32 devices in a mesh: batch: 4 (over y, core), chan: 8 (over z, x).
Axes of the slice: x: 2, y: 2, z: 4, core: 2. Of those that a mesh axis runs over, the one named last changes fastest.
Arguments:
- token_ids: int32 [8, 4096], P('batch', 'chan'), may hold values from 7 to 11, as said below
- embedding: float32 [16, 256], P(None, 'chan'), may hold values from -6 to 6
- inward: float32 [2, 3, 256, 256], P(None, None, 'chan'), may hold values from -0.375 to 0.375
- vectors: float32 [2, 9, 256], P(None, None, 'chan'), may hold values from -0.6 to 1.6
- outward: float32 [2, 256, 256], P(None, 'chan'), may hold values from -0.375 to 0.375
- expand: float32 [2, 1024, 256], P(None, 'chan'), may hold values from -0.375 to 0.375
- offsets: float32 [2, 1024], P(None, 'chan'), may hold values from -0.625 to 0.625
- contract: float32 [2, 256, 1024], P(None, 'chan'), may hold values from -0.1875 to 0.1875
- channels: float32 [2, 77, 256], P(None, None, 'chan'), may hold values from -6 to 6
- filters: float32 [2, 136, 64], replicated, may hold values from -6 to 6
- momentum_embedding: float32 [16, 256], P(None, 'chan'), may hold values from -1536 to 1536
- momentum_inward: float32 [2, 3, 256, 256], P(None, None, 'chan'), may hold values from -1024 to 1024
- momentum_vectors: float32 [2, 9, 256], P(None, None, 'chan'), may hold values from -2048 to 2048
- momentum_outward: float32 [2, 256, 256], P(None, 'chan'), may hold values from -1792 to 1792
- momentum_expand: float32 [2, 1024, 256], P(None, 'chan'), may hold values from -640 to 640
- momentum_offsets: float32 [2, 1024], P(None, 'chan'), may hold values from -640 to 640
- momentum_contract: float32 [2, 256, 1024], P(None, 'chan'), may hold values from -1280 to 1280
- momentum_channels: float32 [2, 77, 256], P(None, None, 'chan'), may hold values from -2048 to 2048
- momentum_filters: float32 [2, 136, 64], replicated, may hold values from -4344464 to 4344464
- average_embedding: float32 [16, 256], P(None, 'chan'), may hold values from -6 to 6
- average_inward: float32 [2, 3, 256, 256], P(None, None, 'chan'), may hold values from -0.375 to 0.375
- average_vectors: float32 [2, 9, 256], P(None, None, 'chan'), may hold values from -0.6 to 1.6
- average_outward: float32 [2, 256, 256], P(None, 'chan'), may hold values from -0.375 to 0.375
- average_expand: float32 [2, 1024, 256], P(None, 'chan'), may hold values from -0.375 to 0.375
- average_offsets: float32 [2, 1024], P(None, 'chan'), may hold values from -0.625 to 0.625
- average_contract: float32 [2, 256, 1024], P(None, 'chan'), may hold values from -0.1875 to 0.1875
- average_channels: float32 [2, 77, 256], P(None, None, 'chan'), may hold values from -6 to 6
- average_filters: float32 [2, 136, 64], replicated, may hold values from -6 to 6
- cotangent: float32 [8, 256, 4096], P('batch', None, 'chan'), may hold values from -6 to 6
Outputs:
- activations: float32 [8, 256, 4096], P('batch', None, 'chan')
- input_gradient: float32 [8, 256, 4096], P('batch', None, 'chan')
- velocity_embedding: float32 [16, 256], P(None, 'chan')
- running_embedding: float32 [16, 256], P(None, 'chan')
- updated_embedding: float32 [16, 256], P(None, 'chan')
- compact_embedding: bfloat16 [16, 256], P(None, 'chan')
- velocity_inward: float32 [2, 3, 256, 256], P(None, None, 'chan')
- running_inward: float32 [2, 3, 256, 256], P(None, None, 'chan')
- updated_inward: float32 [2, 3, 256, 256], P(None, None, 'chan')
- compact_inward: bfloat16 [2, 3, 256, 256], P(None, None, 'chan')
- velocity_vectors: float32 [2, 9, 256], P(None, None, 'chan')
- running_vectors: float32 [2, 9, 256], P(None, None, 'chan')
- updated_vectors: float32 [2, 9, 256], P(None, None, 'chan')
- compact_vectors: bfloat16 [2, 9, 256], P(None, None, 'chan')
- velocity_outward: float32 [2, 256, 256], P(None, 'chan')
- running_outward: float32 [2, 256, 256], P(None, 'chan')
- updated_outward: float32 [2, 256, 256], P(None, 'chan')
- compact_outward: bfloat16 [2, 256, 256], P(None, 'chan')
- velocity_expand: float32 [2, 1024, 256], P(None, 'chan')
- running_expand: float32 [2, 1024, 256], P(None, 'chan')
- updated_expand: float32 [2, 1024, 256], P(None, 'chan')
- compact_expand: bfloat16 [2, 1024, 256], P(None, 'chan')
- velocity_offsets: float32 [2, 1024], P(None, 'chan')
- running_offsets: float32 [2, 1024], P(None, 'chan')
- updated_offsets: float32 [2, 1024], P(None, 'chan')
- compact_offsets: bfloat16 [2, 1024], P(None, 'chan')
- velocity_contract: float32 [2, 256, 1024], P(None, 'chan')
- running_contract: float32 [2, 256, 1024], P(None, 'chan')
- updated_contract: float32 [2, 256, 1024], P(None, 'chan')
- compact_contract: bfloat16 [2, 256, 1024], P(None, 'chan')
- velocity_channels: float32 [2, 77, 256], P(None, None, 'chan')
- running_channels: float32 [2, 77, 256], P(None, None, 'chan')
- updated_channels: float32 [2, 77, 256], P(None, None, 'chan')
- compact_channels: bfloat16 [2, 77, 256], P(None, None, 'chan')
- velocity_filters: float32 [2, 136, 64], replicated
- running_filters: float32 [2, 136, 64], replicated
- updated_filters: float32 [2, 136, 64], replicated
- compact_filters: bfloat16 [2, 136, 64], replicated
The draws below stay inside these ranges and needn't reach their ends.
Inputs may be any that keep to these rules, and one draw needn't show every extreme that they name: `token_ids`: row 2 i + 1 is the reverse complement of row 2 i: read backwards with 7 and 10 swapped and 8 and 9 swapped, 11 staying 11.
All inputs are finite; a program needn't handle non-finite values.
Results may differ from the reference program's by a relative error of at most 0.003.
Values sent between devices are 32-bit elements; how exact they have to be, the bound alone decides.
A program may use at most 384 MiB of HBM per device.

```python
import math
import jax
import jax.numpy as jnp
from jax import lax

D = 256
FF = 1024
FO = 64
EMB = 5
VOCAB = 16
LAYERS = 2
LEN = 4096
SEQS = 8
FROWS = 136
CROWS = 77


def vector_values(key):
    rows = jnp.arange(9)
    noise = jnp.clip(jax.random.normal(key, (LAYERS, 9, D), jnp.float32), -6.0, 6.0)
    base = jnp.where((rows == 0) | (rows == 2), 1.0, 0.0)
    return base[None, :, None] + 0.1 * noise


def channel_values(key):
    rows = jnp.arange(CROWS)
    scales = jnp.where(rows < 9, 0.58, jnp.where(rows < 12, 0.1, jnp.where(rows == 12, 1.0, 4.0 / math.sqrt(FO * LEN))))
    noise = jnp.clip(jax.random.normal(key, (LAYERS, CROWS, D), jnp.float32), -6.0, 6.0)
    return noise * scales[None, :, None]


def filter_values(key):
    rows = jnp.arange(FROWS)
    small = (rows == EMB + 1 + FO) | (rows == EMB + 2 + 2 * FO)
    scales = jnp.where(rows <= EMB, 1.0, jnp.where(small, 0.5, 1.5 / math.sqrt(FO)))
    noise = jnp.clip(jax.random.normal(key, (LAYERS, FROWS, FO), jnp.float32), -6.0, 6.0)
    return noise * scales[None, :, None]


def draw_token_ids(key, part):
    key = jax.random.fold_in(key, 5)
    key_base, key_unknown, key_place = jax.random.split(key, 3)
    pairs = SEQS // 2
    bases = jax.random.randint(key_base, (pairs, LEN), 7, 11)
    unknown = jax.random.randint(key_unknown, (pairs, LEN), 0, 32) == 0
    place = jax.random.randint(key_place, (pairs,), 0, LEN)
    indices = jnp.arange(LEN)[None, :]
    forced_unknown = indices == place[:, None]
    forced_first = indices == ((place + 1) % LEN)[:, None]
    items = jnp.where(forced_unknown, 11, jnp.where(forced_first, 7, jnp.where(unknown, 11, bases)))
    complement = jnp.where(items == 11, 11, 17 - items)
    reverse = complement[:, ::-1]
    return jnp.stack([items, reverse], axis=1).reshape(SEQS, LEN).astype(jnp.int32)


def draw_vectors(key, part):
    key = jax.random.fold_in(key, 11)
    return vector_values(key)


def draw_average_vectors(key, part):
    key = jax.random.fold_in(key, 12)
    return vector_values(key)


def draw_channels(key, part):
    key = jax.random.fold_in(key, 13)
    return channel_values(key)


def draw_average_channels(key, part):
    key = jax.random.fold_in(key, 14)
    return channel_values(key)


def draw_filters(key, part):
    key = jax.random.fold_in(key, 15)
    return filter_values(key)


def draw_average_filters(key, part):
    key = jax.random.fold_in(key, 16)
    return filter_values(key)


def draw_momentum_filters(key, part):
    key = jax.random.fold_in(key, 17)
    rows = jnp.arange(FROWS)
    factors = jnp.where(rows <= EMB, 100.0, jnp.where(rows <= EMB + 1 + FO, 10.0, 1.0))
    noise = jnp.clip(jax.random.normal(key, (LAYERS, FROWS, FO), jnp.float32), -6.0, 6.0)
    return noise * factors[None, :, None] * (40.0 * math.sqrt(SEQS * LEN))


def block_levels(rng, extent, pieces, smallest, high):
    def one(dim, parts):
        draws = jax.random.uniform(jax.random.fold_in(jax.random.fold_in(rng, 6), dim), (parts,), jnp.float32, smallest / len(pieces), high / len(pieces))
        return jnp.repeat(jnp.exp(draws), extent[dim] // parts).reshape((-1,) + (1,) * (len(extent) - dim - 1))

    factor_of = one(*pieces[0])
    for cut in pieces[1:]:
        factor_of = factor_of * one(*cut)
    return factor_of


def gaussian(own_key, dims, deviation, limit, cuts=(), kind=jnp.bfloat16):
    result = deviation * jax.random.normal(own_key, dims, jnp.float32)
    if cuts:
        result = result * block_levels(own_key, dims, cuts, -0.22, 0.18)
    return jnp.clip(result, -limit, limit).astype(kind)


def setup_inputs(seed: int = 0) -> dict:
    seeds = jax.random.split(jax.random.key(seed), 30)
    token_ids = draw_token_ids(jax.random.fold_in(seeds[29], 71), 0)
    embedding = gaussian(seeds[1], (VOCAB, D), 1.0, 6.0, ((1, 8),), jnp.float32)
    inward = gaussian(seeds[2], (LAYERS, 3, D, D), D ** -0.5, 0.375, ((2, 8),), jnp.float32)
    vectors = draw_vectors(jax.random.fold_in(seeds[29], 71), 0)
    outward = gaussian(seeds[4], (LAYERS, D, D), D ** -0.5, 0.375, ((1, 8),), jnp.float32)
    expand = gaussian(seeds[5], (LAYERS, FF, D), D ** -0.5, 0.375, ((1, 8),), jnp.float32)
    offsets = gaussian(seeds[6], (LAYERS, FF), 0.1, 0.625, ((1, 8),), jnp.float32)
    contract = gaussian(seeds[7], (LAYERS, D, FF), FF ** -0.5, 0.1875, ((1, 8),), jnp.float32)
    channels = draw_channels(jax.random.fold_in(seeds[29], 71), 0)
    filters = draw_filters(jax.random.fold_in(seeds[29], 71), 0)
    momentum_embedding = gaussian(seeds[10], (VOCAB, D), (1.4 * (SEQS * LEN) ** 0.5), 1536.0, ((1, 8),), jnp.float32)
    momentum_inward = gaussian(seeds[11], (LAYERS, 3, D, D), (1.0 * (SEQS * LEN) ** 0.5), 1024.0, ((2, 8),), jnp.float32)
    momentum_vectors = gaussian(seeds[12], (LAYERS, 9, D), (2.0 * (SEQS * LEN) ** 0.5), 2048.0, ((2, 8),), jnp.float32)
    momentum_outward = gaussian(seeds[13], (LAYERS, D, D), (1.6 * (SEQS * LEN) ** 0.5), 1792.0, ((1, 8),), jnp.float32)
    momentum_expand = gaussian(seeds[14], (LAYERS, FF, D), (0.6 * (SEQS * LEN) ** 0.5), 640.0, ((1, 8),), jnp.float32)
    momentum_offsets = gaussian(seeds[15], (LAYERS, FF), (0.6 * (SEQS * LEN) ** 0.5), 640.0, ((1, 8),), jnp.float32)
    momentum_contract = gaussian(seeds[16], (LAYERS, D, FF), (1.2 * (SEQS * LEN) ** 0.5), 1280.0, ((1, 8),), jnp.float32)
    momentum_channels = gaussian(seeds[17], (LAYERS, CROWS, D), (2.0 * (SEQS * LEN) ** 0.5), 2048.0, ((2, 8),), jnp.float32)
    momentum_filters = draw_momentum_filters(jax.random.fold_in(seeds[29], 71), 0)
    average_embedding = gaussian(seeds[19], (VOCAB, D), 1.0, 6.0, ((1, 8),), jnp.float32)
    average_inward = gaussian(seeds[20], (LAYERS, 3, D, D), D ** -0.5, 0.375, ((2, 8),), jnp.float32)
    average_vectors = draw_average_vectors(jax.random.fold_in(seeds[29], 71), 0)
    average_outward = gaussian(seeds[22], (LAYERS, D, D), D ** -0.5, 0.375, ((1, 8),), jnp.float32)
    average_expand = gaussian(seeds[23], (LAYERS, FF, D), D ** -0.5, 0.375, ((1, 8),), jnp.float32)
    average_offsets = gaussian(seeds[24], (LAYERS, FF), 0.1, 0.625, ((1, 8),), jnp.float32)
    average_contract = gaussian(seeds[25], (LAYERS, D, FF), FF ** -0.5, 0.1875, ((1, 8),), jnp.float32)
    average_channels = draw_average_channels(jax.random.fold_in(seeds[29], 71), 0)
    average_filters = draw_average_filters(jax.random.fold_in(seeds[29], 71), 0)
    cotangent = gaussian(seeds[28], (SEQS, D, LEN), 1.0, 6.0, ((0, 4), (2, 8)), jnp.float32)
    return dict(token_ids=token_ids, embedding=embedding, inward=inward, vectors=vectors, outward=outward, expand=expand, offsets=offsets, contract=contract, channels=channels, filters=filters, momentum_embedding=momentum_embedding, momentum_inward=momentum_inward, momentum_vectors=momentum_vectors, momentum_outward=momentum_outward, momentum_expand=momentum_expand, momentum_offsets=momentum_offsets, momentum_contract=momentum_contract, momentum_channels=momentum_channels, momentum_filters=momentum_filters, average_embedding=average_embedding, average_inward=average_inward, average_vectors=average_vectors, average_outward=average_outward, average_expand=average_expand, average_offsets=average_offsets, average_contract=average_contract, average_channels=average_channels, average_filters=average_filters, cotangent=cotangent)


HIGHEST = lax.Precision.HIGHEST
EPSILON = 1e-05
MOMENTUM = 0.9
AVERAGING = 0.9
WINDOW_SHIFT = 0.05
FREQUENCY = 10.0
STEP_RATES = (0.7, 0.06, 0.1, 0.037, 0.1, 0.16, 0.025, 0.2, 0.0002)

@jax.custom_vjp
def low(v):
    return lax.optimization_barrier(v.astype(jnp.bfloat16)).astype(jnp.float32)

@jax.custom_vjp
def low_back(v):
    return v

def low_keep(v):
    return (low(v), None)

def low_pass(kept, grad):
    return (grad,)

def back_keep(v):
    return (v, None)

def back_low(kept, grad):
    return (low(grad),)
low.defvjp(low_keep, low_pass)
low_back.defvjp(back_keep, back_low)

def positions(length):
    indices = jnp.arange(length, dtype=jnp.float32)
    fraction = indices / (length - 1)
    angles = 2.0 * math.pi * indices / length
    band_count = (EMB - 1) // 2
    frequency = jnp.linspace(0.0001, band_count - 1, band_count, dtype=jnp.float32)
    turned = angles[:, None] * frequency[None, :]
    return jnp.concatenate([fraction[:, None], jnp.cos(turned), -jnp.sin(turned)], axis=1)

def filter_bank(network, fourth, chan_ids, length):
    features = positions(length)
    hidden = jnp.sin(FREQUENCY * (jnp.dot(features, network[:EMB], precision=HIGHEST) + network[EMB]))
    hidden = jnp.sin(FREQUENCY * (jnp.dot(hidden, network[EMB + 1:EMB + 1 + FO], precision=HIGHEST) + network[EMB + 1 + FO]))
    hidden = jnp.sin(FREQUENCY * (jnp.dot(hidden, network[EMB + 2 + FO:EMB + 2 + 2 * FO], precision=HIGHEST) + network[EMB + 2 + 2 * FO]))
    kernel = jnp.einsum('tf,fc->ct', hidden, fourth, precision=HIGHEST)
    slow_rate = math.log(0.01) / 1.5
    fast_rate = math.log(0.01) / 0.3
    deltas = jnp.abs(slow_rate + (fast_rate - slow_rate) * chan_ids / (D - 1))
    fraction = jnp.arange(length, dtype=jnp.float32) / (length - 1)
    return kernel * (jnp.exp(-deltas[:, None] * fraction[None, :]) + WINDOW_SHIFT)

def layer_norm(values, gains, offsets_row):
    center = values - lax.optimization_barrier(jnp.mean(values, axis=1, keepdims=True))
    spread = lax.optimization_barrier(jnp.mean(center * center, axis=1, keepdims=True))
    return center * lax.rsqrt(spread + EPSILON) * gains[None, :, None] + offsets_row[None, :, None]

def front_part(current, inward_l, vectors_l):
    normed = layer_norm(current, vectors_l[0], vectors_l[1])
    projected = jnp.einsum('sit,joi->sjot', normed, inward_l, precision=HIGHEST)
    return projected + vectors_l[4:7][None, :, :, None]

def rear_part(current, mixer_out, outward_l, vectors_l, expand_l, offsets_l, contract_l):
    mixture = current + jnp.einsum('sit,oi->sot', mixer_out, outward_l, precision=HIGHEST) + vectors_l[7][None, :, None]
    normed = layer_norm(mixture, vectors_l[2], vectors_l[3])
    hidden = jax.nn.gelu(jnp.einsum('sit,fi->sft', normed, expand_l, precision=HIGHEST) + offsets_l[None, :, None], approximate=True)
    return mixture + jnp.einsum('sft,of->sot', hidden, contract_l, precision=HIGHEST) + vectors_l[8][None, :, None]

def long_conv(signal, kernel):
    length = signal.shape[-1]
    spectrum = jnp.fft.rfft(signal, n=2 * length) * jnp.fft.rfft(kernel, n=2 * length)[None]
    return jnp.fft.irfft(spectrum, n=2 * length)[..., :length]

def long_mixer(streams, chan_params, network, chan_ids, length):
    conv_taps = chan_params[:9].reshape(3, 3, chan_params.shape[1])
    shifted_one = jnp.pad(streams, ((0, 0), (0, 0), (0, 0), (1, 0)))[..., :-1]
    shifted_two = jnp.pad(streams, ((0, 0), (0, 0), (0, 0), (2, 0)))[..., :-2]
    short_out = chan_params[9:12][None, :, :, None] + conv_taps[None, :, 0, :, None] * shifted_two + conv_taps[None, :, 1, :, None] * shifted_one + conv_taps[None, :, 2, :, None] * streams
    kernel = filter_bank(network, chan_params[13:], chan_ids, length)
    gated_in = short_out[:, 2] * short_out[:, 1]
    mixture = long_conv(gated_in, kernel) + chan_params[12][None, :, None] * gated_in
    return mixture * short_out[:, 0]

def stack_forward(embedded, inward, vectors, outward, expand, offsets, contract, channels, filters):
    current = embedded
    chan_ids = jnp.arange(D, dtype=jnp.float32)
    for layer_index in range(LAYERS):
        projected = front_part(current, inward[layer_index], vectors[layer_index])
        mixer_out = long_mixer(projected, channels[layer_index], filters[layer_index], chan_ids, LEN)
        current = rear_part(current, mixer_out, outward[layer_index], vectors[layer_index], expand[layer_index], offsets[layer_index], contract[layer_index])
    return current

def reference(token_ids, embedding, inward, vectors, outward, expand, offsets, contract, channels, filters, momentum_embedding, momentum_inward, momentum_vectors, momentum_outward, momentum_expand, momentum_offsets, momentum_contract, momentum_channels, momentum_filters, average_embedding, average_inward, average_vectors, average_outward, average_expand, average_offsets, average_contract, average_channels, average_filters, cotangent):
    embedded, pull_embed = jax.vjp(lambda rows_table: jnp.transpose(rows_table[token_ids], (0, 2, 1)), embedding)
    activations, pullback = jax.vjp(stack_forward, embedded, inward, vectors, outward, expand, offsets, contract, channels, filters)
    gradients = pullback(cotangent)
    input_gradient = gradients[0]
    embed_gradient = pull_embed(input_gradient)[0]
    weights = (embedding, inward, vectors, outward, expand, offsets, contract, channels, filters)
    grad_list = (embed_gradient,) + tuple(gradients[1:])
    moments = (momentum_embedding, momentum_inward, momentum_vectors, momentum_outward, momentum_expand, momentum_offsets, momentum_contract, momentum_channels, momentum_filters)
    averages = (average_embedding, average_inward, average_vectors, average_outward, average_expand, average_offsets, average_contract, average_channels, average_filters)
    step_scale = 1.0 / math.sqrt(SEQS * LEN)
    packed = []
    for weight, gradient, moment, average, factor in zip(weights, grad_list, moments, averages, STEP_RATES):
        velocity = MOMENTUM * moment + gradient
        updated = weight - factor * step_scale * (gradient + MOMENTUM * velocity)
        running = AVERAGING * average + (1.0 - AVERAGING) * updated
        packed.extend([velocity, running, updated, updated.astype(jnp.bfloat16)])
    return (activations, input_gradient, packed[0], packed[1], packed[2], packed[3], packed[4], packed[5], packed[6], packed[7], packed[8], packed[9], packed[10], packed[11], packed[12], packed[13], packed[14], packed[15], packed[16], packed[17], packed[18], packed[19], packed[20], packed[21], packed[22], packed[23], packed[24], packed[25], packed[26], packed[27], packed[28], packed[29], packed[30], packed[31], packed[32], packed[33], packed[34], packed[35])
```

```python
from functools import partial
import math

import jax
import jax.numpy as jnp
import numpy as np
from jax import lax
from jax.experimental import pallas as pl
from jax.experimental.pallas import tpu as pltpu
from jax.sharding import PartitionSpec as P

D = 256
FF = 1024
FO = 64
EMB = 5
VOCAB = 16
LAYERS = 2
LANES = 128
TILE = 256

HIGH = lax.Precision.HIGH
HIGHEST = lax.Precision.HIGHEST
EPSILON = 1e-05
MOMENTUM = 0.9
AVERAGING = 0.9
WINDOW_SHIFT = 0.05
FREQUENCY = 10.0
STEP_RATES = (0.7, 0.06, 0.1, 0.037, 0.1, 0.16, 0.025, 0.2, 0.0002)
GELU_SCALE = math.sqrt(2.0 / math.pi)
GELU_CUBE = 0.044715

MESH = pl.DeviceIdType.MESH
VMEM = pltpu.VMEM
WHOLE = pl.BlockSpec(memory_space=pltpu.VMEM)
HBM = pl.BlockSpec(memory_space=pl.ANY)
VMEM_LIMIT = 58 * 1024 * 1024
F32 = jnp.float32

VEC0 = 0
TAP0 = 18
EMB0 = 42
OFF0 = 58
FILTER_ROWS = 16


def dot(a, b, precision=HIGH):
    return jnp.dot(a, b, precision=precision, preferred_element_type=F32)


def dot_nt(a, b, precision=HIGH):
    return lax.dot_general(
        a, b, (((1,), (1,)), ((), ())), precision=precision, preferred_element_type=F32
    )


def dot_tn(a, b, precision=HIGH):
    return lax.dot_general(
        a, b, (((0,), (0,)), ((), ())), precision=precision, preferred_element_type=F32
    )


def sds(*shape):
    return jax.ShapeDtypeStruct(shape, F32)


def cost(flops, moved):
    return pl.CostEstimate(flops=int(flops), bytes_accessed=int(moved), transcendentals=0)


def position_table(length):
    indices = np.arange(length, dtype=np.float32)
    fraction = indices / np.float32(length - 1)
    angles = np.float32(2.0 * math.pi) * indices / np.float32(length)
    bands = (EMB - 1) // 2
    frequency = np.linspace(0.0001, bands - 1, bands).astype(np.float32)
    turned = (frequency[:, None] * angles[None, :]).astype(np.float32).astype(np.float64)
    table = np.zeros((8, length), np.float32)
    table[0] = fraction
    table[1 : 1 + bands] = np.cos(turned)
    table[1 + bands : 1 + 2 * bands] = -np.sin(turned)
    table[EMB] = 1.0
    return table


def fourier_tables(length):
    rows = length // LANES
    outer = 2 * rows
    total = outer * LANES
    turn = 2.0 * np.pi / outer * (np.arange(outer)[:, None] * np.arange(rows)[None, :] % outer)
    c, s = np.cos(turn), np.sin(turn)
    first = np.block([[c, s], [-s, c]])
    last = np.block([[c.T, -s.T], [s.T, c.T]]) / total
    twist = 2.0 * np.pi / total * (np.arange(outer)[:, None] * np.arange(LANES)[None, :])
    twiddle = np.concatenate([np.cos(twist), -np.sin(twist)], axis=1)
    lane = 2.0 * np.pi / LANES * (np.arange(LANES)[:, None] * np.arange(LANES)[None, :] % LANES)
    c, s = np.cos(lane), np.sin(lane)
    second = np.block([[c, -s], [s, c]])
    second_back = np.block([[c, s], [-s, c]])
    return tuple(t.astype(np.float32) for t in (first, twiddle, second, second_back, last))


def sin_cos(x):
    turns = jnp.round(x * (1.0 / math.pi))
    r = x - turns * 3.140625
    r = r - turns * 9.67025756835937500e-4
    r = r - turns * 6.27711415290832520e-7
    r = r - turns * 1.21542010130123850e-10
    half = turns * 0.5
    sign = 1.0 - 4.0 * jnp.abs(half - jnp.round(half))
    r2 = r * r
    s = -2.5052108385441720e-8
    for k in (2.7557319223985893e-6, -1.9841269841269841e-4, 8.3333333333333333e-3, -1.6666666666666667e-1):
        s = s * r2 + k
    s = r + r * (r2 * s)
    c = 2.0876756987868099e-9
    for k in (-2.7557319223985888e-7, 2.4801587301587302e-5, -1.3888888888888889e-3, 4.1666666666666667e-2, -0.5):
        c = c * r2 + k
    c = 1.0 + r2 * c
    return s * sign, c * sign


def window(delta, length, start, width):
    t = lax.broadcasted_iota(jnp.int32, (1, width), 1) + start
    fraction = t.astype(F32) / (length - 1)
    return jnp.exp(-delta * fraction) + WINDOW_SHIFT


def normalize(x):
    center = x - jnp.mean(x, axis=0, keepdims=True)
    spread = jnp.mean(center * center, axis=0, keepdims=True)
    scale = lax.rsqrt(spread + EPSILON)
    return center * scale, scale


def normalize_back(e, xh, scale):
    return scale * (
        e - jnp.mean(e, axis=0, keepdims=True) - xh * jnp.mean(e * xh, axis=0, keepdims=True)
    )


def gelu_parts(a):
    t = jnp.tanh(GELU_SCALE * (a + GELU_CUBE * a * a * a))
    return 0.5 * (1.0 + t), t


def put_columns(pairs, width=D):
    rows = pairs[0][1].shape[0]
    lane = lax.broadcasted_iota(jnp.int32, (rows, width), 1)
    out = jnp.zeros((rows, width), F32)
    for k, column in pairs:
        out = out + jnp.where(lane == k, column, 0.0)
    return out


def row_sum(x):
    return jnp.sum(x, axis=1, keepdims=True)


def filter_kernel(length, feat, net, fourth, delta, kern, keep):
    step = pl.program_id(0)
    width = feat.shape[1]
    chans = delta.shape[0]
    ones = (lax.broadcasted_iota(jnp.int32, (8, width), 0) == 0).astype(F32)
    h, c = sin_cos(FREQUENCY * dot_tn(net[0:8, :], feat[...] , HIGHEST))
    keep[0] = h
    keep[3] = FREQUENCY * c
    for k, row in ((1, EMB + 1), (2, EMB + 2 + FO)):
        weights = net[row : row + FO + 8, :]
        h, c = sin_cos(FREQUENCY * dot_tn(weights, jnp.concatenate([h, ones], axis=0), HIGHEST))
        keep[k] = h
        keep[3 + k] = FREQUENCY * c
    out = dot_tn(fourth[...], h, HIGHEST) * window(delta[...], length, step * width, width)
    for b in range(width // LANES):
        kern[b * chans : (b + 1) * chans, :] = out[:, b * LANES : (b + 1) * LANES]


def filter_forward(net, fourth, delta, length):
    chans = fourth.shape[1]
    width = 512
    return pl.pallas_call(
        partial(filter_kernel, length),
        grid=(length // width,),
        in_specs=[
            pl.BlockSpec((8, width), lambda i: (0, i)),
            WHOLE, WHOLE, WHOLE,
        ],
        out_specs=[
            pl.BlockSpec((width // LANES * chans, LANES), lambda i: (i, 0)),
            pl.BlockSpec((6, FO, width), lambda i: (0, 0, i)),
        ],
        out_shape=[sds(length // LANES * chans, LANES), sds(6, FO, length)],
        compiler_params=pltpu.CompilerParams(vmem_limit_bytes=VMEM_LIMIT),
        name="filter_forward",
    )(jnp.asarray(position_table(length)), net, fourth, delta)


def filter_back_kernel(length, feat, net, fourth, delta, keep, dk, dnet, dfourth):
    step = pl.program_id(0)
    width = feat.shape[1]
    chans = delta.shape[0]
    ones = (lax.broadcasted_iota(jnp.int32, (8, width), 0) == 0).astype(F32)
    dkw = jnp.concatenate(
        [dk[b * chans : (b + 1) * chans, :] for b in range(width // LANES)], axis=1
    ) * window(delta[...], length, step * width, width)

    @pl.when(step == 0)
    def _():
        dnet[...] = jnp.zeros_like(dnet)
        dfourth[...] = jnp.zeros_like(dfourth)

    dfourth[...] += dot_nt(keep[2], dkw)
    dpre = dot(fourth[...], dkw) * keep[5]
    dnet[80:152, :] += dot_nt(jnp.concatenate([keep[1], ones], axis=0), dpre)
    dpre = dot(net[EMB + 2 + FO : EMB + 2 + 2 * FO, :], dpre) * keep[4]
    dnet[8:80, :] += dot_nt(jnp.concatenate([keep[0], ones], axis=0), dpre)
    dpre = dot(net[EMB + 1 : EMB + 1 + FO, :], dpre) * keep[3]
    dnet[0:8, :] += dot_nt(feat[...], dpre)


def filter_backward(net, fourth, delta, keep, dk, length):
    chans = fourth.shape[1]
    width = 512
    dnet, dfourth = pl.pallas_call(
        partial(filter_back_kernel, length),
        grid=(length // width,),
        in_specs=[
            pl.BlockSpec((8, width), lambda i: (0, i)),
            WHOLE, WHOLE, WHOLE,
            pl.BlockSpec((6, FO, width), lambda i: (0, 0, i)),
            pl.BlockSpec((width // LANES * chans, LANES), lambda i: (i, 0)),
        ],
        out_specs=[
            pl.BlockSpec((152, FO), lambda i: (0, 0)),
            pl.BlockSpec((FO, chans), lambda i: (0, 0)),
        ],
        out_shape=[sds(152, FO), sds(FO, chans)],
        compiler_params=pltpu.CompilerParams(vmem_limit_bytes=VMEM_LIMIT),
        name="filter_backward",
    )(jnp.asarray(position_table(length)), net, fourth, delta, keep, dk)
    whole = jnp.concatenate([dnet[:6], dnet[8:73], dnet[80:145]], axis=0)
    return whole, dfourth


def spectrum_of(x, first, twiddle, second):
    outer = twiddle.shape[0]
    y = dot(first, x)
    tr, ti = twiddle[:, :LANES], twiddle[:, LANES:]
    parts = []
    for b in range(x.shape[1] // LANES):
        yr = y[:outer, b * LANES : (b + 1) * LANES]
        yi = y[outer:, b * LANES : (b + 1) * LANES]
        parts.append(jnp.concatenate([yr * tr - yi * ti, yr * ti + yi * tr], axis=1))
    return dot(jnp.concatenate(parts, axis=0), second)


def signal_of(v, twiddle, second_back, last):
    outer = twiddle.shape[0]
    a = dot(v, second_back)
    tr, ti = twiddle[:, :LANES], twiddle[:, LANES:]
    parts = []
    for b in range(v.shape[0] // outer):
        ar = a[b * outer : (b + 1) * outer, :LANES]
        ai = a[b * outer : (b + 1) * outer, LANES:]
        parts.append(jnp.concatenate([ar * tr + ai * ti, ai * tr - ar * ti], axis=0))
    return dot(last, jnp.concatenate(parts, axis=1))


def load_pairs(ref, start, blocks, chans):
    rows = ref.shape[1] // chans
    parts = []
    for b in range(blocks):
        parts.append(
            jnp.concatenate(
                [ref[s, pl.ds(start + b, rows, stride=chans), :] for s in range(2)], axis=0
            )
        )
    return jnp.concatenate(parts, axis=1)


def store_pairs(ref, start, value, chans):
    rows = ref.shape[1] // chans
    for b in range(value.shape[1] // LANES):
        for s in range(2):
            ref[s, pl.ds(start + b, rows, stride=chans), :] = value[
                s * rows : (s + 1) * rows, b * LANES : (b + 1) * LANES
            ]


def times(a, b):
    ar, ai, br, bi = a[:, :LANES], a[:, LANES:], b[:, :LANES], b[:, LANES:]
    return jnp.concatenate([ar * br - ai * bi, ar * bi + ai * br], axis=1)


def times_conj(a, b):
    ar, ai, br, bi = a[:, :LANES], a[:, LANES:], b[:, :LANES], b[:, LANES:]
    return jnp.concatenate([ar * br + ai * bi, ai * br - ar * bi], axis=1)


GROUP = 4


def kernel_spectrum_kernel(kern, skip, first, twiddle, second, out):
    chans = skip.shape[0]
    rows = kern.shape[0] // chans
    outer = twiddle.shape[0]
    lane = lax.broadcasted_iota(jnp.int32, (outer, 2 * LANES), 1)

    def body(g, _):
        start = g * GROUP
        x = jnp.concatenate(
            [kern[pl.ds(start + b, rows, stride=chans), :] for b in range(GROUP)], axis=1
        )
        u = spectrum_of(x, first[:, :rows], twiddle[...], second[...])
        for b in range(GROUP):
            gain = skip[pl.ds(start + b, 1), :]
            wide = jnp.broadcast_to(gain, (outer, LANES))
            both = jnp.concatenate([wide, jnp.zeros_like(wide)], axis=1)
            out[pl.ds((start + b) * outer, outer), :] = u[b * outer : (b + 1) * outer] + both
        return 0

    lax.fori_loop(0, chans // GROUP, body, 0)


def kernel_spectrum(kern, skip, tables):
    chans = skip.shape[0]
    first, twiddle, second, _, _ = tables
    outer = twiddle.shape[0]
    return pl.pallas_call(
        kernel_spectrum_kernel,
        in_specs=[WHOLE] * 5,
        out_specs=WHOLE,
        out_shape=sds(chans * outer, 2 * LANES),
        compiler_params=pltpu.CompilerParams(vmem_limit_bytes=VMEM_LIMIT),
        name="kernel_spectrum",
    )(kern, skip, first, twiddle, second)


def conv_kernel(chans, g, spec, first, twiddle, second, second_back, last, z, gspec):
    outer = twiddle.shape[0]

    def body(k, _):
        start = k * GROUP
        rows = pl.ds(pl.multiple_of(start * outer, 8), GROUP * outer)
        u = spectrum_of(load_pairs(g, start, GROUP, chans), first[...], twiddle[...], second[...])
        gspec[rows, :] = u
        o = signal_of(times(u, spec[rows, :]), twiddle[...], second_back[...], last[...])
        store_pairs(z, start, o, chans)
        return 0

    lax.fori_loop(0, chans // GROUP, body, 0)


def conv_forward(g, spec, tables, chans):
    return pl.pallas_call(
        partial(conv_kernel, chans),
        in_specs=[WHOLE] * 7,
        out_specs=[WHOLE] * 2,
        out_shape=[sds(*g.shape), sds(*spec.shape)],
        compiler_params=pltpu.CompilerParams(vmem_limit_bytes=VMEM_LIMIT),
        name="conv_forward",
    )(g, spec, *tables)


def conv_back_kernel(chans, dz, spec, gspec, first, twiddle, second, second_back, last, dg, dk):
    outer = twiddle.shape[0]
    length_rows = dz.shape[1] // chans

    def body(k, _):
        start = k * GROUP
        rows = pl.ds(pl.multiple_of(start * outer, 8), GROUP * outer)
        u = spectrum_of(load_pairs(dz, start, GROUP, chans), first[...], twiddle[...], second[...])
        o = signal_of(times_conj(u, spec[rows, :]), twiddle[...], second_back[...], last[...])
        store_pairs(dg, start, o, chans)
        r = signal_of(
            times_conj(u, gspec[rows, :]), twiddle[...], second_back[...], last[:length_rows, :]
        )
        for b in range(GROUP):
            dk[pl.ds(start + b, length_rows, stride=chans), :] = r[:, b * LANES : (b + 1) * LANES]
        return 0

    lax.fori_loop(0, chans // GROUP, body, 0)


def conv_backward(dz, spec, gspec, tables, chans):
    return pl.pallas_call(
        partial(conv_back_kernel, chans),
        in_specs=[WHOLE] * 8,
        out_specs=[WHOLE] * 2,
        out_shape=[sds(*dz.shape), sds(*dz.shape[1:])],
        compiler_params=pltpu.CompilerParams(vmem_limit_bytes=VMEM_LIMIT),
        name="conv_backward",
    )(dz, spec, gspec, *tables)


def greet(axis, size):
    me = lax.axis_index(axis)
    barrier = pltpu.get_barrier_semaphore()
    for d in range(1, size):
        pl.semaphore_signal(
            barrier, inc=1, device_id={axis: lax.rem(me + d, size)}, device_id_type=MESH
        )
    pl.semaphore_wait(barrier, size - 1)


def token_a2a_kernel(n, chans, back, src, dst, send, recv, local):
    me = lax.axis_index("chan")
    greet("chan", n)
    move(n, chans, back, src, dst, send, recv, local)


def views(chans, back, src, dst, me, j):
    if back:
        blocks = dst.shape[1]
        a = src.at[:, pl.ds(j * blocks, blocks), :, :]
        b = dst.at[:, :, pl.ds(pl.multiple_of(me * chans, 8), chans), :]
    else:
        blocks = src.shape[1]
        a = src.at[:, :, pl.ds(pl.multiple_of(j * chans, 8), chans), :]
        b = dst.at[:, pl.ds(me * blocks, blocks), :, :]
    return a, b


def move(n, chans, back, src, dst, send, recv, local):
    me = lax.axis_index("chan")
    a, b = views(chans, back, src, dst, me, me)
    own = pltpu.make_async_copy(a, b, local)
    own.start()
    copies = []
    for d in range(1, n):
        j = lax.rem(me + d, n)
        a, b = views(chans, back, src, dst, me, j)
        copy = pltpu.make_async_remote_copy(
            src_ref=a, dst_ref=b, send_sem=send.at[d], recv_sem=recv.at[d],
            device_id={"chan": j}, device_id_type=MESH,
        )
        copy.start()
        copies.append(copy)
    for copy in copies:
        copy.wait()
    own.wait()


def a2a_scratch(n):
    return [
        pltpu.SemaphoreType.DMA((n,)),
        pltpu.SemaphoreType.DMA((n,)),
        pltpu.SemaphoreType.DMA,
    ]


def comm_params(cid):
    return pltpu.CompilerParams(
        collective_id=cid, has_side_effects=True, vmem_limit_bytes=VMEM_LIMIT
    )


def token_a2a(x, n, chans, back, cid):
    seqs = x.shape[0]
    if back:
        out = sds(seqs, x.shape[1] // n, chans * n, LANES)
    else:
        out = sds(seqs, x.shape[1] * n, chans, LANES)
    return pl.pallas_call(
        partial(token_a2a_kernel, n, chans, back),
        in_specs=[HBM],
        out_specs=HBM,
        out_shape=out,
        scratch_shapes=a2a_scratch(n),
        compiler_params=comm_params(cid),
        name="to_positions" if back else "to_owners",
    )(x)


def mixer_in_kernel(n, chans, lane0, p, misc, q, g, halo, gpos, tails, send, recv, local, hsend, hrecv):
    me = lax.axis_index("chan")
    seqs, width = p.shape[1], p.shape[3]
    greet("chan", n)
    lane = lax.broadcasted_iota(jnp.int32, (D, LANES), 1)
    pack = jnp.zeros((D, LANES), F32)
    for j in range(3):
        for s in range(seqs):
            slot = 2 * (j * seqs + s)
            tail = pltpu.roll(p[j, s, :, width - LANES :], slot + 2, 1)
            pack = jnp.where((lane == slot) | (lane == slot + 1), tail, pack)
    tails[...] = pack
    copy = pltpu.make_async_remote_copy(
        src_ref=tails, dst_ref=halo, send_sem=hsend, recv_sem=hrecv,
        device_id={"chan": lax.rem(me + 1, n)}, device_id_type=MESH,
    )
    copy.start()
    copy.wait()
    inner = (me > 0).astype(F32)

    def body(i, _):
        rows = pl.ds(pl.multiple_of(i * 32, 32), 32)
        side = misc[rows, :]
        edge = halo[rows, :] * inner
        for s in range(seqs):
            made = []
            for j in range(3):
                here = p[j, s, rows, :]
                before = pltpu.roll(edge, LANES - 2 - 2 * (j * seqs + s), 1)
                long = jnp.concatenate([before, here], axis=1)
                one = pltpu.roll(long, 1, 1)[:, LANES:]
                two = pltpu.roll(long, 2, 1)[:, LANES:]
                k = lane0 + 3 * j
                made.append(
                    side[:, lane0 + 9 + j : lane0 + 10 + j]
                    + side[:, k : k + 1] * two
                    + side[:, k + 1 : k + 2] * one
                    + side[:, k + 2 : k + 3] * here
                )
                q[j, s, rows, :] = made[j]
            gate = made[2] * made[1]
            for b in range(width // LANES):
                gpos[s, b, rows, :] = gate[:, b * LANES : (b + 1) * LANES]
        return 0

    lax.fori_loop(0, D // 32, body, 0)
    move(n, chans, False, gpos, g, send, recv, local)


def mixer_in(p, misc, n, chans, lane0, cid):
    seqs, width = p.shape[1], p.shape[3]
    blocks = width // LANES
    return pl.pallas_call(
        partial(mixer_in_kernel, n, chans, lane0),
        in_specs=[WHOLE, WHOLE],
        out_specs=[WHOLE, WHOLE],
        out_shape=[sds(*p.shape), sds(seqs, n * blocks, chans, LANES)],
        scratch_shapes=[
            VMEM((D, LANES), F32),
            VMEM((seqs, blocks, D, LANES), F32),
            VMEM((D, LANES), F32),
        ]
        + a2a_scratch(n)
        + [pltpu.SemaphoreType.DMA, pltpu.SemaphoreType.DMA],
        compiler_params=comm_params(cid),
        name="mixer_in",
    )(p, misc)


def mixer_back_kernel(
    n, chans, lane0, dgch, q, dq0, p, misc, dp, dcols, dgpos, halo, heads, send, recv, local, hsend, hrecv
):
    me = lax.axis_index("chan")
    seqs, width = p.shape[1], p.shape[3]
    greet("chan", n)
    move(n, chans, True, dgch, dgpos, send, recv, local)
    lane = lax.broadcasted_iota(jnp.int32, (D, LANES), 1)
    pack = jnp.zeros((D, LANES), F32)
    for s in range(seqs):
        dg = dgpos[s, 0]
        parts = (
            dq0[s, :, :LANES],
            dg * q[2, s, :, :LANES],
            dg * q[1, s, :, :LANES],
        )
        for j in range(3):
            slot = 2 * (j * seqs + s)
            head = pltpu.roll(parts[j], slot, 1) if slot else parts[j]
            pack = jnp.where((lane == slot) | (lane == slot + 1), head, pack)
    heads[...] = pack
    copy = pltpu.make_async_remote_copy(
        src_ref=heads, dst_ref=halo, send_sem=hsend, recv_sem=hrecv,
        device_id={"chan": lax.rem(me + n - 1, n)}, device_id_type=MESH,
    )
    copy.start()
    copy.wait()
    inner = (me < n - 1).astype(F32)

    def body(i, _):
        rows = pl.ds(pl.multiple_of(i * 32, 32), 32)
        side = misc[rows, :]
        edge = halo[rows, :] * inner
        sums = [jnp.zeros((32, 1), F32)] * 12
        for s in range(seqs):
            dg = jnp.concatenate([dgpos[s, b, rows, :] for b in range(width // LANES)], axis=1)
            parts = (dq0[s, rows, :], dg * q[2, s, rows, :], dg * q[1, s, rows, :])
            for j in range(3):
                here = parts[j]
                slot = 2 * (j * seqs + s)
                after = pltpu.roll(edge, LANES - slot, 1) if slot else edge
                long = jnp.concatenate([here, after], axis=1)
                full = width + LANES
                one = pltpu.roll(long, full - 1, 1)[:, :width]
                two = pltpu.roll(long, full - 2, 1)[:, :width]
                k = lane0 + 3 * j
                dp[j, s, rows, :] = (
                    side[:, k : k + 1] * two
                    + side[:, k + 1 : k + 2] * one
                    + side[:, k + 2 : k + 3] * here
                )
                source = p[j, s, rows, :]
                sums[3 * j] = sums[3 * j] + row_sum(two * source)
                sums[3 * j + 1] = sums[3 * j + 1] + row_sum(one * source)
                sums[3 * j + 2] = sums[3 * j + 2] + row_sum(here * source)
                sums[9 + j] = sums[9 + j] + row_sum(here)
        dcols[rows, :] = put_columns([(lane0 + k, sums[k]) for k in range(12)])
        return 0

    lax.fori_loop(0, D // 32, body, 0)


def mixer_back(dgch, q, dq0, p, misc, n, chans, lane0, cid):
    seqs, width = p.shape[1], p.shape[3]
    blocks = width // LANES
    return pl.pallas_call(
        partial(mixer_back_kernel, n, chans, lane0),
        in_specs=[WHOLE] * 5,
        out_specs=[WHOLE, WHOLE],
        out_shape=[sds(*p.shape), sds(D, D)],
        scratch_shapes=[
            VMEM((seqs, blocks, D, LANES), F32),
            VMEM((D, LANES), F32),
            VMEM((D, LANES), F32),
        ]
        + a2a_scratch(n)
        + [pltpu.SemaphoreType.DMA, pltpu.SemaphoreType.DMA],
        compiler_params=comm_params(cid),
        name="mixer_back",
    )(dgch, q, dq0, p, misc)


def exchange(refs, peers, send, recv, base):
    copies = []
    for k, ((a, b), peer) in enumerate(zip(refs, peers)):
        copy = pltpu.make_async_remote_copy(
            src_ref=a, dst_ref=b, send_sem=send.at[base + k], recv_sem=recv.at[base + k],
            device_id=peer, device_id_type=MESH,
        )
        copy.start()
        copies.append(copy)
    return copies


def gather_kernel(n, m, own, out, send, recv, local):
    me, b = lax.axis_index("chan"), lax.axis_index("batch")
    barrier = pltpu.get_barrier_semaphore()
    for d in range(1, n):
        pl.semaphore_signal(
            barrier, inc=1, device_id={"chan": lax.rem(me + d, n)}, device_id_type=MESH
        )
    for d in range(1, m):
        pl.semaphore_signal(
            barrier, inc=1, device_id={"batch": lax.rem(b + d, m)}, device_id_type=MESH
        )
    quarter = own.shape[0] // m
    part = pl.ds(pl.multiple_of(b * quarter, 8), quarter)
    keep = pltpu.make_async_copy(own.at[part], out.at[me, part], local)
    keep.start()
    pl.semaphore_wait(barrier, n - 1 + m - 1)
    half = n // 2
    x, z = lax.rem(me, 2), me // 2
    sends = []
    for d in range(1, half):
        j = 2 * lax.rem(z + d, half) + x
        sends += exchange([(own.at[part], out.at[me, part])], [{"chan": j}], send, recv, d)
    pair = 1 - x
    sends += exchange(
        [(own.at[part], out.at[me, part])], [{"chan": 2 * z + pair}], send, recv, half
    )
    for d in range(1, half):
        j = 2 * lax.rem(z + half - d, half) + x
        sends[d - 1].wait_recv()
        sends += exchange(
            [(out.at[j, part], out.at[j, part])], [{"chan": 2 * z + pair}], send, recv, half + d
        )
    for copy in sends[half - 1 :]:
        copy.wait_recv()
    base = 2 * half
    keep.wait()
    last = []
    for d in range(1, m):
        peer = lax.rem(b + d, m)
        last += exchange([(out.at[:, part], out.at[:, part])], [{"batch": peer}], send, recv, base + d)
    for copy in sends:
        copy.wait_send()
    for copy in last:
        copy.wait()


def gather_weights(own, n, m, cid):
    count = n + m + 2
    return pl.pallas_call(
        partial(gather_kernel, n, m),
        in_specs=[HBM],
        out_specs=HBM,
        out_shape=sds(n, *own.shape),
        scratch_shapes=[
            pltpu.SemaphoreType.DMA((count,)),
            pltpu.SemaphoreType.DMA((count,)),
            pltpu.SemaphoreType.DMA,
        ],
        compiler_params=comm_params(cid),
        name="gather_weights",
    )(own)


def reduce_kernel(
    n, m, g, chan, out, filt, chan_out, r0, sum0, r1, sum1, r2, sum2, r3, rchan, send, recv
):
    me, b = lax.axis_index("chan"), lax.axis_index("batch")
    barrier = pltpu.get_barrier_semaphore()
    for d in range(1, n):
        pl.semaphore_signal(
            barrier, inc=1, device_id={"chan": lax.rem(me + d, n)}, device_id_type=MESH
        )
    for d in range(1, m):
        pl.semaphore_signal(
            barrier, inc=1, device_id={"batch": lax.rem(b + d, m)}, device_id_type=MESH
        )
    pl.semaphore_wait(barrier, n - 1 + m - 1)
    quarter = g.shape[1] // m
    half = n // 2
    x, z = lax.rem(me, 2), me // 2
    core, y = lax.rem(b, 2), b // 2

    def part(k):
        return pl.ds(pl.multiple_of(k * quarter, 8), quarter)

    mate = {"batch": 2 * y + 1 - core}
    copies = exchange(
        [(g.at[:, part(2 * k + 1 - core)], r0.at[k]) for k in range(2)], [mate] * 2, send, recv, 0
    )
    small = exchange(
        [(chan, rchan.at[d - 1]) for d in range(1, m)],
        [{"batch": lax.rem(b + d, m)} for d in range(1, m)],
        send, recv, 2,
    )
    for k in range(2):
        copies[k].wait()

        def add0(i, _, k=k):
            sum0[k, i] = g[i, part(2 * k + core), :] + r0[k, i]
            return 0

        lax.fori_loop(0, n, add0, 0)
    copies = exchange([(sum0.at[1 - y], r1)], [{"batch": 2 * (1 - y) + core}], send, recv, 5)
    for copy in small:
        copy.wait()
    chan_out[...] = chan[...] + rchan[0] + rchan[1] + rchan[2]
    copies[0].wait()

    def add1(i, _):
        sum1[lax.rem(i, 2), i // 2] = sum0[y, i] + r1[i]
        return 0

    lax.fori_loop(0, n, add1, 0)
    copies = exchange([(sum1.at[1 - x], r2)], [{"chan": 2 * z + 1 - x}], send, recv, 6)
    copies[0].wait()

    def add2(i, _):
        sum2[i] = sum1[x, i] + r2[i]
        return 0

    lax.fori_loop(0, half, add2, 0)
    copies = []
    for d in range(1, half):
        to = lax.rem(z + d, half)
        copies += exchange(
            [(sum2.at[to], r3.at[d - 1])], [{"chan": 2 * to + x}], send, recv, 6 + d
        )
    for copy in copies:
        copy.wait()
    total = sum2[z]
    for d in range(1, half):
        total = total + r3[d - 1]
    mine = part(b)
    out[mine, :] = total
    copies = exchange(
        [(out.at[mine], out.at[mine]) for d in range(1, m)],
        [{"batch": lax.rem(b + d, m)} for d in range(1, m)],
        send, recv, 6 + half,
    )
    for copy in copies:
        copy.wait()
    last = pl.ds(out.shape[0] - FILTER_ROWS, FILTER_ROWS)
    filt[me] = out[last, :]
    copies = exchange(
        [(filt.at[me], filt.at[me]) for d in range(1, n)],
        [{"chan": lax.rem(me + d, n)} for d in range(1, n)],
        send, recv, 6 + half + m,
    )
    for copy in copies:
        copy.wait()


def reduce_gradients(g, chan, n, m, cid):
    quarter = g.shape[1] // m
    half = n // 2
    count = 6 + half + m + n
    return pl.pallas_call(
        partial(reduce_kernel, n, m),
        in_specs=[WHOLE, WHOLE],
        out_specs=[WHOLE] * 3,
        out_shape=[sds(*g.shape[1:]), sds(n, FILTER_ROWS, D), sds(*chan.shape)],
        scratch_shapes=[
            VMEM((2, n, quarter, D), F32),
            VMEM((2, n, quarter, D), F32),
            VMEM((n, quarter, D), F32),
            VMEM((2, half, quarter, D), F32),
            VMEM((half, quarter, D), F32),
            VMEM((half, quarter, D), F32),
            VMEM((half - 1, quarter, D), F32),
            VMEM((m - 1, *chan.shape), F32),
            pltpu.SemaphoreType.DMA((count,)),
            pltpu.SemaphoreType.DMA((count,)),
        ],
        compiler_params=comm_params(cid),
        name="reduce_gradients",
    )(g, chan)


def onehot_rows(tokens):
    row = lax.broadcasted_iota(jnp.int32, (D, tokens.shape[1]), 0)
    return (row == tokens + EMB0).astype(F32)


class Layer:
    def __init__(self, w, misc, index):
        self.n, rows, _ = w.shape
        self.c = rows // 12
        self.w = w
        self.side = misc[...].reshape(D, D)
        self.index = index

    def rows(self, start, count):
        return self.w[:, start * self.c : (start + count) * self.c, :].reshape(
            self.n * count * self.c, D
        )

    def column(self, lane):
        return self.side[:, lane : lane + 1]

    def vec(self, k):
        return self.column(VEC0 + 9 * self.index + k)

    def off(self, k):
        return self.column(OFF0 + 4 * self.index + k)

    def inward(self):
        return self.rows(0, 3)

    def outward(self):
        return self.rows(3, 1)

    def expand(self, k):
        return self.rows(4 + k, 1)

    def contract(self, k):
        return self.rows(8 + k, 1)


def front_forward(lay, x):
    xh, _ = normalize(x)
    normed = xh * lay.vec(0) + lay.vec(1)
    p = dot(lay.inward(), normed).reshape(lay.n, 3, lay.c, x.shape[1])
    return [p[:, j].reshape(D, x.shape[1]) + lay.vec(4 + j) for j in range(3)]


def front_backward(lay, x, dp, dh, dw):
    xh, scale = normalize(x)
    normed = xh * lay.vec(0) + lay.vec(1)
    width = x.shape[1]
    stacked = jnp.stack([d.reshape(lay.n, lay.c, width) for d in dp], axis=1)
    stacked = stacked.reshape(3 * D, width)
    dn = dot_tn(lay.inward(), stacked)
    dw[...] += dot_nt(stacked, normed).reshape(dw.shape)
    base = VEC0 + 9 * lay.index
    columns = [(base + 4 + j, row_sum(dp[j])) for j in range(3)]
    columns += [(base, row_sum(dn * xh)), (base + 1, row_sum(dn))]
    return dh + normalize_back(dn * lay.vec(0), xh, scale), columns


def rear_mix(lay, x, y):
    return x + dot(lay.outward(), y) + lay.vec(7)


def rear_hidden(lay, h):
    xh, scale = normalize(h)
    m = xh * lay.vec(2) + lay.vec(3)
    a = [dot(lay.expand(k), m) + lay.off(k) for k in range(4)]
    return xh, scale, m, a


def rear_out(lay, h, u):
    out = h + lay.vec(8)
    for k in range(4):
        out = out + dot(lay.contract(k), u[k])
    return out


def rear_backward(lay, h, a, y, dout, dw):
    n, c = lay.n, lay.c
    xh, scale = normalize(h)
    m = xh * lay.vec(2) + lay.vec(3)
    base = VEC0 + 9 * lay.index
    columns = [(base + 8, row_sum(dout))]
    dm = None
    for k in range(4):
        ak = a[k]
        g, t = gelu_parts(ak)
        u = ak * g
        dw[:, (5 + k) * c : (6 + k) * c, :] += dot_nt(dout, u).reshape(n, c, D)
        slope = g + 0.5 * ak * (1.0 - t * t) * (GELU_SCALE * (1.0 + 3.0 * GELU_CUBE * ak * ak))
        dpre = dot_tn(lay.contract(k), dout) * slope
        dw[:, (1 + k) * c : (2 + k) * c, :] += dot_nt(dpre, m).reshape(n, c, D)
        columns.append((OFF0 + 4 * lay.index + k, row_sum(dpre)))
        term = dot_tn(lay.expand(k), dpre)
        dm = term if dm is None else dm + term
    dh = dout + normalize_back(dm * lay.vec(2), xh, scale)
    columns += [(base + 2, row_sum(dm * xh)), (base + 3, row_sum(dm)), (base + 7, row_sum(dh))]
    dw[:, 0:c, :] += dot_nt(dh, y).reshape(n, c, D)
    return dh, dot_tn(lay.outward(), dh), columns


def joined(ref):
    return jnp.concatenate([ref[0, b] for b in range(ref.shape[1])], axis=1)


def split(ref, value):
    for b in range(ref.shape[1]):
        ref[0, b] = value[:, b * LANES : (b + 1) * LANES]


def first_step():
    return (pl.program_id(0) == 0) & (pl.program_id(1) == 0)


def front0_kernel(tok, w0, misc, p):
    lay = Layer(w0, misc, 0)
    x = dot(lay.side, onehot_rows(tok[0]), HIGHEST)
    for j, value in enumerate(front_forward(lay, x)):
        p[j, 0] = value


def mid_kernel(tok, z, q0, w0, w1, misc, h, a, x1, p):
    lay = Layer(w0, misc, 0)
    x = dot(lay.side, onehot_rows(tok[0]), HIGHEST)
    mixed = rear_mix(lay, x, joined(z) * q0[0, 0])
    h[0] = mixed
    _, _, _, pre = rear_hidden(lay, mixed)
    u = []
    for k in range(4):
        a[0, k] = pre[k]
        u.append(pre[k] * gelu_parts(pre[k])[0])
    x = rear_out(lay, mixed, u)
    x1[0] = x
    for j, value in enumerate(front_forward(Layer(w1, misc, 1), x)):
        p[j, 0] = value


def top_kernel(x1, z, q0, cot, w1, misc, x2, dz, dq0, dh_out, dw, cols):
    @pl.when(first_step())
    def _():
        dw[...] = jnp.zeros_like(dw)
        cols[...] = jnp.zeros_like(cols)

    lay = Layer(w1, misc, 1)
    zt, qt = joined(z), q0[0, 0]
    y = zt * qt
    h = rear_mix(lay, x1[0], y)
    _, _, _, pre = rear_hidden(lay, h)
    x2[0] = rear_out(lay, h, [v * gelu_parts(v)[0] for v in pre])
    dh, dy, columns = rear_backward(lay, h, pre, y, cot[0], dw)
    split(dz, dy * qt)
    dq0[0] = dy * zt
    dh_out[0] = dh
    cols[...] += put_columns(columns)


def mid_back_kernel(
    dp, x1, dh1, h, a, z, q0, w0, w1, misc, dz, dq0, dh_out, dw_front, dw, cols
):
    @pl.when(first_step())
    def _():
        dw_front[...] = jnp.zeros_like(dw_front)
        dw[...] = jnp.zeros_like(dw)
        cols[...] = jnp.zeros_like(cols)

    upper = Layer(w1, misc, 1)
    dout, columns = front_backward(upper, x1[0], [dp[j, 0] for j in range(3)], dh1[0], dw_front)
    lay = Layer(w0, misc, 0)
    zt, qt = joined(z), q0[0, 0]
    dh, dy, more = rear_backward(lay, h[0], [a[0, k] for k in range(4)], zt * qt, dout, dw)
    split(dz, dy * qt)
    dq0[0] = dy * zt
    dh_out[0] = dh
    cols[...] += put_columns(columns + more)


def front0_back_kernel(dp, tok, dh0, w0, misc, dx, dw_front, cols):
    @pl.when(first_step())
    def _():
        dw_front[...] = jnp.zeros_like(dw_front)
        cols[...] = jnp.zeros_like(cols)

    lay = Layer(w0, misc, 0)
    places = onehot_rows(tok[0])
    x = dot(lay.side, places, HIGHEST)
    grad, columns = front_backward(lay, x, [dp[j, 0] for j in range(3)], dh0[0], dw_front)
    dx[0] = grad
    cols[...] += put_columns(columns) + dot_nt(grad, places)


def token_call(kernel, name, seqs, width, ins, outs, args, out_shape, gflops):
    specs = {
        "tok": pl.BlockSpec((1, 1, TILE), lambda s, t: (s, 0, t)),
        "pos": pl.BlockSpec((1, D, TILE), lambda s, t: (s, 0, t)),
        "blk": pl.BlockSpec((1, TILE // LANES, D, LANES), lambda s, t: (s, t, 0, 0)),
        "q0": pl.BlockSpec((1, 1, D, TILE), lambda s, t: (0, s, 0, t)),
        "three": pl.BlockSpec((3, 1, D, TILE), lambda s, t: (0, s, 0, t)),
        "hid": pl.BlockSpec((1, 4, D, TILE), lambda s, t: (s, 0, 0, t)),
    }

    def spec(item):
        if isinstance(item, str):
            return specs[item]
        return item

    return pl.pallas_call(
        kernel,
        grid=(seqs, width // TILE),
        in_specs=[spec(i) for i in ins],
        out_specs=[spec(o) for o in outs],
        out_shape=out_shape,
        compiler_params=pltpu.CompilerParams(vmem_limit_bytes=VMEM_LIMIT),
        cost_estimate=cost(gflops * 1e9, 1e7),
        name=name,
    )(*args)


def per_device(*arguments):
    (token_ids, embedding, inward, vectors, outward, expand, offsets, contract, channels, filters) = arguments[:10]
    moments = arguments[10:19]
    averages = arguments[19:28]
    cotangent = arguments[28]
    n, m = lax.axis_size("chan"), lax.axis_size("batch")
    seqs, width = token_ids.shape
    length = width * n
    chans = channels.shape[2]
    tables = tuple(jnp.asarray(t) for t in fourier_tables(length))

    def shard_rows(layer):
        folded = contract[layer].reshape(chans, n, 4, chans).transpose(2, 0, 1, 3)
        return [
            inward[layer].reshape(3 * chans, D),
            outward[layer],
            expand[layer],
            folded.reshape(4 * chans, D),
        ]

    side = jnp.concatenate(
        [
            vectors.reshape(18, chans).T,
            channels[:, :12].reshape(24, chans).T,
            embedding.T,
            offsets.reshape(8, chans).T,
            jnp.zeros((chans, D - OFF0 - 8), F32),
        ],
        axis=1,
    )
    pad = -(25 * chans) % 32
    own = shard_rows(0) + shard_rows(1) + [side]
    if pad:
        own.append(jnp.zeros((pad, D), F32))
    gathered = gather_weights(jnp.concatenate(own, axis=0), n, m, 1)
    weight_spec = [
        pl.BlockSpec((n, 12 * chans, D), lambda s, t, k=k: (0, k, 0)) for k in range(LAYERS)
    ]
    misc_spec = pl.BlockSpec((n, chans, D), lambda s, t: (0, 24, 0))
    misc = gathered[:, 24 * chans : 25 * chans].reshape(D, D)
    tokens = token_ids.reshape(seqs, 1, width)

    first_chan = lax.axis_index("chan") * chans
    chan_ids = (first_chan + jnp.arange(chans)).astype(F32)
    slow = math.log(0.01) / 1.5
    fast = math.log(0.01) / 0.3
    delta = jnp.abs(slow + (fast - slow) * chan_ids / (D - 1))[:, None]
    nets = [jnp.pad(filters[k], ((0, 8), (0, 0))) for k in range(LAYERS)]
    fourths = [channels[k, 13:] for k in range(LAYERS)]
    specs, keeps = [], []
    for k in range(LAYERS):
        kern, keep = filter_forward(nets[k], fourths[k], delta, length)
        specs.append(kernel_spectrum(kern, channels[k, 12][:, None], tables))
        keeps.append(keep)

    pos = sds(seqs, D, width)
    blk = sds(seqs, width // LANES, D, LANES)
    three = sds(3, seqs, D, width)
    front_sum = pl.BlockSpec((n, 3 * chans, D), lambda s, t: (0, 0, 0))
    rear_sum = pl.BlockSpec((n, 9 * chans, D), lambda s, t: (0, 0, 0))
    col_sum = pl.BlockSpec((D, D), lambda s, t: (0, 0))
    call = partial(token_call, seqs=seqs, width=width)

    def mixer(p, layer):
        q, g = mixer_in(p, misc, n, chans, TAP0 + 12 * layer, 2 + layer)
        z, gspec = conv_forward(
            g.reshape(seqs, -1, LANES), specs[layer], tables, chans
        )
        z = token_a2a(z.reshape(seqs, -1, chans, LANES), n, chans, True, 4)
        return q, z, gspec

    def mixer_backward(dz, dq0, q, p, gspec, layer):
        dzch = token_a2a(dz, n, chans, False, 5)
        dgch, dk = conv_backward(
            dzch.reshape(seqs, -1, LANES), specs[layer], gspec, tables, chans
        )
        dp, cols = mixer_back(
            dgch.reshape(seqs, -1, chans, LANES), q, dq0, p, misc, n, chans, TAP0 + 12 * layer, 6 + layer
        )
        return dp, cols, dk

    (p0,) = call(
        front0_kernel, "front0", ins=["tok", weight_spec[0], misc_spec], outs=["three"],
        args=(tokens, gathered, gathered), out_shape=[three], gflops=1,
    )
    qa, za, gspec0 = mixer(p0, 0)
    h0, a0, x1, p1 = call(
        mid_kernel, "mid", ins=["tok", "blk", "q0", *weight_spec, misc_spec],
        outs=["pos", "hid", "pos", "three"],
        args=(tokens, za, qa, gathered, gathered, gathered),
        out_shape=[pos, sds(seqs, 4, D, width), pos, three], gflops=5,
    )
    qb, zb, gspec1 = mixer(p1, 1)
    activations, dz1, dq1, dh1, dw_rear1, cols_top = call(
        top_kernel, "top",
        ins=["pos", "blk", "q0", "pos", weight_spec[1], misc_spec],
        outs=["pos", "blk", "pos", "pos", rear_sum, col_sum],
        args=(x1, zb, qb, cotangent, gathered, gathered),
        out_shape=[pos, blk, pos, pos, sds(n, 9 * chans, D), sds(D, D)], gflops=9,
    )
    dp1, cols_taps1, dk1 = mixer_backward(dz1, dq1, qb, p1, gspec1, 1)
    dz0, dq0, dh0, dw_front1, dw_rear0, cols_mid = call(
        mid_back_kernel, "mid_back",
        ins=["three", "pos", "pos", "pos", "hid", "blk", "q0", *weight_spec, misc_spec],
        outs=["blk", "pos", "pos", front_sum, rear_sum, col_sum],
        args=(dp1, x1, dh1, h0, a0, za, qa, gathered, gathered, gathered),
        out_shape=[blk, pos, pos, sds(n, 3 * chans, D), sds(n, 9 * chans, D), sds(D, D)],
        gflops=9,
    )
    dp0, cols_taps0, dk0 = mixer_backward(dz0, dq0, qa, p0, gspec0, 0)
    input_gradient, dw_front0, cols_low = call(
        front0_back_kernel, "front0_back",
        ins=["three", "tok", "pos", weight_spec[0], misc_spec],
        outs=["pos", front_sum, col_sum],
        args=(dp0, tokens, dh0, gathered, gathered),
        out_shape=[pos, sds(n, 3 * chans, D), sds(D, D)], gflops=2,
    )
    dnets, dchans = [], []
    for k, dk in ((0, dk0), (1, dk1)):
        dnet, dfourth = filter_backward(nets[k], fourths[k], delta, keeps[k], dk, length)
        dnets.append(dnet)
        dchans += [dk[:chans, :1], dfourth.T]

    cols = cols_top + cols_taps1 + cols_mid + cols_taps0 + cols_low
    dnet = jnp.stack(dnets).reshape(-1, D)
    dnet = jnp.pad(dnet, ((0, n * FILTER_ROWS - dnet.shape[0]), (0, 0)))
    pad = -(25 * chans + FILTER_ROWS) % 32
    grads = jnp.concatenate(
        [
            dw_front0, dw_rear0, dw_front1, dw_rear1,
            cols.reshape(n, chans, D),
            jnp.zeros((n, pad, D), F32),
            dnet.reshape(n, FILTER_ROWS, D),
        ],
        axis=1,
    )
    dchan = jnp.concatenate(dchans + [jnp.zeros((chans, D - 2 * (FO + 1)), F32)], axis=1)
    rows, filt, chan = reduce_gradients(grads, dchan, n, m, 8)

    per = []
    for k in range(LAYERS):
        base = 12 * chans * k
        block = rows[base : base + 12 * chans]
        folded = block[8 * chans :].reshape(4, chans, n, chans).transpose(1, 2, 0, 3)
        per.append(
            (
                block[: 3 * chans].reshape(3, chans, D),
                block[3 * chans : 4 * chans],
                block[4 * chans : 8 * chans],
                folded.reshape(chans, FF),
            )
        )
    flat = rows[24 * chans : 25 * chans].T
    filter_total = filt.reshape(-1, D)[: LAYERS * 136 * FO // D].reshape(LAYERS, 136, FO)
    chan_rows = chan.T
    chan_grads = jnp.stack(
        [
            jnp.concatenate(
                [
                    flat[TAP0 + 12 * k : TAP0 + 12 * k + 12],
                    chan_rows[(FO + 1) * k : (FO + 1) * (k + 1)],
                ],
                axis=0,
            )
            for k in range(LAYERS)
        ]
    )
    reduced = (
        flat[EMB0 : EMB0 + VOCAB],
        jnp.stack([per[k][0] for k in range(LAYERS)]),
        flat[VEC0 : VEC0 + 18].reshape(LAYERS, 9, chans),
        jnp.stack([per[k][1] for k in range(LAYERS)]),
        jnp.stack([per[k][2] for k in range(LAYERS)]),
        flat[OFF0 : OFF0 + 8].reshape(LAYERS, 4 * chans),
        jnp.stack([per[k][3] for k in range(LAYERS)]),
        chan_grads,
        filter_total,
    )
    weights = (embedding, inward, vectors, outward, expand, offsets, contract, channels, filters)
    step_scale = 1.0 / math.sqrt(seqs * m * length)
    packed = [activations, input_gradient]
    for weight, gradient, moment, average, factor in zip(
        weights, reduced, moments, averages, STEP_RATES
    ):
        velocity = MOMENTUM * moment + gradient
        updated = weight - factor * step_scale * (gradient + MOMENTUM * velocity)
        running = AVERAGING * average + (1.0 - AVERAGING) * updated
        packed.extend([velocity, running, updated, updated.astype(jnp.bfloat16)])
    return tuple(packed)


def solution(mesh):
    in_weights = (
        P(None, "chan"),
        P(None, None, "chan", None),
        P(None, None, "chan"),
        P(None, "chan", None),
        P(None, "chan", None),
        P(None, "chan"),
        P(None, "chan", None),
        P(None, None, "chan"),
        P(),
    )
    tokens = P("batch", None, "chan")
    in_specs = (P("batch", "chan"),) + in_weights * 3 + (tokens,)
    out_specs = (tokens, tokens) + tuple(spec for spec in in_weights for _ in range(4))
    return jax.shard_map(
        per_device, mesh=mesh, in_specs=in_specs, out_specs=out_specs, check_vma=False
    )
```

```python
from functools import partial
import math

import jax
import jax.numpy as jnp
import numpy as np
from jax import lax
from jax.experimental import pallas as pl
from jax.experimental.pallas import tpu as pltpu
from jax.sharding import PartitionSpec as P

D = 256
FF = 1024
FO = 64
EMB = 5
VOCAB = 16
LAYERS = 2
LANES = 128
TILE = 256

HIGH = lax.Precision.HIGH
HIGHEST = lax.Precision.HIGHEST
EPSILON = 1e-05
MOMENTUM = 0.9
AVERAGING = 0.9
WINDOW_SHIFT = 0.05
FREQUENCY = 10.0
STEP_RATES = (0.7, 0.06, 0.1, 0.037, 0.1, 0.16, 0.025, 0.2, 0.0002)
GELU_SCALE = math.sqrt(2.0 / math.pi)
GELU_CUBE = 0.044715

MESH = pl.DeviceIdType.MESH
VMEM = pltpu.VMEM
WHOLE = pl.BlockSpec(memory_space=pltpu.VMEM)
HBM = pl.BlockSpec(memory_space=pl.ANY)
VMEM_LIMIT = 58 * 1024 * 1024
F32 = jnp.float32
BF16 = jnp.bfloat16

VEC0 = 0
TAP0 = 18
EMB0 = 42
OFF0 = 58
EIGHT = 8


def dot(a, b, precision=HIGH):
    return jnp.dot(a, b, precision=precision, preferred_element_type=F32)


def dot_nt(a, b, precision=HIGH):
    return lax.dot_general(
        a, b, (((1,), (1,)), ((), ())), precision=precision, preferred_element_type=F32
    )


def dot_tn(a, b, precision=HIGH):
    return lax.dot_general(
        a, b, (((0,), (0,)), ((), ())), precision=precision, preferred_element_type=F32
    )


def sds(*shape):
    return jax.ShapeDtypeStruct(shape, F32)


def cost(flops, moved):
    return pl.CostEstimate(flops=int(flops), bytes_accessed=int(moved), transcendentals=0)


def position_table(length):
    indices = np.arange(length, dtype=np.float32)
    fraction = indices / np.float32(length - 1)
    angles = np.float32(2.0 * math.pi) * indices / np.float32(length)
    bands = (EMB - 1) // 2
    frequency = np.linspace(0.0001, bands - 1, bands).astype(np.float32)
    turned = (frequency[:, None] * angles[None, :]).astype(np.float32).astype(np.float64)
    table = np.zeros((8, length), np.float32)
    table[0] = fraction
    table[1 : 1 + bands] = np.cos(turned)
    table[1 + bands : 1 + 2 * bands] = -np.sin(turned)
    table[EMB] = 1.0
    return table


def split_table(table):
    high = table.astype(np.float32).astype(jnp.bfloat16)
    low = (table.astype(np.float32) - high.astype(np.float32)).astype(jnp.bfloat16)
    return high, low


def left_table(table):
    high, low = split_table(table)
    return np.concatenate([high, high, low], axis=1)


def right_table(table):
    high, low = split_table(table)
    return np.concatenate([high, high, low], axis=0)


def fourier_tables(length):
    rows = length // LANES
    outer = 2 * rows
    total = outer * LANES
    turn = 2.0 * np.pi / outer * (np.arange(outer)[:, None] * np.arange(rows)[None, :] % outer)
    c, s = np.cos(turn), np.sin(turn)
    first = np.block([[c, s], [-s, c]])
    first_real = np.block([[c], [-s]])
    last = np.block([[c.T, -s.T], [s.T, c.T]]) / total
    last_real = np.block([[c.T, -s.T]]) / total
    twist = 2.0 * np.pi / total * (np.arange(outer)[:, None] * np.arange(LANES)[None, :])
    twiddle = np.concatenate([np.cos(twist), -np.sin(twist)], axis=1).astype(np.float32)
    lane = 2.0 * np.pi / LANES * (np.arange(LANES)[:, None] * np.arange(LANES)[None, :] % LANES)
    c, s = np.cos(lane), np.sin(lane)
    second = np.block([[c, -s], [s, c]])
    second_back = np.block([[c, s], [-s, c]])
    return (
        left_table(first),
        left_table(first_real),
        twiddle,
        right_table(second),
        right_table(second_back),
        left_table(last),
        left_table(last_real),
    )


def sin_cos(x):
    turns = jnp.round(x * (1.0 / math.pi))
    r = x - turns * 3.140625
    r = r - turns * 9.67025756835937500e-4
    r = r - turns * 6.27711415290832520e-7
    r = r - turns * 1.21542010130123850e-10
    half = turns * 0.5
    sign = 1.0 - 4.0 * jnp.abs(half - jnp.round(half))
    r2 = r * r
    s = -2.5052108385441720e-8
    for k in (2.7557319223985893e-6, -1.9841269841269841e-4, 8.3333333333333333e-3, -1.6666666666666667e-1):
        s = s * r2 + k
    s = r + r * (r2 * s)
    c = 2.0876756987868099e-9
    for k in (-2.7557319223985888e-7, 2.4801587301587302e-5, -1.3888888888888889e-3, 4.1666666666666667e-2, -0.5):
        c = c * r2 + k
    c = 1.0 + r2 * c
    return s * sign, c * sign


def window(delta, length, start, width):
    t = lax.broadcasted_iota(jnp.int32, (1, width), 1) + start
    fraction = t.astype(F32) / (length - 1)
    return jnp.exp(-delta * fraction) + WINDOW_SHIFT


def normalize(x):
    center = x - jnp.mean(x, axis=0, keepdims=True)
    spread = jnp.mean(center * center, axis=0, keepdims=True)
    scale = lax.rsqrt(spread + EPSILON)
    return center * scale, scale


def normalize_back(e, xh, scale):
    return scale * (
        e - jnp.mean(e, axis=0, keepdims=True) - xh * jnp.mean(e * xh, axis=0, keepdims=True)
    )


def gelu_parts(a):
    t = jnp.tanh(GELU_SCALE * (a + GELU_CUBE * a * a * a))
    return 0.5 * (1.0 + t), t


def put_columns(pairs, width=D):
    rows = pairs[0][1].shape[0]
    lane = lax.broadcasted_iota(jnp.int32, (rows, width), 1)
    out = jnp.zeros((rows, width), F32)
    for k, column in pairs:
        out = out + jnp.where(lane == k, column, 0.0)
    return out


def row_sum(x):
    return jnp.sum(x, axis=1, keepdims=True)


def ones_rows(width):
    return (lax.broadcasted_iota(jnp.int32, (EIGHT, width), 0) == 0).astype(F32)


def filter_block(length, start, feat, net, fourth, delta):
    width = feat.shape[1]
    ones = ones_rows(width)
    kept = []
    h, c = sin_cos(FREQUENCY * dot_tn(net[0:8, :], feat, HIGHEST))
    kept.append((h, FREQUENCY * c))
    for row in (EMB + 1, EMB + 2 + FO):
        weights = net[row : row + FO + 8, :]
        h, c = sin_cos(FREQUENCY * dot_tn(weights, jnp.concatenate([h, ones], axis=0), HIGHEST))
        kept.append((h, FREQUENCY * c))
    return dot_tn(fourth[...], h, HIGHEST) * window(delta, length, start, width), kept


def filter_back_block(length, start, feat, net, fourth, delta, keep, dk, dnet, dfourth):
    width = feat.shape[1]
    ones = ones_rows(width)
    dkw = dk * window(delta, length, start, width)
    dfourth[...] += dot_nt(keep[2], dkw)
    dpre = dot(fourth[...], dkw) * keep[5]
    dnet[80:152, :] += dot_nt(jnp.concatenate([keep[1], ones], axis=0), dpre)
    dpre = dot(net[EMB + 2 + FO : EMB + 2 + 2 * FO, :], dpre) * keep[4]
    dnet[8:80, :] += dot_nt(jnp.concatenate([keep[0], ones], axis=0), dpre)
    dpre = dot(net[EMB + 1 : EMB + 1 + FO, :], dpre) * keep[3]
    dnet[0:8, :] += dot_nt(feat, dpre)


def halves(x):
    high = x.astype(BF16)
    return high, (x - high.astype(F32)).astype(BF16)


def left_dot(table, x):
    high, low = halves(x)
    return jnp.dot(
        table, jnp.concatenate([high, low, high], axis=0), preferred_element_type=F32
    )


def right_dot(x, table):
    high, low = halves(x)
    return jnp.dot(
        jnp.concatenate([high, low, high], axis=1), table, preferred_element_type=F32
    )


def spectrum_of(x, first, twiddle, second):
    outer = twiddle.shape[0]
    y = left_dot(first, x)
    tr, ti = twiddle[:, :LANES], twiddle[:, LANES:]
    parts = []
    for b in range(x.shape[1] // LANES):
        yr = y[:outer, b * LANES : (b + 1) * LANES]
        yi = y[outer:, b * LANES : (b + 1) * LANES]
        parts.append(jnp.concatenate([yr * tr - yi * ti, yr * ti + yi * tr], axis=1))
    return right_dot(jnp.concatenate(parts, axis=0), second)


def signal_of(v, twiddle, second_back, last):
    outer = twiddle.shape[0]
    a = right_dot(v, second_back)
    tr, ti = twiddle[:, :LANES], twiddle[:, LANES:]
    parts = []
    for b in range(v.shape[0] // outer):
        ar = a[b * outer : (b + 1) * outer, :LANES]
        ai = a[b * outer : (b + 1) * outer, LANES:]
        parts.append(jnp.concatenate([ar * tr + ai * ti, ai * tr - ar * ti], axis=0))
    return left_dot(last, jnp.concatenate(parts, axis=1))


def load_pairs(ref):
    rows = ref.shape[1] // EIGHT
    parts = []
    for b in range(EIGHT):
        parts.append(
            jnp.concatenate([ref[s, pl.ds(b, rows, stride=EIGHT), :] for s in range(2)], axis=0)
        )
    return jnp.concatenate(parts, axis=1)


def store_pairs(ref, value):
    rows = ref.shape[1] // EIGHT
    for b in range(EIGHT):
        for s in range(2):
            ref[s, pl.ds(b, rows, stride=EIGHT), :] = value[
                s * rows : (s + 1) * rows, b * LANES : (b + 1) * LANES
            ]


def times(a, b):
    ar, ai, br, bi = a[:, :LANES], a[:, LANES:], b[:, :LANES], b[:, LANES:]
    return jnp.concatenate([ar * br - ai * bi, ar * bi + ai * br], axis=1)


def times_conj(a, b):
    ar, ai, br, bi = a[:, :LANES], a[:, LANES:], b[:, :LANES], b[:, LANES:]
    return jnp.concatenate([ar * br + ai * bi, ai * br - ar * bi], axis=1)


def send(a, b, sems, index, device):
    copy = remote(a, b, sems, index, device)
    copy.start()
    return copy


def remote(a, b, sems, index, device):
    return pltpu.make_async_remote_copy(
        src_ref=a, dst_ref=b, send_sem=sems[0].at[index], recv_sem=sems[1].at[index],
        device_id=device, device_id_type=MESH,
    )


def exchange(refs, peers, send_sem, recv_sem, base):
    return [
        send(a, b, (send_sem, recv_sem), base + k, peer)
        for k, ((a, b), peer) in enumerate(zip(refs, peers))
    ]


def greet(n, mates=()):
    me, b = lax.axis_index("chan"), lax.axis_index("batch")
    barrier = pltpu.get_barrier_semaphore()
    for d in range(1, n):
        pl.semaphore_signal(
            barrier, inc=1, device_id={"chan": lax.rem(me + d, n)}, device_id_type=MESH
        )
    for mate in mates:
        pl.semaphore_signal(barrier, inc=1, device_id={"batch": mate}, device_id_type=MESH)
    pl.semaphore_wait(barrier, n - 1 + len(mates))


def core_mate(b):
    return b + 1 - 2 * lax.rem(b, 2)


def y_mate(b):
    return b + 2 - 4 * (b // 2)


def comm_params(cid):
    return pltpu.CompilerParams(
        collective_id=cid, has_side_effects=True, vmem_limit_bytes=VMEM_LIMIT
    )


def pair_sems(*shape):
    return [pltpu.SemaphoreType.DMA(shape), pltpu.SemaphoreType.DMA(shape)]


class Blocks:
    def __init__(self, n, span, sems, own):
        self.n, self.span, self.sems, self.own = n, span, sems, own
        self.me = lax.axis_index("chan")

    def rows(self, j):
        return pl.ds(pl.multiple_of(j * self.span, 8), self.span)

    def out_refs(self, k, j, src, dst):
        return src.at[k, j], dst.at[k, :, self.rows(self.me), :]

    def back_refs(self, k, j, src, dst):
        return src.at[k, :, self.rows(j), :], dst.at[k, self.me]

    def each(self, refs, k, src, dst):
        for d in range(1, self.n):
            j = lax.rem(self.me + d, self.n)
            a, b = refs(k, j, src, dst)
            yield remote(a, b, self.sems, (k, d), {"chan": j})

    def start(self, refs, k, src, dst):
        a, b = refs(k, self.me, src, dst)
        pltpu.make_async_copy(a, b, self.own.at[k]).start()
        for copy in self.each(refs, k, src, dst):
            copy.start()

    def arrived(self, refs, k, src, dst):
        for copy in self.each(refs, k, src, dst):
            copy.wait_recv()
        a, b = refs(k, self.me, src, dst)
        pltpu.make_async_copy(a, b, self.own.at[k]).wait()

    def sent(self, refs, k, src, dst):
        for copy in self.each(refs, k, src, dst):
            copy.wait_send()


def loop(count, body):
    def step(i, _):
        body(i)
        return 0

    lax.fori_loop(0, count, step, 0)


def conv_chunk(k, g, spec, gspec, z, first, twiddle, second, second_back, last):
    outer = twiddle.shape[0]
    rows = pl.ds(pl.multiple_of(k * EIGHT * outer, 8), EIGHT * outer)
    u = spectrum_of(load_pairs(g.at[k]), first[...], twiddle[...], second[...])
    gspec[rows, :] = u
    o = signal_of(times(u, spec[rows, :]), twiddle[...], second_back[...], last[...])
    store_pairs(z.at[k], o)


def prepare_kernel(
    n, length, chans,
    wown, sown, town, inw, net0, net1, fourth0, fourth1, delta, skip0, skip1, feat,
    first, first_real, twiddle, second, second_back, last, last_real,
    wall, misc, toks, tokx, spec0, spec1, gspec, keep0, keep1, zpos,
    kern, gch, zch, kbuf, ssem, rsem, wsem, vsem, zsem, ysem, local, ksem, zown,
):
    me, b = lax.axis_index("chan"), lax.axis_index("batch")
    groups = chans // EIGHT
    seqs, span = zpos.shape[2], zpos.shape[3]
    width = span // EIGHT * LANES
    greet(n, (core_mate(b), y_mate(b)))
    mine = pl.ds(pl.multiple_of(me * chans, 8), chans)
    small = []
    for d in range(1, n):
        peer = {"chan": lax.rem(me + d, n)}
        small.append(send(sown, misc.at[mine, :], (ssem, rsem), d, peer))
        small.append(send(town, toks.at[me], (ssem, rsem), n + d, peer))
    misc[mine, :] = sown[...]
    toks[me] = town[...]
    half = n // 2
    x, z = lax.rem(me, 2), me // 2
    side = {"chan": 2 * z + 1 - x}
    count = wown.shape[0] // 2
    quarter = count // 4
    weights = (wsem, vsem)

    def part(c, k):
        return pl.ds(pl.multiple_of(c * count + k * quarter, 8), quarter)

    def hop_z(c):
        keep = pltpu.make_async_copy(wown.at[part(c, b)], wall.at[me, part(c, b)], local.at[c])
        keep.start()
        copies = []
        for d in range(1, half):
            j = 2 * lax.rem(z + d, half) + x
            copies.append(
                send(wown.at[part(c, b)], wall.at[me, part(c, b)], weights, (c, d), {"chan": j})
            )
        return keep, copies

    def hop_x(c, keep, copies):
        out = [send(wown.at[part(c, b)], wall.at[me, part(c, b)], weights, (c, half), side)]
        for d in range(1, half):
            j = 2 * lax.rem(z + half - d, half) + x
            copies[d - 1].wait_recv()
            out.append(
                send(wall.at[j, part(c, b)], wall.at[j, part(c, b)], weights, (c, half + d), side)
            )
        keep.wait()
        return out

    def hop_y(c, copies):
        for copy in copies:
            copy.wait_recv()
        return send(
            wall.at[:, part(c, b)], wall.at[:, part(c, b)], weights, (c, n), {"batch": y_mate(b)}
        )

    def hop_core(c, copy):
        copy.wait_recv()
        mate = {"batch": core_mate(b)}
        return [
            send(wall.at[:, part(c, k)], wall.at[:, part(c, k)], weights, (c, n + 1 + i), mate)
            for i, k in enumerate((b, y_mate(b)))
        ]

    keep_a, z_a = hop_z(0)
    keep_b, z_b = hop_z(1)

    block = 512

    def filters(net, fourth, keep):
        def saved(i, slot):
            return pltpu.make_async_copy(
                kbuf.at[slot],
                keep.at[:, :, pl.ds(pl.multiple_of(i * block, block), block)],
                ksem.at[slot],
            )

        def body(i):
            slot = lax.rem(i, 2)
            out, kept = filter_block(
                length, i * block, feat[:, pl.ds(pl.multiple_of(i * block, block), block)],
                net, fourth, delta[...],
            )

            @pl.when(i >= 2)
            def _():
                saved(i - 2, slot).wait()

            for k, (sine, cosine) in enumerate(kept):
                kbuf[slot, k] = sine
                kbuf[slot, 3 + k] = cosine
            saved(i, slot).start()
            for q in range(block // LANES):
                rows = pl.ds(pl.multiple_of((i * (block // LANES) + q) * EIGHT, 8), EIGHT)
                for k in range(groups):
                    kern[k, rows, :] = out[
                        k * EIGHT : (k + 1) * EIGHT, q * LANES : (q + 1) * LANES
                    ]

        total = length // block
        loop(total, body)
        for i in (total - 2, total - 1):
            saved(i, i % 2).wait()

    def spectra(skip, spec):
        outer = twiddle.shape[0]
        rows = length // LANES

        def body(k):
            taps = jnp.concatenate(
                [kern[k, pl.ds(c, rows, stride=EIGHT), :] for c in range(EIGHT)], axis=1
            )
            u = spectrum_of(taps, first_real[...], twiddle[...], second[...])
            for c in range(EIGHT):
                wide = jnp.broadcast_to(skip[pl.ds(k * EIGHT + c, 1), :], (outer, LANES))
                both = jnp.concatenate([wide, jnp.zeros_like(wide)], axis=1)
                place = pl.ds(pl.multiple_of((k * EIGHT + c) * outer, 8), outer)
                spec[place, :] = u[c * outer : (c + 1) * outer] + both

        loop(groups, body)

    filters(net0, fourth0, keep0)
    spectra(skip0, spec0)
    x_a = hop_x(0, keep_a, z_a)

    for copy in small:
        copy.wait()
    table = misc[...]
    xh, _ = normalize(table)
    normed = xh * table[:, VEC0 : VEC0 + 1] + table[:, VEC0 + 1 : VEC0 + 2]
    lane = lax.broadcasted_iota(jnp.int32, (chans, LANES), 1)
    own = sown[...]
    mixes, biases = [], []
    for j in (1, 2):
        rows = dot(inw[j * chans : (j + 1) * chans, :], normed, HIGHEST)
        rows = rows + own[:, VEC0 + 4 + j : VEC0 + 5 + j]
        rows = pltpu.roll(rows, D - EMB0, 1)[:, :LANES]
        rows = jnp.where(lane < VOCAB, rows, 0.0)
        k = TAP0 + 3 * j
        mixes.append(
            own[:, k : k + 1] * rows
            + own[:, k + 1 : k + 2] * pltpu.roll(rows, VOCAB, 1)
            + own[:, k + 2 : k + 3] * pltpu.roll(rows, 2 * VOCAB, 1)
        )
        biases.append(own[:, TAP0 + 9 + j : TAP0 + 10 + j])
    mix = jnp.concatenate(mixes, axis=0)[:, : 3 * VOCAB]
    names = lax.broadcasted_iota(jnp.int32, (VOCAB, width), 0).astype(F32)
    parts = width // D

    def shifted(i, s):
        here = jnp.concatenate(
            [toks[i, s * parts + h : s * parts + h + 1, :] for h in range(parts)], axis=1
        )
        before = toks[jnp.maximum(i - 1, 0), (s + 1) * parts - 1 : (s + 1) * parts, D - LANES :]
        long = jnp.concatenate([jnp.where(i > 0, before, -1.0), here], axis=1)
        return here, pltpu.roll(long, 1, 1)[:, LANES:], pltpu.roll(long, 2, 1)[:, LANES:]

    for s in range(seqs):
        for k, row in enumerate(shifted(me, s)):
            tokx[s, k : k + 1, :] = row

    def gates(i):
        for s in range(seqs):
            here, one, two = shifted(i, s)
            places = jnp.concatenate(
                [(names == row).astype(F32) for row in (two, one, here)], axis=0
            )
            out = dot(mix, places, HIGHEST)
            gate = (out[:chans] + biases[0]) * (out[chans:] + biases[1])
            for q in range(width // LANES):
                rows = pl.ds(pl.multiple_of(i * span + q * EIGHT, 8), EIGHT)
                for k in range(groups):
                    gch[k, s, rows, :] = gate[
                        k * EIGHT : (k + 1) * EIGHT, q * LANES : (q + 1) * LANES
                    ]

    loop(n, gates)
    y_a = hop_y(0, x_a)
    x_b = hop_x(1, keep_b, z_b)
    back = Blocks(n, span, (zsem, ysem), zown)

    def chunk(k):
        conv_chunk(
            k, gch, spec0, gspec, zch, first, twiddle, second, second_back, last
        )
        back.start(back.back_refs, k, zch, zpos)

    loop(groups, chunk)
    core_a = hop_core(0, y_a)
    y_b = hop_y(1, x_b)
    filters(net1, fourth1, keep1)
    spectra(skip1, spec1)
    core_b = hop_core(1, y_b)

    def finish(k):
        back.arrived(back.back_refs, k, zch, zpos)
        back.sent(back.back_refs, k, zch, zpos)

    loop(groups, finish)
    for copy in z_a + z_b + x_a + x_b + [y_a, y_b]:
        copy.wait_send()
    for copy in core_a + core_b:
        copy.wait()


def prepare(wown, sown, town, inw, nets, fourths, delta, skips, tables, n, seqs, length, cid):
    chans = fourths[0].shape[1]
    groups = chans // EIGHT
    rows = length // LANES
    span = rows // n * EIGHT
    outer = 2 * rows
    width = length // n
    spec = sds(chans * outer, 2 * LANES)
    keep = sds(6, FO, length)
    return pl.pallas_call(
        partial(prepare_kernel, n, length, chans),
        in_specs=[HBM] + [WHOLE] * 18,
        out_specs=[HBM] + [WHOLE] * 6 + [HBM] * 3,
        out_shape=[
            sds(n, *wown.shape), sds(D, D), sds(n, EIGHT, D), sds(seqs, EIGHT, width),
            spec, spec, spec, keep, keep, sds(groups, n, seqs, span, LANES),
        ],
        scratch_shapes=[
            VMEM((groups, rows * EIGHT, LANES), F32),
            VMEM((groups, seqs, rows * EIGHT, LANES), F32),
            VMEM((groups, seqs, rows * EIGHT, LANES), F32),
            VMEM((2, 6, FO, 512), F32),
            *pair_sems(2 * n),
            *pair_sems(2, n + 3),
            *pair_sems(groups, n),
            pltpu.SemaphoreType.DMA((2,)),
            pltpu.SemaphoreType.DMA((2,)),
            pltpu.SemaphoreType.DMA((groups,)),
        ],
        compiler_params=comm_params(cid),
        name="prepare",
    )(
        wown, sown, town, inw, *nets, *fourths, delta, *skips,
        position_table(length), *tables,
    )


def mixer_kernel(
    n, chans, lane0, p, misc, spec,
    first, first_real, twiddle, second, second_back, last, last_real,
    q, gspec, zpos,
    qv, gpos, gch, zch, tails, halo, gsem, hsem, zsem, ysem, gown, zown, hs, hr, qsem,
):
    me = lax.axis_index("chan")
    seqs, width = p.shape[1], p.shape[3]
    groups = chans // EIGHT
    span = zpos.shape[3]
    greet(n)
    lane = lax.broadcasted_iota(jnp.int32, (D, LANES), 1)
    pack = jnp.zeros((D, LANES), F32)
    for j in range(3):
        for s in range(seqs):
            slot = 2 * (j * seqs + s)
            tail = pltpu.roll(p[j, s, :, width - LANES :], slot + 2, 1)
            pack = jnp.where((lane == slot) | (lane == slot + 1), tail, pack)
    tails[...] = pack
    copy = send(tails, halo, (hs, hr), 0, {"chan": lax.rem(me + 1, n)})
    copy.wait()
    inner = (me > 0).astype(F32)
    out = Blocks(n, span, (gsem, hsem), gown)
    back = Blocks(n, span, (zsem, ysem), zown)

    def gates(k):
        def body(owner):
            rows = pl.ds(pl.multiple_of(owner * chans + k * EIGHT, 8), EIGHT)
            side = misc[rows, :]
            edge = halo[rows, :] * inner
            for s in range(seqs):
                made = []
                for j in range(3):
                    here = p[j, s, rows, :]
                    before = pltpu.roll(edge, LANES - 2 - 2 * (j * seqs + s), 1)
                    long = jnp.concatenate([before, here], axis=1)
                    one = pltpu.roll(long, 1, 1)[:, LANES:]
                    two = pltpu.roll(long, 2, 1)[:, LANES:]
                    t = lane0 + 3 * j
                    made.append(
                        side[:, lane0 + 9 + j : lane0 + 10 + j]
                        + side[:, t : t + 1] * two
                        + side[:, t + 1 : t + 2] * one
                        + side[:, t + 2 : t + 3] * here
                    )
                    qv[j, s, rows, :] = made[j]
                gate = made[2] * made[1]
                for b in range(width // LANES):
                    gpos[k, owner, s, b * EIGHT : (b + 1) * EIGHT, :] = gate[
                        :, b * LANES : (b + 1) * LANES
                    ]

        loop(n, body)
        out.start(out.out_refs, k, gpos, gch)

    loop(groups, gates)
    saved = pltpu.make_async_copy(qv, q, qsem)
    saved.start()

    def chunk(k):
        out.arrived(out.out_refs, k, gpos, gch)
        conv_chunk(k, gch, spec, gspec, zch, first, twiddle, second, second_back, last)
        back.start(back.back_refs, k, zch, zpos)

    loop(groups, chunk)

    def finish(k):
        out.sent(out.out_refs, k, gpos, gch)
        back.arrived(back.back_refs, k, zch, zpos)
        back.sent(back.back_refs, k, zch, zpos)

    loop(groups, finish)
    saved.wait()


def mixer(p, misc, spec, tables, n, chans, lane0, cid):
    seqs, width = p.shape[1], p.shape[3]
    groups = chans // EIGHT
    span = width // LANES * EIGHT
    by_position = (groups, n, seqs, span, LANES)
    by_channel = (groups, seqs, n * span, LANES)
    return pl.pallas_call(
        partial(mixer_kernel, n, chans, lane0),
        in_specs=[WHOLE] * 10,
        out_specs=[HBM, WHOLE, HBM],
        out_shape=[sds(*p.shape), sds(*spec.shape), sds(*by_position)],
        scratch_shapes=[
            VMEM(p.shape, F32),
            VMEM(by_position, F32),
            VMEM(by_channel, F32),
            VMEM(by_channel, F32),
            VMEM((D, LANES), F32),
            VMEM((D, LANES), F32),
            *pair_sems(groups, n),
            *pair_sems(groups, n),
            pltpu.SemaphoreType.DMA((groups,)),
            pltpu.SemaphoreType.DMA((groups,)),
            *pair_sems(1),
            pltpu.SemaphoreType.DMA,
        ],
        compiler_params=comm_params(cid),
        name="mixer",
    )(p, misc, spec, *tables)


def mixer_back_kernel(
    n, chans, lane0, length,
    dz, q, dq0, p, keep, misc, spec, gspec, net, fourth, delta, feat,
    first, first_real, twiddle, second, second_back, last, last_real,
    dp, dcols, dnet, dfourth, dkhead,
    qv, dq0v, pv, dzch, dzspec, dgch, dgpos, dk, kbuf, heads, halo,
    gsem, hsem, zsem, ysem, gown, zown, hs, hr, lsem, ksem,
):
    me = lax.axis_index("chan")
    seqs, width = pv.shape[1], pv.shape[3]
    groups = chans // EIGHT
    span = dgpos.shape[3]
    rows_all = length // LANES
    outer = twiddle.shape[0]
    block = kbuf.shape[3]
    loads = [
        pltpu.make_async_copy(q.at[pl.ds(1, 2)], qv, lsem.at[0]),
        pltpu.make_async_copy(dq0, dq0v, lsem.at[1]),
        pltpu.make_async_copy(p, pv, lsem.at[2]),
    ]
    greet(n)
    out = Blocks(n, span, (gsem, hsem), gown)
    back = Blocks(n, span, (zsem, ysem), zown)
    loop(groups, lambda k: out.start(out.out_refs, k, dz, dzch))
    for load in loads:
        load.start()

    def kept(i, slot):
        return pltpu.make_async_copy(
            keep.at[:, :, pl.ds(pl.multiple_of(i * block, block), block)],
            kbuf.at[slot],
            ksem.at[slot],
        )

    kept(0, 0).start()

    def chunk(k):
        out.arrived(out.out_refs, k, dz, dzch)
        rows = pl.ds(pl.multiple_of(k * EIGHT * outer, 8), EIGHT * outer)
        u = spectrum_of(load_pairs(dzch.at[k]), first[...], twiddle[...], second[...])
        dzspec[rows, :] = u
        o = signal_of(times_conj(u, spec[rows, :]), twiddle[...], second_back[...], last[...])
        store_pairs(dgch.at[k], o)
        back.start(back.back_refs, k, dgch, dgpos)

    loop(groups, chunk)

    def lag(k):
        rows = pl.ds(pl.multiple_of(k * EIGHT * outer, 8), EIGHT * outer)
        v = times_conj(dzspec[rows, :], gspec[rows, :])
        r = signal_of(v, twiddle[...], second_back[...], last_real[...])
        for b in range(EIGHT):
            dk[k, pl.ds(b, rows_all, stride=EIGHT), :] = r[:, b * LANES : (b + 1) * LANES]

    loop(groups, lag)
    for k in range(groups):
        dkhead[k * EIGHT : (k + 1) * EIGHT, :] = dk[k, 0:EIGHT, :]
    dnet[...] = jnp.zeros_like(dnet)
    dfourth[...] = jnp.zeros_like(dfourth)
    steps = length // block

    def network(i):
        slot = lax.rem(i, 2)
        kept(i, slot).wait()

        @pl.when(i + 1 < steps)
        def _():
            kept(i + 1, 1 - slot).start()

        wide = []
        for b in range(block // LANES):
            place = pl.ds(pl.multiple_of((i * (block // LANES) + b) * EIGHT, 8), EIGHT)
            wide.append(jnp.concatenate([dk[k, place, :] for k in range(groups)], axis=0))
        filter_back_block(
            length, i * block, feat[:, pl.ds(pl.multiple_of(i * block, block), block)],
            net, fourth, delta[...], kbuf.at[slot], jnp.concatenate(wide, axis=1), dnet, dfourth,
        )

    loop(steps, network)
    loop(groups, lambda k: back.arrived(back.back_refs, k, dgch, dgpos))
    for load in loads:
        load.wait()

    lane = lax.broadcasted_iota(jnp.int32, (D, LANES), 1)
    pack = jnp.zeros((D, LANES), F32)
    for s in range(seqs):
        dg = jnp.concatenate(
            [dgpos[k, j, s, 0:EIGHT, :] for j in range(n) for k in range(groups)], axis=0
        )
        parts = (dq0v[s, :, :LANES], dg * qv[1, s, :, :LANES], dg * qv[0, s, :, :LANES])
        for j in range(3):
            slot = 2 * (j * seqs + s)
            head = pltpu.roll(parts[j], slot, 1) if slot else parts[j]
            pack = jnp.where((lane == slot) | (lane == slot + 1), head, pack)
    heads[...] = pack
    copy = send(heads, halo, (hs, hr), 0, {"chan": lax.rem(me + n - 1, n)})
    copy.wait()
    inner = (me < n - 1).astype(F32)
    full = width + LANES

    def body(owner):
        rows = pl.ds(pl.multiple_of(owner * chans, 8), chans)
        side = misc[rows, :]
        edge = halo[rows, :] * inner
        sums = [jnp.zeros((chans, 1), F32)] * 12
        for s in range(seqs):
            dg = jnp.concatenate(
                [
                    jnp.concatenate(
                        [
                            dgpos[k, owner, s, b * EIGHT : (b + 1) * EIGHT, :]
                            for k in range(groups)
                        ],
                        axis=0,
                    )
                    for b in range(width // LANES)
                ],
                axis=1,
            )
            parts = (dq0v[s, rows, :], dg * qv[1, s, rows, :], dg * qv[0, s, rows, :])
            for j in range(3):
                here = parts[j]
                slot = 2 * (j * seqs + s)
                after = pltpu.roll(edge, LANES - slot, 1) if slot else edge
                long = jnp.concatenate([here, after], axis=1)
                one = pltpu.roll(long, full - 1, 1)[:, :width]
                two = pltpu.roll(long, full - 2, 1)[:, :width]
                t = lane0 + 3 * j
                dp[j, s, rows, :] = (
                    side[:, t : t + 1] * two
                    + side[:, t + 1 : t + 2] * one
                    + side[:, t + 2 : t + 3] * here
                )
                source = pv[j, s, rows, :]
                sums[3 * j] = sums[3 * j] + row_sum(two * source)
                sums[3 * j + 1] = sums[3 * j + 1] + row_sum(one * source)
                sums[3 * j + 2] = sums[3 * j + 2] + row_sum(here * source)
                sums[9 + j] = sums[9 + j] + row_sum(here)
        dcols[rows, :] = put_columns([(lane0 + k, sums[k]) for k in range(12)])

    loop(n, body)

    def finish(k):
        out.sent(out.out_refs, k, dz, dzch)
        back.sent(back.back_refs, k, dgch, dgpos)

    loop(groups, finish)


def mixer_back(
    dz, q, dq0, p, keep, misc, spec, gspec, net, fourth, delta, tables, n, chans, lane0, cid
):
    seqs, width = p.shape[1], p.shape[3]
    groups = chans // EIGHT
    span = width // LANES * EIGHT
    length = width * n
    by_position = (groups, n, seqs, span, LANES)
    by_channel = (groups, seqs, n * span, LANES)
    return pl.pallas_call(
        partial(mixer_back_kernel, n, chans, lane0, length),
        in_specs=[HBM] * 5 + [WHOLE] * 14,
        out_specs=[WHOLE] * 5,
        out_shape=[
            sds(*p.shape), sds(D, D), sds(152, FO), sds(FO, chans), sds(chans, LANES),
        ],
        scratch_shapes=[
            VMEM((2,) + p.shape[1:], F32),
            VMEM(p.shape[1:], F32),
            VMEM(p.shape, F32),
            VMEM(by_channel, F32),
            VMEM(spec.shape, F32),
            VMEM(by_channel, F32),
            VMEM(by_position, F32),
            VMEM((groups, n * span, LANES), F32),
            VMEM((2, 6, FO, 512), F32),
            VMEM((D, LANES), F32),
            VMEM((D, LANES), F32),
            *pair_sems(groups, n),
            *pair_sems(groups, n),
            pltpu.SemaphoreType.DMA((groups,)),
            pltpu.SemaphoreType.DMA((groups,)),
            *pair_sems(1),
            pltpu.SemaphoreType.DMA((3,)),
            pltpu.SemaphoreType.DMA((2,)),
        ],
        compiler_params=comm_params(cid),
        name="mixer_back",
    )(
        dz, q, dq0, p, keep, misc, spec, gspec, net, fourth, delta,
        position_table(length), *tables,
    )

def reduce_kernel(
    n, m, g, chan, out, filt, chan_out, r0, sum0, r1, sum1, r2, sum2, r3, rchan, send_sem, recv_sem
):
    me, b = lax.axis_index("chan"), lax.axis_index("batch")
    barrier = pltpu.get_barrier_semaphore()
    for d in range(1, n):
        pl.semaphore_signal(
            barrier, inc=1, device_id={"chan": lax.rem(me + d, n)}, device_id_type=MESH
        )
    for d in range(1, m):
        pl.semaphore_signal(
            barrier, inc=1, device_id={"batch": lax.rem(b + d, m)}, device_id_type=MESH
        )
    pl.semaphore_wait(barrier, n - 1 + m - 1)
    quarter = g.shape[1] // m
    half = n // 2
    x, z = lax.rem(me, 2), me // 2
    core, y = lax.rem(b, 2), b // 2

    def part(k):
        return pl.ds(pl.multiple_of(k * quarter, 8), quarter)

    mate = {"batch": 2 * y + 1 - core}
    copies = exchange(
        [(g.at[:, part(2 * k + 1 - core)], r0.at[k]) for k in range(2)], [mate] * 2, send_sem, recv_sem, 0
    )
    small = exchange(
        [(chan, rchan.at[d - 1]) for d in range(1, m)],
        [{"batch": lax.rem(b + d, m)} for d in range(1, m)],
        send_sem, recv_sem, 2,
    )
    for k in range(2):
        copies[k].wait()

        def add0(i, _, k=k):
            sum0[k, i] = g[i, part(2 * k + core), :] + r0[k, i]
            return 0

        lax.fori_loop(0, n, add0, 0)
    copies = exchange([(sum0.at[1 - y], r1)], [{"batch": 2 * (1 - y) + core}], send_sem, recv_sem, 5)
    for copy in small:
        copy.wait()
    chan_out[...] = chan[...] + rchan[0] + rchan[1] + rchan[2]
    copies[0].wait()

    def add1(i, _):
        sum1[lax.rem(i, 2), i // 2] = sum0[y, i] + r1[i]
        return 0

    lax.fori_loop(0, n, add1, 0)
    copies = exchange([(sum1.at[1 - x], r2)], [{"chan": 2 * z + 1 - x}], send_sem, recv_sem, 6)
    copies[0].wait()

    def add2(i, _):
        sum2[i] = sum1[x, i] + r2[i]
        return 0

    lax.fori_loop(0, half, add2, 0)
    copies = []
    for d in range(1, half):
        to = lax.rem(z + d, half)
        copies += exchange(
            [(sum2.at[to], r3.at[d - 1])], [{"chan": 2 * to + x}], send_sem, recv_sem, 6 + d
        )
    for copy in copies:
        copy.wait()
    total = sum2[z]
    for d in range(1, half):
        total = total + r3[d - 1]
    mine = part(b)
    out[mine, :] = total
    copy = send(out.at[mine], out.at[mine], (send_sem, recv_sem), 6 + half, {"batch": y_mate(b)})
    copy.wait()
    copies = exchange(
        [(out.at[part(k)], out.at[part(k)]) for k in (b, y_mate(b))], [mate] * 2,
        send_sem, recv_sem, 7 + half,
    )
    for copy in copies:
        copy.wait()
    last = pl.ds(out.shape[0] - filt.shape[1], filt.shape[1])
    filt[me] = out[last, :]
    copies = exchange(
        [(filt.at[me], filt.at[me]) for d in range(1, n)],
        [{"chan": lax.rem(me + d, n)} for d in range(1, n)],
        send_sem, recv_sem, 6 + half + m,
    )
    for copy in copies:
        copy.wait()


def reduce_gradients(g, chan, filter_rows, n, m, cid):
    quarter = g.shape[1] // m
    half = n // 2
    count = 6 + half + m + n
    return pl.pallas_call(
        partial(reduce_kernel, n, m),
        in_specs=[WHOLE, WHOLE],
        out_specs=[WHOLE] * 3,
        out_shape=[sds(*g.shape[1:]), sds(n, filter_rows, D), sds(*chan.shape)],
        scratch_shapes=[
            VMEM((2, n, quarter, D), F32),
            VMEM((2, n, quarter, D), F32),
            VMEM((n, quarter, D), F32),
            VMEM((2, half, quarter, D), F32),
            VMEM((half, quarter, D), F32),
            VMEM((half, quarter, D), F32),
            VMEM((half - 1, quarter, D), F32),
            VMEM((m - 1, *chan.shape), F32),
            pltpu.SemaphoreType.DMA((count,)),
            pltpu.SemaphoreType.DMA((count,)),
        ],
        compiler_params=comm_params(cid),
        name="reduce_gradients",
    )(g, chan)


def onehot_rows(tokens):
    row = lax.broadcasted_iota(jnp.int32, (D, tokens.shape[1]), 0)
    return (row == tokens + EMB0).astype(F32)


class Layer:
    def __init__(self, w, misc, index):
        self.n, rows, _ = w.shape
        self.c = rows // 12
        self.w = w
        self.side = misc[...]
        self.index = index

    def rows(self, start, count):
        return self.w[:, start * self.c : (start + count) * self.c, :].reshape(
            self.n * count * self.c, D
        )

    def column(self, lane):
        return self.side[:, lane : lane + 1]

    def vec(self, k):
        return self.column(VEC0 + 9 * self.index + k)

    def off(self, k):
        return self.column(OFF0 + 4 * self.index + k)

    def inward(self):
        return self.rows(0, 3)

    def outward(self):
        return self.rows(3, 1)

    def expand(self, k):
        return self.rows(4 + k, 1)

    def contract(self, k):
        return self.rows(8 + k, 1)


def front_forward(lay, x):
    xh, _ = normalize(x)
    normed = xh * lay.vec(0) + lay.vec(1)
    p = dot(lay.inward(), normed).reshape(lay.n, 3, lay.c, x.shape[1])
    return [p[:, j].reshape(D, x.shape[1]) + lay.vec(4 + j) for j in range(3)]


def front_backward(lay, x, dp, dh, dw):
    xh, scale = normalize(x)
    normed = xh * lay.vec(0) + lay.vec(1)
    width = x.shape[1]
    stacked = jnp.stack([d.reshape(lay.n, lay.c, width) for d in dp], axis=1)
    stacked = stacked.reshape(3 * D, width)
    dn = dot_tn(lay.inward(), stacked)
    dw[...] += dot_nt(stacked, normed).reshape(dw.shape)
    base = VEC0 + 9 * lay.index
    columns = [(base + 4 + j, row_sum(dp[j])) for j in range(3)]
    columns += [(base, row_sum(dn * xh)), (base + 1, row_sum(dn))]
    return dh + normalize_back(dn * lay.vec(0), xh, scale), columns


def rear_mix(lay, x, y):
    return x + dot(lay.outward(), y) + lay.vec(7)


def rear_hidden(lay, h):
    xh, scale = normalize(h)
    m = xh * lay.vec(2) + lay.vec(3)
    a = [dot(lay.expand(k), m) + lay.off(k) for k in range(4)]
    return xh, scale, m, a


def rear_out(lay, h, u):
    out = h + lay.vec(8)
    for k in range(4):
        out = out + dot(lay.contract(k), u[k])
    return out


def rear_backward(lay, h, a, y, dout, dw):
    n, c = lay.n, lay.c
    xh, scale = normalize(h)
    m = xh * lay.vec(2) + lay.vec(3)
    base = VEC0 + 9 * lay.index
    columns = [(base + 8, row_sum(dout))]
    dm = None
    for k in range(4):
        ak = a[k]
        g, t = gelu_parts(ak)
        u = ak * g
        dw[:, (5 + k) * c : (6 + k) * c, :] += dot_nt(dout, u).reshape(n, c, D)
        slope = g + 0.5 * ak * (1.0 - t * t) * (GELU_SCALE * (1.0 + 3.0 * GELU_CUBE * ak * ak))
        dpre = dot_tn(lay.contract(k), dout) * slope
        dw[:, (1 + k) * c : (2 + k) * c, :] += dot_nt(dpre, m).reshape(n, c, D)
        columns.append((OFF0 + 4 * lay.index + k, row_sum(dpre)))
        term = dot_tn(lay.expand(k), dpre)
        dm = term if dm is None else dm + term
    dh = dout + normalize_back(dm * lay.vec(2), xh, scale)
    columns += [(base + 2, row_sum(dm * xh)), (base + 3, row_sum(dm)), (base + 7, row_sum(dh))]
    dw[:, 0:c, :] += dot_nt(dh, y).reshape(n, c, D)
    return dh, dot_tn(lay.outward(), dh), columns


def joined(ref):
    groups, n, _, span, _ = ref.shape
    return jnp.concatenate(
        [
            jnp.concatenate(
                [ref[k, j, 0, b : b + EIGHT, :] for j in range(n) for k in range(groups)], axis=0
            )
            for b in range(0, span, EIGHT)
        ],
        axis=1,
    )


def split(ref, value):
    groups, n, _, span, _ = ref.shape
    for q in range(span // EIGHT):
        for j in range(n):
            for k in range(groups):
                row = (j * groups + k) * EIGHT
                ref[k, j, 0, q * EIGHT : (q + 1) * EIGHT, :] = value[
                    row : row + EIGHT, q * LANES : (q + 1) * LANES
                ]


def first_step():
    return (pl.program_id(0) == 0) & (pl.program_id(1) == 0)


def front0_kernel(tokx, w0, misc, p, q):
    lay = Layer(w0, misc, 0)
    xh, _ = normalize(lay.side)
    normed = xh * lay.vec(0) + lay.vec(1)
    rows = dot(lay.inward(), normed, HIGHEST).reshape(lay.n, 3, lay.c, D)
    width = tokx.shape[2]
    names = lax.broadcasted_iota(jnp.int32, (VOCAB, width), 0).astype(F32)
    here, one, two = [(names == tokx[0, k : k + 1, :]).astype(F32) for k in range(3)]
    places = jnp.concatenate([two, one, here], axis=0)
    lane = lax.broadcasted_iota(jnp.int32, (D, LANES), 1)
    for j in range(3):
        table = rows[:, j].reshape(D, D) + lay.vec(4 + j)
        table = jnp.where(lane < VOCAB, pltpu.roll(table, D - EMB0, 1)[:, :LANES], 0.0)
        p[j, 0] = dot(table[:, :VOCAB], here, HIGHEST)
        t = TAP0 + 3 * j
        mix = (
            lay.column(t) * table
            + lay.column(t + 1) * pltpu.roll(table, VOCAB, 1)
            + lay.column(t + 2) * pltpu.roll(table, 2 * VOCAB, 1)
        )
        q[j, 0] = dot(mix[:, : 3 * VOCAB], places, HIGHEST) + lay.column(TAP0 + 9 + j)


def mid_kernel(tok, z, q0, w0, w1, misc, h, a, x1, p):
    lay = Layer(w0, misc, 0)
    x = dot(lay.side, onehot_rows(tok[0]), HIGHEST)
    mixed = rear_mix(lay, x, joined(z) * q0[0, 0])
    h[0] = mixed
    _, _, _, pre = rear_hidden(lay, mixed)
    u = []
    for k in range(4):
        a[0, k] = pre[k]
        u.append(pre[k] * gelu_parts(pre[k])[0])
    x = rear_out(lay, mixed, u)
    x1[0] = x
    for j, value in enumerate(front_forward(Layer(w1, misc, 1), x)):
        p[j, 0] = value


def top_kernel(x1, z, q0, cot, w1, misc, x2, dz, dq0, dh_out, dw, cols):
    @pl.when(first_step())
    def _():
        dw[...] = jnp.zeros_like(dw)
        cols[...] = jnp.zeros_like(cols)

    lay = Layer(w1, misc, 1)
    zt, qt = joined(z), q0[0, 0]
    y = zt * qt
    h = rear_mix(lay, x1[0], y)
    _, _, _, pre = rear_hidden(lay, h)
    x2[0] = rear_out(lay, h, [v * gelu_parts(v)[0] for v in pre])
    dh, dy, columns = rear_backward(lay, h, pre, y, cot[0], dw)
    split(dz, dy * qt)
    dq0[0] = dy * zt
    dh_out[0] = dh
    cols[...] += put_columns(columns)


def mid_back_kernel(
    dp, x1, dh1, h, a, z, q0, w0, w1, misc, dz, dq0, dh_out, dw_front, dw, cols
):
    @pl.when(first_step())
    def _():
        dw_front[...] = jnp.zeros_like(dw_front)
        dw[...] = jnp.zeros_like(dw)
        cols[...] = jnp.zeros_like(cols)

    upper = Layer(w1, misc, 1)
    dout, columns = front_backward(upper, x1[0], [dp[j, 0] for j in range(3)], dh1[0], dw_front)
    lay = Layer(w0, misc, 0)
    zt, qt = joined(z), q0[0, 0]
    dh, dy, more = rear_backward(lay, h[0], [a[0, k] for k in range(4)], zt * qt, dout, dw)
    split(dz, dy * qt)
    dq0[0] = dy * zt
    dh_out[0] = dh
    cols[...] += put_columns(columns + more)


def front0_back_kernel(dp, tok, dh0, w0, misc, dx, dw_front, cols):
    @pl.when(first_step())
    def _():
        dw_front[...] = jnp.zeros_like(dw_front)
        cols[...] = jnp.zeros_like(cols)

    lay = Layer(w0, misc, 0)
    places = onehot_rows(tok[0])
    x = dot(lay.side, places, HIGHEST)
    grad, columns = front_backward(lay, x, [dp[j, 0] for j in range(3)], dh0[0], dw_front)
    dx[0] = grad
    cols[...] += put_columns(columns) + dot_nt(grad, places)


def token_call(kernel, name, seqs, width, n, ins, outs, args, out_shape, gflops):
    specs = {
        "tok": pl.BlockSpec((1, 1, TILE), lambda s, t: (s, 0, t)),
        "pos": pl.BlockSpec((1, D, TILE), lambda s, t: (s, 0, t)),
        "blk": pl.BlockSpec(
            (D // n // EIGHT, n, 1, TILE // LANES * EIGHT, LANES), lambda s, t: (0, 0, s, t, 0)
        ),
        "tokx": pl.BlockSpec((1, EIGHT, TILE), lambda s, t: (s, 0, t)),
        "q0": pl.BlockSpec((1, 1, D, TILE), lambda s, t: (0, s, 0, t)),
        "three": pl.BlockSpec((3, 1, D, TILE), lambda s, t: (0, s, 0, t)),
        "hid": pl.BlockSpec((1, 4, D, TILE), lambda s, t: (s, 0, 0, t)),
    }

    def spec(item):
        if isinstance(item, str):
            return specs[item]
        return item

    return pl.pallas_call(
        kernel,
        grid=(seqs, width // TILE),
        in_specs=[spec(i) for i in ins],
        out_specs=[spec(o) for o in outs],
        out_shape=out_shape,
        compiler_params=pltpu.CompilerParams(vmem_limit_bytes=VMEM_LIMIT),
        cost_estimate=cost(gflops * 1e9, 1e7),
        name=name,
    )(*args)


def update_kernel(scale, *refs):
    rows, filt, chan, folded, off = refs[:5]
    weights, moments, averages = refs[5:14], refs[14:23], refs[23:32]
    outs = refs[32:]
    chans = chan.shape[0]
    flat = rows[24 * chans : 25 * chans, :].T
    chan_rows = chan[...].T

    def step(which, index, gradient):
        factor = STEP_RATES[which] * scale
        velocity = MOMENTUM * moments[which][index] + gradient
        updated = weights[which][index] - factor * (gradient + MOMENTUM * velocity)
        running = AVERAGING * averages[which][index] + (1.0 - AVERAGING) * updated
        base = 4 * which
        outs[base][index] = velocity
        outs[base + 1][index] = running
        outs[base + 2][index] = updated
        outs[base + 3][index] = updated.astype(BF16)

    step(0, Ellipsis, flat[EMB0 : EMB0 + VOCAB])
    step(5, Ellipsis, off[...])
    step(6, Ellipsis, folded[...])
    filters = filt[...].reshape(-1, D)[:136, :LANES]
    for k in range(LAYERS):
        base = 12 * chans * k
        for j in range(3):
            step(1, (k, j), rows[base + j * chans : base + (j + 1) * chans, :])
        step(2, k, flat[VEC0 + 9 * k : VEC0 + 9 * k + 9])
        step(3, k, rows[base + 3 * chans : base + 4 * chans, :])
        step(4, k, rows[base + 4 * chans : base + 8 * chans, :])
        step(
            7,
            k,
            jnp.concatenate(
                [
                    flat[TAP0 + 12 * k : TAP0 + 12 * k + 12],
                    chan_rows[(FO + 1) * k : (FO + 1) * (k + 1)],
                ],
                axis=0,
            ),
        )
        step(8, k, filters[:, k * FO : (k + 1) * FO])


def per_device(*arguments):
    (token_ids, embedding, inward, vectors, outward, expand, offsets, contract, channels, filters) = arguments[:10]
    weights = arguments[1:10]
    moments = arguments[10:19]
    averages = arguments[19:28]
    cotangent = arguments[28]
    n, m = lax.axis_size("chan"), lax.axis_size("batch")
    seqs, width = token_ids.shape
    length = width * n
    chans = channels.shape[2]
    groups = chans // EIGHT
    tables = fourier_tables(length)

    def shard_rows(layer):
        folded = contract[layer].reshape(chans, n, 4, chans).transpose(2, 0, 1, 3)
        return [
            inward[layer].reshape(3 * chans, D),
            outward[layer],
            expand[layer],
            folded.reshape(4 * chans, D),
        ]

    side = jnp.concatenate(
        [
            vectors.reshape(18, chans).T,
            channels[:, :12].reshape(24, chans).T,
            embedding.T,
            offsets.reshape(8, chans).T,
            jnp.zeros((chans, D - OFF0 - 8), F32),
        ],
        axis=1,
    )
    own = jnp.concatenate(shard_rows(0) + shard_rows(1), axis=0)
    names = token_ids.astype(F32).reshape(-1, D)
    names = jnp.pad(names, ((0, EIGHT - names.shape[0]), (0, 0)))
    first_chan = lax.axis_index("chan") * chans
    chan_ids = (first_chan + jnp.arange(chans)).astype(F32)
    slow = math.log(0.01) / 1.5
    fast = math.log(0.01) / 0.3
    delta = jnp.abs(slow + (fast - slow) * chan_ids / (D - 1))[:, None]
    nets = [jnp.pad(filters[k], ((0, 8), (0, 0))) for k in range(LAYERS)]
    fourths = [channels[k, 13:] for k in range(LAYERS)]
    skips = [channels[k, 12][:, None] for k in range(LAYERS)]
    gathered, misc, _, tokx, spec0, spec1, gspec0, keep0, keep1, z0 = prepare(
        own, side, names, inward[0].reshape(3 * chans, D), nets, fourths, delta, skips, tables,
        n, seqs, length, 1,
    )
    weight_spec = [
        pl.BlockSpec((n, 12 * chans, D), lambda s, t, k=k: (0, k, 0)) for k in range(LAYERS)
    ]
    misc_spec = pl.BlockSpec((D, D), lambda s, t: (0, 0))
    tokens = token_ids.reshape(seqs, 1, width)

    pos = sds(seqs, D, width)
    blk = sds(groups, n, seqs, width // LANES * EIGHT, LANES)
    three = sds(3, seqs, D, width)
    front_sum = pl.BlockSpec((n, 3 * chans, D), lambda s, t: (0, 0, 0))
    rear_sum = pl.BlockSpec((n, 9 * chans, D), lambda s, t: (0, 0, 0))
    col_sum = pl.BlockSpec((D, D), lambda s, t: (0, 0))
    call = partial(token_call, seqs=seqs, width=width, n=n)

    p0, q0 = call(
        front0_kernel, "front0", ins=["tokx", weight_spec[0], misc_spec], outs=["three", "three"],
        args=(tokx, gathered, misc), out_shape=[three, three], gflops=1,
    )
    h0, a0, x1, p1 = call(
        mid_kernel, "mid", ins=["tok", "blk", "q0", *weight_spec, misc_spec],
        outs=["pos", "hid", "pos", "three"],
        args=(tokens, z0, q0, gathered, gathered, misc),
        out_shape=[pos, sds(seqs, 4, D, width), pos, three], gflops=5,
    )
    q1, gspec1, z1 = mixer(p1, misc, spec1, tables, n, chans, TAP0 + 12, 2)
    activations, dz1, dq1, dh1, dw_rear1, cols_top = call(
        top_kernel, "top",
        ins=["pos", "blk", "q0", "pos", weight_spec[1], misc_spec],
        outs=["pos", "blk", "pos", "pos", rear_sum, col_sum],
        args=(x1, z1, q1, cotangent, gathered, misc),
        out_shape=[pos, blk, pos, pos, sds(n, 9 * chans, D), sds(D, D)], gflops=9,
    )
    dp1, cols_taps1, dnet1, dfourth1, dk1 = mixer_back(
        dz1, q1, dq1, p1, keep1, misc, spec1, gspec1, nets[1], fourths[1], delta, tables,
        n, chans, TAP0 + 12, 3,
    )
    dz0, dq0, dh0, dw_front1, dw_rear0, cols_mid = call(
        mid_back_kernel, "mid_back",
        ins=["three", "pos", "pos", "pos", "hid", "blk", "q0", *weight_spec, misc_spec],
        outs=["blk", "pos", "pos", front_sum, rear_sum, col_sum],
        args=(dp1, x1, dh1, h0, a0, z0, q0, gathered, gathered, misc),
        out_shape=[blk, pos, pos, sds(n, 3 * chans, D), sds(n, 9 * chans, D), sds(D, D)],
        gflops=9,
    )
    dp0, cols_taps0, dnet0, dfourth0, dk0 = mixer_back(
        dz0, q0, dq0, p0, keep0, misc, spec0, gspec0, nets[0], fourths[0], delta, tables,
        n, chans, TAP0, 4,
    )
    input_gradient, dw_front0, cols_low = call(
        front0_back_kernel, "front0_back",
        ins=["three", "tok", "pos", weight_spec[0], misc_spec],
        outs=["pos", front_sum, col_sum],
        args=(dp0, tokens, dh0, gathered, misc),
        out_shape=[pos, sds(n, 3 * chans, D), sds(D, D)], gflops=2,
    )

    cols = cols_top + cols_taps1 + cols_mid + cols_taps0 + cols_low
    filter_rows = -(-136 // (n * EIGHT)) * EIGHT
    dnet = jnp.concatenate(
        [
            jnp.concatenate([v[:6], v[8:73], v[80:145]], axis=0)
            for v in (dnet0, dnet1)
        ],
        axis=1,
    )
    dnet = jnp.pad(dnet, ((0, n * filter_rows - 136), (0, D - 2 * FO)))
    pad = -(25 * chans + filter_rows) % 32
    grads = jnp.concatenate(
        [
            dw_front0, dw_rear0, dw_front1, dw_rear1,
            cols.reshape(n, chans, D),
            jnp.zeros((n, pad, D), F32),
            dnet.reshape(n, filter_rows, D),
        ],
        axis=1,
    )
    dchan = jnp.concatenate(
        [
            dk0[:, :1], dfourth0.T, dk1[:, :1], dfourth1.T,
            jnp.zeros((chans, D - 2 * (FO + 1)), F32),
        ],
        axis=1,
    )
    rows, filt, chan = reduce_gradients(grads, dchan, filter_rows, n, m, 5)

    blocks = rows[: 24 * chans].reshape(LAYERS, 12, chans, n, chans)
    folded = blocks[:, 8:].transpose(0, 2, 3, 1, 4).reshape(LAYERS, chans, FF)
    off = rows[24 * chans : 25 * chans, OFF0 : OFF0 + 8].T.reshape(LAYERS, 4 * chans)
    scale = 1.0 / math.sqrt(seqs * m * length)
    shapes = []
    for weight in weights:
        shapes += [sds(*weight.shape)] * 3 + [jax.ShapeDtypeStruct(weight.shape, BF16)]
    updates = pl.pallas_call(
        partial(update_kernel, scale),
        in_specs=[WHOLE] * 32,
        out_specs=[WHOLE] * 36,
        out_shape=shapes,
        compiler_params=pltpu.CompilerParams(vmem_limit_bytes=VMEM_LIMIT),
        name="update",
    )(rows, filt, chan, folded, off, *weights, *moments, *averages)
    return (activations, input_gradient) + tuple(updates)


def solution(mesh):
    in_weights = (
        P(None, "chan"),
        P(None, None, "chan", None),
        P(None, None, "chan"),
        P(None, "chan", None),
        P(None, "chan", None),
        P(None, "chan"),
        P(None, "chan", None),
        P(None, None, "chan"),
        P(),
    )
    tokens = P("batch", None, "chan")
    in_specs = (P("batch", "chan"),) + in_weights * 3 + (tokens,)
    out_specs = (tokens, tokens) + tuple(spec for spec in in_weights for _ in range(4))
    return jax.shard_map(
        per_device, mesh=mesh, in_specs=in_specs, out_specs=out_specs, check_vma=False
    )
```

```python
from functools import partial
import math

import jax
import jax.numpy as jnp
import numpy as np
from jax import lax
from jax.experimental import pallas as pl
from jax.experimental.pallas import tpu as pltpu
from jax.sharding import PartitionSpec as P

D = 256
FF = 1024
FO = 64
EMB = 5
VOCAB = 16
LAYERS = 2
LANES = 128
TILE = 256

HIGH = lax.Precision.HIGH
HIGHEST = lax.Precision.HIGHEST
EPSILON = 1e-05
MOMENTUM = 0.9
AVERAGING = 0.9
WINDOW_SHIFT = 0.05
FREQUENCY = 10.0
STEP_RATES = (0.7, 0.06, 0.1, 0.037, 0.1, 0.16, 0.025, 0.2, 0.0002)
GELU_SCALE = math.sqrt(2.0 / math.pi)
GELU_CUBE = 0.044715

MESH = pl.DeviceIdType.MESH
VMEM = pltpu.VMEM
WHOLE = pl.BlockSpec(memory_space=pltpu.VMEM)
HBM = pl.BlockSpec(memory_space=pl.ANY)
VMEM_LIMIT = 58 * 1024 * 1024
F32 = jnp.float32
BF16 = jnp.bfloat16

VEC0 = 0
TAP0 = 18
EMB0 = 42
OFF0 = 58
EIGHT = 8


def dot(a, b, precision=HIGH):
    return jnp.dot(a, b, precision=precision, preferred_element_type=F32)


def dot_nt(a, b, precision=HIGH):
    return lax.dot_general(
        a, b, (((1,), (1,)), ((), ())), precision=precision, preferred_element_type=F32
    )


def dot_tn(a, b, precision=HIGH):
    return lax.dot_general(
        a, b, (((0,), (0,)), ((), ())), precision=precision, preferred_element_type=F32
    )


def sds(*shape):
    return jax.ShapeDtypeStruct(shape, F32)


def cost(flops, moved):
    return pl.CostEstimate(flops=int(flops), bytes_accessed=int(moved), transcendentals=0)


def position_table(length):
    indices = np.arange(length, dtype=np.float32)
    fraction = indices / np.float32(length - 1)
    angles = np.float32(2.0 * math.pi) * indices / np.float32(length)
    bands = (EMB - 1) // 2
    frequency = np.linspace(0.0001, bands - 1, bands).astype(np.float32)
    turned = (frequency[:, None] * angles[None, :]).astype(np.float32).astype(np.float64)
    table = np.zeros((8, length), np.float32)
    table[0] = fraction
    table[1 : 1 + bands] = np.cos(turned)
    table[1 + bands : 1 + 2 * bands] = -np.sin(turned)
    table[EMB] = 1.0
    return table


def split_table(table):
    high = table.astype(np.float32).astype(jnp.bfloat16)
    low = (table.astype(np.float32) - high.astype(np.float32)).astype(jnp.bfloat16)
    return high, low


def left_table(table):
    high, low = split_table(table)
    return np.concatenate([high, high, low], axis=1)


def right_table(table):
    high, low = split_table(table)
    return np.concatenate([high, high, low], axis=0)


def fourier_tables(length):
    rows = length // LANES
    outer = 2 * rows
    total = outer * LANES
    turn = 2.0 * np.pi / outer * (np.arange(outer)[:, None] * np.arange(rows)[None, :] % outer)
    c, s = np.cos(turn), np.sin(turn)
    first = np.block([[c, s], [-s, c]])
    first_real = np.block([[c], [-s]])
    last = np.block([[c.T, -s.T], [s.T, c.T]]) / total
    last_real = np.block([[c.T, -s.T]]) / total
    twist = 2.0 * np.pi / total * (np.arange(outer)[:, None] * np.arange(LANES)[None, :])
    twiddle = np.concatenate([np.cos(twist), -np.sin(twist)], axis=1).astype(np.float32)
    lane = 2.0 * np.pi / LANES * (np.arange(LANES)[:, None] * np.arange(LANES)[None, :] % LANES)
    c, s = np.cos(lane), np.sin(lane)
    second = np.block([[c, -s], [s, c]])
    second_back = np.block([[c, s], [-s, c]])
    return (
        left_table(first),
        left_table(first_real),
        twiddle,
        right_table(second),
        right_table(second_back),
        left_table(last),
        left_table(last_real),
    )


def sin_cos(x):
    turns = jnp.round(x * (1.0 / math.pi))
    r = x - turns * 3.140625
    r = r - turns * 9.67025756835937500e-4
    r = r - turns * 6.27711415290832520e-7
    r = r - turns * 1.21542010130123850e-10
    half = turns * 0.5
    sign = 1.0 - 4.0 * jnp.abs(half - jnp.round(half))
    r2 = r * r
    s = -2.5052108385441720e-8
    for k in (2.7557319223985893e-6, -1.9841269841269841e-4, 8.3333333333333333e-3, -1.6666666666666667e-1):
        s = s * r2 + k
    s = r + r * (r2 * s)
    c = 2.0876756987868099e-9
    for k in (-2.7557319223985888e-7, 2.4801587301587302e-5, -1.3888888888888889e-3, 4.1666666666666667e-2, -0.5):
        c = c * r2 + k
    c = 1.0 + r2 * c
    return s * sign, c * sign


def window(delta, length, start, width):
    t = lax.broadcasted_iota(jnp.int32, (1, width), 1) + start
    fraction = t.astype(F32) / (length - 1)
    return jnp.exp(-delta * fraction) + WINDOW_SHIFT


def normalize(x):
    center = x - jnp.mean(x, axis=0, keepdims=True)
    spread = jnp.mean(center * center, axis=0, keepdims=True)
    scale = lax.rsqrt(spread + EPSILON)
    return center * scale, scale


def normalize_back(e, xh, scale):
    return scale * (
        e - jnp.mean(e, axis=0, keepdims=True) - xh * jnp.mean(e * xh, axis=0, keepdims=True)
    )


def gelu_parts(a):
    t = jnp.tanh(GELU_SCALE * (a + GELU_CUBE * a * a * a))
    return 0.5 * (1.0 + t), t


def put_columns(pairs, width=D):
    rows = pairs[0][1].shape[0]
    lane = lax.broadcasted_iota(jnp.int32, (rows, width), 1)
    out = jnp.zeros((rows, width), F32)
    for k, column in pairs:
        out = out + jnp.where(lane == k, column, 0.0)
    return out


def row_sum(x):
    return jnp.sum(x, axis=1, keepdims=True)


def ones_rows(width):
    return (lax.broadcasted_iota(jnp.int32, (EIGHT, width), 0) == 0).astype(F32)


def filter_block(length, start, feat, net, fourth, delta):
    width = feat.shape[1]
    kept = []
    h, c = sin_cos(FREQUENCY * dot(net[:, 0:EIGHT], feat, HIGHEST))
    kept.append((h, FREQUENCY * c))
    for row in (EMB + 1, EMB + 2 + FO):
        v = dot(net[:, row : row + FO], h, HIGHEST) + net[:, row + FO : row + FO + 1]
        h, c = sin_cos(FREQUENCY * v)
        kept.append((h, FREQUENCY * c))
    return dot(fourth, h, HIGHEST) * window(delta, length, start, width), kept


def filter_back_block(length, start, feat, net, fourth, delta, keep, dk, dnet, dfourth):
    width = feat.shape[1]
    ones = ones_rows(width)
    dkw = dk * window(delta, length, start, width)
    dfourth[:, 0:FO] += dot_nt(dkw, keep[2])
    dpre = dot_tn(fourth, dkw) * keep[5]
    row = EMB + 2 + FO
    dnet[2, :, 0 : FO + EIGHT] += dot_nt(dpre, jnp.concatenate([keep[1], ones], axis=0))
    dpre = dot_tn(net[:, row : row + FO], dpre) * keep[4]
    row = EMB + 1
    dnet[1, :, 0 : FO + EIGHT] += dot_nt(dpre, jnp.concatenate([keep[0], ones], axis=0))
    dpre = dot_tn(net[:, row : row + FO], dpre) * keep[3]
    dnet[0, :, 0:EIGHT] += dot_nt(dpre, feat)


def widened(value, width=LANES):
    rows, lanes = value.shape
    return jnp.concatenate([value, jnp.zeros((rows, width - lanes), F32)], axis=1)


def paired(tile, count):
    high = tile.astype(BF16).astype(F32)
    return (high + pltpu.roll(tile - high, count, 1)).astype(BF16)


def named_dot(table, places):
    rows = jnp.concatenate(places + places, axis=0)
    rest = LANES - rows.shape[0]
    rows = jnp.concatenate([rows, jnp.zeros((rest, rows.shape[1]), F32)], axis=0)
    return jnp.dot(table, rows.astype(BF16), preferred_element_type=F32)


def halves(x):
    high = x.astype(BF16)
    return high, (x - high.astype(F32)).astype(BF16)


def left_dot(table, x):
    high, low = halves(x)
    return jnp.dot(
        table, jnp.concatenate([high, low, high], axis=0), preferred_element_type=F32
    )


def right_dot(x, table):
    high, low = halves(x)
    return jnp.dot(
        jnp.concatenate([high, low, high], axis=1), table, preferred_element_type=F32
    )


def spectrum_of(x, first, twiddle, second):
    outer = twiddle.shape[0]
    y = left_dot(first, x)
    tr, ti = twiddle[:, :LANES], twiddle[:, LANES:]
    parts = []
    for b in range(x.shape[1] // LANES):
        yr = y[:outer, b * LANES : (b + 1) * LANES]
        yi = y[outer:, b * LANES : (b + 1) * LANES]
        parts.append(jnp.concatenate([yr * tr - yi * ti, yr * ti + yi * tr], axis=1))
    return right_dot(jnp.concatenate(parts, axis=0), second)


def signal_of(v, twiddle, second_back, last):
    outer = twiddle.shape[0]
    a = right_dot(v, second_back)
    tr, ti = twiddle[:, :LANES], twiddle[:, LANES:]
    parts = []
    for b in range(v.shape[0] // outer):
        ar = a[b * outer : (b + 1) * outer, :LANES]
        ai = a[b * outer : (b + 1) * outer, LANES:]
        parts.append(jnp.concatenate([ar * tr + ai * ti, ai * tr - ar * ti], axis=0))
    return left_dot(last, jnp.concatenate(parts, axis=1))


def load_pairs(ref):
    rows = ref.shape[1] // EIGHT
    parts = []
    for b in range(EIGHT):
        parts.append(
            jnp.concatenate([ref[s, pl.ds(b, rows, stride=EIGHT), :] for s in range(2)], axis=0)
        )
    return jnp.concatenate(parts, axis=1)


def store_pairs(ref, value):
    rows = ref.shape[1] // EIGHT
    for b in range(EIGHT):
        for s in range(2):
            ref[s, pl.ds(b, rows, stride=EIGHT), :] = value[
                s * rows : (s + 1) * rows, b * LANES : (b + 1) * LANES
            ]


def times(a, b):
    ar, ai, br, bi = a[:, :LANES], a[:, LANES:], b[:, :LANES], b[:, LANES:]
    return jnp.concatenate([ar * br - ai * bi, ar * bi + ai * br], axis=1)


def times_conj(a, b):
    ar, ai, br, bi = a[:, :LANES], a[:, LANES:], b[:, :LANES], b[:, LANES:]
    return jnp.concatenate([ar * br + ai * bi, ai * br - ar * bi], axis=1)


def send(a, b, sems, index, device):
    copy = remote(a, b, sems, index, device)
    copy.start()
    return copy


def remote(a, b, sems, index, device):
    return pltpu.make_async_remote_copy(
        src_ref=a, dst_ref=b, send_sem=sems[0].at[index], recv_sem=sems[1].at[index],
        device_id=device, device_id_type=MESH,
    )


def exchange(refs, peers, send_sem, recv_sem, base):
    return [
        send(a, b, (send_sem, recv_sem), base + k, peer)
        for k, ((a, b), peer) in enumerate(zip(refs, peers))
    ]


def greet(n, mates=()):
    me, b = lax.axis_index("chan"), lax.axis_index("batch")
    barrier = pltpu.get_barrier_semaphore()
    for d in range(1, n):
        pl.semaphore_signal(
            barrier, inc=1, device_id={"chan": lax.rem(me + d, n)}, device_id_type=MESH
        )
    for mate in mates:
        pl.semaphore_signal(barrier, inc=1, device_id={"batch": mate}, device_id_type=MESH)
    pl.semaphore_wait(barrier, n - 1 + len(mates))


def core_mate(b):
    return b + 1 - 2 * lax.rem(b, 2)


def y_mate(b):
    return b + 2 - 4 * (b // 2)


def comm_params(cid):
    return pltpu.CompilerParams(
        collective_id=cid, has_side_effects=True, vmem_limit_bytes=VMEM_LIMIT
    )


def pair_sems(*shape):
    return [pltpu.SemaphoreType.DMA(shape), pltpu.SemaphoreType.DMA(shape)]


class Blocks:
    def __init__(self, n, span, sems, own):
        self.n, self.span, self.sems, self.own = n, span, sems, own
        self.me = lax.axis_index("chan")

    def rows(self, j):
        return pl.ds(pl.multiple_of(j * self.span, 8), self.span)

    def out_refs(self, k, j, src, dst):
        return src.at[k, j], dst.at[k, :, self.rows(self.me), :]

    def back_refs(self, k, j, src, dst):
        return src.at[k, :, self.rows(j), :], dst.at[k, self.me]

    def each(self, refs, k, src, dst):
        for d in range(1, self.n):
            j = lax.rem(self.me + d, self.n)
            a, b = refs(k, j, src, dst)
            yield remote(a, b, self.sems, (k, d), {"chan": j})

    def start(self, refs, k, src, dst):
        a, b = refs(k, self.me, src, dst)
        pltpu.make_async_copy(a, b, self.own.at[k]).start()
        for copy in self.each(refs, k, src, dst):
            copy.start()

    def arrived(self, refs, k, src, dst):
        for copy in self.each(refs, k, src, dst):
            copy.wait_recv()
        a, b = refs(k, self.me, src, dst)
        pltpu.make_async_copy(a, b, self.own.at[k]).wait()

    def sent(self, refs, k, src, dst):
        for copy in self.each(refs, k, src, dst):
            copy.wait_send()


def loop(count, body):
    def step(i, _):
        body(i)
        return 0

    lax.fori_loop(0, count, step, 0)


def round_up(value, step):
    return -(-value // step) * step


def quarter_rows(refs_rows, k):
    quarter = refs_rows // 4
    return pl.ds(pl.multiple_of(k * quarter, 8), quarter)


def fold(value, n, chans, back=False):
    lane = lax.broadcasted_iota(jnp.int32, (chans, LANES), 1)
    wide = 4 * n * chans // LANES
    narrow = n * chans // LANES
    if back:
        tiles = [[value[c][:, t * LANES : (t + 1) * LANES] for t in range(narrow)] for c in range(4)]
        out = [None] * wide
    else:
        tiles = [value[:, t * LANES : (t + 1) * LANES] for t in range(wide)]
        out = [[None] * narrow for _ in range(4)]
    for c in range(4):
        for i in range(n):
            a, b = i * 4 * chans + c * chans, i * chans
            if back:
                source, to, at = tiles[c][b // LANES], a % LANES, b % LANES
                row, k = out, a // LANES
            else:
                source, to, at = tiles[a // LANES], b % LANES, a % LANES
                row, k = out[c], b // LANES
            shift = (to - at) % LANES
            moved = pltpu.roll(source, shift, 1) if shift else source
            inside = (lane >= to) & (lane < to + chans)
            row[k] = jnp.where(inside, moved, 0.0 if row[k] is None else row[k])
    if back:
        return jnp.concatenate(out, axis=1)
    return [jnp.concatenate(tiles, axis=1) for tiles in out]


def conv_chunk(k, g, spec, gspec, z, first, twiddle, second, second_back, last):
    outer = twiddle.shape[0]
    rows = pl.ds(pl.multiple_of(k * EIGHT * outer, 8), EIGHT * outer)
    u = spectrum_of(load_pairs(g.at[k]), first[...], twiddle[...], second[...])
    gspec[rows, :] = u
    o = signal_of(times(u, spec[rows, :]), twiddle[...], second_back[...], last[...])
    store_pairs(z.at[k], o)


def decay(me, chans):
    ids = lax.broadcasted_iota(jnp.int32, (chans, 1), 0) + me * chans
    slow = math.log(0.01) / 1.5
    fast = math.log(0.01) / 0.3
    return jnp.abs(slow + (fast - slow) * ids.astype(F32) / (D - 1))


def hops(n, b, me, sems, local):
    half = n // 2
    x, z = lax.rem(me, 2), me // 2
    side = {"chan": 2 * z + 1 - x}

    def hop_z(c, src, dst):
        keep = pltpu.make_async_copy(src, dst.at[me], local.at[c])
        keep.start()
        copies = [
            send(src, dst.at[me], sems, (c, d), {"chan": 2 * lax.rem(z + d, half) + x})
            for d in range(1, half)
        ]
        return keep, copies

    def hop_x(c, src, dst, keep, copies):
        out = [send(src, dst.at[me], sems, (c, half), side)]
        for d in range(1, half):
            j = 2 * lax.rem(z + half - d, half) + x
            copies[d - 1].wait_recv()
            out.append(send(dst.at[j], dst.at[j], sems, (c, half + d), side))
        keep.wait()
        return out

    return hop_z, hop_x


def prepare_kernel(
    n, length, chans,
    ids, embedding, inward, vectors, outward, expand, offsets, contract, chan_t, filt_t, feat,
    first, first_real, twiddle, second, second_back, last, last_real,
    wall, wpart, misc, toks, tokx, spec0, spec1, gspec, keep0, keep1, zpos,
    owned, upper, side, town, flip, kern, gch, zch,
    ssem, rsem, wsem, vsem, ksem, lsem, zsem, ysem, local, zown,
):
    me, b = lax.axis_index("chan"), lax.axis_index("batch")
    groups = chans // EIGHT
    seqs, span = zpos.shape[2], zpos.shape[3]
    width = span // EIGHT * LANES
    parts = width // D
    flip[...] = jnp.zeros_like(flip)
    for k in range(9):
        for l in range(LAYERS):
            flip[VEC0 + 9 * l + k : VEC0 + 9 * l + k + 1, 0:chans] = vectors[k, l : l + 1, :]
    flip[EMB0 : EMB0 + VOCAB, 0:chans] = embedding[...]
    for l in range(LAYERS):
        for c in range(4):
            row = OFF0 + 4 * l + c
            flip[row : row + 1, 0:chans] = offsets[l : l + 1, c * chans : (c + 1) * chans]
    columns = flip[...].T[:chans, :]
    lane = lax.broadcasted_iota(jnp.int32, (chans, LANES), 1)
    for l in range(LAYERS):
        taps = jnp.where(lane < 12, widened(chan_t[l]), 0.0)
        columns = columns + pltpu.roll(taps, TAP0 + 12 * l, 1)
    side[:, 0:LANES] = columns
    side[:, LANES:] = jnp.zeros((chans, LANES), F32)
    town[...] = jnp.zeros_like(town)
    for s in range(seqs):
        for h in range(parts):
            town[s * parts + h : s * parts + h + 1, :] = ids[
                s : s + 1, h * D : (h + 1) * D
            ].astype(F32)
    for l in range(LAYERS):
        folded = fold(contract[l], n, chans)
        rear = owned if l == 0 else upper
        base = 0 if l == 0 else 12 * chans
        for j in range(3):
            owned[base + j * chans : base + (j + 1) * chans, :] = inward[l, j]
        base = 3 * chans if l == 0 else 0
        rear[base : base + chans, :] = outward[l]
        rear[base + chans : base + 5 * chans, :] = expand[l]
        for c in range(4):
            rear[base + (5 + c) * chans : base + (6 + c) * chans, :] = folded[c]
    greet(n, (core_mate(b), y_mate(b)))
    mine = pl.ds(pl.multiple_of(me * chans, 8), chans)
    small = []
    for d in range(1, n):
        peer = {"chan": lax.rem(me + d, n)}
        small.append(send(side, misc.at[mine, :], (ssem, rsem), d, peer))
        small.append(send(town, toks.at[me], (ssem, rsem), n + d, peer))
    misc[mine, :] = side[...]
    toks[me] = town[...]
    weights = (wsem, vsem)
    hop_z, hop_x = hops(n, b, me, weights, local)
    part = quarter_rows(wall.shape[1], b)
    low = (owned.at[part], wall.at[:, part])
    high = (upper.at[quarter_rows(upper.shape[0], b)], wpart)
    keep_a, z_a = hop_z(0, *low)
    keep_b, z_b = hop_z(1, *high)

    block = 512
    steps = length // 4 // block
    delta = decay(me, chans)
    lag = pl.ds(pl.multiple_of(b * (kern.shape[2] // 4), 8), kern.shape[2] // 4)
    lag_y = pl.ds(pl.multiple_of(y_mate(b) * (kern.shape[2] // 4), 8), kern.shape[2] // 4)

    def filters(l, keep):
        fourth = chan_t[l, :, 13 : 13 + FO]

        def body(i):
            start = b * (length // 4) + i * block
            out, kept = filter_block(
                length, start, feat[:, pl.ds(pl.multiple_of(start, block), block)],
                filt_t.at[l], fourth, delta,
            )
            place = pl.ds(pl.multiple_of(i * block, block), block)
            for k, (sine, cosine) in enumerate(kept):
                keep[k, :, place] = sine
                keep[3 + k, :, place] = cosine
            for q in range(block // LANES):
                row = start // LANES + q
                rows = pl.ds(pl.multiple_of(row * EIGHT, 8), EIGHT)
                for k in range(groups):
                    kern[l, k, rows, :] = out[
                        k * EIGHT : (k + 1) * EIGHT, q * LANES : (q + 1) * LANES
                    ]

        loop(steps, body)
        place = kern.at[l, :, lag, :]
        return send(place, place, (ksem, lsem), (l, 0), {"batch": y_mate(b)})

    def share(l, copy):
        copy.wait_recv()
        return [
            send(kern.at[l, :, k, :], kern.at[l, :, k, :], (ksem, lsem), (l, 1 + i), {"batch": core_mate(b)})
            for i, k in enumerate((lag, lag_y))
        ]

    def spectra(l, copies, spec):
        for copy in copies:
            copy.wait_recv()
        outer = twiddle.shape[0]
        rows = length // LANES

        def body(k):
            taps = jnp.concatenate(
                [kern[l, k, pl.ds(c, rows, stride=EIGHT), :] for c in range(EIGHT)], axis=1
            )
            u = spectrum_of(taps, first_real[...], twiddle[...], second[...])
            here = pl.ds(pl.multiple_of(k * EIGHT, 8), EIGHT)
            gain = jnp.broadcast_to(chan_t[l, here, 12:13], (EIGHT, LANES))
            for c in range(EIGHT):
                wide = jnp.broadcast_to(gain[c : c + 1, :], (outer, LANES))
                both = jnp.concatenate([wide, jnp.zeros_like(wide)], axis=1)
                place = pl.ds(pl.multiple_of((k * EIGHT + c) * outer, 8), outer)
                spec[place, :] = u[c * outer : (c + 1) * outer] + both

        loop(groups, body)

    y_k0 = filters(0, keep0)
    for copy in small:
        copy.wait()
    table = misc[...]
    xh, _ = normalize(table)
    normed = xh * table[:, VEC0 : VEC0 + 1] + table[:, VEC0 + 1 : VEC0 + 2]
    own = side[...]
    mixes, biases = [], []
    for j in (1, 2):
        rows = dot(inward[0, j], normed, HIGHEST)
        rows = rows + own[:, VEC0 + 4 + j : VEC0 + 5 + j]
        rows = pltpu.roll(rows, D - EMB0, 1)[:, :LANES]
        rows = jnp.where(lane < VOCAB, rows, 0.0)
        k = TAP0 + 3 * j
        mixes.append(
            own[:, k : k + 1] * rows
            + own[:, k + 1 : k + 2] * pltpu.roll(rows, VOCAB, 1)
            + own[:, k + 2 : k + 3] * pltpu.roll(rows, 2 * VOCAB, 1)
        )
        biases.append(own[:, TAP0 + 9 + j : TAP0 + 10 + j])
    mix = paired(jnp.concatenate(mixes, axis=0), 3 * VOCAB)
    names = lax.broadcasted_iota(jnp.int32, (VOCAB, width), 0).astype(F32)

    def shifted(i, s):
        here = jnp.concatenate(
            [toks[i, s * parts + h : s * parts + h + 1, :] for h in range(parts)], axis=1
        )
        before = toks[jnp.maximum(i - 1, 0), (s + 1) * parts - 1 : (s + 1) * parts, D - LANES :]
        long = jnp.concatenate([jnp.where(i > 0, before, -1.0), here], axis=1)
        return here, pltpu.roll(long, 1, 1)[:, LANES:], pltpu.roll(long, 2, 1)[:, LANES:]

    for s in range(seqs):
        for k, row in enumerate(shifted(me, s)):
            tokx[s, k : k + 1, :] = row

    def gates(i):
        for s in range(seqs):
            here, one, two = shifted(i, s)
            places = [(names == row).astype(F32) for row in (two, one, here)]
            out = named_dot(mix, places)
            gate = (out[:chans] + biases[0]) * (out[chans:] + biases[1])
            for q in range(width // LANES):
                rows = pl.ds(pl.multiple_of(i * span + q * EIGHT, 8), EIGHT)
                for k in range(groups):
                    gch[k, s, rows, :] = gate[
                        k * EIGHT : (k + 1) * EIGHT, q * LANES : (q + 1) * LANES
                    ]

    loop(n, gates)
    core_k0 = share(0, y_k0)
    x_a = hop_x(0, *low, keep_a, z_a)
    y_k1 = filters(1, keep1)
    spectra(0, core_k0, spec0)
    core_k1 = share(1, y_k1)
    for copy in x_a:
        copy.wait_recv()
    whole = wall.at[:, part]
    y_a = send(whole, whole, weights, (0, n), {"batch": y_mate(b)})
    back = Blocks(n, span, (zsem, ysem), zown)

    def chunk(k):
        conv_chunk(
            k, gch, spec0, gspec, zch, first, twiddle, second, second_back, last
        )
        back.start(back.back_refs, k, zch, zpos)

    loop(groups, chunk)
    x_b = hop_x(1, *high, keep_b, z_b)
    spectra(1, core_k1, spec1)
    y_a.wait_recv()
    core_a = []
    for i, k in enumerate((b, y_mate(b))):
        here = wall.at[:, quarter_rows(wall.shape[1], k)]
        core_a.append(send(here, here, weights, (0, n + 1 + i), {"batch": core_mate(b)}))

    def finish(k):
        back.arrived(back.back_refs, k, zch, zpos)
        back.sent(back.back_refs, k, zch, zpos)

    loop(groups, finish)
    for copy in x_b:
        copy.wait_recv()
    for copy in z_a + z_b + x_a + x_b + [y_a, y_k0, y_k1] + core_k0 + core_k1:
        copy.wait_send()
    for copy in core_a:
        copy.wait()


def prepare(arrays, tables, n, seqs, length, cid):
    chan_t = arrays[8]
    chans = chan_t.shape[1]
    groups = chans // EIGHT
    rows = length // LANES
    span = rows // n * EIGHT
    outer = 2 * rows
    width = length // n
    spec = sds(chans * outer, 2 * LANES)
    keep = sds(6, FO, length // 4)
    low, high = round_up(15 * chans, 32), round_up(9 * chans, 32)
    return pl.pallas_call(
        partial(prepare_kernel, n, length, chans),
        in_specs=[WHOLE] * 18,
        out_specs=[HBM] * 2 + [WHOLE] * 8 + [HBM],
        out_shape=[
            sds(n, low, D), sds(n, high // 4, D),
            sds(D, D), sds(n, EIGHT, D), sds(seqs, EIGHT, width),
            spec, spec, spec, keep, keep, sds(groups, n, seqs, span, LANES),
        ],
        scratch_shapes=[
            VMEM((low, D), F32),
            VMEM((high, D), F32),
            VMEM((chans, D), F32),
            VMEM((EIGHT, D), F32),
            VMEM((LANES, LANES), F32),
            VMEM((LAYERS, groups, rows * EIGHT, LANES), F32),
            VMEM((groups, seqs, rows * EIGHT, LANES), F32),
            VMEM((groups, seqs, rows * EIGHT, LANES), F32),
            *pair_sems(2 * n),
            *pair_sems(2, n + 3),
            *pair_sems(LAYERS, 3),
            *pair_sems(groups, n),
            pltpu.SemaphoreType.DMA((2,)),
            pltpu.SemaphoreType.DMA((groups,)),
        ],
        compiler_params=comm_params(cid),
        name="prepare",
    )(*arrays, position_table(length), *tables)


def mixer_kernel(
    n, chans, lane0, p, wpart, misc, spec,
    first, first_real, twiddle, second, second_back, last, last_real,
    q, wrear, gspec, zpos,
    qv, gpos, gch, zch, tails, halo, gsem, hsem, zsem, ysem, gown, zown, hs, hr, qsem, ws, wr,
):
    me, b = lax.axis_index("chan"), lax.axis_index("batch")
    seqs, width = p.shape[1], p.shape[3]
    groups = chans // EIGHT
    span = zpos.shape[3]
    greet(n, (core_mate(b), y_mate(b)))
    part = wrear.at[:, quarter_rows(wrear.shape[1], b)]
    other = wrear.at[:, quarter_rows(wrear.shape[1], y_mate(b))]
    kept = pltpu.make_async_copy(wpart, part, qsem.at[1])
    kept.start()
    weights = [
        send(wpart, part, (ws, wr), 0, {"batch": y_mate(b)}),
        send(wpart, part, (ws, wr), 1, {"batch": core_mate(b)}),
    ]
    lane = lax.broadcasted_iota(jnp.int32, (D, LANES), 1)
    pack = jnp.zeros((D, LANES), F32)
    for j in range(3):
        for s in range(seqs):
            slot = 2 * (j * seqs + s)
            tail = pltpu.roll(p[j, s, :, width - LANES :], slot + 2, 1)
            pack = jnp.where((lane == slot) | (lane == slot + 1), tail, pack)
    tails[...] = pack
    copy = send(tails, halo, (hs, hr), 0, {"chan": lax.rem(me + 1, n)})
    copy.wait()
    inner = (me > 0).astype(F32)
    out = Blocks(n, span, (gsem, hsem), gown)
    back = Blocks(n, span, (zsem, ysem), zown)

    def gates(k):
        def body(owner):
            rows = pl.ds(pl.multiple_of(owner * chans + k * EIGHT, 8), EIGHT)
            side = misc[rows, :]
            edge = halo[rows, :] * inner
            for s in range(seqs):
                made = []
                for j in range(3):
                    here = p[j, s, rows, :]
                    before = pltpu.roll(edge, LANES - 2 - 2 * (j * seqs + s), 1)
                    long = jnp.concatenate([before, here], axis=1)
                    one = pltpu.roll(long, 1, 1)[:, LANES:]
                    two = pltpu.roll(long, 2, 1)[:, LANES:]
                    t = lane0 + 3 * j
                    made.append(
                        side[:, lane0 + 9 + j : lane0 + 10 + j]
                        + side[:, t : t + 1] * two
                        + side[:, t + 1 : t + 2] * one
                        + side[:, t + 2 : t + 3] * here
                    )
                    qv[j, s, rows, :] = made[j]
                gate = made[2] * made[1]
                for b in range(width // LANES):
                    gpos[k, owner, s, b * EIGHT : (b + 1) * EIGHT, :] = gate[
                        :, b * LANES : (b + 1) * LANES
                    ]

        loop(n, body)
        out.start(out.out_refs, k, gpos, gch)

    loop(groups, gates)
    saved = pltpu.make_async_copy(qv, q, qsem.at[0])
    saved.start()

    def chunk(k):
        out.arrived(out.out_refs, k, gpos, gch)
        conv_chunk(k, gch, spec, gspec, zch, first, twiddle, second, second_back, last)
        back.start(back.back_refs, k, zch, zpos)

    loop(groups, chunk)
    weights[0].wait_recv()
    weights.append(send(other, other, (ws, wr), 2, {"batch": core_mate(b)}))

    def finish(k):
        out.sent(out.out_refs, k, gpos, gch)
        back.arrived(back.back_refs, k, zch, zpos)
        back.sent(back.back_refs, k, zch, zpos)

    loop(groups, finish)
    saved.wait()
    kept.wait()
    weights[0].wait_send()
    for copy in weights[1:]:
        copy.wait()


def mixer(p, wpart, misc, spec, tables, n, chans, lane0, cid):
    seqs, width = p.shape[1], p.shape[3]
    groups = chans // EIGHT
    span = width // LANES * EIGHT
    by_position = (groups, n, seqs, span, LANES)
    by_channel = (groups, seqs, n * span, LANES)
    return pl.pallas_call(
        partial(mixer_kernel, n, chans, lane0),
        in_specs=[WHOLE, HBM] + [WHOLE] * 9,
        out_specs=[HBM, HBM, WHOLE, HBM],
        out_shape=[
            sds(*p.shape), sds(n, 4 * wpart.shape[1], D), sds(*spec.shape), sds(*by_position),
        ],
        scratch_shapes=[
            VMEM(p.shape, F32),
            VMEM(by_position, F32),
            VMEM(by_channel, F32),
            VMEM(by_channel, F32),
            VMEM((D, LANES), F32),
            VMEM((D, LANES), F32),
            *pair_sems(groups, n),
            *pair_sems(groups, n),
            pltpu.SemaphoreType.DMA((groups,)),
            pltpu.SemaphoreType.DMA((groups,)),
            *pair_sems(1),
            pltpu.SemaphoreType.DMA((2,)),
            *pair_sems(3),
        ],
        compiler_params=comm_params(cid),
        name="mixer",
    )(p, wpart, misc, spec, *tables)


class GroupSum:
    def __init__(self, n, g, out, r0, sum0, r1, sum1, r2, send_sem, recv_sem):
        self.n, self.g, self.out = n, g, out
        self.r0, self.sum0, self.r1, self.sum1, self.r2 = r0, sum0, r1, sum1, r2
        self.sems = (send_sem, recv_sem)
        me, b = lax.axis_index("chan"), lax.axis_index("batch")
        self.x, self.z = lax.rem(me, 2), me // 2
        self.core, self.y = lax.rem(b, 2), b // 2
        self.b = b
        self.copies = []

    def part(self, k):
        return quarter_rows(self.g.shape[1], k)

    def cores(self):
        mate = {"batch": core_mate(self.b)}
        for k in range(2):
            source = self.g.at[:, self.part(2 * k + 1 - self.core)]
            self.copies.append(send(source, self.r0.at[k], self.sems, k, mate))

    def along_y(self):
        for k in range(2):
            self.copies[k].wait_recv()

            def add(i, k=k):
                mine = self.g[i, self.part(2 * k + self.core), :]
                self.sum0[k, i] = mine + self.r0[k, i]

            loop(self.n, add)
        self.copies.append(
            send(self.sum0.at[1 - self.y], self.r1, self.sems, 2, {"batch": y_mate(self.b)})
        )

    def along_x(self):
        self.copies[2].wait_recv()

        def add(i):
            self.sum1[lax.rem(i, 2), i // 2] = self.sum0[self.y, i] + self.r1[i]

        loop(self.n, add)
        to = {"chan": 2 * self.z + 1 - self.x}
        self.copies.append(send(self.sum1.at[1 - self.x], self.r2, self.sems, 3, to))

    def close(self):
        self.copies[3].wait_recv()

        def add(i):
            self.out[i] = self.sum1[self.x, i] + self.r2[i]

        loop(self.n // 2, add)
        for copy in self.copies:
            copy.wait_send()


def group_scratch(n, rows):
    quarter, half = rows // 4, n // 2
    return [
        VMEM((2, n, quarter, D), F32),
        VMEM((2, n, quarter, D), F32),
        VMEM((n, quarter, D), F32),
        VMEM((2, half, quarter, D), F32),
        VMEM((half, quarter, D), F32),
        *pair_sems(4),
    ]


def mixer_back_kernel(
    n, chans, lane0, layer, length,
    dz, q, dq0, p, keep, misc, spec, gspec, chan_t, filt_t, feat, grads,
    first, first_real, twiddle, second, second_back, last, last_real,
    dp, dcols, dnet, dchan, summed,
    qv, dq0v, pv, dzch, dzspec, dgch, dgpos, dk, dkin, dnets, heads, halo,
    gsem, hsem, zsem, ysem, gown, zown, hs, hr, lsem, ks, kr, *group,
):
    me, b = lax.axis_index("chan"), lax.axis_index("batch")
    seqs, width = pv.shape[1], pv.shape[3]
    groups = chans // EIGHT
    span = dgpos.shape[3]
    rows_all = length // LANES
    outer = twiddle.shape[0]
    total = GroupSum(n, grads, summed, *group)
    loads = [
        pltpu.make_async_copy(q.at[pl.ds(1, 2)], qv, lsem.at[0]),
        pltpu.make_async_copy(dq0, dq0v, lsem.at[1]),
        pltpu.make_async_copy(p, pv, lsem.at[2]),
    ]
    greet(n, [lax.rem(b + d, 4) for d in range(1, 4)])
    out = Blocks(n, span, (gsem, hsem), gown)
    back = Blocks(n, span, (zsem, ysem), zown)
    loop(groups, lambda k: out.start(out.out_refs, k, dz, dzch))
    total.cores()
    for load in loads:
        load.start()
    total.along_y()

    def chunk(k):
        out.arrived(out.out_refs, k, dz, dzch)
        rows = pl.ds(pl.multiple_of(k * EIGHT * outer, 8), EIGHT * outer)
        u = spectrum_of(load_pairs(dzch.at[k]), first[...], twiddle[...], second[...])
        dzspec[rows, :] = u
        o = signal_of(times_conj(u, spec[rows, :]), twiddle[...], second_back[...], last[...])
        store_pairs(dgch.at[k], o)
        back.start(back.back_refs, k, dgch, dgpos)

    loop(groups, chunk)
    total.along_x()

    def lag(k):
        rows = pl.ds(pl.multiple_of(k * EIGHT * outer, 8), EIGHT * outer)
        v = times_conj(dzspec[rows, :], gspec[rows, :])
        r = signal_of(v, twiddle[...], second_back[...], last_real[...])
        for c in range(EIGHT):
            dk[k, pl.ds(c, rows_all, stride=EIGHT), :] = r[:, c * LANES : (c + 1) * LANES]

    loop(groups, lag)
    count = dk.shape[1] // 4

    def lags(j):
        return pl.ds(pl.multiple_of(j * count, 8), count)

    shares = []
    for d in range(1, 4):
        j = lax.rem(b + d, 4)
        shares.append(
            send(dk.at[:, lags(j)], dkin.at[d - 1], (ks, kr), d - 1, {"batch": j})
        )
    for share in shares:
        share.wait_recv()
    dk[:, lags(b), :] = dk[:, lags(b), :] + dkin[0] + dkin[1] + dkin[2]
    dnets[...] = jnp.zeros_like(dnets)
    dchan[...] = jnp.zeros_like(dchan)
    block = 512
    delta = decay(me, chans)
    fourth = chan_t[layer, :, 13 : 13 + FO]

    def network(i):
        start = b * (length // 4) + i * block
        wide = []
        for c in range(block // LANES):
            place = pl.ds(pl.multiple_of((start // LANES + c) * EIGHT, 8), EIGHT)
            wide.append(jnp.concatenate([dk[k, place, :] for k in range(groups)], axis=0))
        filter_back_block(
            length, start, feat[:, pl.ds(pl.multiple_of(start, block), block)],
            filt_t.at[layer], fourth, delta,
            keep.at[:, :, pl.ds(pl.multiple_of(i * block, block), block)],
            jnp.concatenate(wide, axis=1), dnets, dchan,
        )

    loop(length // 4 // block, network)
    head = jnp.concatenate([dk[k, 0:EIGHT, :] for k in range(groups)], axis=0)
    lane = lax.broadcasted_iota(jnp.int32, (chans, LANES), 1)
    head = jnp.where(lane == 0, head, 0.0) * (b == 0).astype(F32)
    dchan[...] += pltpu.roll(head, FO, 1)
    dnet[...] = (
        widened(dnets[0], D)
        + pltpu.roll(widened(dnets[1], D), EMB + 1, 1)
        + pltpu.roll(widened(dnets[2], D), EMB + 2 + FO, 1)
    )
    loop(groups, lambda k: back.arrived(back.back_refs, k, dgch, dgpos))
    for load in loads:
        load.wait()

    lane = lax.broadcasted_iota(jnp.int32, (D, LANES), 1)
    pack = jnp.zeros((D, LANES), F32)
    for s in range(seqs):
        dg = jnp.concatenate(
            [dgpos[k, j, s, 0:EIGHT, :] for j in range(n) for k in range(groups)], axis=0
        )
        parts = (dq0v[s, :, :LANES], dg * qv[1, s, :, :LANES], dg * qv[0, s, :, :LANES])
        for j in range(3):
            slot = 2 * (j * seqs + s)
            head = pltpu.roll(parts[j], slot, 1) if slot else parts[j]
            pack = jnp.where((lane == slot) | (lane == slot + 1), head, pack)
    heads[...] = pack
    copy = send(heads, halo, (hs, hr), 0, {"chan": lax.rem(me + n - 1, n)})
    copy.wait()
    inner = (me < n - 1).astype(F32)
    full = width + LANES

    def body(owner):
        rows = pl.ds(pl.multiple_of(owner * chans, 8), chans)
        side = misc[rows, :]
        edge = halo[rows, :] * inner
        sums = [jnp.zeros((chans, 1), F32)] * 12
        for s in range(seqs):
            dg = jnp.concatenate(
                [
                    jnp.concatenate(
                        [
                            dgpos[k, owner, s, b * EIGHT : (b + 1) * EIGHT, :]
                            for k in range(groups)
                        ],
                        axis=0,
                    )
                    for b in range(width // LANES)
                ],
                axis=1,
            )
            parts = (dq0v[s, rows, :], dg * qv[1, s, rows, :], dg * qv[0, s, rows, :])
            for j in range(3):
                here = parts[j]
                slot = 2 * (j * seqs + s)
                after = pltpu.roll(edge, LANES - slot, 1) if slot else edge
                long = jnp.concatenate([here, after], axis=1)
                one = pltpu.roll(long, full - 1, 1)[:, :width]
                two = pltpu.roll(long, full - 2, 1)[:, :width]
                t = lane0 + 3 * j
                dp[j, s, rows, :] = (
                    side[:, t : t + 1] * two
                    + side[:, t + 1 : t + 2] * one
                    + side[:, t + 2 : t + 3] * here
                )
                source = pv[j, s, rows, :]
                sums[3 * j] = sums[3 * j] + row_sum(two * source)
                sums[3 * j + 1] = sums[3 * j + 1] + row_sum(one * source)
                sums[3 * j + 2] = sums[3 * j + 2] + row_sum(here * source)
                sums[9 + j] = sums[9 + j] + row_sum(here)
        dcols[rows, :] = put_columns([(lane0 + k, sums[k]) for k in range(12)])

    loop(n, body)
    total.close()
    for share in shares:
        share.wait_send()

    def finish(k):
        out.sent(out.out_refs, k, dz, dzch)
        back.sent(back.back_refs, k, dgch, dgpos)

    loop(groups, finish)


def mixer_back(
    dz, q, dq0, p, keep, misc, spec, gspec, chan_t, filt_t, grads, tables, n, chans, layer, cid
):
    seqs, width = p.shape[1], p.shape[3]
    groups = chans // EIGHT
    span = width // LANES * EIGHT
    length = width * n
    by_position = (groups, n, seqs, span, LANES)
    by_channel = (groups, seqs, n * span, LANES)
    rows = grads.shape[1]
    return pl.pallas_call(
        partial(mixer_back_kernel, n, chans, TAP0 + 12 * layer, layer, length),
        in_specs=[HBM] * 4 + [WHOLE] * 15,
        out_specs=[WHOLE] * 5,
        out_shape=[
            sds(*p.shape), sds(D, D), sds(FO, D), sds(chans, LANES), sds(n // 2, rows // 4, D),
        ],
        scratch_shapes=[
            VMEM((2,) + p.shape[1:], F32),
            VMEM(p.shape[1:], F32),
            VMEM(p.shape, F32),
            VMEM(by_channel, F32),
            VMEM(spec.shape, F32),
            VMEM(by_channel, F32),
            VMEM(by_position, F32),
            VMEM((groups, n * span, LANES), F32),
            VMEM((3, groups, n * span // 4, LANES), F32),
            VMEM((3, FO, LANES), F32),
            VMEM((D, LANES), F32),
            VMEM((D, LANES), F32),
            *pair_sems(groups, n),
            *pair_sems(groups, n),
            pltpu.SemaphoreType.DMA((groups,)),
            pltpu.SemaphoreType.DMA((groups,)),
            *pair_sems(1),
            pltpu.SemaphoreType.DMA((3,)),
            *pair_sems(3),
            *group_scratch(n, rows),
        ],
        compiler_params=comm_params(cid),
        name="mixer_back",
    )(
        dz, q, dq0, p, keep, misc, spec, gspec, chan_t, filt_t, position_table(length), grads,
        *tables,
    )


def total_kernel(n, *refs):
    part1, part2, front0, cols, dnets, dchans = refs[0], refs[1], refs[2], refs[3:8], refs[8:10], refs[10:12]
    rows1, rows2, rows3, filt, chan = refs[12:17]
    (low, last, in1, in2, in3, dchan, rchan, zs, zr, bs, br, cs, cr, fs, fr) = refs[17:32]
    group = refs[32:]
    me, b = lax.axis_index("chan"), lax.axis_index("batch")
    x, z = lax.rem(me, 2), me // 2
    half = n // 2
    chans = front0.shape[1] // 3
    filter_rows = filt.shape[1]
    greet(n, [lax.rem(b + d, 4) for d in range(1, 4)])

    def column(k, source, landing):
        return [
            send(
                source.at[lax.rem(z + d, half)], landing.at[d - 1], (zs, zr), (k, d - 1),
                {"chan": 2 * lax.rem(z + d, half) + x},
            )
            for d in range(1, half)
        ]

    def gather(k, rows):
        mine = rows.at[quarter_rows(rows.shape[0], b)]
        other = rows.at[quarter_rows(rows.shape[0], y_mate(b))]
        mate = {"batch": core_mate(b)}
        first = send(mine, mine, (bs, br), (k, 0), {"batch": y_mate(b)})
        second = send(mine, mine, (bs, br), (k, 1), mate)
        first.wait_recv()
        third = send(other, other, (bs, br), (k, 2), mate)
        return [first, second, third]

    def add_column(copies, source, landing, rows):
        total = source[z]
        for d, copy in enumerate(copies):
            copy.wait_recv()
            total = total + landing[d]
        rows[quarter_rows(rows.shape[0], b), :] = total

    low[...] = jnp.zeros_like(low)
    side = cols[0][...] + cols[1][...] + cols[2][...] + cols[3][...] + cols[4][...]
    for i in range(n):
        low[i, 0 : 3 * chans, :] = front0[i]
        low[i, 3 * chans : 4 * chans, :] = side[i * chans : (i + 1) * chans, :]
        row = i * filter_rows
        if row < LAYERS * FO:
            low[i, 4 * chans : 4 * chans + filter_rows, :] = dnets[row // FO][
                row % FO : row % FO + filter_rows, :
            ]
    total = GroupSum(n, low, last, *group)
    total.cores()
    for l in range(LAYERS):
        dchan[l] = dchans[l][...]
    small = [
        send(dchan, rchan.at[d - 1], (cs, cr), d - 1, {"batch": lax.rem(b + d, 4)})
        for d in range(1, 4)
    ]
    z1 = column(0, part1, in1)
    z2 = column(1, part2, in2)
    total.along_y()
    total.along_x()
    total.close()
    z3 = column(2, last, in3)
    add_column(z1, part1, in1, rows1)
    g1 = gather(0, rows1)
    add_column(z2, part2, in2, rows2)
    g2 = gather(1, rows2)
    add_column(z3, last, in3, rows3)
    g3 = gather(2, rows3)
    for copy in g3[1:]:
        copy.wait_recv()
    filt[me] = rows3[4 * chans : 4 * chans + filter_rows, :]
    shares = [
        send(filt.at[me], filt.at[me], (fs, fr), d - 1, {"chan": lax.rem(me + d, n)})
        for d in range(1, n)
    ]
    for copy in g1[1:] + g2[1:]:
        copy.wait_recv()
    for copy in small:
        copy.wait_recv()

    for l in range(LAYERS):
        chan[l] = dchan[l] + rchan[0, l] + rchan[1, l] + rchan[2, l]
    for copy in shares:
        copy.wait_recv()
    for copy in z1 + z2 + z3 + g1 + g2 + g3 + small + shares:
        copy.wait_send()


def update_kernel(n, scale, *refs):
    rows1, rows2, rows3, filt, chan = refs[:5]
    weights, moments, averages = refs[5:14], refs[14:23], refs[23:32]
    outs = refs[32:]
    chans = chan.shape[1]
    filter_rows = filt.shape[1]

    def step(which, index, gradient):
        factor = STEP_RATES[which] * scale
        velocity = MOMENTUM * moments[which][index] + gradient
        updated = weights[which][index] - factor * (gradient + MOMENTUM * velocity)
        running = AVERAGING * averages[which][index] + (1.0 - AVERAGING) * updated
        base = 4 * which
        outs[base][index] = velocity
        outs[base + 1][index] = running
        outs[base + 2][index] = updated
        outs[base + 3][index] = updated.astype(BF16)

    columns = rows3[3 * chans : 4 * chans, 0:LANES]
    flat = columns
    if chans < LANES:
        flat = jnp.concatenate([columns, jnp.zeros((LANES - chans, LANES), F32)], axis=0)
    flat = flat.T
    step(0, Ellipsis, flat[EMB0 : EMB0 + VOCAB, :chans])
    lane = lax.broadcasted_iota(jnp.int32, (chans, LANES), 1)
    off = []
    for l in range(LAYERS):
        front, base = (rows3, 0) if l == 0 else (rows2, 0)
        for j in range(3):
            step(1, (l, j), front[base + j * chans : base + (j + 1) * chans, :])
        for k in range(9):
            row = VEC0 + 9 * l + k
            step(2, (k, slice(l, l + 1)), flat[row : row + 1, :chans])
        rear, base = (rows2, 3 * chans) if l == 0 else (rows1, 0)
        step(3, l, rear[base : base + chans, :])
        step(4, l, rear[base + chans : base + 5 * chans, :])
        pieces = [rear[base + (5 + c) * chans : base + (6 + c) * chans, :] for c in range(4)]
        step(6, l, fold(pieces, n, chans, back=True))
        row = jnp.zeros((1, LANES), F32)
        for c in range(4):
            piece = flat[OFF0 + 4 * l + c : OFF0 + 4 * l + c + 1, :]
            row = row + (pltpu.roll(piece, c * chans, 1) if c else piece)
        off.append(row[:, : 4 * chans])
        taps = pltpu.roll(columns, LANES - TAP0 - 12 * l, 1)
        own = chan[l]
        skip = pltpu.roll(own, LANES - FO + 12, 1)
        gradient = jnp.where(lane < 12, taps, jnp.where(lane == 12, skip, pltpu.roll(own, 13, 1)))
        step(7, l, gradient[:, : 13 + FO])
    step(5, Ellipsis, jnp.concatenate(off, axis=0))
    whole = filt[...].reshape(n * filter_rows, D)
    for l in range(LAYERS):
        step(8, l, whole[l * FO : (l + 1) * FO, :136])
def finish(part1, part2, front0, cols, dnets, dchans, weights, moments, averages, n, scale, cid):
    chans = front0.shape[1] // 3
    filter_rows = round_up(LAYERS * FO, n * EIGHT) // n
    low = round_up(4 * chans + filter_rows, 32)
    q1, q2, q3 = part1.shape[1], part2.shape[1], low // 4
    half = n // 2
    sums = pl.pallas_call(
        partial(total_kernel, n),
        in_specs=[WHOLE] * 12,
        out_specs=[WHOLE] * 5,
        out_shape=[
            sds(4 * q1, D), sds(4 * q2, D), sds(4 * q3, D), sds(n, filter_rows, D),
            sds(LAYERS, chans, LANES),
        ],
        scratch_shapes=[
            VMEM((n, low, D), F32),
            VMEM((half, q3, D), F32),
            VMEM((half - 1, q1, D), F32),
            VMEM((half - 1, q2, D), F32),
            VMEM((half - 1, q3, D), F32),
            VMEM((LAYERS, chans, LANES), F32),
            VMEM((3, LAYERS, chans, LANES), F32),
            *pair_sems(3, half - 1),
            *pair_sems(3, 3),
            *pair_sems(3),
            *pair_sems(n - 1),
            *group_scratch(n, low),
        ],
        compiler_params=comm_params(cid),
        name="total",
    )(part1, part2, front0, *cols, *dnets, *dchans)
    shapes = []
    for weight in weights:
        shapes += [sds(*weight.shape)] * 3 + [jax.ShapeDtypeStruct(weight.shape, BF16)]
    return pl.pallas_call(
        partial(update_kernel, n, scale),
        in_specs=[WHOLE] * 32,
        out_specs=[WHOLE] * 36,
        out_shape=shapes,
        compiler_params=pltpu.CompilerParams(vmem_limit_bytes=VMEM_LIMIT),
        name="update",
    )(*sums, *weights, *moments, *averages)


def onehot_rows(tokens):
    row = lax.broadcasted_iota(jnp.int32, (D, tokens.shape[1]), 0)
    return (row == tokens + EMB0).astype(F32)


class Layer:
    def __init__(self, front, rear, misc, index, base=0):
        some = rear if front is None else front
        self.n = some.shape[0]
        self.c = D // self.n
        self.front, self.rear, self.base = front, rear, base
        self.side = misc[...]
        self.index = index

    def rows(self, ref, start, count):
        return ref[:, start * self.c : (start + count) * self.c, :].reshape(
            self.n * count * self.c, D
        )

    def column(self, lane):
        return self.side[:, lane : lane + 1]

    def vec(self, k):
        return self.column(VEC0 + 9 * self.index + k)

    def off(self, k):
        return self.column(OFF0 + 4 * self.index + k)

    def inward(self):
        return self.rows(self.front, 0, 3)

    def outward(self):
        return self.rows(self.rear, self.base, 1)

    def expand(self, k):
        return self.rows(self.rear, self.base + 1 + k, 1)

    def contract(self, k):
        return self.rows(self.rear, self.base + 5 + k, 1)


def front_forward(lay, x):
    xh, _ = normalize(x)
    normed = xh * lay.vec(0) + lay.vec(1)
    p = dot(lay.inward(), normed).reshape(lay.n, 3, lay.c, x.shape[1])
    return [p[:, j].reshape(D, x.shape[1]) + lay.vec(4 + j) for j in range(3)]


def front_backward(lay, x, dp, dh, dw):
    xh, scale = normalize(x)
    normed = xh * lay.vec(0) + lay.vec(1)
    width = x.shape[1]
    stacked = jnp.stack([d.reshape(lay.n, lay.c, width) for d in dp], axis=1)
    stacked = stacked.reshape(3 * D, width)
    dn = dot_tn(lay.inward(), stacked)
    dw[:, 0 : 3 * lay.c, :] += dot_nt(stacked, normed).reshape(lay.n, 3 * lay.c, D)
    base = VEC0 + 9 * lay.index
    columns = [(base + 4 + j, row_sum(dp[j])) for j in range(3)]
    columns += [(base, row_sum(dn * xh)), (base + 1, row_sum(dn))]
    return dh + normalize_back(dn * lay.vec(0), xh, scale), columns


def rear_mix(lay, x, y):
    return x + dot(lay.outward(), y) + lay.vec(7)


def rear_hidden(lay, h):
    xh, scale = normalize(h)
    m = xh * lay.vec(2) + lay.vec(3)
    a = [dot(lay.expand(k), m) + lay.off(k) for k in range(4)]
    return xh, scale, m, a


def rear_out(lay, h, u):
    out = h + lay.vec(8)
    for k in range(4):
        out = out + dot(lay.contract(k), u[k])
    return out


def rear_backward(lay, h, a, y, dout, dw, base=0):
    n, c = lay.n, lay.c

    def add(row, value):
        dw[:, (base + row) * c : (base + row + 1) * c, :] += value.reshape(n, c, D)

    xh, scale = normalize(h)
    m = xh * lay.vec(2) + lay.vec(3)
    vec = VEC0 + 9 * lay.index
    columns = [(vec + 8, row_sum(dout))]
    dm = None
    for k in range(4):
        ak = a[k]
        g, t = gelu_parts(ak)
        u = ak * g
        add(5 + k, dot_nt(dout, u))
        slope = g + 0.5 * ak * (1.0 - t * t) * (GELU_SCALE * (1.0 + 3.0 * GELU_CUBE * ak * ak))
        dpre = dot_tn(lay.contract(k), dout) * slope
        add(1 + k, dot_nt(dpre, m))
        columns.append((OFF0 + 4 * lay.index + k, row_sum(dpre)))
        term = dot_tn(lay.expand(k), dpre)
        dm = term if dm is None else dm + term
    dh = dout + normalize_back(dm * lay.vec(2), xh, scale)
    columns += [(vec + 2, row_sum(dm * xh)), (vec + 3, row_sum(dm)), (vec + 7, row_sum(dh))]
    add(0, dot_nt(dh, y))
    return dh, dot_tn(lay.outward(), dh), columns


def joined(ref):
    groups, n, _, span, _ = ref.shape
    return jnp.concatenate(
        [
            jnp.concatenate(
                [ref[k, j, 0, b : b + EIGHT, :] for j in range(n) for k in range(groups)], axis=0
            )
            for b in range(0, span, EIGHT)
        ],
        axis=1,
    )


def split(ref, value):
    groups, n, _, span, _ = ref.shape
    for q in range(span // EIGHT):
        for j in range(n):
            for k in range(groups):
                row = (j * groups + k) * EIGHT
                ref[k, j, 0, q * EIGHT : (q + 1) * EIGHT, :] = value[
                    row : row + EIGHT, q * LANES : (q + 1) * LANES
                ]


def first_step():
    return (pl.program_id(0) == 0) & (pl.program_id(1) == 0)


def front0_kernel(tokx, w0, misc, p, q, ptab, qtab):
    lay = Layer(w0, w0, misc, 0, 3)

    @pl.when(first_step())
    def _():
        xh, _ = normalize(lay.side)
        normed = xh * lay.vec(0) + lay.vec(1)
        rows = dot(lay.inward(), normed, HIGHEST).reshape(lay.n, 3, lay.c, D)
        lane = lax.broadcasted_iota(jnp.int32, (D, LANES), 1)
        for j in range(3):
            table = rows[:, j].reshape(D, D) + lay.vec(4 + j)
            table = jnp.where(lane < VOCAB, pltpu.roll(table, D - EMB0, 1)[:, :LANES], 0.0)
            ptab[j] = paired(table, VOCAB)
            t = TAP0 + 3 * j
            mix = (
                lay.column(t) * table
                + lay.column(t + 1) * pltpu.roll(table, VOCAB, 1)
                + lay.column(t + 2) * pltpu.roll(table, 2 * VOCAB, 1)
            )
            qtab[j] = paired(mix, 3 * VOCAB)

    names = lax.broadcasted_iota(jnp.int32, (VOCAB, tokx.shape[2]), 0).astype(F32)
    here, one, two = [(names == tokx[0, k : k + 1, :]).astype(F32) for k in range(3)]
    for j in range(3):
        p[j, 0] = named_dot(ptab[j], [here])
        q[j, 0] = named_dot(qtab[j], [two, one, here]) + lay.column(TAP0 + 9 + j)


def mid_kernel(tok, z, q0, w0, f1, misc, h, a, x1, p):
    lay = Layer(w0, w0, misc, 0, 3)
    x = dot(lay.side, onehot_rows(tok[0]), HIGHEST)
    mixed = rear_mix(lay, x, joined(z) * q0[0, 0])
    h[0] = mixed
    _, _, _, pre = rear_hidden(lay, mixed)
    u = []
    for k in range(4):
        a[0, k] = pre[k]
        u.append(pre[k] * gelu_parts(pre[k])[0])
    x = rear_out(lay, mixed, u)
    x1[0] = x
    for j, value in enumerate(front_forward(Layer(f1, None, misc, 1), x)):
        p[j, 0] = value


def top_kernel(x1, z, q0, cot, r1, misc, x2, dz, dq0, dh_out, dw, cols):
    @pl.when(first_step())
    def _():
        dw[...] = jnp.zeros_like(dw)
        cols[...] = jnp.zeros_like(cols)

    lay = Layer(None, r1, misc, 1)
    zt, qt = joined(z), q0[0, 0]
    y = zt * qt
    h = rear_mix(lay, x1[0], y)
    _, _, _, pre = rear_hidden(lay, h)
    x2[0] = rear_out(lay, h, [v * gelu_parts(v)[0] for v in pre])
    dh, dy, columns = rear_backward(lay, h, pre, y, cot[0], dw)
    split(dz, dy * qt)
    dq0[0] = dy * zt
    dh_out[0] = dh
    cols[...] += put_columns(columns)


def mid_back_kernel(dp, x1, dh1, h, a, z, q0, w0, f1, misc, dz, dq0, dh_out, dw, cols):
    @pl.when(first_step())
    def _():
        dw[...] = jnp.zeros_like(dw)
        cols[...] = jnp.zeros_like(cols)

    upper = Layer(f1, None, misc, 1)
    dout, columns = front_backward(upper, x1[0], [dp[j, 0] for j in range(3)], dh1[0], dw)
    lay = Layer(w0, w0, misc, 0, 3)
    zt, qt = joined(z), q0[0, 0]
    dh, dy, more = rear_backward(lay, h[0], [a[0, k] for k in range(4)], zt * qt, dout, dw, 3)
    split(dz, dy * qt)
    dq0[0] = dy * zt
    dh_out[0] = dh
    cols[...] += put_columns(columns + more)


def front0_back_kernel(dp, tok, dh0, w0, misc, dx, dw_front, cols):
    @pl.when(first_step())
    def _():
        dw_front[...] = jnp.zeros_like(dw_front)
        cols[...] = jnp.zeros_like(cols)

    lay = Layer(w0, w0, misc, 0, 3)
    places = onehot_rows(tok[0])
    x = dot(lay.side, places, HIGHEST)
    grad, columns = front_backward(lay, x, [dp[j, 0] for j in range(3)], dh0[0], dw_front)
    dx[0] = grad
    cols[...] += put_columns(columns) + dot_nt(grad, places)


def token_call(kernel, name, seqs, width, n, ins, outs, args, out_shape, gflops, scratch=()):
    specs = {
        "tok": pl.BlockSpec((1, 1, TILE), lambda s, t: (s, 0, t)),
        "pos": pl.BlockSpec((1, D, TILE), lambda s, t: (s, 0, t)),
        "blk": pl.BlockSpec(
            (D // n // EIGHT, n, 1, TILE // LANES * EIGHT, LANES), lambda s, t: (0, 0, s, t, 0)
        ),
        "tokx": pl.BlockSpec((1, EIGHT, TILE), lambda s, t: (s, 0, t)),
        "q0": pl.BlockSpec((1, 1, D, TILE), lambda s, t: (0, s, 0, t)),
        "three": pl.BlockSpec((3, 1, D, TILE), lambda s, t: (0, s, 0, t)),
        "hid": pl.BlockSpec((1, 4, D, TILE), lambda s, t: (s, 0, 0, t)),
    }

    def spec(item):
        if isinstance(item, str):
            return specs[item]
        return item

    return pl.pallas_call(
        kernel,
        grid=(seqs, width // TILE),
        in_specs=[spec(i) for i in ins],
        out_specs=[spec(o) for o in outs],
        out_shape=out_shape,
        scratch_shapes=scratch,
        compiler_params=pltpu.CompilerParams(vmem_limit_bytes=VMEM_LIMIT),
        cost_estimate=cost(gflops * 1e9, 1e7),
        name=name,
    )(*args)


def turned(arrays):
    out = list(arrays)
    out[2] = arrays[2].transpose(1, 0, 2)
    out[7] = arrays[7].transpose(0, 2, 1)
    out[8] = arrays[8].transpose(0, 2, 1)
    return out


def per_device(*arguments):
    token_ids, cotangent = arguments[0], arguments[28]
    weights = turned(arguments[1:10])
    moments = turned(arguments[10:19])
    averages = turned(arguments[19:28])
    n, m = lax.axis_size("chan"), lax.axis_size("batch")
    seqs, width = token_ids.shape
    length = width * n
    chan_t, filt_t = weights[7], weights[8]
    chans = chan_t.shape[1]
    groups = chans // EIGHT
    tables = fourier_tables(length)
    tokens = token_ids.reshape(seqs, 1, width)
    wall, wpart, misc, _, tokx, spec0, spec1, gspec0, keep0, keep1, z0 = prepare(
        (token_ids, *weights), tables, n, seqs, length, 1
    )
    lower = pl.BlockSpec((n, 12 * chans, D), lambda s, t: (0, 0, 0))
    upper_front = pl.BlockSpec((n, 3 * chans, D), lambda s, t: (0, 4, 0))
    high = 4 * wpart.shape[1]
    upper_rear = pl.BlockSpec((n, high, D), lambda s, t: (0, 0, 0))
    square = pl.BlockSpec((D, D), lambda s, t: (0, 0))
    front_sum = pl.BlockSpec((n, 3 * chans, D), lambda s, t: (0, 0, 0))

    pos = sds(seqs, D, width)
    blk = sds(groups, n, seqs, width // LANES * EIGHT, LANES)
    three = sds(3, seqs, D, width)
    call = partial(token_call, seqs=seqs, width=width, n=n)

    p0, q0 = call(
        front0_kernel, "front0", ins=["tokx", lower, square], outs=["three", "three"],
        args=(tokx, wall, misc), out_shape=[three, three], gflops=1,
        scratch=[VMEM((3, D, LANES), BF16), VMEM((3, D, LANES), BF16)],
    )
    h0, a0, x1, p1 = call(
        mid_kernel, "mid", ins=["tok", "blk", "q0", lower, upper_front, square],
        outs=["pos", "hid", "pos", "three"],
        args=(tokens, z0, q0, wall, wall, misc),
        out_shape=[pos, sds(seqs, 4, D, width), pos, three], gflops=5,
    )
    q1, wrear, gspec1, z1 = mixer(p1, wpart, misc, spec1, tables, n, chans, TAP0 + 12, 2)
    activations, dz1, dq1, dh1, dw1, cols_top = call(
        top_kernel, "top",
        ins=["pos", "blk", "q0", "pos", upper_rear, square],
        outs=["pos", "blk", "pos", "pos", upper_rear, square],
        args=(x1, z1, q1, cotangent, wrear, misc),
        out_shape=[pos, blk, pos, pos, sds(n, high, D), sds(D, D)], gflops=9,
    )
    dp1, cols_taps1, dnet1, dchan1, part1 = mixer_back(
        dz1, q1, dq1, p1, keep1, misc, spec1, gspec1, chan_t, filt_t, dw1, tables, n, chans, 1, 3
    )
    dz0, dq0, dh0, dw0, cols_mid = call(
        mid_back_kernel, "mid_back",
        ins=["three", "pos", "pos", "pos", "hid", "blk", "q0", lower, upper_front, square],
        outs=["blk", "pos", "pos", lower, square],
        args=(dp1, x1, dh1, h0, a0, z0, q0, wall, wall, misc),
        out_shape=[blk, pos, pos, sds(n, 12 * chans, D), sds(D, D)],
        gflops=9,
    )
    dp0, cols_taps0, dnet0, dchan0, part2 = mixer_back(
        dz0, q0, dq0, p0, keep0, misc, spec0, gspec0, chan_t, filt_t, dw0, tables, n, chans, 0, 4
    )
    input_gradient, dw_front0, cols_low = call(
        front0_back_kernel, "front0_back",
        ins=["three", "tok", "pos", lower, square],
        outs=["pos", front_sum, square],
        args=(dp0, tokens, dh0, wall, misc),
        out_shape=[pos, sds(n, 3 * chans, D), sds(D, D)], gflops=2,
    )
    updates = finish(
        part1, part2, dw_front0, (cols_top, cols_taps1, cols_mid, cols_taps0, cols_low),
        (dnet0, dnet1), (dchan0, dchan1), weights, moments, averages, n,
        1.0 / math.sqrt(seqs * m * length), 5,
    )
    kinds = [turned(updates[k::4]) for k in range(4)]
    return (activations, input_gradient) + tuple(
        kinds[k][w] for w in range(9) for k in range(4)
    )


def solution(mesh):
    in_weights = (
        P(None, "chan"),
        P(None, None, "chan", None),
        P(None, None, "chan"),
        P(None, "chan", None),
        P(None, "chan", None),
        P(None, "chan"),
        P(None, "chan", None),
        P(None, None, "chan"),
        P(),
    )
    tokens = P("batch", None, "chan")
    in_specs = (P("batch", "chan"),) + in_weights * 3 + (tokens,)
    out_specs = (tokens, tokens) + tuple(spec for spec in in_weights for _ in range(4))
    return jax.shard_map(
        per_device, mesh=mesh, in_specs=in_specs, out_specs=out_specs, check_vma=False
    )
```

```python
from functools import partial
import math

import jax
import jax.numpy as jnp
import numpy as np
from jax import lax
from jax.experimental import pallas as pl
from jax.experimental.pallas import tpu as pltpu
from jax.sharding import PartitionSpec as P

D = 256
FF = 1024
FO = 64
EMB = 5
VOCAB = 16
LAYERS = 2
LANES = 128
TILE = 256

HIGH = lax.Precision.HIGH
HIGHEST = lax.Precision.HIGHEST
DW = lax.Precision.HIGH
EPSILON = 1e-05
MOMENTUM = 0.9
AVERAGING = 0.9
WINDOW_SHIFT = 0.05
FREQUENCY = 10.0
STEP_RATES = (0.7, 0.06, 0.1, 0.037, 0.1, 0.16, 0.025, 0.2, 0.0002)
GELU_SCALE = math.sqrt(2.0 / math.pi)
GELU_CUBE = 0.044715

MESH = pl.DeviceIdType.MESH
VMEM = pltpu.VMEM
WHOLE = pl.BlockSpec(memory_space=pltpu.VMEM)
HBM = pl.BlockSpec(memory_space=pl.ANY)
VMEM_LIMIT = 60 * 1024 * 1024
F32 = jnp.float32
BF16 = jnp.bfloat16

VEC0 = 0
TAP0 = 18
EMB0 = 42
OFF0 = 58
EIGHT = 8


def dot(a, b, precision=HIGH):
    return jnp.dot(a, b, precision=precision, preferred_element_type=F32)


def dot_nt(a, b, precision=HIGH):
    return lax.dot_general(
        a, b, (((1,), (1,)), ((), ())), precision=precision, preferred_element_type=F32
    )


def dot_tn(a, b, precision=HIGH):
    return lax.dot_general(
        a, b, (((0,), (0,)), ((), ())), precision=precision, preferred_element_type=F32
    )


def sds(*shape):
    return jax.ShapeDtypeStruct(shape, F32)


def cost(flops, moved):
    return pl.CostEstimate(flops=int(flops), bytes_accessed=int(moved), transcendentals=0)


def position_table(length):
    indices = np.arange(length, dtype=np.float32)
    fraction = indices / np.float32(length - 1)
    angles = np.float32(2.0 * math.pi) * indices / np.float32(length)
    bands = (EMB - 1) // 2
    frequency = np.linspace(0.0001, bands - 1, bands).astype(np.float32)
    turned = (frequency[:, None] * angles[None, :]).astype(np.float32).astype(np.float64)
    table = np.zeros((8, length), np.float32)
    table[0] = fraction
    table[1 : 1 + bands] = np.cos(turned)
    table[1 + bands : 1 + 2 * bands] = -np.sin(turned)
    table[EMB] = 1.0
    return table


def split_table(table):
    high = table.astype(np.float32).astype(jnp.bfloat16)
    low = (table.astype(np.float32) - high.astype(np.float32)).astype(jnp.bfloat16)
    return high, low


def left_table(table):
    high, low = split_table(table)
    return np.concatenate([high, high, low], axis=1)


def right_table(table):
    high, low = split_table(table)
    return np.concatenate([high, high, low], axis=0)


def fourier_tables(length):
    rows = length // LANES
    outer = 2 * rows
    total = outer * LANES
    turn = 2.0 * np.pi / outer * (np.arange(outer)[:, None] * np.arange(rows)[None, :] % outer)
    c, s = np.cos(turn), np.sin(turn)
    first = np.block([[c, s], [-s, c]])
    first_real = np.block([[c], [-s]])
    last = np.block([[c.T, -s.T], [s.T, c.T]]) / total
    last_real = np.block([[c.T, -s.T]]) / total
    twist = 2.0 * np.pi / total * (np.arange(outer)[:, None] * np.arange(LANES)[None, :])
    twiddle = np.concatenate([np.cos(twist), -np.sin(twist)], axis=1).astype(np.float32)
    lane = 2.0 * np.pi / LANES * (np.arange(LANES)[:, None] * np.arange(LANES)[None, :] % LANES)
    c, s = np.cos(lane), np.sin(lane)
    second = np.block([[c, -s], [s, c]])
    second_back = np.block([[c, s], [-s, c]])
    return (
        left_table(first),
        left_table(first_real),
        twiddle,
        right_table(second),
        right_table(second_back),
        left_table(last),
        left_table(last_real),
    )


def sin_cos(x):
    turns = jnp.round(x * (1.0 / math.pi))
    r = x - turns * 3.140625
    r = r - turns * 9.67025756835937500e-4
    r = r - turns * 6.27711415290832520e-7
    r = r - turns * 1.21542010130123850e-10
    half = turns * 0.5
    sign = 1.0 - 4.0 * jnp.abs(half - jnp.round(half))
    r2 = r * r
    s = -2.5052108385441720e-8
    for k in (2.7557319223985893e-6, -1.9841269841269841e-4, 8.3333333333333333e-3, -1.6666666666666667e-1):
        s = s * r2 + k
    s = r + r * (r2 * s)
    c = 2.0876756987868099e-9
    for k in (-2.7557319223985888e-7, 2.4801587301587302e-5, -1.3888888888888889e-3, 4.1666666666666667e-2, -0.5):
        c = c * r2 + k
    c = 1.0 + r2 * c
    return s * sign, c * sign


def window(delta, length, start, width):
    t = lax.broadcasted_iota(jnp.int32, (1, width), 1) + start
    fraction = t.astype(F32) / (length - 1)
    return jnp.exp(-delta * fraction) + WINDOW_SHIFT


def normalize(x):
    center = x - jnp.mean(x, axis=0, keepdims=True)
    spread = jnp.mean(center * center, axis=0, keepdims=True)
    scale = lax.rsqrt(spread + EPSILON)
    return center * scale, scale


def normalize_back(e, xh, scale):
    return scale * (
        e - jnp.mean(e, axis=0, keepdims=True) - xh * jnp.mean(e * xh, axis=0, keepdims=True)
    )


def gelu_parts(a):
    t = jnp.tanh(GELU_SCALE * (a + GELU_CUBE * a * a * a))
    return 0.5 * (1.0 + t), t


def put_columns(pairs, width=D):
    rows = pairs[0][1].shape[0]
    lane = lax.broadcasted_iota(jnp.int32, (rows, width), 1)
    out = jnp.zeros((rows, width), F32)
    for k, column in pairs:
        out = out + jnp.where(lane == k, column, 0.0)
    return out


def row_sum(x):
    return jnp.sum(x, axis=1, keepdims=True)


def ones_rows(width):
    return (lax.broadcasted_iota(jnp.int32, (EIGHT, width), 0) == 0).astype(F32)


def filter_block(length, start, feat, net, fourth, delta):
    width = feat.shape[1]
    kept = []
    h, c = sin_cos(FREQUENCY * dot(net[:, 0:EIGHT], feat, HIGHEST))
    kept.append((h, FREQUENCY * c))
    for row in (EMB + 1, EMB + 2 + FO):
        v = dot(net[:, row : row + FO], h, HIGHEST) + net[:, row + FO : row + FO + 1]
        h, c = sin_cos(FREQUENCY * v)
        kept.append((h, FREQUENCY * c))
    return dot(fourth, h, HIGHEST) * window(delta, length, start, width), kept


def filter_back_block(length, start, feat, net, fourth, delta, keep, dk, dnet, dfourth):
    width = feat.shape[1]
    ones = ones_rows(width)
    dkw = dk * window(delta, length, start, width)
    dfourth[:, 0:FO] += dot_nt(dkw, keep[2])
    dpre = dot_tn(fourth, dkw) * keep[5]
    row = EMB + 2 + FO
    dnet[2, :, 0 : FO + EIGHT] += dot_nt(dpre, jnp.concatenate([keep[1], ones], axis=0))
    dpre = dot_tn(net[:, row : row + FO], dpre) * keep[4]
    row = EMB + 1
    dnet[1, :, 0 : FO + EIGHT] += dot_nt(dpre, jnp.concatenate([keep[0], ones], axis=0))
    dpre = dot_tn(net[:, row : row + FO], dpre) * keep[3]
    dnet[0, :, 0:EIGHT] += dot_nt(dpre, feat)


def widened(value, width=LANES):
    rows, lanes = value.shape
    return jnp.concatenate([value, jnp.zeros((rows, width - lanes), F32)], axis=1)


def paired(tile, count):
    high = tile.astype(BF16).astype(F32)
    return (high + pltpu.roll(tile - high, count, 1)).astype(BF16)


def named_dot(table, places, repeat=2):
    rows = jnp.concatenate(places * repeat, axis=0)
    rest = LANES - rows.shape[0]
    rows = jnp.concatenate([rows, jnp.zeros((rest, rows.shape[1]), F32)], axis=0)
    return jnp.dot(table, rows.astype(BF16), preferred_element_type=F32)


def halves(x):
    high = x.astype(BF16)
    return high, (x - high.astype(F32)).astype(BF16)


def left_dot(table, x):
    high, low = halves(x)
    return jnp.dot(
        table, jnp.concatenate([high, low, high], axis=0), preferred_element_type=F32
    )


def right_dot(x, table):
    high, low = halves(x)
    return jnp.dot(
        jnp.concatenate([high, low, high], axis=1), table, preferred_element_type=F32
    )


def spectrum_of(x, first, twiddle, second):
    outer = twiddle.shape[0]
    y = left_dot(first, x)
    tr, ti = twiddle[:, :LANES], twiddle[:, LANES:]
    parts = []
    for b in range(x.shape[1] // LANES):
        yr = y[:outer, b * LANES : (b + 1) * LANES]
        yi = y[outer:, b * LANES : (b + 1) * LANES]
        parts.append(jnp.concatenate([yr * tr - yi * ti, yr * ti + yi * tr], axis=1))
    return right_dot(jnp.concatenate(parts, axis=0), second)


def signal_of(v, twiddle, second_back, last):
    outer = twiddle.shape[0]
    a = right_dot(v, second_back)
    tr, ti = twiddle[:, :LANES], twiddle[:, LANES:]
    parts = []
    for b in range(v.shape[0] // outer):
        ar = a[b * outer : (b + 1) * outer, :LANES]
        ai = a[b * outer : (b + 1) * outer, LANES:]
        parts.append(jnp.concatenate([ar * tr + ai * ti, ai * tr - ar * ti], axis=0))
    return left_dot(last, jnp.concatenate(parts, axis=1))


def load_pairs(ref):
    rows = ref.shape[1] // EIGHT
    parts = []
    for b in range(EIGHT):
        parts.append(
            jnp.concatenate([ref[s, pl.ds(b, rows, stride=EIGHT), :] for s in range(2)], axis=0)
        )
    return jnp.concatenate(parts, axis=1)


def store_pairs(ref, value):
    rows = ref.shape[1] // EIGHT
    for b in range(EIGHT):
        for s in range(2):
            ref[s, pl.ds(b, rows, stride=EIGHT), :] = value[
                s * rows : (s + 1) * rows, b * LANES : (b + 1) * LANES
            ]


def times(a, b):
    ar, ai, br, bi = a[:, :LANES], a[:, LANES:], b[:, :LANES], b[:, LANES:]
    return jnp.concatenate([ar * br - ai * bi, ar * bi + ai * br], axis=1)


def times_conj(a, b):
    ar, ai, br, bi = a[:, :LANES], a[:, LANES:], b[:, :LANES], b[:, LANES:]
    return jnp.concatenate([ar * br + ai * bi, ai * br - ar * bi], axis=1)


def send(a, b, sems, index, device):
    copy = remote(a, b, sems, index, device)
    copy.start()
    return copy


def remote(a, b, sems, index, device):
    return pltpu.make_async_remote_copy(
        src_ref=a, dst_ref=b, send_sem=sems[0].at[index], recv_sem=sems[1].at[index],
        device_id=device, device_id_type=MESH,
    )


def exchange(refs, peers, send_sem, recv_sem, base):
    return [
        send(a, b, (send_sem, recv_sem), base + k, peer)
        for k, ((a, b), peer) in enumerate(zip(refs, peers))
    ]


def greet(n, mates=()):
    me, b = lax.axis_index("chan"), lax.axis_index("batch")
    barrier = pltpu.get_barrier_semaphore()
    for d in range(1, n):
        pl.semaphore_signal(
            barrier, inc=1, device_id={"chan": lax.rem(me + d, n)}, device_id_type=MESH
        )
    for mate in mates:
        pl.semaphore_signal(barrier, inc=1, device_id={"batch": mate}, device_id_type=MESH)
    pl.semaphore_wait(barrier, n - 1 + len(mates))


def core_mate(b):
    return b + 1 - 2 * lax.rem(b, 2)


def y_mate(b):
    return b + 2 - 4 * (b // 2)


def comm_params(cid):
    return pltpu.CompilerParams(
        collective_id=cid, has_side_effects=True, vmem_limit_bytes=VMEM_LIMIT
    )


def pair_sems(*shape):
    return [pltpu.SemaphoreType.DMA(shape), pltpu.SemaphoreType.DMA(shape)]


class Blocks:
    def __init__(self, n, span, sems, own):
        self.n, self.span, self.sems, self.own = n, span, sems, own
        self.me = lax.axis_index("chan")

    def rows(self, j):
        return pl.ds(pl.multiple_of(j * self.span, 8), self.span)

    def out_refs(self, k, j, src, dst):
        return src.at[k, j], dst.at[k, :, self.rows(self.me), :]

    def back_refs(self, k, j, src, dst):
        return src.at[k, :, self.rows(j), :], dst.at[k, self.me]

    def each(self, refs, k, src, dst):
        for d in range(1, self.n):
            j = lax.rem(self.me + d, self.n)
            a, b = refs(k, j, src, dst)
            yield remote(a, b, self.sems, (k, d), {"chan": j})

    def start(self, refs, k, src, dst):
        a, b = refs(k, self.me, src, dst)
        pltpu.make_async_copy(a, b, self.own.at[k]).start()
        for copy in self.each(refs, k, src, dst):
            copy.start()

    def arrived(self, refs, k, src, dst):
        for copy in self.each(refs, k, src, dst):
            copy.wait_recv()
        a, b = refs(k, self.me, src, dst)
        pltpu.make_async_copy(a, b, self.own.at[k]).wait()

    def sent(self, refs, k, src, dst):
        for copy in self.each(refs, k, src, dst):
            copy.wait_send()


class Tiles:
    def __init__(self, n, tiles, sems, own, src, dst):
        self.n, self.tiles, self.sems, self.own = n, tiles, sems, own
        self.src, self.dst = src, dst
        self.me = lax.axis_index("chan")

    def refs(self, q, j):
        here = pl.ds(pl.multiple_of(q * EIGHT, 8), EIGHT)
        there = pl.ds(pl.multiple_of((self.me * self.tiles + q) * EIGHT, 8), EIGHT)
        return self.src.at[:, j, :, here, :], self.dst.at[:, :, there, :]

    def each(self, q):
        for d in range(1, self.n):
            j = lax.rem(self.me + d, self.n)
            yield remote(*self.refs(q, j), self.sems, (q, d), {"chan": j})

    def start(self, q):
        for copy in self.each(q):
            copy.start()
        pltpu.make_async_copy(*self.refs(q, self.me), self.own.at[q]).start()

    def arrived(self, q):
        for copy in self.each(q):
            copy.wait_recv()
        pltpu.make_async_copy(*self.refs(q, self.me), self.own.at[q]).wait()

    def sent(self, q):
        for copy in self.each(q):
            copy.wait_send()


class Names:
    def __init__(self, values):
        self.__dict__.update(values)


def loop(count, body):
    def step(i, _):
        body(i)
        return 0

    lax.fori_loop(0, count, step, 0)


def round_up(value, step):
    return -(-value // step) * step


def quarter_rows(refs_rows, k):
    quarter = refs_rows // 4
    return pl.ds(pl.multiple_of(k * quarter, 8), quarter)


def fold(value, n, chans, back=False):
    lane = lax.broadcasted_iota(jnp.int32, (chans, LANES), 1)
    wide = 4 * n * chans // LANES
    narrow = n * chans // LANES
    if back:
        tiles = [[value[c][:, t * LANES : (t + 1) * LANES] for t in range(narrow)] for c in range(4)]
        out = [None] * wide
    else:
        tiles = [value[:, t * LANES : (t + 1) * LANES] for t in range(wide)]
        out = [[None] * narrow for _ in range(4)]
    for c in range(4):
        for i in range(n):
            a, b = i * 4 * chans + c * chans, i * chans
            if back:
                source, to, at = tiles[c][b // LANES], a % LANES, b % LANES
                row, k = out, a // LANES
            else:
                source, to, at = tiles[a // LANES], b % LANES, a % LANES
                row, k = out[c], b // LANES
            shift = (to - at) % LANES
            moved = pltpu.roll(source, shift, 1) if shift else source
            inside = (lane >= to) & (lane < to + chans)
            row[k] = jnp.where(inside, moved, 0.0 if row[k] is None else row[k])
    if back:
        return jnp.concatenate(out, axis=1)
    return [jnp.concatenate(tiles, axis=1) for tiles in out]


def conv_chunk(k, g, spec, gspec, z, first, twiddle, second, second_back, last):
    outer = twiddle.shape[0]
    rows = pl.ds(pl.multiple_of(k * EIGHT * outer, 8), EIGHT * outer)
    u = spectrum_of(load_pairs(g.at[k]), first[...], twiddle[...], second[...])
    gspec[rows, :] = u
    o = signal_of(times(u, spec[rows, :]), twiddle[...], second_back[...], last[...])
    store_pairs(z.at[k], o)


def decay(me, chans):
    ids = lax.broadcasted_iota(jnp.int32, (chans, 1), 0) + me * chans
    slow = math.log(0.01) / 1.5
    fast = math.log(0.01) / 0.3
    return jnp.abs(slow + (fast - slow) * ids.astype(F32) / (D - 1))


def hops(n, b, me, sems, local):
    half = n // 2
    x, z = lax.rem(me, 2), me // 2
    side = {"chan": 2 * z + 1 - x}

    def hop_z(c, src, dst):
        keep = pltpu.make_async_copy(src, dst.at[me], local.at[c])
        keep.start()
        copies = [
            send(src, dst.at[me], sems, (c, d), {"chan": 2 * lax.rem(z + d, half) + x})
            for d in range(1, half)
        ]
        return keep, copies

    def hop_x(c, src, dst, keep, copies):
        out = [send(src, dst.at[me], sems, (c, half), side)]
        for d in range(1, half):
            j = 2 * lax.rem(z + half - d, half) + x
            copies[d - 1].wait_recv()
            out.append(send(dst.at[j], dst.at[j], sems, (c, half + d), side))
        keep.wait()
        return out

    return hop_z, hop_x


def filter_steps(r, l, b, length, groups, keep, delta):
    block = 512
    fourth = r.chan_t[l, :, 13 : 13 + FO]

    def body(i):
        start = b * (length // 4) + i * block
        out, kept = filter_block(
            length, start, r.feat[:, pl.ds(pl.multiple_of(start, block), block)],
            r.filt_t.at[l], fourth, delta,
        )
        place = pl.ds(pl.multiple_of(i * block, block), block)
        for k, (sine, cosine) in enumerate(kept):
            keep[k, :, place] = sine
            keep[3 + k, :, place] = cosine
        for q in range(block // LANES):
            rows = pl.ds(pl.multiple_of((start // LANES + q) * EIGHT, 8), EIGHT)
            for k in range(groups):
                r.kern[l, k, rows, :] = out[
                    k * EIGHT : (k + 1) * EIGHT, q * LANES : (q + 1) * LANES
                ]

    loop(length // 4 // block, body)


def name_rows(tokx, s, lanes):
    width = tokx.shape[2] if lanes is None else LANES
    names = lax.broadcasted_iota(jnp.int32, (VOCAB, width), 0).astype(F32)
    rows = [tokx[s, k : k + 1, :] if lanes is None else tokx[s, k : k + 1, lanes] for k in range(3)]
    here, one, two = [(names == row).astype(F32) for row in rows]
    return [two, one, here]


def name_tables(shared, misc, j):
    lane = lax.broadcasted_iota(jnp.int32, (D, LANES), 1)
    rows = pltpu.roll(shared, LANES - j * VOCAB, 1) if j else shared
    rows = jnp.where(lane < VOCAB, rows, 0.0)
    t = TAP0 + 3 * j
    mix = (
        misc[:, t : t + 1] * rows
        + misc[:, t + 1 : t + 2] * pltpu.roll(rows, VOCAB, 1)
        + misc[:, t + 2 : t + 3] * pltpu.roll(rows, 2 * VOCAB, 1)
    )
    return paired(rows, VOCAB), paired(mix, 3 * VOCAB)


def prepare_kernel(
    n, length, chans, ids, embedding, inward, vectors, outward, expand, offsets, contract,
    chan_t, filt_t, feat, first, first_real, twiddle, second, second_back, last, last_real,
    wall, late, spec0, spec1, gspec, keep0, keep1, zpos, misc, toks, tokx, shared, owned,
    upper, side, town, rows, flip, kern, gch, zch, spec0v, spec1v, gspecv, keep0v, keep1v,
    osem, ss, sr, ws, wr, ks, kr, zs, zr, local, zown,
):
    r = Names(locals())
    me, b = lax.axis_index("chan"), lax.axis_index("batch")
    groups = chans // EIGHT
    seqs, span = r.zpos.shape[2], r.zpos.shape[3]
    width = span // EIGHT * LANES
    parts = width // D
    tabs = (r.first, r.twiddle, r.second, r.second_back, r.last)
    flip, side, town = r.flip, r.side, r.town
    flip[...] = jnp.zeros_like(flip)
    for k in range(9):
        for l in range(LAYERS):
            row = VEC0 + 9 * l + k
            flip[row : row + 1, 0:chans] = r.vectors[k, l : l + 1, :]
    flip[EMB0 : EMB0 + VOCAB, 0:chans] = r.embedding[...]
    for l in range(LAYERS):
        for c in range(4):
            row = OFF0 + 4 * l + c
            flip[row : row + 1, 0:chans] = r.offsets[l : l + 1, c * chans : (c + 1) * chans]
    columns = flip[...].T[:chans, :]
    lane = lax.broadcasted_iota(jnp.int32, (chans, LANES), 1)
    for l in range(LAYERS):
        taps = jnp.where(lane < 12, widened(r.chan_t[l]), 0.0)
        columns = columns + pltpu.roll(taps, TAP0 + 12 * l, 1)
    side[:, 0:LANES] = columns
    side[:, LANES:] = jnp.zeros((chans, LANES), F32)
    town[...] = jnp.zeros_like(town)
    for s in range(seqs):
        for h in range(parts):
            town[s * parts + h : s * parts + h + 1, :] = r.ids[
                s : s + 1, h * D : (h + 1) * D
            ].astype(F32)
    for l, rear, front in ((0, r.owned, r.upper), (1, r.upper, r.owned)):
        for j in range(3):
            front[(9 + j) * chans : (10 + j) * chans, :] = r.inward[l, j]
        rear[0:chans, :] = r.outward[l]
        rear[chans : 5 * chans, :] = r.expand[l]
        for c, piece in enumerate(fold(r.contract[l], n, chans)):
            rear[(5 + c) * chans : (6 + c) * chans, :] = piece
    greet(n, (core_mate(b), y_mate(b)))
    mine = pl.ds(pl.multiple_of(me * chans, 8), chans)
    small = []
    for d in range(1, n):
        peer = {"chan": lax.rem(me + d, n)}
        small.append(send(side, r.misc.at[mine, :], (r.ss, r.sr), d, peer))
        small.append(send(town, r.toks.at[me], (r.ss, r.sr), n + d, peer))
    r.misc[mine, :] = side[...]
    r.toks[me] = town[...]
    weights = (r.ws, r.wr)
    hop_z, hop_x = hops(n, b, me, weights, r.local)
    count = r.wall.shape[1] // 2
    core = lax.rem(b, 2)

    def part(c, k):
        size = count // (2 if c else 4)
        return pl.ds(pl.multiple_of(c * count + k * size, 8), size)

    low = [(r.owned.at[part(c, k)], r.wall.at[:, part(c, k)]) for c, k in ((0, b), (1, core))]
    z_w = [hop_z(0, *low[0]), None]
    x_w, y_w, core_w = [None] * 2, [], []
    saves = []

    def save(src, dst):
        copy = pltpu.make_async_copy(src, dst, r.osem.at[len(saves)])
        copy.start()
        saves.append(copy)

    save(r.upper, r.late)

    def hop_y():
        for copy in x_w[0]:
            copy.wait_recv()
        here = r.wall.at[:, part(0, b)]
        y_w.append(send(here, here, weights, (0, n), {"batch": y_mate(b)}))
        core_w.append(send(here, here, weights, (0, n + 1), {"batch": core_mate(b)}))

    def hop_core():
        for copy in x_w[1]:
            copy.wait_recv()
        here = r.wall.at[:, part(1, core)]
        core_w.append(send(here, here, weights, (1, n), {"batch": core_mate(b)}))
        y_w[0].wait_recv()
        here = r.wall.at[:, part(0, y_mate(b))]
        core_w.append(send(here, here, weights, (0, n + 2), {"batch": core_mate(b)}))

    delta = decay(me, chans)
    count_lag = r.kern.shape[2] // 4
    lags = [pl.ds(pl.multiple_of(k * count_lag, 8), count_lag) for k in (b, y_mate(b))]

    def offer(l):
        place = r.kern.at[l, :, lags[0], :]
        return send(place, place, (r.ks, r.kr), (l, 0), {"batch": y_mate(b)})

    def share(l, copy):
        copy.wait_recv()
        return [
            send(
                r.kern.at[l, :, k, :], r.kern.at[l, :, k, :], (r.ks, r.kr), (l, 1 + i),
                {"batch": core_mate(b)},
            )
            for i, k in enumerate(lags)
        ]

    def spectra(l, copies, spec):
        for copy in copies:
            copy.wait_recv()
        outer = r.twiddle.shape[0]
        rows = length // LANES

        def body(k):
            taps = jnp.concatenate(
                [r.kern[l, k, pl.ds(c, rows, stride=EIGHT), :] for c in range(EIGHT)], axis=1
            )
            u = spectrum_of(taps, r.first_real[...], r.twiddle[...], r.second[...])
            here = pl.ds(pl.multiple_of(k * EIGHT, 8), EIGHT)
            gain = jnp.broadcast_to(r.chan_t[l, here, 12:13], (EIGHT, LANES))
            for c in range(EIGHT):
                wide = jnp.broadcast_to(gain[c : c + 1, :], (outer, LANES))
                both = jnp.concatenate([wide, jnp.zeros_like(wide)], axis=1)
                place = pl.ds(pl.multiple_of((k * EIGHT + c) * outer, 8), outer)
                spec[place, :] = u[c * outer : (c + 1) * outer] + both

        loop(groups, body)

    filter_steps(r, 0, b, length, groups, r.keep0v, delta)
    y_k0 = offer(0)
    save(r.keep0v, r.keep0)
    for copy in small:
        copy.wait()
    table = r.misc[...]
    xh, _ = normalize(table)
    normed = xh * table[:, VEC0 : VEC0 + 1] + table[:, VEC0 + 1 : VEC0 + 2]
    own = side[...]
    shared = jnp.zeros((chans, LANES), F32)
    mixes, biases = [], []
    for j in range(3):
        rows = dot(r.inward[0, j], normed, HIGHEST)
        rows = rows + own[:, VEC0 + 4 + j : VEC0 + 5 + j]
        rows = pltpu.roll(rows, D - EMB0, 1)[:, :LANES]
        rows = jnp.where(lane < VOCAB, rows, 0.0)
        shared = shared + (pltpu.roll(rows, j * VOCAB, 1) if j else rows)
        if j:
            k = TAP0 + 3 * j
            mixes.append(
                own[:, k : k + 1] * rows
                + own[:, k + 1 : k + 2] * pltpu.roll(rows, VOCAB, 1)
                + own[:, k + 2 : k + 3] * pltpu.roll(rows, 2 * VOCAB, 1)
            )
            biases.append(own[:, TAP0 + 9 + j : TAP0 + 10 + j])
    r.rows[...] = shared
    r.shared[mine, :] = shared
    for d in range(1, n):
        peer = {"chan": lax.rem(me + d, n)}
        small.append(send(r.rows, r.shared.at[mine, :], (r.ss, r.sr), 2 * n + d, peer))
    mix = paired(jnp.concatenate(mixes, axis=0), 3 * VOCAB)
    names = lax.broadcasted_iota(jnp.int32, (VOCAB, width), 0).astype(F32)
    toks = r.toks

    def shifted(i, s):
        here = jnp.concatenate(
            [toks[i, s * parts + h : s * parts + h + 1, :] for h in range(parts)], axis=1
        )
        before = toks[jnp.maximum(i - 1, 0), (s + 1) * parts - 1 : (s + 1) * parts, D - LANES :]
        long = jnp.concatenate([jnp.where(i > 0, before, -1.0), here], axis=1)
        return here, pltpu.roll(long, 1, 1)[:, LANES:], pltpu.roll(long, 2, 1)[:, LANES:]

    for s in range(seqs):
        for k, row in enumerate(shifted(me, s)):
            r.tokx[s, k : k + 1, :] = row

    def gates(i):
        for s in range(seqs):
            here, one, two = shifted(i, s)
            out = named_dot(mix, [(names == row).astype(F32) for row in (two, one, here)])
            gate = (out[:chans] + biases[0]) * (out[chans:] + biases[1])
            for q in range(width // LANES):
                rows = pl.ds(pl.multiple_of(i * span + q * EIGHT, 8), EIGHT)
                for k in range(groups):
                    r.gch[k, s, rows, :] = gate[
                        k * EIGHT : (k + 1) * EIGHT, q * LANES : (q + 1) * LANES
                    ]

    loop(n // 2, gates)
    core_k0 = share(0, y_k0)
    x_w[0] = hop_x(0, *low[0], *z_w[0])
    z_w[1] = hop_z(1, *low[1])
    loop(n // 2, lambda i: gates(i + n // 2))
    spectra(0, core_k0, r.spec0v)
    hop_y()
    save(r.spec0v, r.spec0)
    back = Blocks(n, span, (r.zs, r.zr), r.zown)

    def chunk(k):
        conv_chunk(
            k, r.gch, r.spec0v, r.gspecv, r.zch, *tabs
        )
        back.start(back.back_refs, k, r.zch, r.zpos)

    early = max(groups // 2, 1)
    loop(early, chunk)
    x_w[1] = hop_x(1, *low[1], *z_w[1])
    loop(groups - early, lambda k: chunk(k + early))
    save(r.gspecv, r.gspec)
    filter_steps(r, 1, b, length, groups, r.keep1v, delta)
    y_k1 = offer(1)
    save(r.keep1v, r.keep1)
    hop_core()
    core_k1 = share(1, y_k1)
    spectra(1, core_k1, r.spec1v)
    save(r.spec1v, r.spec1)

    def finish(k):
        back.arrived(back.back_refs, k, r.zch, r.zpos)
        back.sent(back.back_refs, k, r.zch, r.zpos)

    loop(groups, finish)
    for _, copies in z_w:
        for copy in copies:
            copy.wait_send()
    for copy in saves:
        copy.wait()
    for copy in x_w[0] + x_w[1] + y_w + [y_k0, y_k1] + core_k0 + core_k1:
        copy.wait_send()
    for copy in core_w + small[2 * (n - 1) :]:
        copy.wait()


def prepare(arrays, tables, n, seqs, length, cid):
    chan_t = arrays[8]
    chans = chan_t.shape[1]
    groups = chans // EIGHT
    rows = length // LANES
    span = rows // n * EIGHT
    outer = 2 * rows
    width = length // n
    spec = sds(chans * outer, 2 * LANES)
    keep = sds(6, FO, length // 4)
    low, high = round_up(12 * chans, 64), round_up(12 * chans, 32)
    return pl.pallas_call(
        partial(prepare_kernel, n, length, chans),
        in_specs=[WHOLE] * 18,
        out_specs=[HBM] * 8 + [WHOLE] * 4,
        out_shape=[
            sds(n, low, D), sds(high, D),
            spec, spec, spec, keep, keep, sds(groups, n, seqs, span, LANES),
            sds(D, D), sds(n, EIGHT, D), sds(seqs, EIGHT, width), sds(D, LANES),
        ],
        scratch_shapes=[
            VMEM((low, D), F32),
            VMEM((high, D), F32),
            VMEM((chans, D), F32),
            VMEM((EIGHT, D), F32),
            VMEM((chans, LANES), F32),
            VMEM((LANES, LANES), F32),
            VMEM((LAYERS, groups, rows * EIGHT, LANES), F32),
            VMEM((groups, seqs, rows * EIGHT, LANES), F32),
            VMEM((groups, seqs, rows * EIGHT, LANES), F32),
            *[VMEM(spec.shape, F32)] * 3,
            *[VMEM(keep.shape, F32)] * 2,
            pltpu.SemaphoreType.DMA((6,)),
            *pair_sems(3 * n),
            *pair_sems(2, n + 3),
            *pair_sems(LAYERS, 3),
            *pair_sems(groups, n),
            pltpu.SemaphoreType.DMA((2,)),
            pltpu.SemaphoreType.DMA((groups,)),
        ],
        compiler_params=comm_params(cid),
        name="prepare",
    )(*arrays, position_table(length), *tables)


def middle_kernel(
    n, chans, z, wall, late, spec, misc, shared, tokx, first, first_real, twiddle, second,
    second_back, last, last_real, wlate, h, a, x1, p, q, gspec, zpos, zv, wv, hv, av, x1v,
    pv, qv, table, gpos, gch, zch, tails, halo, gspecv, gs, gr, gown, zs, zr, zown, hs, hr,
    ws, wr, wown, lsem,
):
    r = Names(locals())
    me, b = lax.axis_index("chan"), lax.axis_index("batch")
    seqs, width = r.x1v.shape[0], r.x1v.shape[2]
    groups, tiles = chans // EIGHT, width // LANES
    lane0 = TAP0 + 12
    loads = [
        pltpu.make_async_copy(r.z, r.zv, r.lsem.at[0]),
        pltpu.make_async_copy(r.wall.at[:, 0 : r.wv.shape[1]], r.wv, r.lsem.at[1]),
    ]
    for copy in loads:
        copy.start()
    r.table[...] = name_tables(r.shared[...], r.misc[...], 0)[1]
    greet(n, (core_mate(b), y_mate(b)))
    weights = (r.ws, r.wr)
    hop_z, hop_x = hops(n, b, me, weights, r.wown)
    mine = quarter_rows(r.wlate.shape[1], b)
    other = quarter_rows(r.wlate.shape[1], y_mate(b))
    late = (r.late.at[mine], r.wlate.at[:, mine])
    z_w = hop_z(0, *late)
    out = Tiles(n, tiles, (r.gs, r.gr), r.gown, r.gpos, r.gch)
    back = Blocks(n, tiles * EIGHT, (r.zs, r.zr), r.zown)
    for copy in loads:
        copy.wait()
    low = Layer(None, r.wv, r.misc, 0)
    high = Layer(r.wv.at[:, 9 * chans :], None, r.misc, 1)
    edge_lane = lax.broadcasted_iota(jnp.int32, (D, LANES), 1)
    inner = (me > 0).astype(F32)
    halo_copy = remote(r.tails, r.halo, (r.hs, r.hr), 0, {"chan": lax.rem(me + 1, n)})

    def tile(q):
        places = places_of(r.tokx, q)
        x = embedded(low.side, places[2])
        first_gate = named_dot(r.table[...], places) + low.column(TAP0 + 9)
        mixed = rear_mix(low, x, take_blocks(r.zv, q) * first_gate)
        put(r.hv, q, mixed)
        _, _, _, pre = rear_hidden(low, mixed)
        u = []
        for k in range(4):
            put(r.av.at[:, k], q, pre[k])
            u.append(pre[k] * gelu_parts(pre[k])[0])
        x = rear_out(low, mixed, u)
        put(r.x1v, q, x)
        for j, value in enumerate(front_forward(high, x)):
            put(r.pv.at[j], q, value)

    def gates(q):
        here = pl.ds(pl.multiple_of(q * LANES, LANES), LANES)
        prior = pl.ds(pl.multiple_of(jnp.maximum(q - 1, 0) * LANES, LANES), LANES)
        made = []
        for j in range(3):
            t = lane0 + 3 * j
            row = []
            for s in range(seqs):
                edge = pltpu.roll(r.halo[...], LANES - 2 - 2 * (j * seqs + s), 1) * inner
                before = jnp.where(q > 0, r.pv[j, s, :, prior], edge)
                now = r.pv[j, s, :, here]
                long = jnp.concatenate([before, now], axis=1)
                one = pltpu.roll(long, 1, 1)[:, LANES:]
                two = pltpu.roll(long, 2, 1)[:, LANES:]
                value = (
                    r.misc[:, lane0 + 9 + j : lane0 + 10 + j]
                    + r.misc[:, t : t + 1] * two
                    + r.misc[:, t + 1 : t + 2] * one
                    + r.misc[:, t + 2 : t + 3] * now
                )
                r.qv[j, s, :, here] = value
                row.append(value)
            made.append(row)
        gate = [made[2][s] * made[1][s] for s in range(seqs)]
        put_blocks(r.gpos, q, jnp.concatenate(gate, axis=1))
        out.start(q)

    def step(i):
        q = lax.rem(i + tiles - 1, tiles)
        tile(q)

        @pl.when(i == 0)
        def _():
            pack = jnp.zeros((D, LANES), F32)
            for j in range(3):
                for s in range(seqs):
                    slot = 2 * (j * seqs + s)
                    tail = pltpu.roll(r.pv[j, s, :, width - LANES :], slot + 2, 1)
                    pack = jnp.where((edge_lane == slot) | (edge_lane == slot + 1), tail, pack)
            r.tails[...] = pack
            halo_copy.start()

        @pl.when(i == 1)
        def _():
            halo_copy.wait_recv()

        @pl.when(i > 0)
        def _():
            gates(q)

    loop(tiles - 1, step)
    x_w = hop_x(0, *late, *z_w)
    step(tiles - 1)
    gates(tiles - 1)
    saves = [
        pltpu.make_async_copy(src, dst, r.lsem.at[3 + i])
        for i, (src, dst) in enumerate(
            ((r.hv, r.h), (r.av, r.a), (r.x1v, r.x1), (r.pv, r.p), (r.qv, r.q))
        )
    ]
    for copy in saves:
        copy.start()
    loop(tiles, out.arrived)

    def chunk(k):
        conv_chunk(
            k, r.gch, r.spec, r.gspecv, r.zch, r.first, r.twiddle, r.second, r.second_back, r.last
        )
        back.start(back.back_refs, k, r.zch, r.zpos)

    chunk(0)
    for copy in x_w:
        copy.wait_recv()
    here, there = r.wlate.at[:, mine], r.wlate.at[:, other]
    y_w = send(here, here, weights, (0, n), {"batch": y_mate(b)})
    core_w = [send(here, here, weights, (0, n + 1), {"batch": core_mate(b)})]
    loop(groups - 1, lambda k: chunk(k + 1))
    saves.append(pltpu.make_async_copy(r.gspecv, r.gspec, r.lsem.at[2]))
    saves[-1].start()
    loop(tiles, out.sent)
    loop(groups - 1, lambda k: back.arrived(back.back_refs, k, r.zch, r.zpos))
    y_w.wait_recv()
    core_w.append(send(there, there, weights, (0, n + 2), {"batch": core_mate(b)}))
    back.arrived(back.back_refs, groups - 1, r.zch, r.zpos)

    loop(groups, lambda k: back.sent(back.back_refs, k, r.zch, r.zpos))
    for copy in saves:
        copy.wait()
    halo_copy.wait_send()
    for copy in z_w[1] + x_w + [y_w]:
        copy.wait_send()
    for copy in core_w:
        copy.wait()


def middle(z, wall, late, spec, misc, shared, tokx, tables, n, chans, cid):
    groups, _, seqs, span, _ = z.shape
    width = span // EIGHT * LANES
    tiles = width // LANES
    by_channel = (groups, seqs, n * span, LANES)
    pos = (seqs, D, width)
    return pl.pallas_call(
        partial(middle_kernel, n, chans),
        in_specs=[HBM] * 3 + [WHOLE] * 11,
        out_specs=[HBM] * 8,
        out_shape=[
            sds(n, *late.shape), sds(*pos), sds(seqs, 4, D, width), sds(*pos),
            sds(3, *pos), sds(3, *pos), sds(*spec.shape), sds(*z.shape),
        ],
        scratch_shapes=[
            VMEM(z.shape, F32),
            VMEM((n, 12 * chans, D), F32),
            VMEM(pos, F32),
            VMEM((seqs, 4, D, width), F32),
            VMEM(pos, F32),
            VMEM((3,) + pos, F32),
            VMEM((3,) + pos, F32),
            VMEM((D, LANES), BF16),
            VMEM(z.shape, F32),
            VMEM(by_channel, F32),
            VMEM(by_channel, F32),
            VMEM((D, LANES), F32),
            VMEM((D, LANES), F32),
            VMEM(spec.shape, F32),
            *pair_sems(tiles, n),
            pltpu.SemaphoreType.DMA((tiles,)),
            *pair_sems(groups, n),
            pltpu.SemaphoreType.DMA((groups,)),
            *pair_sems(1),
            *pair_sems(1, n + 3),
            pltpu.SemaphoreType.DMA((1,)),
            pltpu.SemaphoreType.DMA((8,)),
        ],
        compiler_params=comm_params(cid),
        name="middle",
    )(z, wall, late, spec, misc, shared, tokx, *tables)


class GroupSum:
    def __init__(self, n, g, out, r0, sum0, r1, sum1, r2, send_sem, recv_sem):
        self.n, self.g, self.out = n, g, out
        self.r0, self.sum0, self.r1, self.sum1, self.r2 = r0, sum0, r1, sum1, r2
        self.sems = (send_sem, recv_sem)
        me, b = lax.axis_index("chan"), lax.axis_index("batch")
        self.x, self.z = lax.rem(me, 2), me // 2
        self.core, self.y = lax.rem(b, 2), b // 2
        self.b = b
        self.copies = []

    def part(self, k):
        return quarter_rows(self.g.shape[1], k)

    def cores(self):
        mate = {"batch": core_mate(self.b)}
        for k in range(2):
            source = self.g.at[:, self.part(2 * k + 1 - self.core)]
            self.copies.append(send(source, self.r0.at[k], self.sems, k, mate))

    def along_y(self):
        for k in range(2):
            self.copies[k].wait_recv()

            def add(i, k=k):
                mine = self.g[i, self.part(2 * k + self.core), :]
                self.sum0[k, i] = mine + self.r0[k, i]

            loop(self.n, add)
        self.copies.append(
            send(self.sum0.at[1 - self.y], self.r1, self.sems, 2, {"batch": y_mate(self.b)})
        )

    def along_x(self):
        self.copies[2].wait_recv()

        def add(i):
            self.sum1[lax.rem(i, 2), i // 2] = self.sum0[self.y, i] + self.r1[i]

        loop(self.n, add)
        to = {"chan": 2 * self.z + 1 - self.x}
        self.copies.append(send(self.sum1.at[1 - self.x], self.r2, self.sems, 3, to))

    def close(self):
        self.copies[3].wait_recv()

        def add(i):
            self.out[i] = self.sum1[self.x, i] + self.r2[i]

        loop(self.n // 2, add)
        for copy in self.copies:
            copy.wait_send()


class ColumnSum:
    def __init__(self, n, source, landing, rows, zs, zr, bs, br):
        self.source, self.landing, self.rows = source, landing, rows
        self.zsems, self.bsems = (zs, zr), (bs, br)
        self.half = n // 2
        me, self.b = lax.axis_index("chan"), lax.axis_index("batch")
        self.x, self.z = lax.rem(me, 2), me // 2

    def column(self):
        for d in range(1, self.half):
            to = lax.rem(self.z + d, self.half)
            yield remote(
                self.source.at[to], self.landing.at[d - 1], self.zsems, d - 1,
                {"chan": 2 * to + self.x},
            )

    def quarter(self, k):
        return self.rows.at[quarter_rows(self.rows.shape[0], k)]

    def hop(self, k):
        mine, other = self.quarter(self.b), self.quarter(y_mate(self.b))
        ref, to = ((mine, y_mate), (mine, core_mate), (other, core_mate))[k]
        return remote(ref, ref, self.bsems, k, {"batch": to(self.b)})

    def start(self):
        for copy in self.column():
            copy.start()

    def share(self):
        total = self.source[self.z]
        for d, copy in enumerate(self.column()):
            copy.wait_recv()
            total = total + self.landing[d]
        self.rows[quarter_rows(self.rows.shape[0], self.b), :] = total
        self.hop(0).start()
        self.hop(1).start()

    def pass_on(self):
        self.hop(0).wait_recv()
        self.hop(2).start()

    def arrived(self):
        self.hop(1).wait_recv()
        self.hop(2).wait_recv()

    def sent(self):
        for copy in self.column():
            copy.wait_send()
        for k in range(3):
            self.hop(k).wait_send()


def column_scratch(n, quarter):
    return [
        VMEM((n // 2 - 1, quarter, D), F32),
        *pair_sems(n // 2 - 1),
        *pair_sems(3),
    ]


def group_scratch(n, rows):
    quarter, half = rows // 4, n // 2
    return [
        VMEM((2, n, quarter, D), F32),
        VMEM((2, n, quarter, D), F32),
        VMEM((n, quarter, D), F32),
        VMEM((2, half, quarter, D), F32),
        VMEM((half, quarter, D), F32),
        *pair_sems(4),
    ]


def take(ref, q):
    lanes = pl.ds(pl.multiple_of(q * LANES, LANES), LANES)
    return jnp.concatenate([ref[s, :, lanes] for s in range(ref.shape[0])], axis=1)


def put(ref, q, value):
    lanes = pl.ds(pl.multiple_of(q * LANES, LANES), LANES)
    for s in range(ref.shape[0]):
        ref[s, :, lanes] = value[:, s * LANES : (s + 1) * LANES]


def take_blocks(ref, q):
    groups, n, seqs, _, _ = ref.shape
    here = pl.ds(pl.multiple_of(q * EIGHT, 8), EIGHT)
    return jnp.concatenate(
        [
            jnp.concatenate(
                [ref[k, j, s, here, :] for j in range(n) for k in range(groups)], axis=0
            )
            for s in range(seqs)
        ],
        axis=1,
    )


def put_blocks(ref, q, value):
    groups, n, seqs, _, _ = ref.shape
    here = pl.ds(pl.multiple_of(q * EIGHT, 8), EIGHT)
    for s in range(seqs):
        for j in range(n):
            for k in range(groups):
                row = (j * groups + k) * EIGHT
                ref[k, j, s, here, :] = value[row : row + EIGHT, s * LANES : (s + 1) * LANES]


def places_of(tokx, q):
    lanes = pl.ds(pl.multiple_of(q * LANES, LANES), LANES)
    rows = [name_rows(tokx, s, lanes) for s in range(tokx.shape[0])]
    return [jnp.concatenate([row[k] for row in rows], axis=1) for k in range(3)]


def embedded(side, places):
    lane = lax.broadcasted_iota(jnp.int32, (D, LANES), 1)
    table = jnp.where(lane < VOCAB, pltpu.roll(side, D - EMB0, 1)[:, :LANES], 0.0)
    high = table.astype(BF16).astype(F32)
    middle = (table - high).astype(BF16).astype(F32)
    low = table - high - middle
    three = high + pltpu.roll(middle, VOCAB, 1) + pltpu.roll(low, 2 * VOCAB, 1)
    return named_dot(three.astype(BF16), [places] * 3, 1)


def top_tile(r, q):
    lay = Layer(None, r.wv, r.misc, 1)
    zt, qt = take_blocks(r.zv, q), take(r.qv.at[0], q)
    y = zt * qt
    h = rear_mix(lay, take(r.x1v, q), y)
    _, _, _, pre = rear_hidden(lay, h)
    put(r.x2, q, rear_out(lay, h, [v * gelu_parts(v)[0] for v in pre]))
    dh, dy, columns = rear_backward(lay, h, pre, y, take(r.cotv, q), r.dw)
    put_blocks(r.dzpos, q, dy * qt)
    put(r.dq0v, q, dy * zt)
    put(r.dh_out, q, dh)
    r.cols[...] += put_columns(columns)


def mid_tile(r, q):
    upper = Layer(r.wv.at[:, 9 * (D // r.wv.shape[0]) :], None, r.misc, 1)
    dout, columns = front_backward(
        upper, take(r.x1v, q), [take(r.pv.at[j], q) for j in range(3)], take(r.dh1v, q), r.dw
    )
    lay = Layer(None, r.wv, r.misc, 0)
    zt = take_blocks(r.zv, q)
    qt = named_dot(r.qtab[0], places_of(r.tokx, q)) + lay.column(TAP0 + 9)
    dh, dy, more = rear_backward(
        lay, take(r.hv, q), [take(r.av.at[:, k], q) for k in range(4)], zt * qt, dout, r.dw, 3
    )
    put_blocks(r.dzpos, q, dy * qt)
    put(r.dq0v, q, dy * zt)
    put(r.dh_out, q, dh)
    r.cols[...] += put_columns(columns + more)


def top_kernel(
    n, chans, length, z, keep, spec, gspec, x1, w, misc, chan_t, filt_t, feat, q, p, cot,
    first, first_real, twiddle, second, second_back, last, last_real, dp, dh_out, cols,
    dnet, dchan, summed, x2, qv, pv, zv, keepv, specv, gspecv, x1v, wv, dw, dq0v, dzpos,
    dzch, dzspec, dgch, dgpos, dk, dkin, dnets, heads, halo, gs, gr, gown, zs, zr, zown, hs,
    hr, ks, kr, lsem, ksem, tsem, r0, sum0, r1, sum1, r2, ts, tr, cotv,
):
    back_body(Names(locals()), n, chans, 1, length)


def mid_kernel(
    n, chans, length, z, keep, spec, gspec, x1, w, misc, chan_t, filt_t, feat, shared, tokx,
    part1, dp1, dh1, h, a, first, first_real, twiddle, second, second_back, last, last_real, dp,
    dh_out, cols, dnet, dchan, summed, rows1, qv, pv, zv, keepv, specv, gspecv, x1v, wv, dw, dq0v,
    dzpos, dzch, dzspec, dgch, dgpos, dk, dkin, dnets, heads, halo, gs, gr, gown, zs, zr,
    zown, hs, hr, ks, kr, lsem, ksem, tsem, r0, sum0, r1, sum1, r2, ts, tr, dh1v, hv, av,
    ptab, qtab, in1, c1s, c1r, b1s, b1r,
):
    back_body(Names(locals()), n, chans, 0, length)


def back_body(r, n, chans, layer, length):
    top = layer == LAYERS - 1
    me, b = lax.axis_index("chan"), lax.axis_index("batch")
    seqs, width = r.x1v.shape[0], r.x1v.shape[2]
    groups, tiles = chans // EIGHT, width // LANES
    rows_all, outer = length // LANES, r.twiddle.shape[0]
    lane0 = TAP0 + 12 * layer
    span = tiles * EIGHT

    def fetch(index, src, dst):
        copy = pltpu.make_async_copy(src, dst, r.lsem.at[index])
        copy.start()
        return copy

    early = [fetch(0, r.w.at[:, 0 : r.wv.shape[1]], r.wv), fetch(1, r.z, r.zv)]
    if top:
        tiled = [(r.x1, r.x1v), (r.cot, r.cotv), (r.q.at[0], r.qv.at[0])]
    else:
        tiled = [(r.x1, r.x1v), (r.dp1, r.pv), (r.dh1, r.dh1v), (r.h, r.hv), (r.a, r.av)]

    def tile_loads(q):
        lanes = pl.ds(pl.multiple_of(q * LANES, LANES), LANES)
        for i, (src, dst) in enumerate(tiled):
            index = (slice(None),) * (len(src.shape) - 1) + (lanes,)
            yield pltpu.make_async_copy(src.at[index], dst.at[index], r.tsem.at[i, q])

    def start_tile(q):
        for copy in tile_loads(q):
            copy.start()

    loop(tiles, start_tile)
    late = [fetch(8, r.spec, r.specv), fetch(9, r.gspec, r.gspecv)]
    block = 512

    def kept(i):
        place = pl.ds(pl.multiple_of(i * block, block), block)
        slot = lax.rem(i, 2)
        return pltpu.make_async_copy(r.keep.at[:, :, place], r.keepv.at[slot], r.ksem.at[slot])

    for i in range(2):
        kept(i).start()
    greet(n, [lax.rem(b + d, 4) for d in range(1, 4)])
    r.dw[...] = jnp.zeros_like(r.dw)
    r.cols[...] = jnp.zeros_like(r.cols)
    if top:
        late.append(fetch(2, r.q.at[pl.ds(1, 2)], r.qv.at[pl.ds(1, 2)]))
        late.append(fetch(3, r.p, r.pv))
    else:
        upper = ColumnSum(n, r.part1, r.in1, r.rows1, r.c1s, r.c1r, r.b1s, r.b1r)
        upper.start()
        for j in range(3):
            r.ptab[j], r.qtab[j] = name_tables(r.shared[...], r.misc[...], j)
    out = Tiles(n, tiles, (r.gs, r.gr), r.gown, r.dzpos, r.dzch)
    back = Blocks(n, span, (r.zs, r.zr), r.zown)
    for copy in early:
        copy.wait()

    def tile(q):
        for copy in tile_loads(q):
            copy.wait()
        (top_tile if top else mid_tile)(r, q)
        out.start(q)

    loop(tiles, tile)
    total = GroupSum(
        n, r.dw, r.summed, r.r0, r.sum0, r.r1, r.sum1, r.r2, r.ts, r.tr
    )
    total.cores()
    if not top:
        upper.share()

        def lower(q):
            places = places_of(r.tokx, q)
            for j in range(3):
                put(r.pv.at[j], q, named_dot(r.ptab[j], places[2:]))
                if j:
                    value = named_dot(r.qtab[j], places)
                    put(r.qv.at[j], q, value + r.misc[:, TAP0 + 9 + j : TAP0 + 10 + j])

        loop(tiles, lower)
    for copy in late[:2]:
        copy.wait()
    total.along_y()
    loop(tiles, out.arrived)
    dgch, dgpos, dk = r.dgch, r.dgpos, r.dk

    def chunk(k):
        rows = pl.ds(pl.multiple_of(k * EIGHT * outer, 8), EIGHT * outer)
        u = spectrum_of(load_pairs(r.dzch.at[k]), r.first[...], r.twiddle[...], r.second[...])
        r.dzspec[rows, :] = u
        o = signal_of(
            times_conj(u, r.specv[rows, :]), r.twiddle[...], r.second_back[...], r.last[...]
        )
        store_pairs(dgch.at[k], o)
        back.start(back.back_refs, k, dgch, dgpos)

    loop(groups, chunk)

    def lag(k):
        rows = pl.ds(pl.multiple_of(k * EIGHT * outer, 8), EIGHT * outer)
        v = times_conj(r.dzspec[rows, :], r.gspecv[rows, :])
        taps = signal_of(v, r.twiddle[...], r.second_back[...], r.last_real[...])
        for c in range(EIGHT):
            dk[k, pl.ds(c, rows_all, stride=EIGHT), :] = taps[:, c * LANES : (c + 1) * LANES]

    loop(groups, lag)
    count = dk.shape[1] // 4

    def lags(j):
        return pl.ds(pl.multiple_of(j * count, 8), count)

    shares = []
    for d in range(1, 4):
        j = lax.rem(b + d, 4)
        shares.append(
            send(dk.at[:, lags(j)], r.dkin.at[d - 1], (r.ks, r.kr), d - 1, {"batch": j})
        )
    total.along_x()
    if not top:
        upper.pass_on()
    for copy in late[2:]:
        copy.wait()
    for share in shares:
        share.wait_recv()
    dk[:, lags(b), :] = dk[:, lags(b), :] + r.dkin[0] + r.dkin[1] + r.dkin[2]
    r.dnets[...] = jnp.zeros_like(r.dnets)
    r.dchan[...] = jnp.zeros_like(r.dchan)
    steps = length // 4 // block
    delta = decay(me, chans)
    fourth = r.chan_t[layer, :, 13 : 13 + FO]

    def network(i):
        start = b * (length // 4) + i * block
        wide = []
        for c in range(block // LANES):
            place = pl.ds(pl.multiple_of((start // LANES + c) * EIGHT, 8), EIGHT)
            wide.append(jnp.concatenate([dk[k, place, :] for k in range(groups)], axis=0))
        kept(i).wait()
        filter_back_block(
            length, start, r.feat[:, pl.ds(pl.multiple_of(start, block), block)],
            r.filt_t.at[layer], fourth, delta,
            r.keepv.at[lax.rem(i, 2)], jnp.concatenate(wide, axis=1), r.dnets, r.dchan,
        )

        @pl.when(i + 2 < steps)
        def _():
            kept(i + 2).start()

    loop(steps, network)
    head = jnp.concatenate([dk[k, 0:EIGHT, :] for k in range(groups)], axis=0)
    lane = lax.broadcasted_iota(jnp.int32, (chans, LANES), 1)
    head = jnp.where(lane == 0, head, 0.0) * (b == 0).astype(F32)
    r.dchan[...] += pltpu.roll(head, FO, 1)
    r.dnet[...] = (
        widened(r.dnets[0], D)
        + pltpu.roll(widened(r.dnets[1], D), EMB + 1, 1)
        + pltpu.roll(widened(r.dnets[2], D), EMB + 2 + FO, 1)
    )
    lane = lax.broadcasted_iota(jnp.int32, (EIGHT, LANES), 1)
    full = width + LANES
    inner = (me < n - 1).astype(F32)

    def halo_copy(k):
        return remote(
            r.heads.at[k], r.halo.at[k], (r.hs, r.hr), k, {"chan": lax.rem(me + n - 1, n)}
        )

    def heads(k):
        back.arrived(back.back_refs, k, dgch, dgpos)

        def body(owner):
            rows = pl.ds(pl.multiple_of(owner * chans + k * EIGHT, 8), EIGHT)
            pack = jnp.zeros((EIGHT, LANES), F32)
            for s in range(seqs):
                dg = dgpos[k, owner, s, 0:EIGHT, :]
                parts = (
                    r.dq0v[s, rows, 0:LANES],
                    dg * r.qv[2, s, rows, 0:LANES],
                    dg * r.qv[1, s, rows, 0:LANES],
                )
                for j in range(3):
                    slot = 2 * (j * seqs + s)
                    head = pltpu.roll(parts[j], slot, 1) if slot else parts[j]
                    pack = jnp.where((lane == slot) | (lane == slot + 1), head, pack)
            r.heads[k, pl.ds(pl.multiple_of(owner * EIGHT, 8), EIGHT), :] = pack

        loop(n, body)
        halo_copy(k).start()

    def short(k):
        halo_copy(k).wait_recv()

        def body(owner):
            rows = pl.ds(pl.multiple_of(owner * chans + k * EIGHT, 8), EIGHT)
            side = r.misc[rows, :]
            edge = r.halo[k, pl.ds(pl.multiple_of(owner * EIGHT, 8), EIGHT), :] * inner
            sums = [jnp.zeros((EIGHT, 1), F32)] * 12
            for s in range(seqs):
                dg = jnp.concatenate(
                    [
                        dgpos[k, owner, s, q * EIGHT : (q + 1) * EIGHT, :]
                        for q in range(tiles)
                    ],
                    axis=1,
                )
                parts = (r.dq0v[s, rows, :], dg * r.qv[2, s, rows, :], dg * r.qv[1, s, rows, :])
                for j in range(3):
                    here = parts[j]
                    slot = 2 * (j * seqs + s)
                    after = pltpu.roll(edge, LANES - slot, 1) if slot else edge
                    long = jnp.concatenate([here, after], axis=1)
                    one = pltpu.roll(long, full - 1, 1)[:, :width]
                    two = pltpu.roll(long, full - 2, 1)[:, :width]
                    t = lane0 + 3 * j
                    r.dp[j, s, rows, :] = (
                        side[:, t : t + 1] * two
                        + side[:, t + 1 : t + 2] * one
                        + side[:, t + 2 : t + 3] * here
                    )
                    source = r.pv[j, s, rows, :]
                    sums[3 * j] = sums[3 * j] + row_sum(two * source)
                    sums[3 * j + 1] = sums[3 * j + 1] + row_sum(one * source)
                    sums[3 * j + 2] = sums[3 * j + 2] + row_sum(here * source)
                    sums[9 + j] = sums[9 + j] + row_sum(here)
            r.cols[rows, :] += put_columns([(lane0 + i, sums[i]) for i in range(12)])

        loop(n, body)

    def step(k):
        @pl.when(k < groups)
        def _():
            heads(k)

        @pl.when(k > 0)
        def _():
            short(k - 1)

    loop(groups + 1, step)
    total.close()
    if not top:
        upper.arrived()
        upper.sent()
    for share in shares:
        share.wait_send()
    loop(tiles, out.sent)

    def finish(k):
        halo_copy(k).wait_send()
        back.sent(back.back_refs, k, dgch, dgpos)

    loop(groups, finish)


def back_call(z, keep, spec, gspec, x1, w, misc, chan_t, filt_t, extra, tables, n, layer, cid):
    top = layer == LAYERS - 1
    seqs, _, width = x1.shape
    chans = chan_t.shape[1]
    groups, tiles = chans // EIGHT, width // LANES
    span = tiles * EIGHT
    length = width * n
    pos = x1.shape
    by_position = (groups, n, seqs, span, LANES)
    by_channel = (groups, seqs, n * span, LANES)
    rows = round_up(9 * chans, 32) if top else 12 * chans
    held = (n, rows, D)
    half = n // 2
    if top:
        mine, places = [VMEM(pos, F32)], [HBM] * 3
    else:
        mine = [
            VMEM(pos, F32), VMEM(pos, F32), VMEM(extra[6].shape, F32),
            VMEM((3, D, LANES), BF16), VMEM((3, D, LANES), BF16),
            *column_scratch(n, extra[2].shape[1]),
        ]
        places = [WHOLE] * 3 + [HBM] * 4
    return pl.pallas_call(
        partial(top_kernel if top else mid_kernel, n, chans, length),
        in_specs=[HBM] * 6 + [WHOLE] * 4 + places + [WHOLE] * 7,
        out_specs=[WHOLE] * 7,
        out_shape=[
            sds(3, *pos), sds(*pos), sds(D, D), sds(FO, D), sds(chans, LANES),
            sds(half, rows // 4, D),
        ]
        + [sds(*pos) if top else sds(4 * extra[2].shape[1], D)],
        scratch_shapes=[
            VMEM((3,) + pos, F32),
            VMEM((3,) + pos, F32),
            VMEM(by_position, F32),
            VMEM((2, 6, FO, 512), F32),
            VMEM(spec.shape, F32),
            VMEM(spec.shape, F32),
            VMEM(pos, F32),
            VMEM(held, F32),
            VMEM(held, F32),
            VMEM(pos, F32),
            VMEM(by_position, F32),
            VMEM(by_channel, F32),
            VMEM(spec.shape, F32),
            VMEM(by_channel, F32),
            VMEM(by_position, F32),
            VMEM((groups, n * span, LANES), F32),
            VMEM((3, groups, n * span // 4, LANES), F32),
            VMEM((3, FO, LANES), F32),
            VMEM((groups, n * EIGHT, LANES), F32),
            VMEM((groups, n * EIGHT, LANES), F32),
            *pair_sems(tiles, n),
            pltpu.SemaphoreType.DMA((tiles,)),
            *pair_sems(groups, n),
            pltpu.SemaphoreType.DMA((groups,)),
            *pair_sems(groups),
            *pair_sems(3),
            pltpu.SemaphoreType.DMA((12,)),
            pltpu.SemaphoreType.DMA((2,)),
            pltpu.SemaphoreType.DMA((5, tiles)),
            *group_scratch(n, rows),
        ]
        + mine,
        compiler_params=comm_params(cid),
        name="top_back" if top else "mid_back",
    )(
        z, keep, spec, gspec, x1, w, misc, chan_t, filt_t, position_table(length),
        *extra, *tables,
    )


def total_kernel(
    n,
    part2, cols0, cols1, dnet0, dnet1, dchan0, dchan1, dp, dh, ids, late, misc,
    rows2, rows3, rows4, filt, chan, dx,
    fourth, last4, dchan, rchan, inward, sums, named, own, cs, cr, fs, fr, isem, *rest,
):
    me, b = lax.axis_index("chan"), lax.axis_index("batch")
    chans = D // n
    filter_rows = filt.shape[1]
    seqs, _, width = dh.shape
    fetch = pltpu.make_async_copy(late.at[:, 9 * chans : 12 * chans], inward, isem)
    fetch.start()
    for l, value in enumerate((dchan0, dchan1)):
        dchan[l] = value[...]
    greet(n, [lax.rem(b + d, 4) for d in range(1, 4)])

    two = ColumnSum(n, part2, rest[0], rows2, *rest[1:5])
    two.start()
    slot = lax.broadcasted_iota(jnp.int32, (LANES, width), 0)

    def by_name(s, total):
        here = ids[pl.ds(s, 1), :]
        for j in range(4):
            places = (slot == here + VOCAB * j).astype(F32)
            total = total + dot_nt(dh[s] if j == 3 else dp[j, s], places)
        return total

    by_names = lax.fori_loop(0, seqs, by_name, jnp.zeros((D, LANES), F32))
    columns = cols0[:, 0:LANES] + cols1[:, 0:LANES]
    for i in range(n):
        here = slice(i * chans, (i + 1) * chans)
        fourth[i, 0:chans, 0:LANES] = columns[here]
        fourth[i, 0:chans, LANES:] = by_names[here]
        row = i * filter_rows
        if row < LAYERS * FO:
            dnet = (dnet0, dnet1)[row // FO]
            fourth[i, chans : chans + filter_rows, :] = dnet[
                row % FO : row % FO + filter_rows, :
            ]
        else:
            fourth[i, chans : chans + filter_rows, :] = jnp.zeros((filter_rows, D), F32)
        spare = fourth.shape[1] - chans - filter_rows
        if spare:
            fourth[i, chans + filter_rows :, :] = jnp.zeros((spare, D), F32)
    four = GroupSum(n, fourth, last4, *rest[10:])
    end = ColumnSum(n, last4, rest[5], rows4, *rest[6:10])
    four.cores()
    small = [
        send(dchan, rchan.at[d - 1], (cs, cr), d - 1, {"batch": lax.rem(b + d, 4)})
        for d in range(1, 4)
    ]
    fetch.wait()
    lay = Layer(inward, None, misc, 0)

    def tile(q):
        lanes = pl.ds(pl.multiple_of(q * LANES, LANES), LANES)
        here = jnp.concatenate([ids[s : s + 1, lanes] for s in range(seqs)], axis=1)
        names = lax.broadcasted_iota(jnp.int32, (VOCAB, here.shape[1]), 0)
        value = embedded(lay.side, (names == here).astype(F32))
        grad, _ = front_backward(
            lay, value, [take(dp.at[j], q) for j in range(3)], take(dh, q)
        )
        put(dx, q, grad)

    tiles = width // LANES
    four.along_y()
    loop(tiles // 2, tile)
    four.along_x()
    loop(tiles - tiles // 2, lambda q: tile(q + tiles // 2))
    four.close()
    end.start()
    two.share()
    end.share()
    end.pass_on()
    end.arrived()
    mine = pl.ds(pl.multiple_of(me * chans, 8), chans)
    filt[me] = rows4[chans : chans + filter_rows, :]
    own[...] = rows4[0:chans, LANES:]
    named[mine, :] = own[...]
    shares = []
    for d in range(1, n):
        peer = {"chan": lax.rem(me + d, n)}
        shares.append(send(own, named.at[mine, :], (fs, fr), d - 1, peer))
        shares.append(send(filt.at[me], filt.at[me], (fs, fr), n - 2 + d, peer))
    two.pass_on()
    for copy in small + shares:
        copy.wait_recv()
    for l in range(LAYERS):
        chan[l] = dchan[l] + rchan[0, l] + rchan[1, l] + rchan[2, l]
    lane = lax.broadcasted_iota(jnp.int32, (D, LANES), 1)

    def name_lanes(value, j):
        value = pltpu.roll(value, LANES - j * VOCAB, 1) if j else value
        return jnp.where(lane[: value.shape[0]] < VOCAB, value, 0.0)

    table = jnp.where(lane < VOCAB, pltpu.roll(lay.side, D - EMB0, 1)[:, :LANES], 0.0)
    xh, scale = normalize(table)
    xh = jnp.where(lane < VOCAB, xh, 0.0)
    normed = xh * lay.vec(0) + lay.vec(1)
    everything = named[...]
    dps = [name_lanes(everything, j) for j in range(3)]
    stacked = jnp.stack([v.reshape(n, chans, LANES) for v in dps], axis=1)
    dn = dot_tn(lay.inward(), stacked.reshape(3 * D, LANES))
    grad = name_lanes(everything, 3) + normalize_back(dn * lay.vec(0), xh, scale)
    grad = jnp.where(lane < VOCAB, grad, 0.0)
    base = VEC0
    pairs = [(base + 4 + j, row_sum(dps[j])) for j in range(3)]
    pairs += [(base, row_sum(dn * xh)), (base + 1, row_sum(dn))]
    sums[...] = put_columns(pairs, LANES) + pltpu.roll(grad, EMB0, 1)
    end.sent()
    rows4[0:chans, 0:LANES] += sums[mine, :]
    for j in range(3):
        rows3[j * chans : (j + 1) * chans, :] = dot_nt(name_lanes(own[...], j), normed)
    two.arrived()
    two.sent()
    for copy in small + shares:
        copy.wait_send()


def update_kernel(n, scale, *refs):
    sem = refs[-1]
    passed = [
        pltpu.make_async_copy(refs[k], refs[k - 3], sem.at[k]) for k in range(2)
    ]
    for copy in passed:
        copy.start()
    refs = refs[2:]
    rows1, rows2, rows3, rows4, filt, chan = refs[:6]
    weights, moments, averages = refs[6:15], refs[15:24], refs[24:33]
    outs = refs[33:69]
    chans = chan.shape[1]
    filter_rows = filt.shape[1]

    def step(which, index, gradient):
        factor = STEP_RATES[which] * scale
        velocity = MOMENTUM * moments[which][index] + gradient
        updated = weights[which][index] - factor * (gradient + MOMENTUM * velocity)
        running = AVERAGING * averages[which][index] + (1.0 - AVERAGING) * updated
        base = 4 * which
        outs[base][index] = velocity
        outs[base + 1][index] = running
        outs[base + 2][index] = updated
        outs[base + 3][index] = updated.astype(BF16)

    columns = rows4[0:chans, 0:LANES]
    flat = columns
    if chans < LANES:
        flat = jnp.concatenate([columns, jnp.zeros((LANES - chans, LANES), F32)], axis=0)
    flat = flat.T
    step(0, Ellipsis, flat[EMB0 : EMB0 + VOCAB, :chans])
    lane = lax.broadcasted_iota(jnp.int32, (chans, LANES), 1)
    off = []
    for l in range(LAYERS):
        front, base = (rows3, 0) if l == 0 else (rows2, 0)
        for j in range(3):
            step(1, (l, j), front[base + j * chans : base + (j + 1) * chans, :])
        for k in range(9):
            row = VEC0 + 9 * l + k
            step(2, (k, slice(l, l + 1)), flat[row : row + 1, :chans])
        rear, base = (rows2, 3 * chans) if l == 0 else (rows1, 0)
        step(3, l, rear[base : base + chans, :])
        step(4, l, rear[base + chans : base + 5 * chans, :])
        pieces = [rear[base + (5 + c) * chans : base + (6 + c) * chans, :] for c in range(4)]
        step(6, l, fold(pieces, n, chans, back=True))
        row = jnp.zeros((1, LANES), F32)
        for c in range(4):
            piece = flat[OFF0 + 4 * l + c : OFF0 + 4 * l + c + 1, :]
            row = row + (pltpu.roll(piece, c * chans, 1) if c else piece)
        off.append(row[:, : 4 * chans])
        taps = pltpu.roll(columns, LANES - TAP0 - 12 * l, 1)
        own = chan[l]
        skip = pltpu.roll(own, LANES - FO + 12, 1)
        gradient = jnp.where(lane < 12, taps, jnp.where(lane == 12, skip, pltpu.roll(own, 13, 1)))
        step(7, l, gradient[:, : 13 + FO])
    step(5, Ellipsis, jnp.concatenate(off, axis=0))
    whole = filt[...].reshape(n * filter_rows, D)
    for l in range(LAYERS):
        step(8, l, whole[l * FO : (l + 1) * FO, :136])
    for copy in passed:
        copy.wait()


def finish(
    rows1, part2, cols, dnets, dchans, dp, dh, ids, late, misc, weights, moments, averages,
    activations, n, scale, cid,
):
    chans = D // n
    filter_rows = round_up(LAYERS * FO, n * EIGHT) // n
    fourth = round_up(chans + filter_rows, 32)
    q2, q4 = part2.shape[1], fourth // 4
    half = n // 2
    *sums, dx = pl.pallas_call(
        partial(total_kernel, n),
        in_specs=[WHOLE] * 10 + [HBM, WHOLE],
        out_specs=[WHOLE] * 6,
        out_shape=[
            sds(4 * q2, D), sds(3 * chans, D), sds(fourth, D),
            sds(n, filter_rows, D), sds(LAYERS, chans, LANES), sds(*dh.shape),
        ],
        scratch_shapes=[
            VMEM((n, fourth, D), F32),
            VMEM((half, q4, D), F32),
            VMEM((LAYERS, chans, LANES), F32),
            VMEM((3, LAYERS, chans, LANES), F32),
            VMEM((n, 3 * chans, D), F32),
            VMEM((D, LANES), F32),
            VMEM((D, LANES), F32),
            VMEM((chans, LANES), F32),
            *pair_sems(3),
            *pair_sems(2 * n),
            pltpu.SemaphoreType.DMA,
            *column_scratch(n, q2),
            *column_scratch(n, q4),
            *group_scratch(n, fourth),
        ],
        compiler_params=comm_params(cid),
        name="total",
    )(part2, *cols, *dnets, *dchans, dp, dh, ids, late, misc)
    shapes = []
    for weight in weights:
        shapes += [sds(*weight.shape)] * 3 + [jax.ShapeDtypeStruct(weight.shape, BF16)]
    shapes += [sds(*dx.shape)] * 2
    return pl.pallas_call(
        partial(update_kernel, n, scale),
        in_specs=[WHOLE] * 35,
        out_specs=[WHOLE] * 36 + [HBM, HBM],
        out_shape=shapes,
        scratch_shapes=[pltpu.SemaphoreType.DMA((2,))],
        compiler_params=pltpu.CompilerParams(vmem_limit_bytes=VMEM_LIMIT),
        name="update",
    )(activations, dx, rows1, *sums, *weights, *moments, *averages)


def onehot_rows(tokens):
    row = lax.broadcasted_iota(jnp.int32, (D, tokens.shape[1]), 0)
    return (row == tokens + EMB0).astype(F32)


class Layer:
    def __init__(self, front, rear, misc, index, base=0):
        some = rear if front is None else front
        self.n = some.shape[0]
        self.c = D // self.n
        self.front, self.rear, self.base = front, rear, base
        self.side = misc[...]
        self.index = index

    def rows(self, ref, start, count):
        return ref[:, start * self.c : (start + count) * self.c, :].reshape(
            self.n * count * self.c, D
        )

    def column(self, lane):
        return self.side[:, lane : lane + 1]

    def vec(self, k):
        return self.column(VEC0 + 9 * self.index + k)

    def off(self, k):
        return self.column(OFF0 + 4 * self.index + k)

    def inward(self):
        return self.rows(self.front, 0, 3)

    def outward(self):
        return self.rows(self.rear, self.base, 1)

    def expand(self, k):
        return self.rows(self.rear, self.base + 1 + k, 1)

    def contract(self, k):
        return self.rows(self.rear, self.base + 5 + k, 1)


def front_forward(lay, x):
    xh, _ = normalize(x)
    normed = xh * lay.vec(0) + lay.vec(1)
    p = dot(lay.inward(), normed).reshape(lay.n, 3, lay.c, x.shape[1])
    return [p[:, j].reshape(D, x.shape[1]) + lay.vec(4 + j) for j in range(3)]


def front_backward(lay, x, dp, dh, dw=None):
    xh, scale = normalize(x)
    normed = xh * lay.vec(0) + lay.vec(1)
    width = x.shape[1]
    stacked = jnp.stack([d.reshape(lay.n, lay.c, width) for d in dp], axis=1)
    stacked = stacked.reshape(3 * D, width)
    dn = dot_tn(lay.inward(), stacked)
    if dw is not None:
        dw[:, 0 : 3 * lay.c, :] += dot_nt(stacked, normed, DW).reshape(lay.n, 3 * lay.c, D)
    base = VEC0 + 9 * lay.index
    columns = [(base + 4 + j, row_sum(dp[j])) for j in range(3)]
    columns += [(base, row_sum(dn * xh)), (base + 1, row_sum(dn))]
    return dh + normalize_back(dn * lay.vec(0), xh, scale), columns


def rear_mix(lay, x, y):
    return x + dot(lay.outward(), y) + lay.vec(7)


def rear_hidden(lay, h):
    xh, scale = normalize(h)
    m = xh * lay.vec(2) + lay.vec(3)
    a = [dot(lay.expand(k), m) + lay.off(k) for k in range(4)]
    return xh, scale, m, a


def rear_out(lay, h, u):
    out = h + lay.vec(8)
    for k in range(4):
        out = out + dot(lay.contract(k), u[k])
    return out


def rear_backward(lay, h, a, y, dout, dw, base=0):
    n, c = lay.n, lay.c

    def add(row, value):
        dw[:, (base + row) * c : (base + row + 1) * c, :] += value.reshape(n, c, D)

    xh, scale = normalize(h)
    m = xh * lay.vec(2) + lay.vec(3)
    vec = VEC0 + 9 * lay.index
    columns = [(vec + 8, row_sum(dout))]
    dm = None
    for k in range(4):
        ak = a[k]
        g, t = gelu_parts(ak)
        u = ak * g
        add(5 + k, dot_nt(dout, u, DW))
        slope = g + 0.5 * ak * (1.0 - t * t) * (GELU_SCALE * (1.0 + 3.0 * GELU_CUBE * ak * ak))
        dpre = dot_tn(lay.contract(k), dout) * slope
        add(1 + k, dot_nt(dpre, m, DW))
        columns.append((OFF0 + 4 * lay.index + k, row_sum(dpre)))
        term = dot_tn(lay.expand(k), dpre)
        dm = term if dm is None else dm + term
    dh = dout + normalize_back(dm * lay.vec(2), xh, scale)
    columns += [(vec + 2, row_sum(dm * xh)), (vec + 3, row_sum(dm)), (vec + 7, row_sum(dh))]
    add(0, dot_nt(dh, y, DW))
    return dh, dot_tn(lay.outward(), dh), columns


def turned(arrays):
    out = list(arrays)
    out[2] = arrays[2].transpose(1, 0, 2)
    out[7] = arrays[7].transpose(0, 2, 1)
    out[8] = arrays[8].transpose(0, 2, 1)
    return out


def per_device(*arguments):
    token_ids, cotangent = arguments[0], arguments[28]
    weights = turned(arguments[1:10])
    moments = turned(arguments[10:19])
    averages = turned(arguments[19:28])
    n, m = lax.axis_size("chan"), lax.axis_size("batch")
    seqs, width = token_ids.shape
    length = width * n
    chan_t, filt_t = weights[7], weights[8]
    chans = chan_t.shape[1]
    groups = chans // EIGHT
    tables = fourier_tables(length)
    wall, late, spec0, spec1, gspec0, keep0, keep1, z0, misc, _, tokx, shared = prepare(
        (token_ids, *weights), tables, n, seqs, length, 1
    )
    wlate, h0, a0, x1, p1, q1, gspec1, z1 = middle(
        z0, wall, late, spec1, misc, shared, tokx, tables, n, chans, 2
    )
    dp1, dh1, cols1, dnet1, dchan1, part1, activations = back_call(
        z1, keep1, spec1, gspec1, x1, wlate, misc, chan_t, filt_t, (q1, p1, cotangent),
        tables, n, 1, 3,
    )
    dp0, dh0, cols0, dnet0, dchan0, part2, rows1 = back_call(
        z0, keep0, spec0, gspec0, x1, wall, misc, chan_t, filt_t,
        (shared, tokx, part1, dp1, dh1, h0, a0), tables, n, 0, 4,
    )
    *updates, activations, input_gradient = finish(
        rows1, part2, (cols0, cols1), (dnet0, dnet1), (dchan0, dchan1), dp0, dh0, token_ids,
        wlate, misc, weights, moments, averages, activations, n,
        1.0 / math.sqrt(seqs * m * length), 5,
    )
    kinds = [turned(updates[k::4]) for k in range(4)]
    return (activations, input_gradient) + tuple(
        kinds[k][w] for w in range(9) for k in range(4)
    )


def solution(mesh):
    in_weights = (
        P(None, "chan"),
        P(None, None, "chan", None),
        P(None, None, "chan"),
        P(None, "chan", None),
        P(None, "chan", None),
        P(None, "chan"),
        P(None, "chan", None),
        P(None, None, "chan"),
        P(),
    )
    tokens = P("batch", None, "chan")
    in_specs = (P("batch", "chan"),) + in_weights * 3 + (tokens,)
    out_specs = (tokens, tokens) + tuple(spec for spec in in_weights for _ in range(4))
    return jax.shard_map(
        per_device, mesh=mesh, in_specs=in_specs, out_specs=out_specs, check_vma=False
    )
```

```python
from functools import partial
import math

import jax
import jax.numpy as jnp
import numpy as np
from jax import lax
from jax.experimental import pallas as pl
from jax.experimental.pallas import tpu as pltpu
from jax.sharding import PartitionSpec as P

D = 256
FF = 1024
FO = 64
EMB = 5
VOCAB = 16
LAYERS = 2
LANES = 128
TILE = 256

HIGH = lax.Precision.HIGH
HIGHEST = lax.Precision.HIGHEST
DW = lax.Precision.HIGH
EPSILON = 1e-05
MOMENTUM = 0.9
AVERAGING = 0.9
WINDOW_SHIFT = 0.05
FREQUENCY = 10.0
STEP_RATES = (0.7, 0.06, 0.1, 0.037, 0.1, 0.16, 0.025, 0.2, 0.0002)
GELU_SCALE = math.sqrt(2.0 / math.pi)
GELU_CUBE = 0.044715

MESH = pl.DeviceIdType.MESH
VMEM = pltpu.VMEM
WHOLE = pl.BlockSpec(memory_space=pltpu.VMEM)
HBM = pl.BlockSpec(memory_space=pl.ANY)
VMEM_LIMIT = 60 * 1024 * 1024
F32 = jnp.float32
BF16 = jnp.bfloat16

VEC0 = 0
TAP0 = 18
EMB0 = 42
OFF0 = 58
EIGHT = 8


def dot(a, b, precision=HIGH):
    return jnp.dot(a, b, precision=precision, preferred_element_type=F32)


def dot_nt(a, b, precision=HIGH):
    return lax.dot_general(
        a, b, (((1,), (1,)), ((), ())), precision=precision, preferred_element_type=F32
    )


def dot_tn(a, b, precision=HIGH):
    return lax.dot_general(
        a, b, (((0,), (0,)), ((), ())), precision=precision, preferred_element_type=F32
    )


def sds(*shape):
    return jax.ShapeDtypeStruct(shape, F32)


def cost(flops, moved):
    return pl.CostEstimate(flops=int(flops), bytes_accessed=int(moved), transcendentals=0)


def position_table(length):
    indices = np.arange(length, dtype=np.float32)
    fraction = indices / np.float32(length - 1)
    angles = np.float32(2.0 * math.pi) * indices / np.float32(length)
    bands = (EMB - 1) // 2
    frequency = np.linspace(0.0001, bands - 1, bands).astype(np.float32)
    turned = (frequency[:, None] * angles[None, :]).astype(np.float32).astype(np.float64)
    table = np.zeros((8, length), np.float32)
    table[0] = fraction
    table[1 : 1 + bands] = np.cos(turned)
    table[1 + bands : 1 + 2 * bands] = -np.sin(turned)
    table[EMB] = 1.0
    return table


def split_table(table):
    high = table.astype(np.float32).astype(jnp.bfloat16)
    low = (table.astype(np.float32) - high.astype(np.float32)).astype(jnp.bfloat16)
    return high, low


def left_table(table):
    high, low = split_table(table)
    return np.concatenate([high, high, low], axis=1)


def right_table(table):
    high, low = split_table(table)
    return np.concatenate([high, high, low], axis=0)


def fourier_tables(length):
    rows = length // LANES
    outer = 2 * rows
    total = outer * LANES
    turn = 2.0 * np.pi / outer * (np.arange(outer)[:, None] * np.arange(rows)[None, :] % outer)
    c, s = np.cos(turn), np.sin(turn)
    first = np.block([[c, s], [-s, c]])
    first_real = np.block([[c], [-s]])
    last = np.block([[c.T, -s.T], [s.T, c.T]]) / total
    last_real = np.block([[c.T, -s.T]]) / total
    twist = 2.0 * np.pi / total * (np.arange(outer)[:, None] * np.arange(LANES)[None, :])
    twiddle = np.concatenate([np.cos(twist), -np.sin(twist)], axis=1).astype(np.float32)
    lane = 2.0 * np.pi / LANES * (np.arange(LANES)[:, None] * np.arange(LANES)[None, :] % LANES)
    c, s = np.cos(lane), np.sin(lane)
    second = np.block([[c, -s], [s, c]])
    second_back = np.block([[c, s], [-s, c]])
    return (
        left_table(first),
        left_table(first_real),
        twiddle,
        right_table(second),
        right_table(second_back),
        left_table(last),
        left_table(last_real),
    )


def sin_cos(x):
    turns = jnp.round(x * (1.0 / math.pi))
    r = x - turns * 3.140625
    r = r - turns * 9.67025756835937500e-4
    r = r - turns * 6.27711415290832520e-7
    r = r - turns * 1.21542010130123850e-10
    half = turns * 0.5
    sign = 1.0 - 4.0 * jnp.abs(half - jnp.round(half))
    r2 = r * r
    s = -2.5052108385441720e-8
    for k in (2.7557319223985893e-6, -1.9841269841269841e-4, 8.3333333333333333e-3, -1.6666666666666667e-1):
        s = s * r2 + k
    s = r + r * (r2 * s)
    c = 2.0876756987868099e-9
    for k in (-2.7557319223985888e-7, 2.4801587301587302e-5, -1.3888888888888889e-3, 4.1666666666666667e-2, -0.5):
        c = c * r2 + k
    c = 1.0 + r2 * c
    return s * sign, c * sign


def window(delta, length, start, width):
    t = lax.broadcasted_iota(jnp.int32, (1, width), 1) + start
    fraction = t.astype(F32) / (length - 1)
    return jnp.exp(-delta * fraction) + WINDOW_SHIFT


def normalize(x):
    center = x - jnp.mean(x, axis=0, keepdims=True)
    spread = jnp.mean(center * center, axis=0, keepdims=True)
    scale = lax.rsqrt(spread + EPSILON)
    return center * scale, scale


def normalize_back(e, xh, scale):
    return scale * (
        e - jnp.mean(e, axis=0, keepdims=True) - xh * jnp.mean(e * xh, axis=0, keepdims=True)
    )


def gelu_parts(a):
    t = jnp.tanh(GELU_SCALE * (a + GELU_CUBE * a * a * a))
    return 0.5 * (1.0 + t), t


def put_columns(pairs, width=D):
    rows = pairs[0][1].shape[0]
    lane = lax.broadcasted_iota(jnp.int32, (rows, width), 1)
    out = jnp.zeros((rows, width), F32)
    for k, column in pairs:
        out = out + jnp.where(lane == k, column, 0.0)
    return out


def row_sum(x):
    return jnp.sum(x, axis=1, keepdims=True)


def ones_rows(width):
    return (lax.broadcasted_iota(jnp.int32, (EIGHT, width), 0) == 0).astype(F32)


def filter_block(length, start, feat, net, fourth, delta):
    width = feat.shape[1]
    kept = []
    h, c = sin_cos(FREQUENCY * dot(net[:, 0:EIGHT], feat, HIGHEST))
    kept.append((h, FREQUENCY * c))
    for row in (EMB + 1, EMB + 2 + FO):
        v = dot(net[:, row : row + FO], h, HIGHEST) + net[:, row + FO : row + FO + 1]
        h, c = sin_cos(FREQUENCY * v)
        kept.append((h, FREQUENCY * c))
    return dot(fourth, h, HIGHEST) * window(delta, length, start, width), kept


def filter_back_block(length, start, feat, net, fourth, delta, keep, dk, dnet, dfourth):
    width = feat.shape[1]
    ones = ones_rows(width)
    dkw = dk * window(delta, length, start, width)
    dfourth[:, 0:FO] += dot_nt(dkw, keep[2])
    dpre = dot_tn(fourth, dkw) * keep[5]
    row = EMB + 2 + FO
    dnet[2, :, 0 : FO + EIGHT] += dot_nt(dpre, jnp.concatenate([keep[1], ones], axis=0))
    dpre = dot_tn(net[:, row : row + FO], dpre) * keep[4]
    row = EMB + 1
    dnet[1, :, 0 : FO + EIGHT] += dot_nt(dpre, jnp.concatenate([keep[0], ones], axis=0))
    dpre = dot_tn(net[:, row : row + FO], dpre) * keep[3]
    dnet[0, :, 0:EIGHT] += dot_nt(dpre, feat)


def widened(value, width=LANES):
    rows, lanes = value.shape
    return jnp.concatenate([value, jnp.zeros((rows, width - lanes), F32)], axis=1)


def paired(tile, count):
    high = tile.astype(BF16).astype(F32)
    return (high + pltpu.roll(tile - high, count, 1)).astype(BF16)


def named_dot(table, places, repeat=2):
    rows = jnp.concatenate(places * repeat, axis=0)
    rest = LANES - rows.shape[0]
    rows = jnp.concatenate([rows, jnp.zeros((rest, rows.shape[1]), F32)], axis=0)
    return jnp.dot(table, rows.astype(BF16), preferred_element_type=F32)


def halves(x):
    high = x.astype(BF16)
    return high, (x - high.astype(F32)).astype(BF16)


def left_dot(table, x):
    high, low = halves(x)
    return jnp.dot(
        table, jnp.concatenate([high, low, high], axis=0), preferred_element_type=F32
    )


def right_dot(x, table):
    high, low = halves(x)
    return jnp.dot(
        jnp.concatenate([high, low, high], axis=1), table, preferred_element_type=F32
    )


def spectrum_of(x, first, twiddle, second):
    outer = twiddle.shape[0]
    y = left_dot(first, x)
    tr, ti = twiddle[:, :LANES], twiddle[:, LANES:]
    parts = []
    for b in range(x.shape[1] // LANES):
        yr = y[:outer, b * LANES : (b + 1) * LANES]
        yi = y[outer:, b * LANES : (b + 1) * LANES]
        parts.append(jnp.concatenate([yr * tr - yi * ti, yr * ti + yi * tr], axis=1))
    return right_dot(jnp.concatenate(parts, axis=0), second)


def signal_of(v, twiddle, second_back, last):
    outer = twiddle.shape[0]
    a = right_dot(v, second_back)
    tr, ti = twiddle[:, :LANES], twiddle[:, LANES:]
    parts = []
    for b in range(v.shape[0] // outer):
        ar = a[b * outer : (b + 1) * outer, :LANES]
        ai = a[b * outer : (b + 1) * outer, LANES:]
        parts.append(jnp.concatenate([ar * tr + ai * ti, ai * tr - ar * ti], axis=0))
    return left_dot(last, jnp.concatenate(parts, axis=1))


def load_pairs(ref):
    rows = ref.shape[1] // EIGHT
    parts = []
    for b in range(EIGHT):
        parts.append(
            jnp.concatenate([ref[s, pl.ds(b, rows, stride=EIGHT), :] for s in range(2)], axis=0)
        )
    return jnp.concatenate(parts, axis=1)


def store_pairs(ref, value):
    rows = ref.shape[1] // EIGHT
    for b in range(EIGHT):
        for s in range(2):
            ref[s, pl.ds(b, rows, stride=EIGHT), :] = value[
                s * rows : (s + 1) * rows, b * LANES : (b + 1) * LANES
            ]


def times(a, b):
    ar, ai, br, bi = a[:, :LANES], a[:, LANES:], b[:, :LANES], b[:, LANES:]
    return jnp.concatenate([ar * br - ai * bi, ar * bi + ai * br], axis=1)


def times_conj(a, b):
    ar, ai, br, bi = a[:, :LANES], a[:, LANES:], b[:, :LANES], b[:, LANES:]
    return jnp.concatenate([ar * br + ai * bi, ai * br - ar * bi], axis=1)


def send(a, b, sems, index, device):
    copy = remote(a, b, sems, index, device)
    copy.start()
    return copy


def remote(a, b, sems, index, device):
    return pltpu.make_async_remote_copy(
        src_ref=a, dst_ref=b, send_sem=sems[0].at[index], recv_sem=sems[1].at[index],
        device_id=device, device_id_type=MESH,
    )


def exchange(refs, peers, send_sem, recv_sem, base):
    return [
        send(a, b, (send_sem, recv_sem), base + k, peer)
        for k, ((a, b), peer) in enumerate(zip(refs, peers))
    ]


def greet(n, mates=()):
    me, b = lax.axis_index("chan"), lax.axis_index("batch")
    barrier = pltpu.get_barrier_semaphore()
    for d in range(1, n):
        pl.semaphore_signal(
            barrier, inc=1, device_id={"chan": lax.rem(me + d, n)}, device_id_type=MESH
        )
    for mate in mates:
        pl.semaphore_signal(barrier, inc=1, device_id={"batch": mate}, device_id_type=MESH)
    pl.semaphore_wait(barrier, n - 1 + len(mates))


def core_mate(b):
    return b + 1 - 2 * lax.rem(b, 2)


def y_mate(b):
    return b + 2 - 4 * (b // 2)


def comm_params(cid):
    return pltpu.CompilerParams(
        collective_id=cid, has_side_effects=True, vmem_limit_bytes=VMEM_LIMIT
    )


def pair_sems(*shape):
    return [pltpu.SemaphoreType.DMA(shape), pltpu.SemaphoreType.DMA(shape)]


class Blocks:
    def __init__(self, n, span, sems, own):
        self.n, self.span, self.sems, self.own = n, span, sems, own
        self.me = lax.axis_index("chan")

    def rows(self, j):
        return pl.ds(pl.multiple_of(j * self.span, 8), self.span)

    def out_refs(self, k, j, src, dst):
        return src.at[k, j], dst.at[k, :, self.rows(self.me), :]

    def back_refs(self, k, j, src, dst):
        return src.at[k, :, self.rows(j), :], dst.at[k, self.me]

    def each(self, refs, k, src, dst):
        for d in range(1, self.n):
            j = lax.rem(self.me + d, self.n)
            a, b = refs(k, j, src, dst)
            yield remote(a, b, self.sems, (k, d), {"chan": j})

    def start(self, refs, k, src, dst):
        a, b = refs(k, self.me, src, dst)
        pltpu.make_async_copy(a, b, self.own.at[k]).start()
        for copy in self.each(refs, k, src, dst):
            copy.start()

    def arrived(self, refs, k, src, dst):
        for copy in self.each(refs, k, src, dst):
            copy.wait_recv()
        a, b = refs(k, self.me, src, dst)
        pltpu.make_async_copy(a, b, self.own.at[k]).wait()

    def sent(self, refs, k, src, dst):
        for copy in self.each(refs, k, src, dst):
            copy.wait_send()


class Tiles:
    def __init__(self, n, tiles, sems, own, src, dst):
        self.n, self.tiles, self.sems, self.own = n, tiles, sems, own
        self.src, self.dst = src, dst
        self.me = lax.axis_index("chan")

    def refs(self, q, j):
        here = pl.ds(pl.multiple_of(q * EIGHT, 8), EIGHT)
        there = pl.ds(pl.multiple_of((self.me * self.tiles + q) * EIGHT, 8), EIGHT)
        return self.src.at[:, j, :, here, :], self.dst.at[:, :, there, :]

    def each(self, q):
        for d in range(1, self.n):
            j = lax.rem(self.me + d, self.n)
            yield remote(*self.refs(q, j), self.sems, (q, d), {"chan": j})

    def start(self, q):
        for copy in self.each(q):
            copy.start()
        pltpu.make_async_copy(*self.refs(q, self.me), self.own.at[q]).start()

    def arrived(self, q):
        for copy in self.each(q):
            copy.wait_recv()
        pltpu.make_async_copy(*self.refs(q, self.me), self.own.at[q]).wait()

    def sent(self, q):
        for copy in self.each(q):
            copy.wait_send()


class Names:
    def __init__(self, values):
        self.__dict__.update(values)


def loop(count, body):
    def step(i, _):
        body(i)
        return 0

    lax.fori_loop(0, count, step, 0)


def round_up(value, step):
    return -(-value // step) * step


def quarter_rows(refs_rows, k):
    quarter = refs_rows // 4
    return pl.ds(pl.multiple_of(k * quarter, 8), quarter)


def fold(value, n, chans, back=False):
    lane = lax.broadcasted_iota(jnp.int32, (chans, LANES), 1)
    wide = 4 * n * chans // LANES
    narrow = n * chans // LANES
    if back:
        tiles = [[value[c][:, t * LANES : (t + 1) * LANES] for t in range(narrow)] for c in range(4)]
        out = [None] * wide
    else:
        tiles = [value[:, t * LANES : (t + 1) * LANES] for t in range(wide)]
        out = [[None] * narrow for _ in range(4)]
    for c in range(4):
        for i in range(n):
            a, b = i * 4 * chans + c * chans, i * chans
            if back:
                source, to, at = tiles[c][b // LANES], a % LANES, b % LANES
                row, k = out, a // LANES
            else:
                source, to, at = tiles[a // LANES], b % LANES, a % LANES
                row, k = out[c], b // LANES
            shift = (to - at) % LANES
            moved = pltpu.roll(source, shift, 1) if shift else source
            inside = (lane >= to) & (lane < to + chans)
            row[k] = jnp.where(inside, moved, 0.0 if row[k] is None else row[k])
    if back:
        return jnp.concatenate(out, axis=1)
    return [jnp.concatenate(tiles, axis=1) for tiles in out]


def conv_chunk(k, g, spec, gspec, z, first, twiddle, second, second_back, last):
    outer = twiddle.shape[0]
    rows = pl.ds(pl.multiple_of(k * EIGHT * outer, 8), EIGHT * outer)
    u = spectrum_of(load_pairs(g.at[k]), first[...], twiddle[...], second[...])
    gspec[rows, :] = u
    o = signal_of(times(u, spec[rows, :]), twiddle[...], second_back[...], last[...])
    store_pairs(z.at[k], o)


def decay(me, chans):
    ids = lax.broadcasted_iota(jnp.int32, (chans, 1), 0) + me * chans
    slow = math.log(0.01) / 1.5
    fast = math.log(0.01) / 0.3
    return jnp.abs(slow + (fast - slow) * ids.astype(F32) / (D - 1))


def hops(n, b, me, sems, local):
    half = n // 2
    x, z = lax.rem(me, 2), me // 2
    side = {"chan": 2 * z + 1 - x}

    def hop_z(c, src, dst):
        keep = pltpu.make_async_copy(src, dst.at[me], local.at[c])
        keep.start()
        copies = [
            send(src, dst.at[me], sems, (c, d), {"chan": 2 * lax.rem(z + d, half) + x})
            for d in range(1, half)
        ]
        return keep, copies

    def hop_x(c, src, dst, keep, copies):
        out = [send(src, dst.at[me], sems, (c, half), side)]
        for d in range(1, half):
            j = 2 * lax.rem(z + half - d, half) + x
            copies[d - 1].wait_recv()
            out.append(send(dst.at[j], dst.at[j], sems, (c, half + d), side))
        keep.wait()
        return out

    return hop_z, hop_x


def filter_steps(r, l, b, length, groups, keep, delta):
    block = 512
    fourth = r.chan_t[l, :, 13 : 13 + FO]

    def body(i):
        start = b * (length // 4) + i * block
        out, kept = filter_block(
            length, start, r.feat[:, pl.ds(pl.multiple_of(start, block), block)],
            r.filt_t.at[l], fourth, delta,
        )
        place = pl.ds(pl.multiple_of(i * block, block), block)
        for k, (sine, cosine) in enumerate(kept):
            keep[k, :, place] = sine
            keep[3 + k, :, place] = cosine
        for q in range(block // LANES):
            rows = pl.ds(pl.multiple_of((start // LANES + q) * EIGHT, 8), EIGHT)
            for k in range(groups):
                r.kern[l, k, rows, :] = out[
                    k * EIGHT : (k + 1) * EIGHT, q * LANES : (q + 1) * LANES
                ]

    loop(length // 4 // block, body)


def name_rows(tokx, s, lanes):
    width = tokx.shape[2] if lanes is None else LANES
    names = lax.broadcasted_iota(jnp.int32, (VOCAB, width), 0).astype(F32)
    rows = [tokx[s, k : k + 1, :] if lanes is None else tokx[s, k : k + 1, lanes] for k in range(3)]
    here, one, two = [(names == row).astype(F32) for row in rows]
    return [two, one, here]


def name_tables(shared, misc, j):
    lane = lax.broadcasted_iota(jnp.int32, (D, LANES), 1)
    rows = pltpu.roll(shared, LANES - j * VOCAB, 1) if j else shared
    rows = jnp.where(lane < VOCAB, rows, 0.0)
    t = TAP0 + 3 * j
    mix = (
        misc[:, t : t + 1] * rows
        + misc[:, t + 1 : t + 2] * pltpu.roll(rows, VOCAB, 1)
        + misc[:, t + 2 : t + 3] * pltpu.roll(rows, 2 * VOCAB, 1)
    )
    return paired(rows, VOCAB), paired(mix, 3 * VOCAB)


def prepare_kernel(
    n, length, chans, ids, embedding, inward, vectors, outward, expand, offsets, contract,
    chan_t, filt_t, feat, first, first_real, twiddle, second, second_back, last, last_real,
    wall, late, spec0, spec1, gspec, keep0, keep1, zpos, misc, toks, tokx, shared, owned,
    upper, side, town, rows, flip, kern, gch, zch, spec0v, spec1v, gspecv, keep0v, keep1v,
    osem, ss, sr, ws, wr, ks, kr, zs, zr, local, zown,
):
    r = Names(locals())
    me, b = lax.axis_index("chan"), lax.axis_index("batch")
    groups = chans // EIGHT
    seqs, span = r.zpos.shape[2], r.zpos.shape[3]
    width = span // EIGHT * LANES
    parts = width // D
    tabs = (r.first, r.twiddle, r.second, r.second_back, r.last)
    flip, side, town = r.flip, r.side, r.town
    flip[...] = jnp.zeros_like(flip)
    for k in range(9):
        for l in range(LAYERS):
            row = VEC0 + 9 * l + k
            flip[row : row + 1, 0:chans] = r.vectors[k, l : l + 1, :]
    flip[EMB0 : EMB0 + VOCAB, 0:chans] = r.embedding[...]
    for l in range(LAYERS):
        for c in range(4):
            row = OFF0 + 4 * l + c
            flip[row : row + 1, 0:chans] = r.offsets[l : l + 1, c * chans : (c + 1) * chans]
    columns = flip[...].T[:chans, :]
    lane = lax.broadcasted_iota(jnp.int32, (chans, LANES), 1)
    for l in range(LAYERS):
        taps = jnp.where(lane < 12, widened(r.chan_t[l]), 0.0)
        columns = columns + pltpu.roll(taps, TAP0 + 12 * l, 1)
    side[:, 0:LANES] = columns
    side[:, LANES:] = jnp.zeros((chans, LANES), F32)
    town[...] = jnp.zeros_like(town)
    for s in range(seqs):
        for h in range(parts):
            town[s * parts + h : s * parts + h + 1, :] = r.ids[
                s : s + 1, h * D : (h + 1) * D
            ].astype(F32)
    for l, rear, front in ((0, r.owned, r.upper), (1, r.upper, r.owned)):
        for j in range(3):
            front[(9 + j) * chans : (10 + j) * chans, :] = r.inward[l, j]
        rear[0:chans, :] = r.outward[l]
        rear[chans : 5 * chans, :] = r.expand[l]
        for c, piece in enumerate(fold(r.contract[l], n, chans)):
            rear[(5 + c) * chans : (6 + c) * chans, :] = piece
    greet(n, (core_mate(b), y_mate(b)))
    mine = pl.ds(pl.multiple_of(me * chans, 8), chans)
    small = []
    for d in range(1, n):
        peer = {"chan": lax.rem(me + d, n)}
        small.append(send(side, r.misc.at[mine, :], (r.ss, r.sr), d, peer))
        small.append(send(town, r.toks.at[me], (r.ss, r.sr), n + d, peer))
    r.misc[mine, :] = side[...]
    r.toks[me] = town[...]
    weights = (r.ws, r.wr)
    hop_z, hop_x = hops(n, b, me, weights, r.local)
    count = r.wall.shape[1] // 2
    core = lax.rem(b, 2)

    def part(c, k):
        size = count // (2 if c else 4)
        return pl.ds(pl.multiple_of(c * count + k * size, 8), size)

    low = [(r.owned.at[part(c, k)], r.wall.at[:, part(c, k)]) for c, k in ((0, b), (1, core))]
    z_w = [hop_z(0, *low[0]), None]
    x_w, y_w, core_w = [None] * 2, [], []
    saves = []

    def save(src, dst):
        copy = pltpu.make_async_copy(src, dst, r.osem.at[len(saves)])
        copy.start()
        saves.append(copy)

    save(r.upper, r.late)

    def hop_y():
        for copy in x_w[0]:
            copy.wait_recv()
        here = r.wall.at[:, part(0, b)]
        y_w.append(send(here, here, weights, (0, n), {"batch": y_mate(b)}))
        core_w.append(send(here, here, weights, (0, n + 1), {"batch": core_mate(b)}))

    def hop_core():
        for copy in x_w[1]:
            copy.wait_recv()
        here = r.wall.at[:, part(1, core)]
        core_w.append(send(here, here, weights, (1, n), {"batch": core_mate(b)}))
        y_w[0].wait_recv()
        here = r.wall.at[:, part(0, y_mate(b))]
        core_w.append(send(here, here, weights, (0, n + 2), {"batch": core_mate(b)}))

    delta = decay(me, chans)
    count_lag = r.kern.shape[2] // 4
    lags = [pl.ds(pl.multiple_of(k * count_lag, 8), count_lag) for k in (b, y_mate(b))]

    def offer(l):
        place = r.kern.at[l, :, lags[0], :]
        return send(place, place, (r.ks, r.kr), (l, 0), {"batch": y_mate(b)})

    def share(l, copy):
        copy.wait_recv()
        return [
            send(
                r.kern.at[l, :, k, :], r.kern.at[l, :, k, :], (r.ks, r.kr), (l, 1 + i),
                {"batch": core_mate(b)},
            )
            for i, k in enumerate(lags)
        ]

    def spectra(l, copies, spec):
        for copy in copies:
            copy.wait_recv()
        outer = r.twiddle.shape[0]
        rows = length // LANES

        def body(k):
            taps = jnp.concatenate(
                [r.kern[l, k, pl.ds(c, rows, stride=EIGHT), :] for c in range(EIGHT)], axis=1
            )
            u = spectrum_of(taps, r.first_real[...], r.twiddle[...], r.second[...])
            here = pl.ds(pl.multiple_of(k * EIGHT, 8), EIGHT)
            gain = jnp.broadcast_to(r.chan_t[l, here, 12:13], (EIGHT, LANES))
            for c in range(EIGHT):
                wide = jnp.broadcast_to(gain[c : c + 1, :], (outer, LANES))
                both = jnp.concatenate([wide, jnp.zeros_like(wide)], axis=1)
                place = pl.ds(pl.multiple_of((k * EIGHT + c) * outer, 8), outer)
                spec[place, :] = u[c * outer : (c + 1) * outer] + both

        loop(groups, body)

    filter_steps(r, 0, b, length, groups, r.keep0v, delta)
    y_k0 = offer(0)
    save(r.keep0v, r.keep0)
    for copy in small:
        copy.wait()
    table = r.misc[...]
    xh, _ = normalize(table)
    normed = xh * table[:, VEC0 : VEC0 + 1] + table[:, VEC0 + 1 : VEC0 + 2]
    own = side[...]
    shared = jnp.zeros((chans, LANES), F32)
    mixes, biases = [], []
    for j in range(3):
        rows = dot(r.inward[0, j], normed, HIGHEST)
        rows = rows + own[:, VEC0 + 4 + j : VEC0 + 5 + j]
        rows = pltpu.roll(rows, D - EMB0, 1)[:, :LANES]
        rows = jnp.where(lane < VOCAB, rows, 0.0)
        shared = shared + (pltpu.roll(rows, j * VOCAB, 1) if j else rows)
        if j:
            k = TAP0 + 3 * j
            mixes.append(
                own[:, k : k + 1] * rows
                + own[:, k + 1 : k + 2] * pltpu.roll(rows, VOCAB, 1)
                + own[:, k + 2 : k + 3] * pltpu.roll(rows, 2 * VOCAB, 1)
            )
            biases.append(own[:, TAP0 + 9 + j : TAP0 + 10 + j])
    r.rows[...] = shared
    r.shared[mine, :] = shared
    for d in range(1, n):
        peer = {"chan": lax.rem(me + d, n)}
        small.append(send(r.rows, r.shared.at[mine, :], (r.ss, r.sr), 2 * n + d, peer))
    mix = paired(jnp.concatenate(mixes, axis=0), 3 * VOCAB)
    names = lax.broadcasted_iota(jnp.int32, (VOCAB, width), 0).astype(F32)
    toks = r.toks

    def shifted(i, s):
        here = jnp.concatenate(
            [toks[i, s * parts + h : s * parts + h + 1, :] for h in range(parts)], axis=1
        )
        before = toks[jnp.maximum(i - 1, 0), (s + 1) * parts - 1 : (s + 1) * parts, D - LANES :]
        long = jnp.concatenate([jnp.where(i > 0, before, -1.0), here], axis=1)
        return here, pltpu.roll(long, 1, 1)[:, LANES:], pltpu.roll(long, 2, 1)[:, LANES:]

    for s in range(seqs):
        for k, row in enumerate(shifted(me, s)):
            r.tokx[s, k : k + 1, :] = row

    def gates(i):
        for s in range(seqs):
            here, one, two = shifted(i, s)
            out = named_dot(mix, [(names == row).astype(F32) for row in (two, one, here)])
            gate = (out[:chans] + biases[0]) * (out[chans:] + biases[1])
            for q in range(width // LANES):
                rows = pl.ds(pl.multiple_of(i * span + q * EIGHT, 8), EIGHT)
                for k in range(groups):
                    r.gch[k, s, rows, :] = gate[
                        k * EIGHT : (k + 1) * EIGHT, q * LANES : (q + 1) * LANES
                    ]

    loop(n // 2, gates)
    core_k0 = share(0, y_k0)
    x_w[0] = hop_x(0, *low[0], *z_w[0])
    z_w[1] = hop_z(1, *low[1])
    loop(n // 2, lambda i: gates(i + n // 2))
    spectra(0, core_k0, r.spec0v)
    hop_y()
    save(r.spec0v, r.spec0)
    back = Blocks(n, span, (r.zs, r.zr), r.zown)

    def chunk(k):
        conv_chunk(
            k, r.gch, r.spec0v, r.gspecv, r.zch, *tabs
        )
        back.start(back.back_refs, k, r.zch, r.zpos)

    early = max(groups // 2, 1)
    loop(early, chunk)
    x_w[1] = hop_x(1, *low[1], *z_w[1])
    loop(groups - early, lambda k: chunk(k + early))
    save(r.gspecv, r.gspec)
    filter_steps(r, 1, b, length, groups, r.keep1v, delta)
    y_k1 = offer(1)
    save(r.keep1v, r.keep1)
    hop_core()
    core_k1 = share(1, y_k1)
    spectra(1, core_k1, r.spec1v)
    save(r.spec1v, r.spec1)

    def finish(k):
        back.arrived(back.back_refs, k, r.zch, r.zpos)
        back.sent(back.back_refs, k, r.zch, r.zpos)

    loop(groups, finish)
    for _, copies in z_w:
        for copy in copies:
            copy.wait_send()
    for copy in saves:
        copy.wait()
    for copy in x_w[0] + x_w[1] + y_w + [y_k0, y_k1] + core_k0 + core_k1:
        copy.wait_send()
    for copy in core_w + small[2 * (n - 1) :]:
        copy.wait()


def prepare(arrays, tables, n, seqs, length, cid):
    chan_t = arrays[8]
    chans = chan_t.shape[1]
    groups = chans // EIGHT
    rows = length // LANES
    span = rows // n * EIGHT
    outer = 2 * rows
    width = length // n
    spec = sds(chans * outer, 2 * LANES)
    keep = sds(6, FO, length // 4)
    low, high = round_up(12 * chans, 64), round_up(12 * chans, 32)
    return pl.pallas_call(
        partial(prepare_kernel, n, length, chans),
        in_specs=[WHOLE] * 18,
        out_specs=[HBM] * 8 + [WHOLE] * 4,
        out_shape=[
            sds(n, low, D), sds(high, D),
            spec, spec, spec, keep, keep, sds(groups, n, seqs, span, LANES),
            sds(D, D), sds(n, EIGHT, D), sds(seqs, EIGHT, width), sds(D, LANES),
        ],
        scratch_shapes=[
            VMEM((low, D), F32),
            VMEM((high, D), F32),
            VMEM((chans, D), F32),
            VMEM((EIGHT, D), F32),
            VMEM((chans, LANES), F32),
            VMEM((LANES, LANES), F32),
            VMEM((LAYERS, groups, rows * EIGHT, LANES), F32),
            VMEM((groups, seqs, rows * EIGHT, LANES), F32),
            VMEM((groups, seqs, rows * EIGHT, LANES), F32),
            *[VMEM(spec.shape, F32)] * 3,
            *[VMEM(keep.shape, F32)] * 2,
            pltpu.SemaphoreType.DMA((6,)),
            *pair_sems(3 * n),
            *pair_sems(2, n + 3),
            *pair_sems(LAYERS, 3),
            *pair_sems(groups, n),
            pltpu.SemaphoreType.DMA((2,)),
            pltpu.SemaphoreType.DMA((groups,)),
        ],
        compiler_params=comm_params(cid),
        name="prepare",
    )(*arrays, position_table(length), *tables)


def middle_kernel(
    n, chans, z, wall, late, spec, misc, shared, tokx, first, first_real, twiddle, second,
    second_back, last, last_real, wlate, h, a, x1, p, q, gspec, zpos, zv, wv, hv, av, x1v,
    pv, qv, table, gpos, gch, zch, tails, halo, gspecv, gs, gr, gown, zs, zr, zown, hs, hr,
    ws, wr, wown, lsem,
):
    r = Names(locals())
    me, b = lax.axis_index("chan"), lax.axis_index("batch")
    seqs, width = r.x1v.shape[0], r.x1v.shape[2]
    groups, tiles = chans // EIGHT, width // LANES
    lane0 = TAP0 + 12
    loads = [
        pltpu.make_async_copy(r.z, r.zv, r.lsem.at[0]),
        pltpu.make_async_copy(r.wall.at[:, 0 : r.wv.shape[1]], r.wv, r.lsem.at[1]),
    ]
    for copy in loads:
        copy.start()
    r.table[...] = name_tables(r.shared[...], r.misc[...], 0)[1]
    greet(n, (core_mate(b), y_mate(b)))
    weights = (r.ws, r.wr)
    hop_z, hop_x = hops(n, b, me, weights, r.wown)
    mine = quarter_rows(r.wlate.shape[1], b)
    other = quarter_rows(r.wlate.shape[1], y_mate(b))
    late = (r.late.at[mine], r.wlate.at[:, mine])
    z_w = hop_z(0, *late)
    out = Tiles(n, tiles, (r.gs, r.gr), r.gown, r.gpos, r.gch)
    back = Blocks(n, tiles * EIGHT, (r.zs, r.zr), r.zown)
    for copy in loads:
        copy.wait()
    low = Layer(None, r.wv, r.misc, 0)
    high = Layer(r.wv.at[:, 9 * chans :], None, r.misc, 1)
    edge_lane = lax.broadcasted_iota(jnp.int32, (D, LANES), 1)
    inner = (me > 0).astype(F32)
    halo_copy = remote(r.tails, r.halo, (r.hs, r.hr), 0, {"chan": lax.rem(me + 1, n)})

    def tile(q):
        places = places_of(r.tokx, q)
        x = embedded(low.side, places[2])
        first_gate = named_dot(r.table[...], places) + low.column(TAP0 + 9)
        mixed = rear_mix(low, x, take_blocks(r.zv, q) * first_gate)
        put(r.hv, q, mixed)
        _, _, _, pre = rear_hidden(low, mixed)
        u = []
        for k in range(4):
            put(r.av.at[:, k], q, pre[k])
            u.append(pre[k] * gelu_parts(pre[k])[0])
        x = rear_out(low, mixed, u)
        put(r.x1v, q, x)
        for j, value in enumerate(front_forward(high, x)):
            put(r.pv.at[j], q, value)

    def gates(q):
        here = pl.ds(pl.multiple_of(q * LANES, LANES), LANES)
        prior = pl.ds(pl.multiple_of(jnp.maximum(q - 1, 0) * LANES, LANES), LANES)
        made = []
        for j in range(3):
            t = lane0 + 3 * j
            row = []
            for s in range(seqs):
                edge = pltpu.roll(r.halo[...], LANES - 2 - 2 * (j * seqs + s), 1) * inner
                before = jnp.where(q > 0, r.pv[j, s, :, prior], edge)
                now = r.pv[j, s, :, here]
                long = jnp.concatenate([before, now], axis=1)
                one = pltpu.roll(long, 1, 1)[:, LANES:]
                two = pltpu.roll(long, 2, 1)[:, LANES:]
                value = (
                    r.misc[:, lane0 + 9 + j : lane0 + 10 + j]
                    + r.misc[:, t : t + 1] * two
                    + r.misc[:, t + 1 : t + 2] * one
                    + r.misc[:, t + 2 : t + 3] * now
                )
                r.qv[j, s, :, here] = value
                row.append(value)
            made.append(row)
        gate = [made[2][s] * made[1][s] for s in range(seqs)]
        put_blocks(r.gpos, q, jnp.concatenate(gate, axis=1))
        out.start(q)

    def step(i):
        q = lax.rem(i + tiles - 1, tiles)
        tile(q)

        @pl.when(i == 0)
        def _():
            pack = jnp.zeros((D, LANES), F32)
            for j in range(3):
                for s in range(seqs):
                    slot = 2 * (j * seqs + s)
                    tail = pltpu.roll(r.pv[j, s, :, width - LANES :], slot + 2, 1)
                    pack = jnp.where((edge_lane == slot) | (edge_lane == slot + 1), tail, pack)
            r.tails[...] = pack
            halo_copy.start()

        @pl.when(i == 1)
        def _():
            halo_copy.wait_recv()

        @pl.when(i > 0)
        def _():
            gates(q)

    loop(tiles - 1, step)
    x_w = hop_x(0, *late, *z_w)
    step(tiles - 1)
    gates(tiles - 1)
    saves = [
        pltpu.make_async_copy(src, dst, r.lsem.at[3 + i])
        for i, (src, dst) in enumerate(
            ((r.hv, r.h), (r.av, r.a), (r.x1v, r.x1), (r.pv, r.p), (r.qv, r.q))
        )
    ]
    for copy in saves:
        copy.start()
    loop(tiles, out.arrived)

    def chunk(k):
        conv_chunk(
            k, r.gch, r.spec, r.gspecv, r.zch, r.first, r.twiddle, r.second, r.second_back, r.last
        )
        back.start(back.back_refs, k, r.zch, r.zpos)

    chunk(0)
    for copy in x_w:
        copy.wait_recv()
    here, there = r.wlate.at[:, mine], r.wlate.at[:, other]
    y_w = send(here, here, weights, (0, n), {"batch": y_mate(b)})
    core_w = [send(here, here, weights, (0, n + 1), {"batch": core_mate(b)})]
    loop(groups - 1, lambda k: chunk(k + 1))
    saves.append(pltpu.make_async_copy(r.gspecv, r.gspec, r.lsem.at[2]))
    saves[-1].start()
    loop(tiles, out.sent)
    loop(groups - 1, lambda k: back.arrived(back.back_refs, k, r.zch, r.zpos))
    y_w.wait_recv()
    core_w.append(send(there, there, weights, (0, n + 2), {"batch": core_mate(b)}))
    back.arrived(back.back_refs, groups - 1, r.zch, r.zpos)

    loop(groups, lambda k: back.sent(back.back_refs, k, r.zch, r.zpos))
    for copy in saves:
        copy.wait()
    halo_copy.wait_send()
    for copy in z_w[1] + x_w + [y_w]:
        copy.wait_send()
    for copy in core_w:
        copy.wait()


def middle(z, wall, late, spec, misc, shared, tokx, tables, n, chans, cid):
    groups, _, seqs, span, _ = z.shape
    width = span // EIGHT * LANES
    tiles = width // LANES
    by_channel = (groups, seqs, n * span, LANES)
    pos = (seqs, D, width)
    return pl.pallas_call(
        partial(middle_kernel, n, chans),
        in_specs=[HBM] * 3 + [WHOLE] * 11,
        out_specs=[HBM] * 8,
        out_shape=[
            sds(n, *late.shape), sds(*pos), sds(seqs, 4, D, width), sds(*pos),
            sds(3, *pos), sds(3, *pos), sds(*spec.shape), sds(*z.shape),
        ],
        scratch_shapes=[
            VMEM(z.shape, F32),
            VMEM((n, 12 * chans, D), F32),
            VMEM(pos, F32),
            VMEM((seqs, 4, D, width), F32),
            VMEM(pos, F32),
            VMEM((3,) + pos, F32),
            VMEM((3,) + pos, F32),
            VMEM((D, LANES), BF16),
            VMEM(z.shape, F32),
            VMEM(by_channel, F32),
            VMEM(by_channel, F32),
            VMEM((D, LANES), F32),
            VMEM((D, LANES), F32),
            VMEM(spec.shape, F32),
            *pair_sems(tiles, n),
            pltpu.SemaphoreType.DMA((tiles,)),
            *pair_sems(groups, n),
            pltpu.SemaphoreType.DMA((groups,)),
            *pair_sems(1),
            *pair_sems(1, n + 3),
            pltpu.SemaphoreType.DMA((1,)),
            pltpu.SemaphoreType.DMA((8,)),
        ],
        compiler_params=comm_params(cid),
        name="middle",
    )(z, wall, late, spec, misc, shared, tokx, *tables)


class GroupSum:
    def __init__(self, n, g, out, r0, sum0, ra, sa, ta, rb, sb, tb, send_sem, recv_sem):
        self.n, self.g, self.out = n, g, out
        self.r0, self.sum0 = r0, sum0
        self.a, self.b_side = (ra, sa, ta), (rb, sb, tb)
        self.sems = (send_sem, recv_sem)
        me, b = lax.axis_index("chan"), lax.axis_index("batch")
        self.x, self.z = lax.rem(me, 2), me // 2
        self.core, self.y = lax.rem(b, 2), b // 2
        self.b = b
        self.quarter = g.shape[1] // 4
        self.cut = first_rows(self.quarter)
        self.to_y = {"batch": y_mate(b)}
        self.to_x = {"chan": 2 * self.z + 1 - self.x}
        self.copies = []

    def start(self, source, landing, device):
        self.copies.append(send(source, landing, self.sems, len(self.copies), device))

    def part(self, k):
        return quarter_rows(self.g.shape[1], k)

    def cores(self):
        mate = {"batch": core_mate(self.b)}
        for k in range(2):
            self.start(self.g.at[:, self.part(2 * k + 1 - self.core)], self.r0.at[k], mate)

    def first(self):
        for k in range(2):
            self.copies[k].wait_recv()

            def add(i, k=k):
                mine = self.g[i, self.part(2 * k + self.core), :]
                self.sum0[k, lax.rem(i, 2), i // 2] = mine + self.r0[k, i]

            loop(self.n, add)
        cut = self.cut
        self.start(self.sum0.at[1 - self.y, :, :, 0:cut], self.a[0], self.to_y)
        if cut < self.quarter:
            self.start(
                self.sum0.at[:, 1 - self.x, :, cut : self.quarter], self.b_side[0], self.to_x
            )

    def second(self):
        cut = self.cut
        landing, sums, last = self.a
        self.copies[2].wait_recv()

        def add_a(i):
            for k in range(2):
                sums[k, i] = self.sum0[self.y, k, i, 0:cut, :] + landing[k, i]

        loop(self.n // 2, add_a)
        self.start(sums.at[1 - self.x], last, self.to_x)
        if cut < self.quarter:
            landing_b, sums_b, last_b = self.b_side
            self.copies[3].wait_recv()

            def add_b(i):
                for k in range(2):
                    mine = self.sum0[k, self.x, i, cut : self.quarter, :]
                    sums_b[k, i] = mine + landing_b[k, i]

            loop(self.n // 2, add_b)
            self.start(sums_b.at[1 - self.y], last_b, self.to_y)

    def close(self):
        cut = self.cut
        split = cut < self.quarter
        self.copies[4 if split else 3].wait_recv()

        def add_a(i):
            self.out[i, 0:cut, :] = self.a[1][self.x, i] + self.a[2][i]

        loop(self.n // 2, add_a)
        if split:
            self.copies[5].wait_recv()

            def add_b(i):
                self.out[i, cut : self.quarter, :] = self.b_side[1][self.y, i] + self.b_side[2][i]

            loop(self.n // 2, add_b)
        for copy in self.copies:
            copy.wait_send()


def first_rows(quarter):
    return quarter if quarter < 16 else round_up(quarter // 2, 8)


class ColumnSum:
    def __init__(self, n, source, landing, rows, zs, zr, bs, br):
        self.source, self.landing, self.rows = source, landing, rows
        self.zsems, self.bsems = (zs, zr), (bs, br)
        self.half = n // 2
        me, self.b = lax.axis_index("chan"), lax.axis_index("batch")
        self.x, self.z = lax.rem(me, 2), me // 2

    def column(self):
        for d in range(1, self.half):
            to = lax.rem(self.z + d, self.half)
            yield remote(
                self.source.at[to], self.landing.at[d - 1], self.zsems, d - 1,
                {"chan": 2 * to + self.x},
            )

    def quarter(self, k):
        return self.rows.at[quarter_rows(self.rows.shape[0], k)]

    def hop(self, k):
        mine, other = self.quarter(self.b), self.quarter(y_mate(self.b))
        ref, to = ((mine, y_mate), (mine, core_mate), (other, core_mate))[k]
        return remote(ref, ref, self.bsems, k, {"batch": to(self.b)})

    def start(self):
        for copy in self.column():
            copy.start()

    def share(self):
        total = self.source[self.z]
        for d, copy in enumerate(self.column()):
            copy.wait_recv()
            total = total + self.landing[d]
        self.rows[quarter_rows(self.rows.shape[0], self.b), :] = total
        self.hop(0).start()
        self.hop(1).start()

    def pass_on(self):
        self.hop(0).wait_recv()
        self.hop(2).start()

    def arrived(self):
        self.hop(1).wait_recv()
        self.hop(2).wait_recv()

    def sent(self):
        for copy in self.column():
            copy.wait_send()
        for k in range(3):
            self.hop(k).wait_send()


def column_scratch(n, quarter):
    return [
        VMEM((n // 2 - 1, quarter, D), F32),
        *pair_sems(n // 2 - 1),
        *pair_sems(3),
    ]


def group_scratch(n, rows):
    quarter, half = rows // 4, n // 2
    cut = first_rows(quarter)
    rest = max(quarter - cut, 8)
    return [
        VMEM((2, n, quarter, D), F32),
        VMEM((2, 2, half, quarter, D), F32),
        VMEM((2, half, cut, D), F32),
        VMEM((2, half, cut, D), F32),
        VMEM((half, cut, D), F32),
        VMEM((2, half, rest, D), F32),
        VMEM((2, half, rest, D), F32),
        VMEM((half, rest, D), F32),
        *pair_sems(6),
    ]


def take(ref, q):
    lanes = pl.ds(pl.multiple_of(q * LANES, LANES), LANES)
    return jnp.concatenate([ref[s, :, lanes] for s in range(ref.shape[0])], axis=1)


def put(ref, q, value):
    lanes = pl.ds(pl.multiple_of(q * LANES, LANES), LANES)
    for s in range(ref.shape[0]):
        ref[s, :, lanes] = value[:, s * LANES : (s + 1) * LANES]


def take_blocks(ref, q):
    groups, n, seqs, _, _ = ref.shape
    here = pl.ds(pl.multiple_of(q * EIGHT, 8), EIGHT)
    return jnp.concatenate(
        [
            jnp.concatenate(
                [ref[k, j, s, here, :] for j in range(n) for k in range(groups)], axis=0
            )
            for s in range(seqs)
        ],
        axis=1,
    )


def put_blocks(ref, q, value):
    groups, n, seqs, _, _ = ref.shape
    here = pl.ds(pl.multiple_of(q * EIGHT, 8), EIGHT)
    for s in range(seqs):
        for j in range(n):
            for k in range(groups):
                row = (j * groups + k) * EIGHT
                ref[k, j, s, here, :] = value[row : row + EIGHT, s * LANES : (s + 1) * LANES]


def places_of(tokx, q):
    lanes = pl.ds(pl.multiple_of(q * LANES, LANES), LANES)
    rows = [name_rows(tokx, s, lanes) for s in range(tokx.shape[0])]
    return [jnp.concatenate([row[k] for row in rows], axis=1) for k in range(3)]


def embedded(side, places):
    lane = lax.broadcasted_iota(jnp.int32, (D, LANES), 1)
    table = jnp.where(lane < VOCAB, pltpu.roll(side, D - EMB0, 1)[:, :LANES], 0.0)
    high = table.astype(BF16).astype(F32)
    middle = (table - high).astype(BF16).astype(F32)
    low = table - high - middle
    three = high + pltpu.roll(middle, VOCAB, 1) + pltpu.roll(low, 2 * VOCAB, 1)
    return named_dot(three.astype(BF16), [places] * 3, 1)


def top_tile(r, q):
    lay = Layer(None, r.wv, r.misc, 1)
    zt, qt = take_blocks(r.zv, q), take(r.qv.at[0], q)
    y = zt * qt
    h = rear_mix(lay, take(r.x1v, q), y)
    _, _, _, pre = rear_hidden(lay, h)
    put(r.x2v, q, rear_out(lay, h, [v * gelu_parts(v)[0] for v in pre]))
    dh, dy, columns = rear_backward(lay, h, pre, y, take(r.cotv, q), r.dw)
    put_blocks(r.dzpos, q, dy * qt)
    put(r.dq0v, q, dy * zt)
    put(r.dhout, q, dh)
    r.cols[...] += put_columns(columns)


def mid_tile(r, q):
    upper = Layer(r.wv.at[:, 9 * (D // r.wv.shape[0]) :], None, r.misc, 1)
    dout, columns = front_backward(
        upper, take(r.x1v, q), [take(r.pv.at[j], q) for j in range(3)], take(r.dh1v, q), r.dw
    )
    lay = Layer(None, r.wv, r.misc, 0)
    zt = take_blocks(r.zv, q)
    qt = named_dot(r.qtab[0], places_of(r.tokx, q)) + lay.column(TAP0 + 9)
    dh, dy, more = rear_backward(
        lay, take(r.hv, q), [take(r.av.at[:, k], q) for k in range(4)], zt * qt, dout, r.dw, 3
    )
    put_blocks(r.dzpos, q, dy * qt)
    put(r.dq0v, q, dy * zt)
    put(r.dhout, q, dh)
    r.cols[...] += put_columns(columns + more)


def top_kernel(
    n, chans, length, z, keep, spec, gspec, x1, w, misc, chan_t, filt_t, feat, q, p, cot,
    first, first_real, twiddle, second, second_back, last, last_real, dp, dh_out, cols,
    dnet, dchan, summed, x2, dpv, dhout, qv, pv, zv, keepv, specv, gspecv, x1v, wv, dw, dq0v, dzpos,
    dzch, dzspec, dgch, dgpos, dk, dkin, dnets, heads, halo, gs, gr, gown, zs, zr, zown, hs,
    hr, ks, kr, lsem, ssem, dsem, ksem, tsem, r0, sum0, ra, sa, ta, rb, sb, tb, ts, tr, cotv, x2v,
):
    back_body(Names(locals()), n, chans, 1, length)


def mid_kernel(
    n, chans, length, z, keep, spec, gspec, x1, w, misc, chan_t, filt_t, feat, shared, tokx,
    part1, dp1, dh1, h, a, first, first_real, twiddle, second, second_back, last, last_real, dp,
    dh_out, cols, dnet, dchan, summed, rows1, dpv, dhout, qv, pv, zv, keepv, specv, gspecv, x1v, wv, dw, dq0v,
    dzpos, dzch, dzspec, dgch, dgpos, dk, dkin, dnets, heads, halo, gs, gr, gown, zs, zr,
    zown, hs, hr, ks, kr, lsem, ssem, dsem, ksem, tsem, r0, sum0, ra, sa, ta, rb, sb, tb, ts, tr, dh1v, hv, av,
    ptab, qtab, in1, c1s, c1r, b1s, b1r,
):
    back_body(Names(locals()), n, chans, 0, length)


def back_body(r, n, chans, layer, length):
    top = layer == LAYERS - 1
    me, b = lax.axis_index("chan"), lax.axis_index("batch")
    seqs, width = r.x1v.shape[0], r.x1v.shape[2]
    groups, tiles = chans // EIGHT, width // LANES
    rows_all, outer = length // LANES, r.twiddle.shape[0]
    lane0 = TAP0 + 12 * layer
    span = tiles * EIGHT

    def fetch(index, src, dst):
        return pltpu.make_async_copy(src, dst, r.lsem.at[index])

    early = [fetch(0, r.w.at[:, 0 : r.wv.shape[1]], r.wv), fetch(1, r.z, r.zv)]
    for copy in early:
        copy.start()
    if top:
        tiled = [(r.x1, r.x1v), (r.cot, r.cotv), (r.q.at[0], r.qv.at[0])]
    else:
        tiled = [(r.x1, r.x1v), (r.dp1, r.pv), (r.dh1, r.dh1v), (r.h, r.hv), (r.a, r.av)]

    def tile_loads(q):
        lanes = pl.ds(pl.multiple_of(q * LANES, LANES), LANES)
        for i, (src, dst) in enumerate(tiled):
            index = (slice(None),) * (len(src.shape) - 1) + (lanes,)
            yield pltpu.make_async_copy(src.at[index], dst.at[index], r.tsem.at[i, q])

    def start_tile(q):
        for copy in tile_loads(q):
            copy.start()

    start_tile(0)
    late = [fetch(8, r.spec, r.specv), fetch(9, r.gspec, r.gspecv)]
    block = 512

    def kept(i):
        place = pl.ds(pl.multiple_of(i * block, block), block)
        slot = lax.rem(i, 2)
        return pltpu.make_async_copy(r.keep.at[:, :, place], r.keepv.at[slot], r.ksem.at[slot])

    greet(n, [lax.rem(b + d, 4) for d in range(1, 4)])
    r.dw[...] = jnp.zeros_like(r.dw)
    r.cols[...] = jnp.zeros_like(r.cols)
    if top:
        late.append(fetch(2, r.q.at[pl.ds(1, 2)], r.qv.at[pl.ds(1, 2)]))
        late.append(fetch(3, r.p, r.pv))
    else:
        upper = ColumnSum(n, r.part1, r.in1, r.rows1, r.c1s, r.c1r, r.b1s, r.b1r)
        upper.start()
        for j in range(3):
            r.ptab[j], r.qtab[j] = name_tables(r.shared[...], r.misc[...], j)
    out = Tiles(n, tiles, (r.gs, r.gr), r.gown, r.dzpos, r.dzch)
    back = Blocks(n, span, (r.zs, r.zr), r.zown)
    for copy in early:
        copy.wait()

    def tile(q):
        for copy in tile_loads(q):
            copy.wait()

        @pl.when(q + 1 < tiles)
        def _():
            start_tile(q + 1)

        @pl.when(q == min(1, tiles - 1))
        def _():
            for copy in late:
                copy.start()
            for i in range(2):
                kept(i).start()

        (top_tile if top else mid_tile)(r, q)
        out.start(q)

    loop(tiles, tile)
    saves = [pltpu.make_async_copy(r.dhout, r.dh_out, r.ssem.at[0])]
    if top:
        saves.append(pltpu.make_async_copy(r.x2v, r.x2, r.ssem.at[1]))
    for copy in saves:
        copy.start()

    def dp_save(k):
        place = pl.ds(pl.multiple_of(k * EIGHT, 8), EIGHT)
        return pltpu.make_async_copy(
            r.dpv.at[:, :, :, place, :], r.dp.at[:, :, :, place, :], r.dsem.at[k]
        )

    total = GroupSum(
        n, r.dw, r.summed, r.r0, r.sum0, r.ra, r.sa, r.ta, r.rb, r.sb, r.tb, r.ts, r.tr
    )
    total.cores()
    if not top:
        upper.share()

    for copy in late[:2]:
        copy.wait()
    total.first()
    loop(tiles, out.arrived)
    dgch, dgpos, dk = r.dgch, r.dgpos, r.dk

    def chunk(k):
        rows = pl.ds(pl.multiple_of(k * EIGHT * outer, 8), EIGHT * outer)
        u = spectrum_of(load_pairs(r.dzch.at[k]), r.first[...], r.twiddle[...], r.second[...])
        r.dzspec[rows, :] = u
        o = signal_of(
            times_conj(u, r.specv[rows, :]), r.twiddle[...], r.second_back[...], r.last[...]
        )
        store_pairs(dgch.at[k], o)
        back.start(back.back_refs, k, dgch, dgpos)

    loop(groups, chunk)

    def lag(k):
        rows = pl.ds(pl.multiple_of(k * EIGHT * outer, 8), EIGHT * outer)
        v = times_conj(r.dzspec[rows, :], r.gspecv[rows, :])
        taps = signal_of(v, r.twiddle[...], r.second_back[...], r.last_real[...])
        for c in range(EIGHT):
            dk[k, pl.ds(c, rows_all, stride=EIGHT), :] = taps[:, c * LANES : (c + 1) * LANES]

    loop(groups, lag)
    count = dk.shape[1] // 4

    def lags(j):
        return pl.ds(pl.multiple_of(j * count, 8), count)

    shares = []
    for d in range(1, 4):
        j = lax.rem(b + d, 4)
        shares.append(
            send(dk.at[:, lags(j)], r.dkin.at[d - 1], (r.ks, r.kr), d - 1, {"batch": j})
        )
    total.second()
    if not top:
        upper.pass_on()

        def lower(q):
            places = places_of(r.tokx, q)
            for j in range(3):
                put(r.pv.at[j], q, named_dot(r.ptab[j], places[2:]))
                if j:
                    value = named_dot(r.qtab[j], places)
                    put(r.qv.at[j], q, value + r.misc[:, TAP0 + 9 + j : TAP0 + 10 + j])

        loop(tiles, lower)

    for copy in late[2:]:
        copy.wait()
    for share in shares:
        share.wait_recv()
    dk[:, lags(b), :] = dk[:, lags(b), :] + r.dkin[0] + r.dkin[1] + r.dkin[2]
    r.dnets[...] = jnp.zeros_like(r.dnets)
    r.dchan[...] = jnp.zeros_like(r.dchan)
    steps = length // 4 // block
    delta = decay(me, chans)
    fourth = r.chan_t[layer, :, 13 : 13 + FO]

    def network(i):
        start = b * (length // 4) + i * block
        wide = []
        for c in range(block // LANES):
            place = pl.ds(pl.multiple_of((start // LANES + c) * EIGHT, 8), EIGHT)
            wide.append(jnp.concatenate([dk[k, place, :] for k in range(groups)], axis=0))
        kept(i).wait()
        filter_back_block(
            length, start, r.feat[:, pl.ds(pl.multiple_of(start, block), block)],
            r.filt_t.at[layer], fourth, delta,
            r.keepv.at[lax.rem(i, 2)], jnp.concatenate(wide, axis=1), r.dnets, r.dchan,
        )

        @pl.when(i + 2 < steps)
        def _():
            kept(i + 2).start()

    loop(steps, network)
    head = jnp.concatenate([dk[k, 0:EIGHT, :] for k in range(groups)], axis=0)
    lane = lax.broadcasted_iota(jnp.int32, (chans, LANES), 1)
    head = jnp.where(lane == 0, head, 0.0) * (b == 0).astype(F32)
    r.dchan[...] += pltpu.roll(head, FO, 1)
    r.dnet[...] = (
        widened(r.dnets[0], D)
        + pltpu.roll(widened(r.dnets[1], D), EMB + 1, 1)
        + pltpu.roll(widened(r.dnets[2], D), EMB + 2 + FO, 1)
    )
    lane = lax.broadcasted_iota(jnp.int32, (EIGHT, LANES), 1)
    full = width + LANES
    inner = (me < n - 1).astype(F32)

    def halo_copy(k):
        return remote(
            r.heads.at[k], r.halo.at[k], (r.hs, r.hr), k, {"chan": lax.rem(me + n - 1, n)}
        )

    def heads(k):
        back.arrived(back.back_refs, k, dgch, dgpos)

        def body(owner):
            rows = pl.ds(pl.multiple_of(owner * chans + k * EIGHT, 8), EIGHT)
            pack = jnp.zeros((EIGHT, LANES), F32)
            for s in range(seqs):
                dg = dgpos[k, owner, s, 0:EIGHT, :]
                parts = (
                    r.dq0v[s, rows, 0:LANES],
                    dg * r.qv[2, s, rows, 0:LANES],
                    dg * r.qv[1, s, rows, 0:LANES],
                )
                for j in range(3):
                    slot = 2 * (j * seqs + s)
                    head = pltpu.roll(parts[j], slot, 1) if slot else parts[j]
                    pack = jnp.where((lane == slot) | (lane == slot + 1), head, pack)
            r.heads[k, pl.ds(pl.multiple_of(owner * EIGHT, 8), EIGHT), :] = pack

        loop(n, body)
        halo_copy(k).start()

    def short(k):
        halo_copy(k).wait_recv()
        eight = pl.ds(pl.multiple_of(k * EIGHT, 8), EIGHT)

        def body(owner):
            rows = pl.ds(pl.multiple_of(owner * chans + k * EIGHT, 8), EIGHT)
            side = r.misc[rows, :]
            edge = r.halo[k, pl.ds(pl.multiple_of(owner * EIGHT, 8), EIGHT), :] * inner
            sums = [jnp.zeros((EIGHT, 1), F32)] * 12
            for s in range(seqs):
                dg = jnp.concatenate(
                    [
                        dgpos[k, owner, s, q * EIGHT : (q + 1) * EIGHT, :]
                        for q in range(tiles)
                    ],
                    axis=1,
                )
                parts = (r.dq0v[s, rows, :], dg * r.qv[2, s, rows, :], dg * r.qv[1, s, rows, :])
                for j in range(3):
                    here = parts[j]
                    slot = 2 * (j * seqs + s)
                    after = pltpu.roll(edge, LANES - slot, 1) if slot else edge
                    long = jnp.concatenate([here, after], axis=1)
                    one = pltpu.roll(long, full - 1, 1)[:, :width]
                    two = pltpu.roll(long, full - 2, 1)[:, :width]
                    t = lane0 + 3 * j
                    r.dpv[j, s, owner, eight, :] = (
                        side[:, t : t + 1] * two
                        + side[:, t + 1 : t + 2] * one
                        + side[:, t + 2 : t + 3] * here
                    )
                    source = r.pv[j, s, rows, :]
                    sums[3 * j] = sums[3 * j] + row_sum(two * source)
                    sums[3 * j + 1] = sums[3 * j + 1] + row_sum(one * source)
                    sums[3 * j + 2] = sums[3 * j + 2] + row_sum(here * source)
                    sums[9 + j] = sums[9 + j] + row_sum(here)
            r.cols[rows, :] += put_columns([(lane0 + i, sums[i]) for i in range(12)])

        loop(n, body)
        dp_save(k).start()

    def step(k):
        @pl.when(k < groups)
        def _():
            heads(k)

        @pl.when(k > 0)
        def _():
            short(k - 1)

    loop(groups + 1, step)
    total.close()
    if not top:
        upper.arrived()
        upper.sent()
    for copy in saves:
        copy.wait()
    loop(groups, lambda k: dp_save(k).wait())
    for share in shares:
        share.wait_send()
    loop(tiles, out.sent)

    def finish(k):
        halo_copy(k).wait_send()
        back.sent(back.back_refs, k, dgch, dgpos)

    loop(groups, finish)


def back_call(z, keep, spec, gspec, x1, w, misc, chan_t, filt_t, extra, tables, n, layer, cid):
    top = layer == LAYERS - 1
    seqs, _, width = x1.shape
    chans = chan_t.shape[1]
    groups, tiles = chans // EIGHT, width // LANES
    span = tiles * EIGHT
    length = width * n
    pos = x1.shape
    by_position = (groups, n, seqs, span, LANES)
    by_channel = (groups, seqs, n * span, LANES)
    rows = round_up(9 * chans, 32) if top else 12 * chans
    held = (n, rows, D)
    half = n // 2
    if top:
        mine, places = [VMEM(pos, F32), VMEM(pos, F32)], [HBM] * 3
    else:
        mine = [
            VMEM(pos, F32), VMEM(pos, F32), VMEM(extra[6].shape, F32),
            VMEM((3, D, LANES), BF16), VMEM((3, D, LANES), BF16),
            *column_scratch(n, extra[2].shape[1]),
        ]
        places = [WHOLE] * 3 + [HBM] * 4
    dp, *rest = pl.pallas_call(
        partial(top_kernel if top else mid_kernel, n, chans, length),
        in_specs=[HBM] * 6 + [WHOLE] * 4 + places + [WHOLE] * 7,
        out_specs=[HBM] * 2 + [WHOLE] * 4 + [HBM if top else WHOLE],
        out_shape=[
            sds(3, seqs, n, chans, width), sds(*pos), sds(D, D), sds(FO, D), sds(chans, LANES),
            sds(half, rows // 4, D),
        ]
        + [sds(*pos) if top else sds(4 * extra[2].shape[1], D)],
        scratch_shapes=[
            VMEM((3, seqs, n, chans, width), F32),
            VMEM(pos, F32),
            VMEM((3,) + pos, F32),
            VMEM((3,) + pos, F32),
            VMEM(by_position, F32),
            VMEM((2, 6, FO, 512), F32),
            VMEM(spec.shape, F32),
            VMEM(spec.shape, F32),
            VMEM(pos, F32),
            VMEM(held, F32),
            VMEM(held, F32),
            VMEM(pos, F32),
            VMEM(by_position, F32),
            VMEM(by_channel, F32),
            VMEM(spec.shape, F32),
            VMEM(by_channel, F32),
            VMEM(by_position, F32),
            VMEM((groups, n * span, LANES), F32),
            VMEM((3, groups, n * span // 4, LANES), F32),
            VMEM((3, FO, LANES), F32),
            VMEM((groups, n * EIGHT, LANES), F32),
            VMEM((groups, n * EIGHT, LANES), F32),
            *pair_sems(tiles, n),
            pltpu.SemaphoreType.DMA((tiles,)),
            *pair_sems(groups, n),
            pltpu.SemaphoreType.DMA((groups,)),
            *pair_sems(groups),
            *pair_sems(3),
            pltpu.SemaphoreType.DMA((12,)),
            pltpu.SemaphoreType.DMA((2,)),
            pltpu.SemaphoreType.DMA((groups,)),
            pltpu.SemaphoreType.DMA((2,)),
            pltpu.SemaphoreType.DMA((5, tiles)),
            *group_scratch(n, rows),
        ]
        + mine,
        compiler_params=comm_params(cid),
        name="top_back" if top else "mid_back",
    )(
        z, keep, spec, gspec, x1, w, misc, chan_t, filt_t, position_table(length),
        *extra, *tables,
    )
    return (dp.reshape(3, *pos), *rest)


def total_kernel(
    n,
    part2, cols0, cols1, dnet0, dnet1, dchan0, dchan1, dp, dh, ids, late, misc,
    rows2, rows3, rows4, filt, chan, dx,
    fourth, last4, dchan, rchan, inward, sums, named, own, cs, cr, fs, fr, isem, *rest,
):
    me, b = lax.axis_index("chan"), lax.axis_index("batch")
    chans = D // n
    filter_rows = filt.shape[1]
    seqs, _, width = dh.shape
    fetch = pltpu.make_async_copy(late.at[:, 9 * chans : 12 * chans], inward, isem)
    fetch.start()
    for l, value in enumerate((dchan0, dchan1)):
        dchan[l] = value[...]
    greet(n, [lax.rem(b + d, 4) for d in range(1, 4)])

    two = ColumnSum(n, part2, rest[0], rows2, *rest[1:5])
    two.start()
    slot = lax.broadcasted_iota(jnp.int32, (LANES, width), 0)

    def by_name(s, total):
        here = ids[pl.ds(s, 1), :]
        for j in range(4):
            places = (slot == here + VOCAB * j).astype(F32)
            total = total + dot_nt(dh[s] if j == 3 else dp[j, s], places)
        return total

    by_names = lax.fori_loop(0, seqs, by_name, jnp.zeros((D, LANES), F32))
    columns = cols0[:, 0:LANES] + cols1[:, 0:LANES]
    for i in range(n):
        here = slice(i * chans, (i + 1) * chans)
        fourth[i, 0:chans, 0:LANES] = columns[here]
        fourth[i, 0:chans, LANES:] = by_names[here]
        row = i * filter_rows
        if row < LAYERS * FO:
            dnet = (dnet0, dnet1)[row // FO]
            fourth[i, chans : chans + filter_rows, :] = dnet[
                row % FO : row % FO + filter_rows, :
            ]
        else:
            fourth[i, chans : chans + filter_rows, :] = jnp.zeros((filter_rows, D), F32)
        spare = fourth.shape[1] - chans - filter_rows
        if spare:
            fourth[i, chans + filter_rows :, :] = jnp.zeros((spare, D), F32)
    four = GroupSum(n, fourth, last4, *rest[10:])
    end = ColumnSum(n, last4, rest[5], rows4, *rest[6:10])
    four.cores()
    small = [
        send(dchan, rchan.at[d - 1], (cs, cr), d - 1, {"batch": lax.rem(b + d, 4)})
        for d in range(1, 4)
    ]
    fetch.wait()
    lay = Layer(inward, None, misc, 0)

    def tile(q):
        lanes = pl.ds(pl.multiple_of(q * LANES, LANES), LANES)
        here = jnp.concatenate([ids[s : s + 1, lanes] for s in range(seqs)], axis=1)
        names = lax.broadcasted_iota(jnp.int32, (VOCAB, here.shape[1]), 0)
        value = embedded(lay.side, (names == here).astype(F32))
        grad, _ = front_backward(
            lay, value, [take(dp.at[j], q) for j in range(3)], take(dh, q)
        )
        put(dx, q, grad)

    tiles = width // LANES
    four.first()
    loop(tiles // 2, tile)
    four.second()
    loop(tiles - tiles // 2, lambda q: tile(q + tiles // 2))
    four.close()
    end.start()
    two.share()
    end.share()
    end.pass_on()
    end.arrived()
    mine = pl.ds(pl.multiple_of(me * chans, 8), chans)
    filt[me] = rows4[chans : chans + filter_rows, :]
    own[...] = rows4[0:chans, LANES:]
    named[mine, :] = own[...]
    shares = []
    for d in range(1, n):
        peer = {"chan": lax.rem(me + d, n)}
        shares.append(send(own, named.at[mine, :], (fs, fr), d - 1, peer))
        shares.append(send(filt.at[me], filt.at[me], (fs, fr), n - 2 + d, peer))
    two.pass_on()
    for copy in small + shares:
        copy.wait_recv()
    for l in range(LAYERS):
        chan[l] = dchan[l] + rchan[0, l] + rchan[1, l] + rchan[2, l]
    lane = lax.broadcasted_iota(jnp.int32, (D, LANES), 1)

    def name_lanes(value, j):
        value = pltpu.roll(value, LANES - j * VOCAB, 1) if j else value
        return jnp.where(lane[: value.shape[0]] < VOCAB, value, 0.0)

    table = jnp.where(lane < VOCAB, pltpu.roll(lay.side, D - EMB0, 1)[:, :LANES], 0.0)
    xh, scale = normalize(table)
    xh = jnp.where(lane < VOCAB, xh, 0.0)
    normed = xh * lay.vec(0) + lay.vec(1)
    everything = named[...]
    dps = [name_lanes(everything, j) for j in range(3)]
    stacked = jnp.stack([v.reshape(n, chans, LANES) for v in dps], axis=1)
    dn = dot_tn(lay.inward(), stacked.reshape(3 * D, LANES))
    grad = name_lanes(everything, 3) + normalize_back(dn * lay.vec(0), xh, scale)
    grad = jnp.where(lane < VOCAB, grad, 0.0)
    base = VEC0
    pairs = [(base + 4 + j, row_sum(dps[j])) for j in range(3)]
    pairs += [(base, row_sum(dn * xh)), (base + 1, row_sum(dn))]
    sums[...] = put_columns(pairs, LANES) + pltpu.roll(grad, EMB0, 1)
    end.sent()
    rows4[0:chans, 0:LANES] += sums[mine, :]
    for j in range(3):
        rows3[j * chans : (j + 1) * chans, :] = dot_nt(name_lanes(own[...], j), normed)
    two.arrived()
    two.sent()
    for copy in small + shares:
        copy.wait_send()


def update_kernel(n, scale, *refs):
    sem = refs[-1]
    passed = [
        pltpu.make_async_copy(refs[k], refs[k - 3], sem.at[k]) for k in range(2)
    ]
    for copy in passed:
        copy.start()
    refs = refs[2:]
    rows1, rows2, rows3, rows4, filt, chan = refs[:6]
    weights, moments, averages = refs[6:15], refs[15:24], refs[24:33]
    outs = refs[33:69]
    chans = chan.shape[1]
    filter_rows = filt.shape[1]

    def step(which, index, gradient):
        factor = STEP_RATES[which] * scale
        velocity = MOMENTUM * moments[which][index] + gradient
        updated = weights[which][index] - factor * (gradient + MOMENTUM * velocity)
        running = AVERAGING * averages[which][index] + (1.0 - AVERAGING) * updated
        base = 4 * which
        outs[base][index] = velocity
        outs[base + 1][index] = running
        outs[base + 2][index] = updated
        outs[base + 3][index] = updated.astype(BF16)

    columns = rows4[0:chans, 0:LANES]
    flat = columns
    if chans < LANES:
        flat = jnp.concatenate([columns, jnp.zeros((LANES - chans, LANES), F32)], axis=0)
    flat = flat.T
    step(0, Ellipsis, flat[EMB0 : EMB0 + VOCAB, :chans])
    lane = lax.broadcasted_iota(jnp.int32, (chans, LANES), 1)
    off = []
    for l in range(LAYERS):
        front, base = (rows3, 0) if l == 0 else (rows2, 0)
        for j in range(3):
            step(1, (l, j), front[base + j * chans : base + (j + 1) * chans, :])
        for k in range(9):
            row = VEC0 + 9 * l + k
            step(2, (k, slice(l, l + 1)), flat[row : row + 1, :chans])
        rear, base = (rows2, 3 * chans) if l == 0 else (rows1, 0)
        step(3, l, rear[base : base + chans, :])
        step(4, l, rear[base + chans : base + 5 * chans, :])
        pieces = [rear[base + (5 + c) * chans : base + (6 + c) * chans, :] for c in range(4)]
        step(6, l, fold(pieces, n, chans, back=True))
        row = jnp.zeros((1, LANES), F32)
        for c in range(4):
            piece = flat[OFF0 + 4 * l + c : OFF0 + 4 * l + c + 1, :]
            row = row + (pltpu.roll(piece, c * chans, 1) if c else piece)
        off.append(row[:, : 4 * chans])
        taps = pltpu.roll(columns, LANES - TAP0 - 12 * l, 1)
        own = chan[l]
        skip = pltpu.roll(own, LANES - FO + 12, 1)
        gradient = jnp.where(lane < 12, taps, jnp.where(lane == 12, skip, pltpu.roll(own, 13, 1)))
        step(7, l, gradient[:, : 13 + FO])
    step(5, Ellipsis, jnp.concatenate(off, axis=0))
    whole = filt[...].reshape(n * filter_rows, D)
    for l in range(LAYERS):
        step(8, l, whole[l * FO : (l + 1) * FO, :136])
    for copy in passed:
        copy.wait()


def finish(
    rows1, part2, cols, dnets, dchans, dp, dh, ids, late, misc, weights, moments, averages,
    activations, n, scale, cid,
):
    chans = D // n
    filter_rows = round_up(LAYERS * FO, n * EIGHT) // n
    fourth = round_up(chans + filter_rows, 32)
    q2, q4 = part2.shape[1], fourth // 4
    half = n // 2
    *sums, dx = pl.pallas_call(
        partial(total_kernel, n),
        in_specs=[WHOLE] * 10 + [HBM, WHOLE],
        out_specs=[WHOLE] * 6,
        out_shape=[
            sds(4 * q2, D), sds(3 * chans, D), sds(fourth, D),
            sds(n, filter_rows, D), sds(LAYERS, chans, LANES), sds(*dh.shape),
        ],
        scratch_shapes=[
            VMEM((n, fourth, D), F32),
            VMEM((half, q4, D), F32),
            VMEM((LAYERS, chans, LANES), F32),
            VMEM((3, LAYERS, chans, LANES), F32),
            VMEM((n, 3 * chans, D), F32),
            VMEM((D, LANES), F32),
            VMEM((D, LANES), F32),
            VMEM((chans, LANES), F32),
            *pair_sems(3),
            *pair_sems(2 * n),
            pltpu.SemaphoreType.DMA,
            *column_scratch(n, q2),
            *column_scratch(n, q4),
            *group_scratch(n, fourth),
        ],
        compiler_params=comm_params(cid),
        name="total",
    )(part2, *cols, *dnets, *dchans, dp, dh, ids, late, misc)
    shapes = []
    for weight in weights:
        shapes += [sds(*weight.shape)] * 3 + [jax.ShapeDtypeStruct(weight.shape, BF16)]
    shapes += [sds(*dx.shape)] * 2
    return pl.pallas_call(
        partial(update_kernel, n, scale),
        in_specs=[WHOLE] * 35,
        out_specs=[WHOLE] * 36 + [HBM, HBM],
        out_shape=shapes,
        scratch_shapes=[pltpu.SemaphoreType.DMA((2,))],
        compiler_params=pltpu.CompilerParams(vmem_limit_bytes=VMEM_LIMIT),
        name="update",
    )(activations, dx, rows1, *sums, *weights, *moments, *averages)


def onehot_rows(tokens):
    row = lax.broadcasted_iota(jnp.int32, (D, tokens.shape[1]), 0)
    return (row == tokens + EMB0).astype(F32)


class Layer:
    def __init__(self, front, rear, misc, index, base=0):
        some = rear if front is None else front
        self.n = some.shape[0]
        self.c = D // self.n
        self.front, self.rear, self.base = front, rear, base
        self.side = misc[...]
        self.index = index

    def rows(self, ref, start, count):
        return ref[:, start * self.c : (start + count) * self.c, :].reshape(
            self.n * count * self.c, D
        )

    def column(self, lane):
        return self.side[:, lane : lane + 1]

    def vec(self, k):
        return self.column(VEC0 + 9 * self.index + k)

    def off(self, k):
        return self.column(OFF0 + 4 * self.index + k)

    def inward(self):
        return self.rows(self.front, 0, 3)

    def outward(self):
        return self.rows(self.rear, self.base, 1)

    def expand(self, k):
        return self.rows(self.rear, self.base + 1 + k, 1)

    def contract(self, k):
        return self.rows(self.rear, self.base + 5 + k, 1)


def front_forward(lay, x):
    xh, _ = normalize(x)
    normed = xh * lay.vec(0) + lay.vec(1)
    p = dot(lay.inward(), normed).reshape(lay.n, 3, lay.c, x.shape[1])
    return [p[:, j].reshape(D, x.shape[1]) + lay.vec(4 + j) for j in range(3)]


def front_backward(lay, x, dp, dh, dw=None):
    xh, scale = normalize(x)
    normed = xh * lay.vec(0) + lay.vec(1)
    width = x.shape[1]
    stacked = jnp.stack([d.reshape(lay.n, lay.c, width) for d in dp], axis=1)
    stacked = stacked.reshape(3 * D, width)
    dn = dot_tn(lay.inward(), stacked)
    if dw is not None:
        dw[:, 0 : 3 * lay.c, :] += dot_nt(stacked, normed, DW).reshape(lay.n, 3 * lay.c, D)
    base = VEC0 + 9 * lay.index
    columns = [(base + 4 + j, row_sum(dp[j])) for j in range(3)]
    columns += [(base, row_sum(dn * xh)), (base + 1, row_sum(dn))]
    return dh + normalize_back(dn * lay.vec(0), xh, scale), columns


def rear_mix(lay, x, y):
    return x + dot(lay.outward(), y) + lay.vec(7)


def rear_hidden(lay, h):
    xh, scale = normalize(h)
    m = xh * lay.vec(2) + lay.vec(3)
    a = [dot(lay.expand(k), m) + lay.off(k) for k in range(4)]
    return xh, scale, m, a


def rear_out(lay, h, u):
    out = h + lay.vec(8)
    for k in range(4):
        out = out + dot(lay.contract(k), u[k])
    return out


def rear_backward(lay, h, a, y, dout, dw, base=0):
    n, c = lay.n, lay.c

    def add(row, value):
        dw[:, (base + row) * c : (base + row + 1) * c, :] += value.reshape(n, c, D)

    xh, scale = normalize(h)
    m = xh * lay.vec(2) + lay.vec(3)
    vec = VEC0 + 9 * lay.index
    columns = [(vec + 8, row_sum(dout))]
    dm = None
    for k in range(4):
        ak = a[k]
        g, t = gelu_parts(ak)
        u = ak * g
        add(5 + k, dot_nt(dout, u, DW))
        slope = g + 0.5 * ak * (1.0 - t * t) * (GELU_SCALE * (1.0 + 3.0 * GELU_CUBE * ak * ak))
        dpre = dot_tn(lay.contract(k), dout) * slope
        add(1 + k, dot_nt(dpre, m, DW))
        columns.append((OFF0 + 4 * lay.index + k, row_sum(dpre)))
        term = dot_tn(lay.expand(k), dpre)
        dm = term if dm is None else dm + term
    dh = dout + normalize_back(dm * lay.vec(2), xh, scale)
    columns += [(vec + 2, row_sum(dm * xh)), (vec + 3, row_sum(dm)), (vec + 7, row_sum(dh))]
    add(0, dot_nt(dh, y, DW))
    return dh, dot_tn(lay.outward(), dh), columns


def turned(arrays):
    out = list(arrays)
    out[2] = arrays[2].transpose(1, 0, 2)
    out[7] = arrays[7].transpose(0, 2, 1)
    out[8] = arrays[8].transpose(0, 2, 1)
    return out


def per_device(*arguments):
    token_ids, cotangent = arguments[0], arguments[28]
    weights = turned(arguments[1:10])
    moments = turned(arguments[10:19])
    averages = turned(arguments[19:28])
    n, m = lax.axis_size("chan"), lax.axis_size("batch")
    seqs, width = token_ids.shape
    length = width * n
    chan_t, filt_t = weights[7], weights[8]
    chans = chan_t.shape[1]
    groups = chans // EIGHT
    tables = fourier_tables(length)
    wall, late, spec0, spec1, gspec0, keep0, keep1, z0, misc, _, tokx, shared = prepare(
        (token_ids, *weights), tables, n, seqs, length, 1
    )
    wlate, h0, a0, x1, p1, q1, gspec1, z1 = middle(
        z0, wall, late, spec1, misc, shared, tokx, tables, n, chans, 2
    )
    dp1, dh1, cols1, dnet1, dchan1, part1, activations = back_call(
        z1, keep1, spec1, gspec1, x1, wlate, misc, chan_t, filt_t, (q1, p1, cotangent),
        tables, n, 1, 3,
    )
    dp0, dh0, cols0, dnet0, dchan0, part2, rows1 = back_call(
        z0, keep0, spec0, gspec0, x1, wall, misc, chan_t, filt_t,
        (shared, tokx, part1, dp1, dh1, h0, a0), tables, n, 0, 4,
    )
    *updates, activations, input_gradient = finish(
        rows1, part2, (cols0, cols1), (dnet0, dnet1), (dchan0, dchan1), dp0, dh0, token_ids,
        wlate, misc, weights, moments, averages, activations, n,
        1.0 / math.sqrt(seqs * m * length), 5,
    )
    kinds = [turned(updates[k::4]) for k in range(4)]
    return (activations, input_gradient) + tuple(
        kinds[k][w] for w in range(9) for k in range(4)
    )


def solution(mesh):
    in_weights = (
        P(None, "chan"),
        P(None, None, "chan", None),
        P(None, None, "chan"),
        P(None, "chan", None),
        P(None, "chan", None),
        P(None, "chan"),
        P(None, "chan", None),
        P(None, None, "chan"),
        P(),
    )
    tokens = P("batch", None, "chan")
    in_specs = (P("batch", "chan"),) + in_weights * 3 + (tokens,)
    out_specs = (tokens, tokens) + tuple(spec for spec in in_weights for _ in range(4))
    return jax.shard_map(
        per_device, mesh=mesh, in_specs=in_specs, out_specs=out_specs, check_vma=False
    )
```

```python
from functools import partial
import math

import jax
import jax.numpy as jnp
import numpy as np
from jax import lax
from jax.experimental import pallas as pl
from jax.experimental.pallas import tpu as pltpu
from jax.sharding import PartitionSpec as P

D = 256
FF = 1024
FO = 64
EMB = 5
VOCAB = 16
LAYERS = 2
LANES = 128
TILE = 256

HIGH = lax.Precision.HIGH
HIGHEST = lax.Precision.HIGHEST
DW = lax.Precision.HIGH
EPSILON = 1e-05
MOMENTUM = 0.9
AVERAGING = 0.9
WINDOW_SHIFT = 0.05
FREQUENCY = 10.0
STEP_RATES = (0.7, 0.06, 0.1, 0.037, 0.1, 0.16, 0.025, 0.2, 0.0002)
GELU_SCALE = math.sqrt(2.0 / math.pi)
GELU_CUBE = 0.044715

MESH = pl.DeviceIdType.MESH
VMEM = pltpu.VMEM
WHOLE = pl.BlockSpec(memory_space=pltpu.VMEM)
HBM = pl.BlockSpec(memory_space=pl.ANY)
VMEM_LIMIT = 60 * 1024 * 1024
F32 = jnp.float32
BF16 = jnp.bfloat16

VEC0 = 0
TAP0 = 18
EMB0 = 42
OFF0 = 58
EIGHT = 8


def dot(a, b, precision=HIGH):
    return jnp.dot(a, b, precision=precision, preferred_element_type=F32)


def dot_nt(a, b, precision=HIGH):
    return lax.dot_general(
        a, b, (((1,), (1,)), ((), ())), precision=precision, preferred_element_type=F32
    )


def dot_tn(a, b, precision=HIGH):
    return lax.dot_general(
        a, b, (((0,), (0,)), ((), ())), precision=precision, preferred_element_type=F32
    )


def sds(*shape):
    return jax.ShapeDtypeStruct(shape, F32)


def cost(flops, moved):
    return pl.CostEstimate(flops=int(flops), bytes_accessed=int(moved), transcendentals=0)


def position_table(length):
    indices = np.arange(length, dtype=np.float32)
    fraction = indices / np.float32(length - 1)
    angles = np.float32(2.0 * math.pi) * indices / np.float32(length)
    bands = (EMB - 1) // 2
    frequency = np.linspace(0.0001, bands - 1, bands).astype(np.float32)
    turned = (frequency[:, None] * angles[None, :]).astype(np.float32).astype(np.float64)
    table = np.zeros((8, length), np.float32)
    table[0] = fraction
    table[1 : 1 + bands] = np.cos(turned)
    table[1 + bands : 1 + 2 * bands] = -np.sin(turned)
    table[EMB] = 1.0
    return table


def split_table(table):
    high = table.astype(np.float32).astype(jnp.bfloat16)
    low = (table.astype(np.float32) - high.astype(np.float32)).astype(jnp.bfloat16)
    return high, low


def left_table(table):
    high, low = split_table(table)
    return np.concatenate([high, high, low], axis=1)


def right_table(table):
    high, low = split_table(table)
    return np.concatenate([high, high, low], axis=0)


def fourier_tables(length):
    rows = length // LANES
    outer = 2 * rows
    total = outer * LANES
    turn = 2.0 * np.pi / outer * (np.arange(outer)[:, None] * np.arange(rows)[None, :] % outer)
    c, s = np.cos(turn), np.sin(turn)
    first = np.block([[c, s], [-s, c]])
    first_real = np.block([[c], [-s]])
    last = np.block([[c.T, -s.T], [s.T, c.T]]) / total
    last_real = np.block([[c.T, -s.T]]) / total
    twist = 2.0 * np.pi / total * (np.arange(outer)[:, None] * np.arange(LANES)[None, :])
    twiddle = np.concatenate([np.cos(twist), -np.sin(twist)], axis=1).astype(np.float32)
    lane = 2.0 * np.pi / LANES * (np.arange(LANES)[:, None] * np.arange(LANES)[None, :] % LANES)
    c, s = np.cos(lane), np.sin(lane)
    second = np.block([[c, -s], [s, c]])
    second_back = np.block([[c, s], [-s, c]])
    return (
        left_table(first),
        left_table(first_real),
        twiddle,
        right_table(second),
        right_table(second_back),
        left_table(last),
        left_table(last_real),
    )


def sin_cos(x):
    turns = jnp.round(x * (1.0 / math.pi))
    r = x - turns * 3.140625
    r = r - turns * 9.67025756835937500e-4
    r = r - turns * 6.27711415290832520e-7
    r = r - turns * 1.21542010130123850e-10
    half = turns * 0.5
    sign = 1.0 - 4.0 * jnp.abs(half - jnp.round(half))
    r2 = r * r
    s = -2.5052108385441720e-8
    for k in (2.7557319223985893e-6, -1.9841269841269841e-4, 8.3333333333333333e-3, -1.6666666666666667e-1):
        s = s * r2 + k
    s = r + r * (r2 * s)
    c = 2.0876756987868099e-9
    for k in (-2.7557319223985888e-7, 2.4801587301587302e-5, -1.3888888888888889e-3, 4.1666666666666667e-2, -0.5):
        c = c * r2 + k
    c = 1.0 + r2 * c
    return s * sign, c * sign


def window(delta, length, start, width):
    t = lax.broadcasted_iota(jnp.int32, (1, width), 1) + start
    fraction = t.astype(F32) / (length - 1)
    return jnp.exp(-delta * fraction) + WINDOW_SHIFT


def normalize(x):
    center = x - jnp.mean(x, axis=0, keepdims=True)
    spread = jnp.mean(center * center, axis=0, keepdims=True)
    scale = lax.rsqrt(spread + EPSILON)
    return center * scale, scale


def normalize_back(e, xh, scale):
    return scale * (
        e - jnp.mean(e, axis=0, keepdims=True) - xh * jnp.mean(e * xh, axis=0, keepdims=True)
    )


def gelu_parts(a):
    t = jnp.tanh(GELU_SCALE * (a + GELU_CUBE * a * a * a))
    return 0.5 * (1.0 + t), t


def put_columns(pairs, width=D):
    rows = pairs[0][1].shape[0]
    lane = lax.broadcasted_iota(jnp.int32, (rows, width), 1)
    out = jnp.zeros((rows, width), F32)
    for k, column in pairs:
        out = out + jnp.where(lane == k, column, 0.0)
    return out


def row_sum(x):
    return jnp.sum(x, axis=1, keepdims=True)


def ones_rows(width):
    return (lax.broadcasted_iota(jnp.int32, (EIGHT, width), 0) == 0).astype(F32)


def filter_block(length, start, feat, net, fourth, delta):
    width = feat.shape[1]
    kept = []
    h, c = sin_cos(FREQUENCY * dot(net[:, 0:EIGHT], feat, HIGHEST))
    kept.append((h, FREQUENCY * c))
    for row in (EMB + 1, EMB + 2 + FO):
        v = dot(net[:, row : row + FO], h, HIGHEST) + net[:, row + FO : row + FO + 1]
        h, c = sin_cos(FREQUENCY * v)
        kept.append((h, FREQUENCY * c))
    return dot(fourth, h, HIGHEST) * window(delta, length, start, width), kept


def filter_back_block(length, start, feat, net, fourth, delta, keep, dk, dnet, dfourth):
    width = feat.shape[1]
    ones = ones_rows(width)
    dkw = dk * window(delta, length, start, width)
    dfourth[:, 0:FO] += dot_nt(dkw, keep[2])
    dpre = dot_tn(fourth, dkw) * keep[5]
    row = EMB + 2 + FO
    dnet[2, :, 0 : FO + EIGHT] += dot_nt(dpre, jnp.concatenate([keep[1], ones], axis=0))
    dpre = dot_tn(net[:, row : row + FO], dpre) * keep[4]
    row = EMB + 1
    dnet[1, :, 0 : FO + EIGHT] += dot_nt(dpre, jnp.concatenate([keep[0], ones], axis=0))
    dpre = dot_tn(net[:, row : row + FO], dpre) * keep[3]
    dnet[0, :, 0:EIGHT] += dot_nt(dpre, feat)


def widened(value, width=LANES):
    rows, lanes = value.shape
    return jnp.concatenate([value, jnp.zeros((rows, width - lanes), F32)], axis=1)


def paired(tile, count):
    high = tile.astype(BF16).astype(F32)
    return (high + pltpu.roll(tile - high, count, 1)).astype(BF16)


def named_dot(table, places, repeat=2):
    rows = jnp.concatenate(places * repeat, axis=0)
    rest = LANES - rows.shape[0]
    rows = jnp.concatenate([rows, jnp.zeros((rest, rows.shape[1]), F32)], axis=0)
    return jnp.dot(table, rows.astype(BF16), preferred_element_type=F32)


def halves(x):
    high = x.astype(BF16)
    return high, (x - high.astype(F32)).astype(BF16)


def left_dot(table, x):
    high, low = halves(x)
    return jnp.dot(
        table, jnp.concatenate([high, low, high], axis=0), preferred_element_type=F32
    )


def right_dot(x, table):
    high, low = halves(x)
    return jnp.dot(
        jnp.concatenate([high, low, high], axis=1), table, preferred_element_type=F32
    )


def spectrum_of(x, first, twiddle, second):
    outer = twiddle.shape[0]
    y = left_dot(first, x)
    tr, ti = twiddle[:, :LANES], twiddle[:, LANES:]
    parts = []
    for b in range(x.shape[1] // LANES):
        yr = y[:outer, b * LANES : (b + 1) * LANES]
        yi = y[outer:, b * LANES : (b + 1) * LANES]
        parts.append(jnp.concatenate([yr * tr - yi * ti, yr * ti + yi * tr], axis=1))
    return right_dot(jnp.concatenate(parts, axis=0), second)


def signal_of(v, twiddle, second_back, last):
    outer = twiddle.shape[0]
    a = right_dot(v, second_back)
    tr, ti = twiddle[:, :LANES], twiddle[:, LANES:]
    parts = []
    for b in range(v.shape[0] // outer):
        ar = a[b * outer : (b + 1) * outer, :LANES]
        ai = a[b * outer : (b + 1) * outer, LANES:]
        parts.append(jnp.concatenate([ar * tr + ai * ti, ai * tr - ar * ti], axis=0))
    return left_dot(last, jnp.concatenate(parts, axis=1))


def load_pairs(ref):
    rows = ref.shape[1] // EIGHT
    parts = []
    for b in range(EIGHT):
        parts.append(
            jnp.concatenate([ref[s, pl.ds(b, rows, stride=EIGHT), :] for s in range(2)], axis=0)
        )
    return jnp.concatenate(parts, axis=1)


def store_pairs(ref, value):
    rows = ref.shape[1] // EIGHT
    for b in range(EIGHT):
        for s in range(2):
            ref[s, pl.ds(b, rows, stride=EIGHT), :] = value[
                s * rows : (s + 1) * rows, b * LANES : (b + 1) * LANES
            ]


def times(a, b):
    ar, ai, br, bi = a[:, :LANES], a[:, LANES:], b[:, :LANES], b[:, LANES:]
    return jnp.concatenate([ar * br - ai * bi, ar * bi + ai * br], axis=1)


def times_conj(a, b):
    ar, ai, br, bi = a[:, :LANES], a[:, LANES:], b[:, :LANES], b[:, LANES:]
    return jnp.concatenate([ar * br + ai * bi, ai * br - ar * bi], axis=1)


def send(a, b, sems, index, device):
    copy = remote(a, b, sems, index, device)
    copy.start()
    return copy


def remote(a, b, sems, index, device):
    return pltpu.make_async_remote_copy(
        src_ref=a, dst_ref=b, send_sem=sems[0].at[index], recv_sem=sems[1].at[index],
        device_id=device, device_id_type=MESH,
    )


def exchange(refs, peers, send_sem, recv_sem, base):
    return [
        send(a, b, (send_sem, recv_sem), base + k, peer)
        for k, ((a, b), peer) in enumerate(zip(refs, peers))
    ]


def greet(n, mates=()):
    me, b = lax.axis_index("chan"), lax.axis_index("batch")
    barrier = pltpu.get_barrier_semaphore()
    for d in range(1, n):
        pl.semaphore_signal(
            barrier, inc=1, device_id={"chan": lax.rem(me + d, n)}, device_id_type=MESH
        )
    for mate in mates:
        pl.semaphore_signal(barrier, inc=1, device_id={"batch": mate}, device_id_type=MESH)
    pl.semaphore_wait(barrier, n - 1 + len(mates))


def core_mate(b):
    return b + 1 - 2 * lax.rem(b, 2)


def y_mate(b):
    return b + 2 - 4 * (b // 2)


def comm_params(cid):
    return pltpu.CompilerParams(
        collective_id=cid, has_side_effects=True, vmem_limit_bytes=VMEM_LIMIT
    )


def pair_sems(*shape):
    return [pltpu.SemaphoreType.DMA(shape), pltpu.SemaphoreType.DMA(shape)]


class Blocks:
    def __init__(self, n, span, sems, own):
        self.n, self.span, self.sems, self.own = n, span, sems, own
        self.me = lax.axis_index("chan")

    def rows(self, j):
        return pl.ds(pl.multiple_of(j * self.span, 8), self.span)

    def out_refs(self, k, j, src, dst):
        return src.at[k, j], dst.at[k, :, self.rows(self.me), :]

    def back_refs(self, k, j, src, dst):
        return src.at[k, :, self.rows(j), :], dst.at[k, self.me]

    def each(self, refs, k, src, dst):
        for d in range(1, self.n):
            j = lax.rem(self.me + d, self.n)
            a, b = refs(k, j, src, dst)
            yield remote(a, b, self.sems, (k, d), {"chan": j})

    def start(self, refs, k, src, dst):
        a, b = refs(k, self.me, src, dst)
        pltpu.make_async_copy(a, b, self.own.at[k]).start()
        for copy in self.each(refs, k, src, dst):
            copy.start()

    def arrived(self, refs, k, src, dst):
        for copy in self.each(refs, k, src, dst):
            copy.wait_recv()
        a, b = refs(k, self.me, src, dst)
        pltpu.make_async_copy(a, b, self.own.at[k]).wait()

    def sent(self, refs, k, src, dst):
        for copy in self.each(refs, k, src, dst):
            copy.wait_send()


class Tiles:
    def __init__(self, n, tiles, sems, own, src, dst):
        self.n, self.tiles, self.sems, self.own = n, tiles, sems, own
        self.src, self.dst = src, dst
        self.me = lax.axis_index("chan")

    def refs(self, q, j):
        here = pl.ds(pl.multiple_of(q * EIGHT, 8), EIGHT)
        there = pl.ds(pl.multiple_of((self.me * self.tiles + q) * EIGHT, 8), EIGHT)
        return self.src.at[:, j, :, here, :], self.dst.at[:, :, there, :]

    def each(self, q):
        for d in range(1, self.n):
            j = lax.rem(self.me + d, self.n)
            yield remote(*self.refs(q, j), self.sems, (q, d), {"chan": j})

    def start(self, q):
        for copy in self.each(q):
            copy.start()
        pltpu.make_async_copy(*self.refs(q, self.me), self.own.at[q]).start()

    def arrived(self, q):
        for copy in self.each(q):
            copy.wait_recv()
        pltpu.make_async_copy(*self.refs(q, self.me), self.own.at[q]).wait()

    def sent(self, q):
        for copy in self.each(q):
            copy.wait_send()


class Names:
    def __init__(self, values):
        self.__dict__.update(values)


def loop(count, body):
    def step(i, _):
        body(i)
        return 0

    lax.fori_loop(0, count, step, 0)


def round_up(value, step):
    return -(-value // step) * step


def quarter_rows(refs_rows, k):
    quarter = refs_rows // 4
    return pl.ds(pl.multiple_of(k * quarter, 8), quarter)


def fold(value, n, chans, back=False):
    lane = lax.broadcasted_iota(jnp.int32, (chans, LANES), 1)
    wide = 4 * n * chans // LANES
    narrow = n * chans // LANES
    if back:
        tiles = [[value[c][:, t * LANES : (t + 1) * LANES] for t in range(narrow)] for c in range(4)]
        out = [None] * wide
    else:
        tiles = [value[:, t * LANES : (t + 1) * LANES] for t in range(wide)]
        out = [[None] * narrow for _ in range(4)]
    for c in range(4):
        for i in range(n):
            a, b = i * 4 * chans + c * chans, i * chans
            if back:
                source, to, at = tiles[c][b // LANES], a % LANES, b % LANES
                row, k = out, a // LANES
            else:
                source, to, at = tiles[a // LANES], b % LANES, a % LANES
                row, k = out[c], b // LANES
            shift = (to - at) % LANES
            moved = pltpu.roll(source, shift, 1) if shift else source
            inside = (lane >= to) & (lane < to + chans)
            row[k] = jnp.where(inside, moved, 0.0 if row[k] is None else row[k])
    if back:
        return jnp.concatenate(out, axis=1)
    return [jnp.concatenate(tiles, axis=1) for tiles in out]


def conv_chunk(k, g, spec, gspec, z, first, twiddle, second, second_back, last):
    outer = twiddle.shape[0]
    rows = pl.ds(pl.multiple_of(k * EIGHT * outer, 8), EIGHT * outer)
    u = spectrum_of(load_pairs(g.at[k]), first[...], twiddle[...], second[...])
    gspec[rows, :] = u
    o = signal_of(times(u, spec[rows, :]), twiddle[...], second_back[...], last[...])
    store_pairs(z.at[k], o)


def decay(me, chans):
    ids = lax.broadcasted_iota(jnp.int32, (chans, 1), 0) + me * chans
    slow = math.log(0.01) / 1.5
    fast = math.log(0.01) / 0.3
    return jnp.abs(slow + (fast - slow) * ids.astype(F32) / (D - 1))


def hops(n, b, me, sems, local):
    half = n // 2
    x, z = lax.rem(me, 2), me // 2
    side = {"chan": 2 * z + 1 - x}

    def hop_z(c, src, dst):
        keep = pltpu.make_async_copy(src, dst.at[me], local.at[c])
        keep.start()
        copies = [
            send(src, dst.at[me], sems, (c, d), {"chan": 2 * lax.rem(z + d, half) + x})
            for d in range(1, half)
        ]
        return keep, copies

    def hop_x(c, src, dst, keep, copies):
        out = [send(src, dst.at[me], sems, (c, half), side)]
        for d in range(1, half):
            j = 2 * lax.rem(z + half - d, half) + x
            copies[d - 1].wait_recv()
            out.append(send(dst.at[j], dst.at[j], sems, (c, half + d), side))
        keep.wait()
        return out

    return hop_z, hop_x


def filter_steps(r, l, b, length, groups, keep, delta):
    block = 512
    fourth = r.chan_t[l, :, 13 : 13 + FO]

    def body(i):
        start = b * (length // 4) + i * block
        out, kept = filter_block(
            length, start, r.feat[:, pl.ds(pl.multiple_of(start, block), block)],
            r.filt_t.at[l], fourth, delta,
        )
        place = pl.ds(pl.multiple_of(i * block, block), block)
        for k, (sine, cosine) in enumerate(kept):
            keep[k, :, place] = sine
            keep[3 + k, :, place] = cosine
        for q in range(block // LANES):
            rows = pl.ds(pl.multiple_of((start // LANES + q) * EIGHT, 8), EIGHT)
            for k in range(groups):
                r.kern[l, k, rows, :] = out[
                    k * EIGHT : (k + 1) * EIGHT, q * LANES : (q + 1) * LANES
                ]

    loop(length // 4 // block, body)


def name_rows(tokx, s, lanes):
    width = tokx.shape[2] if lanes is None else LANES
    names = lax.broadcasted_iota(jnp.int32, (VOCAB, width), 0).astype(F32)
    rows = [tokx[s, k : k + 1, :] if lanes is None else tokx[s, k : k + 1, lanes] for k in range(3)]
    here, one, two = [(names == row).astype(F32) for row in rows]
    return [two, one, here]


def name_tables(shared, misc, j):
    lane = lax.broadcasted_iota(jnp.int32, (D, LANES), 1)
    rows = pltpu.roll(shared, LANES - j * VOCAB, 1) if j else shared
    rows = jnp.where(lane < VOCAB, rows, 0.0)
    t = TAP0 + 3 * j
    mix = (
        misc[:, t : t + 1] * rows
        + misc[:, t + 1 : t + 2] * pltpu.roll(rows, VOCAB, 1)
        + misc[:, t + 2 : t + 3] * pltpu.roll(rows, 2 * VOCAB, 1)
    )
    return paired(rows, VOCAB), paired(mix, 3 * VOCAB)


def prepare_kernel(
    n, length, chans, ids, embedding, inward, vectors, outward, expand, offsets, contract,
    chan_t, filt_t, feat, first, first_real, twiddle, second, second_back, last, last_real,
    wall, late, spec0, spec1, gspec, keep0, keep1, zpos, misc, toks, tokx, shared, owned,
    upper, side, town, rows, flip, kern, gch, zch, spec0v, spec1v, gspecv, keep0v, keep1v,
    osem, ss, sr, ws, wr, ks, kr, zs, zr, local, zown,
):
    r = Names(locals())
    me, b = lax.axis_index("chan"), lax.axis_index("batch")
    groups = chans // EIGHT
    seqs, span = r.zpos.shape[2], r.zpos.shape[3]
    width = span // EIGHT * LANES
    parts = width // D
    tabs = (r.first, r.twiddle, r.second, r.second_back, r.last)
    flip, side, town = r.flip, r.side, r.town
    flip[...] = jnp.zeros_like(flip)
    for k in range(9):
        for l in range(LAYERS):
            row = VEC0 + 9 * l + k
            flip[row : row + 1, 0:chans] = r.vectors[k, l : l + 1, :]
    flip[EMB0 : EMB0 + VOCAB, 0:chans] = r.embedding[...]
    for l in range(LAYERS):
        for c in range(4):
            row = OFF0 + 4 * l + c
            flip[row : row + 1, 0:chans] = r.offsets[l : l + 1, c * chans : (c + 1) * chans]
    columns = flip[...].T[:chans, :]
    lane = lax.broadcasted_iota(jnp.int32, (chans, LANES), 1)
    for l in range(LAYERS):
        taps = jnp.where(lane < 12, widened(r.chan_t[l]), 0.0)
        columns = columns + pltpu.roll(taps, TAP0 + 12 * l, 1)
    side[:, 0:LANES] = columns
    side[:, LANES:] = jnp.zeros((chans, LANES), F32)
    town[...] = jnp.zeros_like(town)
    for s in range(seqs):
        for h in range(parts):
            town[s * parts + h : s * parts + h + 1, :] = r.ids[
                s : s + 1, h * D : (h + 1) * D
            ].astype(F32)
    for l, rear, front in ((0, r.owned, r.upper), (1, r.upper, r.owned)):
        for j in range(3):
            front[(9 + j) * chans : (10 + j) * chans, :] = r.inward[l, j]
        rear[0:chans, :] = r.outward[l]
        rear[chans : 5 * chans, :] = r.expand[l]
        for c, piece in enumerate(fold(r.contract[l], n, chans)):
            rear[(5 + c) * chans : (6 + c) * chans, :] = piece
    greet(n, (core_mate(b), y_mate(b)))
    mine = pl.ds(pl.multiple_of(me * chans, 8), chans)
    small = []
    for d in range(1, n):
        peer = {"chan": lax.rem(me + d, n)}
        small.append(send(side, r.misc.at[mine, :], (r.ss, r.sr), d, peer))
        small.append(send(town, r.toks.at[me], (r.ss, r.sr), n + d, peer))
    r.misc[mine, :] = side[...]
    r.toks[me] = town[...]
    weights = (r.ws, r.wr)
    hop_z, hop_x = hops(n, b, me, weights, r.local)
    count = r.wall.shape[1] // 2
    core = lax.rem(b, 2)

    def part(c, k):
        size = count // (2 if c else 4)
        return pl.ds(pl.multiple_of(c * count + k * size, 8), size)

    low = [(r.owned.at[part(c, k)], r.wall.at[:, part(c, k)]) for c, k in ((0, b), (1, core))]
    z_w = [hop_z(0, *low[0]), None]
    x_w, y_w, core_w = [None] * 2, [], []
    saves = []

    def save(src, dst):
        copy = pltpu.make_async_copy(src, dst, r.osem.at[len(saves)])
        copy.start()
        saves.append(copy)

    save(r.upper, r.late)

    def hop_y():
        for copy in x_w[0]:
            copy.wait_recv()
        here = r.wall.at[:, part(0, b)]
        y_w.append(send(here, here, weights, (0, n), {"batch": y_mate(b)}))
        core_w.append(send(here, here, weights, (0, n + 1), {"batch": core_mate(b)}))

    def hop_core():
        for copy in x_w[1]:
            copy.wait_recv()
        here = r.wall.at[:, part(1, core)]
        core_w.append(send(here, here, weights, (1, n), {"batch": core_mate(b)}))
        y_w[0].wait_recv()
        here = r.wall.at[:, part(0, y_mate(b))]
        core_w.append(send(here, here, weights, (0, n + 2), {"batch": core_mate(b)}))

    delta = decay(me, chans)
    count_lag = r.kern.shape[2] // 4
    lags = [pl.ds(pl.multiple_of(k * count_lag, 8), count_lag) for k in (b, y_mate(b))]

    def offer(l):
        place = r.kern.at[l, :, lags[0], :]
        return send(place, place, (r.ks, r.kr), (l, 0), {"batch": y_mate(b)})

    def share(l, copy):
        copy.wait_recv()
        return [
            send(
                r.kern.at[l, :, k, :], r.kern.at[l, :, k, :], (r.ks, r.kr), (l, 1 + i),
                {"batch": core_mate(b)},
            )
            for i, k in enumerate(lags)
        ]

    def spectra(l, copies, spec):
        for copy in copies:
            copy.wait_recv()
        outer = r.twiddle.shape[0]
        rows = length // LANES

        def body(k):
            taps = jnp.concatenate(
                [r.kern[l, k, pl.ds(c, rows, stride=EIGHT), :] for c in range(EIGHT)], axis=1
            )
            u = spectrum_of(taps, r.first_real[...], r.twiddle[...], r.second[...])
            here = pl.ds(pl.multiple_of(k * EIGHT, 8), EIGHT)
            gain = jnp.broadcast_to(r.chan_t[l, here, 12:13], (EIGHT, LANES))
            for c in range(EIGHT):
                wide = jnp.broadcast_to(gain[c : c + 1, :], (outer, LANES))
                both = jnp.concatenate([wide, jnp.zeros_like(wide)], axis=1)
                place = pl.ds(pl.multiple_of((k * EIGHT + c) * outer, 8), outer)
                spec[place, :] = u[c * outer : (c + 1) * outer] + both

        loop(groups, body)

    filter_steps(r, 0, b, length, groups, r.keep0v, delta)
    y_k0 = offer(0)
    save(r.keep0v, r.keep0)
    for copy in small:
        copy.wait()
    table = r.misc[...]
    xh, _ = normalize(table)
    normed = xh * table[:, VEC0 : VEC0 + 1] + table[:, VEC0 + 1 : VEC0 + 2]
    own = side[...]
    shared = jnp.zeros((chans, LANES), F32)
    mixes, biases = [], []
    for j in range(3):
        rows = dot(r.inward[0, j], normed, HIGHEST)
        rows = rows + own[:, VEC0 + 4 + j : VEC0 + 5 + j]
        rows = pltpu.roll(rows, D - EMB0, 1)[:, :LANES]
        rows = jnp.where(lane < VOCAB, rows, 0.0)
        shared = shared + (pltpu.roll(rows, j * VOCAB, 1) if j else rows)
        if j:
            k = TAP0 + 3 * j
            mixes.append(
                own[:, k : k + 1] * rows
                + own[:, k + 1 : k + 2] * pltpu.roll(rows, VOCAB, 1)
                + own[:, k + 2 : k + 3] * pltpu.roll(rows, 2 * VOCAB, 1)
            )
            biases.append(own[:, TAP0 + 9 + j : TAP0 + 10 + j])
    r.rows[...] = shared
    r.shared[mine, :] = shared
    for d in range(1, n):
        peer = {"chan": lax.rem(me + d, n)}
        small.append(send(r.rows, r.shared.at[mine, :], (r.ss, r.sr), 2 * n + d, peer))
    mix = paired(jnp.concatenate(mixes, axis=0), 3 * VOCAB)
    names = lax.broadcasted_iota(jnp.int32, (VOCAB, width), 0).astype(F32)
    toks = r.toks

    def shifted(i, s):
        here = jnp.concatenate(
            [toks[i, s * parts + h : s * parts + h + 1, :] for h in range(parts)], axis=1
        )
        before = toks[jnp.maximum(i - 1, 0), (s + 1) * parts - 1 : (s + 1) * parts, D - LANES :]
        long = jnp.concatenate([jnp.where(i > 0, before, -1.0), here], axis=1)
        return here, pltpu.roll(long, 1, 1)[:, LANES:], pltpu.roll(long, 2, 1)[:, LANES:]

    for s in range(seqs):
        for k, row in enumerate(shifted(me, s)):
            r.tokx[s, k : k + 1, :] = row

    def gates(i):
        for s in range(seqs):
            here, one, two = shifted(i, s)
            out = named_dot(mix, [(names == row).astype(F32) for row in (two, one, here)])
            gate = (out[:chans] + biases[0]) * (out[chans:] + biases[1])
            for q in range(width // LANES):
                rows = pl.ds(pl.multiple_of(i * span + q * EIGHT, 8), EIGHT)
                for k in range(groups):
                    r.gch[k, s, rows, :] = gate[
                        k * EIGHT : (k + 1) * EIGHT, q * LANES : (q + 1) * LANES
                    ]

    loop(n // 2, gates)
    core_k0 = share(0, y_k0)
    x_w[0] = hop_x(0, *low[0], *z_w[0])
    z_w[1] = hop_z(1, *low[1])
    loop(n // 2, lambda i: gates(i + n // 2))
    spectra(0, core_k0, r.spec0v)
    hop_y()
    save(r.spec0v, r.spec0)
    back = Blocks(n, span, (r.zs, r.zr), r.zown)

    def chunk(k):
        conv_chunk(
            k, r.gch, r.spec0v, r.gspecv, r.zch, *tabs
        )
        back.start(back.back_refs, k, r.zch, r.zpos)

    early = max(groups // 2, 1)
    loop(early, chunk)
    x_w[1] = hop_x(1, *low[1], *z_w[1])
    loop(groups - early, lambda k: chunk(k + early))
    save(r.gspecv, r.gspec)
    filter_steps(r, 1, b, length, groups, r.keep1v, delta)
    y_k1 = offer(1)
    save(r.keep1v, r.keep1)
    hop_core()
    core_k1 = share(1, y_k1)
    spectra(1, core_k1, r.spec1v)
    save(r.spec1v, r.spec1)

    def finish(k):
        back.arrived(back.back_refs, k, r.zch, r.zpos)
        back.sent(back.back_refs, k, r.zch, r.zpos)

    loop(groups, finish)
    for _, copies in z_w:
        for copy in copies:
            copy.wait_send()
    for copy in saves:
        copy.wait()
    for copy in x_w[0] + x_w[1] + y_w + [y_k0, y_k1] + core_k0 + core_k1:
        copy.wait_send()
    for copy in core_w + small[2 * (n - 1) :]:
        copy.wait()


def prepare(arrays, tables, n, seqs, length, cid):
    chan_t = arrays[8]
    chans = chan_t.shape[1]
    groups = chans // EIGHT
    rows = length // LANES
    span = rows // n * EIGHT
    outer = 2 * rows
    width = length // n
    spec = sds(chans * outer, 2 * LANES)
    keep = sds(6, FO, length // 4)
    low, high = round_up(12 * chans, 64), round_up(12 * chans, 32)
    return pl.pallas_call(
        partial(prepare_kernel, n, length, chans),
        in_specs=[WHOLE] * 18,
        out_specs=[HBM] * 8 + [WHOLE] * 4,
        out_shape=[
            sds(n, low, D), sds(high, D),
            spec, spec, spec, keep, keep, sds(groups, n, seqs, span, LANES),
            sds(D, D), sds(n, EIGHT, D), sds(seqs, EIGHT, width), sds(D, LANES),
        ],
        scratch_shapes=[
            VMEM((low, D), F32),
            VMEM((high, D), F32),
            VMEM((chans, D), F32),
            VMEM((EIGHT, D), F32),
            VMEM((chans, LANES), F32),
            VMEM((LANES, LANES), F32),
            VMEM((LAYERS, groups, rows * EIGHT, LANES), F32),
            VMEM((groups, seqs, rows * EIGHT, LANES), F32),
            VMEM((groups, seqs, rows * EIGHT, LANES), F32),
            *[VMEM(spec.shape, F32)] * 3,
            *[VMEM(keep.shape, F32)] * 2,
            pltpu.SemaphoreType.DMA((6,)),
            *pair_sems(3 * n),
            *pair_sems(2, n + 3),
            *pair_sems(LAYERS, 3),
            *pair_sems(groups, n),
            pltpu.SemaphoreType.DMA((2,)),
            pltpu.SemaphoreType.DMA((groups,)),
        ],
        compiler_params=comm_params(cid),
        name="prepare",
    )(*arrays, position_table(length), *tables)


def middle_kernel(
    n, chans, z, wall, late, spec, misc, shared, tokx, first, first_real, twiddle, second,
    second_back, last, last_real, wlate, h, a, x1, p, q, gspec, zpos, zv, wv, hv, av, x1v,
    pv, qv, table, gpos, gch, zch, tails, halo, gspecv, gs, gr, gown, zs, zr, zown, hs, hr,
    ws, wr, wown, lsem,
):
    r = Names(locals())
    me, b = lax.axis_index("chan"), lax.axis_index("batch")
    seqs, width = r.x1v.shape[0], r.x1v.shape[2]
    groups, tiles = chans // EIGHT, width // LANES
    lane0 = TAP0 + 12
    loads = [
        pltpu.make_async_copy(r.z, r.zv, r.lsem.at[0]),
        pltpu.make_async_copy(r.wall.at[:, 0 : r.wv.shape[1]], r.wv, r.lsem.at[1]),
    ]
    for copy in loads:
        copy.start()
    r.table[...] = name_tables(r.shared[...], r.misc[...], 0)[1]
    greet(n, (core_mate(b), y_mate(b)))
    weights = (r.ws, r.wr)
    hop_z, hop_x = hops(n, b, me, weights, r.wown)
    mine = quarter_rows(r.wlate.shape[1], b)
    other = quarter_rows(r.wlate.shape[1], y_mate(b))
    late = (r.late.at[mine], r.wlate.at[:, mine])
    z_w = hop_z(0, *late)
    out = Tiles(n, tiles, (r.gs, r.gr), r.gown, r.gpos, r.gch)
    back = Blocks(n, tiles * EIGHT, (r.zs, r.zr), r.zown)
    for copy in loads:
        copy.wait()
    low = Layer(None, r.wv, r.misc, 0)
    high = Layer(r.wv.at[:, 9 * chans :], None, r.misc, 1)
    edge_lane = lax.broadcasted_iota(jnp.int32, (D, LANES), 1)
    inner = (me > 0).astype(F32)
    halo_copy = remote(r.tails, r.halo, (r.hs, r.hr), 0, {"chan": lax.rem(me + 1, n)})

    def tile(q):
        places = places_of(r.tokx, q)
        x = embedded(low.side, places[2])
        first_gate = named_dot(r.table[...], places) + low.column(TAP0 + 9)
        mixed = rear_mix(low, x, take_blocks(r.zv, q) * first_gate)
        put(r.hv, q, mixed)
        _, _, _, pre = rear_hidden(low, mixed)
        u = []
        for k in range(4):
            put(r.av.at[:, k], q, pre[k])
            u.append(pre[k] * gelu_parts(pre[k])[0])
        x = rear_out(low, mixed, u)
        put(r.x1v, q, x)
        for j, value in enumerate(front_forward(high, x)):
            put(r.pv.at[j], q, value)

    def gates(q):
        here = pl.ds(pl.multiple_of(q * LANES, LANES), LANES)
        prior = pl.ds(pl.multiple_of(jnp.maximum(q - 1, 0) * LANES, LANES), LANES)
        made = []
        for j in range(3):
            t = lane0 + 3 * j
            row = []
            for s in range(seqs):
                edge = pltpu.roll(r.halo[...], LANES - 2 - 2 * (j * seqs + s), 1) * inner
                before = jnp.where(q > 0, r.pv[j, s, :, prior], edge)
                now = r.pv[j, s, :, here]
                long = jnp.concatenate([before, now], axis=1)
                one = pltpu.roll(long, 1, 1)[:, LANES:]
                two = pltpu.roll(long, 2, 1)[:, LANES:]
                value = (
                    r.misc[:, lane0 + 9 + j : lane0 + 10 + j]
                    + r.misc[:, t : t + 1] * two
                    + r.misc[:, t + 1 : t + 2] * one
                    + r.misc[:, t + 2 : t + 3] * now
                )
                r.qv[j, s, :, here] = value
                row.append(value)
            made.append(row)
        gate = [made[2][s] * made[1][s] for s in range(seqs)]
        put_blocks(r.gpos, q, jnp.concatenate(gate, axis=1))
        out.start(q)

    def step(i):
        q = lax.rem(i + tiles - 1, tiles)
        tile(q)

        @pl.when(i == 0)
        def _():
            pack = jnp.zeros((D, LANES), F32)
            for j in range(3):
                for s in range(seqs):
                    slot = 2 * (j * seqs + s)
                    tail = pltpu.roll(r.pv[j, s, :, width - LANES :], slot + 2, 1)
                    pack = jnp.where((edge_lane == slot) | (edge_lane == slot + 1), tail, pack)
            r.tails[...] = pack
            halo_copy.start()

        @pl.when(i == 1)
        def _():
            halo_copy.wait_recv()

        @pl.when(i > 0)
        def _():
            gates(q)

    loop(tiles - 1, step)
    x_w = hop_x(0, *late, *z_w)
    step(tiles - 1)
    gates(tiles - 1)
    saves = [
        pltpu.make_async_copy(src, dst, r.lsem.at[3 + i])
        for i, (src, dst) in enumerate(
            ((r.hv, r.h), (r.av, r.a), (r.x1v, r.x1), (r.pv, r.p), (r.qv, r.q))
        )
    ]
    for copy in saves:
        copy.start()
    loop(tiles, out.arrived)

    def chunk(k):
        conv_chunk(
            k, r.gch, r.spec, r.gspecv, r.zch, r.first, r.twiddle, r.second, r.second_back, r.last
        )
        back.start(back.back_refs, k, r.zch, r.zpos)

    chunk(0)
    for copy in x_w:
        copy.wait_recv()
    here, there = r.wlate.at[:, mine], r.wlate.at[:, other]
    y_w = send(here, here, weights, (0, n), {"batch": y_mate(b)})
    core_w = [send(here, here, weights, (0, n + 1), {"batch": core_mate(b)})]
    loop(groups - 1, lambda k: chunk(k + 1))
    saves.append(pltpu.make_async_copy(r.gspecv, r.gspec, r.lsem.at[2]))
    saves[-1].start()
    loop(tiles, out.sent)
    loop(groups - 1, lambda k: back.arrived(back.back_refs, k, r.zch, r.zpos))
    y_w.wait_recv()
    core_w.append(send(there, there, weights, (0, n + 2), {"batch": core_mate(b)}))
    back.arrived(back.back_refs, groups - 1, r.zch, r.zpos)

    loop(groups, lambda k: back.sent(back.back_refs, k, r.zch, r.zpos))
    for copy in saves:
        copy.wait()
    halo_copy.wait_send()
    for copy in z_w[1] + x_w + [y_w]:
        copy.wait_send()
    for copy in core_w:
        copy.wait()


def middle(z, wall, late, spec, misc, shared, tokx, tables, n, chans, cid):
    groups, _, seqs, span, _ = z.shape
    width = span // EIGHT * LANES
    tiles = width // LANES
    by_channel = (groups, seqs, n * span, LANES)
    pos = (seqs, D, width)
    return pl.pallas_call(
        partial(middle_kernel, n, chans),
        in_specs=[HBM] * 3 + [WHOLE] * 11,
        out_specs=[HBM] * 8,
        out_shape=[
            sds(n, *late.shape), sds(*pos), sds(seqs, 4, D, width), sds(*pos),
            sds(3, *pos), sds(3, *pos), sds(*spec.shape), sds(*z.shape),
        ],
        scratch_shapes=[
            VMEM(z.shape, F32),
            VMEM((n, 12 * chans, D), F32),
            VMEM(pos, F32),
            VMEM((seqs, 4, D, width), F32),
            VMEM(pos, F32),
            VMEM((3,) + pos, F32),
            VMEM((3,) + pos, F32),
            VMEM((D, LANES), BF16),
            VMEM(z.shape, F32),
            VMEM(by_channel, F32),
            VMEM(by_channel, F32),
            VMEM((D, LANES), F32),
            VMEM((D, LANES), F32),
            VMEM(spec.shape, F32),
            *pair_sems(tiles, n),
            pltpu.SemaphoreType.DMA((tiles,)),
            *pair_sems(groups, n),
            pltpu.SemaphoreType.DMA((groups,)),
            *pair_sems(1),
            *pair_sems(1, n + 3),
            pltpu.SemaphoreType.DMA((1,)),
            pltpu.SemaphoreType.DMA((8,)),
        ],
        compiler_params=comm_params(cid),
        name="middle",
    )(z, wall, late, spec, misc, shared, tokx, *tables)


class GroupSum:
    def __init__(self, n, g, out, r0, sum0, ra, sa, ta, rb, sb, tb, send_sem, recv_sem):
        self.n, self.g, self.out = n, g, out
        self.r0, self.sum0 = r0, sum0
        self.a, self.b_side = (ra, sa, ta), (rb, sb, tb)
        self.sems = (send_sem, recv_sem)
        me, b = lax.axis_index("chan"), lax.axis_index("batch")
        self.x, self.z = lax.rem(me, 2), me // 2
        self.core, self.y = lax.rem(b, 2), b // 2
        self.b = b
        self.quarter = g.shape[1] // 4
        self.cut = first_rows(self.quarter)
        self.to_y = {"batch": y_mate(b)}
        self.to_x = {"chan": 2 * self.z + 1 - self.x}
        self.copies = []

    def start(self, source, landing, device):
        self.copies.append(send(source, landing, self.sems, len(self.copies), device))

    def part(self, k):
        return quarter_rows(self.g.shape[1], k)

    def cores(self):
        mate = {"batch": core_mate(self.b)}
        for k in range(2):
            self.start(self.g.at[:, self.part(2 * k + 1 - self.core)], self.r0.at[k], mate)

    def first(self):
        for k in range(2):
            self.copies[k].wait_recv()

            def add(i, k=k):
                mine = self.g[i, self.part(2 * k + self.core), :]
                self.sum0[k, lax.rem(i, 2), i // 2] = mine + self.r0[k, i]

            loop(self.n, add)
        cut = self.cut
        self.start(self.sum0.at[1 - self.y, :, :, 0:cut], self.a[0], self.to_y)
        if cut < self.quarter:
            self.start(
                self.sum0.at[:, 1 - self.x, :, cut : self.quarter], self.b_side[0], self.to_x
            )

    def second(self):
        cut = self.cut
        landing, sums, last = self.a
        self.copies[2].wait_recv()

        def add_a(i):
            for k in range(2):
                sums[k, i] = self.sum0[self.y, k, i, 0:cut, :] + landing[k, i]

        loop(self.n // 2, add_a)
        self.start(sums.at[1 - self.x], last, self.to_x)
        if cut < self.quarter:
            landing_b, sums_b, last_b = self.b_side
            self.copies[3].wait_recv()

            def add_b(i):
                for k in range(2):
                    mine = self.sum0[k, self.x, i, cut : self.quarter, :]
                    sums_b[k, i] = mine + landing_b[k, i]

            loop(self.n // 2, add_b)
            self.start(sums_b.at[1 - self.y], last_b, self.to_y)

    def close(self):
        cut = self.cut
        split = cut < self.quarter
        self.copies[4 if split else 3].wait_recv()

        def add_a(i):
            self.out[i, 0:cut, :] = self.a[1][self.x, i] + self.a[2][i]

        loop(self.n // 2, add_a)
        if split:
            self.copies[5].wait_recv()

            def add_b(i):
                self.out[i, cut : self.quarter, :] = self.b_side[1][self.y, i] + self.b_side[2][i]

            loop(self.n // 2, add_b)
        for copy in self.copies:
            copy.wait_send()


def first_rows(quarter):
    return quarter if quarter < 16 else round_up(quarter // 2, 8)


class ColumnSum:
    def __init__(self, n, source, landing, rows, zs, zr, bs, br):
        self.source, self.landing, self.rows = source, landing, rows
        self.zsems, self.bsems = (zs, zr), (bs, br)
        self.half = n // 2
        me, self.b = lax.axis_index("chan"), lax.axis_index("batch")
        self.x, self.z = lax.rem(me, 2), me // 2

    def column(self):
        for d in range(1, self.half):
            to = lax.rem(self.z + d, self.half)
            yield remote(
                self.source.at[to], self.landing.at[d - 1], self.zsems, d - 1,
                {"chan": 2 * to + self.x},
            )

    def quarter(self, k):
        return self.rows.at[quarter_rows(self.rows.shape[0], k)]

    def hop(self, k):
        mine, other = self.quarter(self.b), self.quarter(y_mate(self.b))
        ref, to = ((mine, y_mate), (mine, core_mate), (other, core_mate))[k]
        return remote(ref, ref, self.bsems, k, {"batch": to(self.b)})

    def start(self):
        for copy in self.column():
            copy.start()

    def share(self):
        total = self.source[self.z]
        for d, copy in enumerate(self.column()):
            copy.wait_recv()
            total = total + self.landing[d]
        self.rows[quarter_rows(self.rows.shape[0], self.b), :] = total
        self.hop(0).start()
        self.hop(1).start()

    def pass_on(self):
        self.hop(0).wait_recv()
        self.hop(2).start()

    def arrived(self):
        self.hop(1).wait_recv()
        self.hop(2).wait_recv()

    def sent(self):
        for copy in self.column():
            copy.wait_send()
        for k in range(3):
            self.hop(k).wait_send()


def column_scratch(n, quarter):
    return [
        VMEM((n // 2 - 1, quarter, D), F32),
        *pair_sems(n // 2 - 1),
        *pair_sems(3),
    ]


def group_scratch(n, rows):
    quarter, half = rows // 4, n // 2
    cut = first_rows(quarter)
    rest = max(quarter - cut, 8)
    return [
        VMEM((2, n, quarter, D), F32),
        VMEM((2, 2, half, quarter, D), F32),
        VMEM((2, half, cut, D), F32),
        VMEM((2, half, cut, D), F32),
        VMEM((half, cut, D), F32),
        VMEM((2, half, rest, D), F32),
        VMEM((2, half, rest, D), F32),
        VMEM((half, rest, D), F32),
        *pair_sems(6),
    ]


def take(ref, q):
    lanes = pl.ds(pl.multiple_of(q * LANES, LANES), LANES)
    return jnp.concatenate([ref[s, :, lanes] for s in range(ref.shape[0])], axis=1)


def put(ref, q, value):
    lanes = pl.ds(pl.multiple_of(q * LANES, LANES), LANES)
    for s in range(ref.shape[0]):
        ref[s, :, lanes] = value[:, s * LANES : (s + 1) * LANES]


def take_blocks(ref, q):
    groups, n, seqs, _, _ = ref.shape
    here = pl.ds(pl.multiple_of(q * EIGHT, 8), EIGHT)
    return jnp.concatenate(
        [
            jnp.concatenate(
                [ref[k, j, s, here, :] for j in range(n) for k in range(groups)], axis=0
            )
            for s in range(seqs)
        ],
        axis=1,
    )


def put_blocks(ref, q, value):
    groups, n, seqs, _, _ = ref.shape
    here = pl.ds(pl.multiple_of(q * EIGHT, 8), EIGHT)
    for s in range(seqs):
        for j in range(n):
            for k in range(groups):
                row = (j * groups + k) * EIGHT
                ref[k, j, s, here, :] = value[row : row + EIGHT, s * LANES : (s + 1) * LANES]


def places_of(tokx, q):
    lanes = pl.ds(pl.multiple_of(q * LANES, LANES), LANES)
    rows = [name_rows(tokx, s, lanes) for s in range(tokx.shape[0])]
    return [jnp.concatenate([row[k] for row in rows], axis=1) for k in range(3)]


def embedded(side, places):
    lane = lax.broadcasted_iota(jnp.int32, (D, LANES), 1)
    table = jnp.where(lane < VOCAB, pltpu.roll(side, D - EMB0, 1)[:, :LANES], 0.0)
    high = table.astype(BF16).astype(F32)
    middle = (table - high).astype(BF16).astype(F32)
    low = table - high - middle
    three = high + pltpu.roll(middle, VOCAB, 1) + pltpu.roll(low, 2 * VOCAB, 1)
    return named_dot(three.astype(BF16), [places] * 3, 1)


def top_tile(r, q):
    lay = Layer(None, r.wv, r.misc, 1)
    zt, qt = take_blocks(r.zv, q), take(r.qv.at[0], q)
    y = zt * qt
    h = rear_mix(lay, take(r.x1v, q), y)
    _, _, _, pre = rear_hidden(lay, h)
    put(r.x2v, q, rear_out(lay, h, [v * gelu_parts(v)[0] for v in pre]))
    dh, dy, columns = rear_backward(lay, h, pre, y, take(r.cotv, q), r.dw)
    put_blocks(r.dzpos, q, dy * qt)
    put(r.dq0v, q, dy * zt)
    put(r.dhout, q, dh)
    r.cols[...] += put_columns(columns)


def mid_tile(r, q):
    upper = Layer(r.wv.at[:, 9 * (D // r.wv.shape[0]) :], None, r.misc, 1)
    dout, columns = front_backward(
        upper, take(r.x1v, q), [take(r.pv.at[j], q) for j in range(3)], take(r.dh1v, q), r.dw
    )
    lay = Layer(None, r.wv, r.misc, 0)
    zt = take_blocks(r.zv, q)
    qt = named_dot(r.qtab[0], places_of(r.tokx, q)) + lay.column(TAP0 + 9)
    dh, dy, more = rear_backward(
        lay, take(r.hv, q), [take(r.av.at[:, k], q) for k in range(4)], zt * qt, dout, r.dw, 3
    )
    put_blocks(r.dzpos, q, dy * qt)
    put(r.dq0v, q, dy * zt)
    put(r.dhout, q, dh)
    r.cols[...] += put_columns(columns + more)


def top_kernel(
    n, chans, length, z, keep, spec, gspec, x1, w, misc, chan_t, filt_t, feat, q, p, cot,
    first, first_real, twiddle, second, second_back, last, last_real, dp, dh_out, cols,
    dnet, dchan, summed, x2, dpv, dhout, qv, pv, zv, keepv, specv, gspecv, x1v, wv, dw, dq0v, dzpos,
    dzch, dzspec, dgch, dgpos, dk, dkin, dnets, heads, halo, gs, gr, gown, zs, zr, zown, hs,
    hr, ks, kr, lsem, ssem, dsem, ksem, tsem, r0, sum0, ra, sa, ta, rb, sb, tb, ts, tr, cotv, x2v,
):
    back_body(Names(locals()), n, chans, 1, length)


def mid_kernel(
    n, chans, length, z, keep, spec, gspec, x1, w, misc, chan_t, filt_t, feat, shared, tokx,
    part1, dp1, dh1, h, a, first, first_real, twiddle, second, second_back, last, last_real, dp,
    dh_out, cols, dnet, dchan, summed, rows1, dpv, dhout, qv, pv, zv, keepv, specv, gspecv, x1v, wv, dw, dq0v,
    dzpos, dzch, dzspec, dgch, dgpos, dk, dkin, dnets, heads, halo, gs, gr, gown, zs, zr,
    zown, hs, hr, ks, kr, lsem, ssem, dsem, ksem, tsem, r0, sum0, ra, sa, ta, rb, sb, tb, ts, tr, dh1v, hv, av,
    ptab, qtab, in1, c1s, c1r, b1s, b1r,
):
    back_body(Names(locals()), n, chans, 0, length)


def back_body(r, n, chans, layer, length):
    top = layer == LAYERS - 1
    me, b = lax.axis_index("chan"), lax.axis_index("batch")
    seqs, width = r.x1v.shape[0], r.x1v.shape[2]
    groups, tiles = chans // EIGHT, width // LANES
    rows_all, outer = length // LANES, r.twiddle.shape[0]
    lane0 = TAP0 + 12 * layer
    span = tiles * EIGHT

    def fetch(index, src, dst):
        return pltpu.make_async_copy(src, dst, r.lsem.at[index])

    early = [fetch(0, r.w.at[:, 0 : r.wv.shape[1]], r.wv), fetch(1, r.z, r.zv)]
    for copy in early:
        copy.start()
    if top:
        tiled = [(r.x1, r.x1v), (r.cot, r.cotv), (r.q.at[0], r.qv.at[0])]
    else:
        tiled = [(r.x1, r.x1v), (r.dp1, r.pv), (r.dh1, r.dh1v), (r.h, r.hv), (r.a, r.av)]

    def tile_loads(q):
        lanes = pl.ds(pl.multiple_of(q * LANES, LANES), LANES)
        for i, (src, dst) in enumerate(tiled):
            index = (slice(None),) * (len(src.shape) - 1) + (lanes,)
            yield pltpu.make_async_copy(src.at[index], dst.at[index], r.tsem.at[i, q])

    def start_tile(q):
        for copy in tile_loads(q):
            copy.start()

    start_tile(0)
    late = [fetch(8, r.spec, r.specv), fetch(9, r.gspec, r.gspecv)]
    block = 512

    def kept(i):
        place = pl.ds(pl.multiple_of(i * block, block), block)
        slot = lax.rem(i, 2)
        return pltpu.make_async_copy(r.keep.at[:, :, place], r.keepv.at[slot], r.ksem.at[slot])

    greet(n, [lax.rem(b + d, 4) for d in range(1, 4)])
    r.dw[...] = jnp.zeros_like(r.dw)
    r.cols[...] = jnp.zeros_like(r.cols)
    if top:
        late.append(fetch(2, r.q.at[pl.ds(1, 2)], r.qv.at[pl.ds(1, 2)]))
        late.append(fetch(3, r.p, r.pv))
    else:
        upper = ColumnSum(n, r.part1, r.in1, r.rows1, r.c1s, r.c1r, r.b1s, r.b1r)
        upper.start()
        for j in range(3):
            r.ptab[j], r.qtab[j] = name_tables(r.shared[...], r.misc[...], j)
    out = Tiles(n, tiles, (r.gs, r.gr), r.gown, r.dzpos, r.dzch)
    back = Blocks(n, span, (r.zs, r.zr), r.zown)
    for copy in early:
        copy.wait()

    def tile(q):
        for copy in tile_loads(q):
            copy.wait()

        @pl.when(q + 1 < tiles)
        def _():
            start_tile(q + 1)

        @pl.when(q == min(1, tiles - 1))
        def _():
            for copy in late:
                copy.start()
            for i in range(2):
                kept(i).start()

        (top_tile if top else mid_tile)(r, q)
        out.start(q)

    loop(tiles, tile)
    saves = [pltpu.make_async_copy(r.dhout, r.dh_out, r.ssem.at[0])]
    if top:
        saves.append(pltpu.make_async_copy(r.x2v, r.x2, r.ssem.at[1]))
    for copy in saves:
        copy.start()

    def dp_save(k):
        place = pl.ds(pl.multiple_of(k * EIGHT, 8), EIGHT)
        return pltpu.make_async_copy(
            r.dpv.at[:, :, :, place, :], r.dp.at[:, :, :, place, :], r.dsem.at[k]
        )

    total = GroupSum(
        n, r.dw, r.summed, r.r0, r.sum0, r.ra, r.sa, r.ta, r.rb, r.sb, r.tb, r.ts, r.tr
    )
    total.cores()
    if not top:
        upper.share()

    for copy in late[:2]:
        copy.wait()
    total.first()
    loop(tiles, out.arrived)
    dgch, dgpos, dk = r.dgch, r.dgpos, r.dk

    def chunk(k):
        rows = pl.ds(pl.multiple_of(k * EIGHT * outer, 8), EIGHT * outer)
        u = spectrum_of(load_pairs(r.dzch.at[k]), r.first[...], r.twiddle[...], r.second[...])
        r.dzspec[rows, :] = u
        o = signal_of(
            times_conj(u, r.specv[rows, :]), r.twiddle[...], r.second_back[...], r.last[...]
        )
        store_pairs(dgch.at[k], o)
        back.start(back.back_refs, k, dgch, dgpos)

    loop(groups, chunk)

    def lag(k):
        rows = pl.ds(pl.multiple_of(k * EIGHT * outer, 8), EIGHT * outer)
        v = times_conj(r.dzspec[rows, :], r.gspecv[rows, :])
        taps = signal_of(v, r.twiddle[...], r.second_back[...], r.last_real[...])
        for c in range(EIGHT):
            dk[k, pl.ds(c, rows_all, stride=EIGHT), :] = taps[:, c * LANES : (c + 1) * LANES]

    loop(groups, lag)
    count = dk.shape[1] // 4

    def lags(j):
        return pl.ds(pl.multiple_of(j * count, 8), count)

    core, y = lax.rem(b, 2), b // 2
    shares = [
        send(
            dk.at[:, lags(2 * k + 1 - core)], r.dkin.at[k], (r.ks, r.kr), k,
            {"batch": core_mate(b)},
        )
        for k in range(2)
    ]
    total.second()
    for share in shares:
        share.wait_recv()
    for j, k in ((y_mate(b), 1 - y), (b, y)):
        dk[:, lags(j), :] = dk[:, lags(j), :] + r.dkin[k]
    shares.append(
        send(dk.at[:, lags(y_mate(b))], r.dkin.at[2], (r.ks, r.kr), 2, {"batch": y_mate(b)})
    )
    if not top:
        upper.pass_on()

        def lower(q):
            places = places_of(r.tokx, q)
            for j in range(3):
                put(r.pv.at[j], q, named_dot(r.ptab[j], places[2:]))
                if j:
                    value = named_dot(r.qtab[j], places)
                    put(r.qv.at[j], q, value + r.misc[:, TAP0 + 9 + j : TAP0 + 10 + j])

        loop(tiles, lower)

    for copy in late[2:]:
        copy.wait()
    shares[2].wait_recv()
    dk[:, lags(b), :] = dk[:, lags(b), :] + r.dkin[2]
    r.dnets[...] = jnp.zeros_like(r.dnets)
    r.dchan[...] = jnp.zeros_like(r.dchan)
    steps = length // 4 // block
    delta = decay(me, chans)
    fourth = r.chan_t[layer, :, 13 : 13 + FO]

    def network(i):
        start = b * (length // 4) + i * block
        wide = []
        for c in range(block // LANES):
            place = pl.ds(pl.multiple_of((start // LANES + c) * EIGHT, 8), EIGHT)
            wide.append(jnp.concatenate([dk[k, place, :] for k in range(groups)], axis=0))
        kept(i).wait()
        filter_back_block(
            length, start, r.feat[:, pl.ds(pl.multiple_of(start, block), block)],
            r.filt_t.at[layer], fourth, delta,
            r.keepv.at[lax.rem(i, 2)], jnp.concatenate(wide, axis=1), r.dnets, r.dchan,
        )

        @pl.when(i + 2 < steps)
        def _():
            kept(i + 2).start()

    loop(steps, network)
    head = jnp.concatenate([dk[k, 0:EIGHT, :] for k in range(groups)], axis=0)
    lane = lax.broadcasted_iota(jnp.int32, (chans, LANES), 1)
    head = jnp.where(lane == 0, head, 0.0) * (b == 0).astype(F32)
    r.dchan[...] += pltpu.roll(head, FO, 1)
    r.dnet[...] = (
        widened(r.dnets[0], D)
        + pltpu.roll(widened(r.dnets[1], D), EMB + 1, 1)
        + pltpu.roll(widened(r.dnets[2], D), EMB + 2 + FO, 1)
    )
    lane = lax.broadcasted_iota(jnp.int32, (EIGHT, LANES), 1)
    full = width + LANES
    inner = (me < n - 1).astype(F32)

    def halo_copy(k):
        return remote(
            r.heads.at[k], r.halo.at[k], (r.hs, r.hr), k, {"chan": lax.rem(me + n - 1, n)}
        )

    def heads(k):
        back.arrived(back.back_refs, k, dgch, dgpos)

        def body(owner):
            rows = pl.ds(pl.multiple_of(owner * chans + k * EIGHT, 8), EIGHT)
            pack = jnp.zeros((EIGHT, LANES), F32)
            for s in range(seqs):
                dg = dgpos[k, owner, s, 0:EIGHT, :]
                parts = (
                    r.dq0v[s, rows, 0:LANES],
                    dg * r.qv[2, s, rows, 0:LANES],
                    dg * r.qv[1, s, rows, 0:LANES],
                )
                for j in range(3):
                    slot = 2 * (j * seqs + s)
                    head = pltpu.roll(parts[j], slot, 1) if slot else parts[j]
                    pack = jnp.where((lane == slot) | (lane == slot + 1), head, pack)
            r.heads[k, pl.ds(pl.multiple_of(owner * EIGHT, 8), EIGHT), :] = pack

        loop(n, body)
        halo_copy(k).start()

    def short(k):
        halo_copy(k).wait_recv()
        eight = pl.ds(pl.multiple_of(k * EIGHT, 8), EIGHT)

        def body(owner):
            rows = pl.ds(pl.multiple_of(owner * chans + k * EIGHT, 8), EIGHT)
            side = r.misc[rows, :]
            edge = r.halo[k, pl.ds(pl.multiple_of(owner * EIGHT, 8), EIGHT), :] * inner
            sums = [jnp.zeros((EIGHT, 1), F32)] * 12
            for s in range(seqs):
                dg = jnp.concatenate(
                    [
                        dgpos[k, owner, s, q * EIGHT : (q + 1) * EIGHT, :]
                        for q in range(tiles)
                    ],
                    axis=1,
                )
                parts = (r.dq0v[s, rows, :], dg * r.qv[2, s, rows, :], dg * r.qv[1, s, rows, :])
                for j in range(3):
                    here = parts[j]
                    slot = 2 * (j * seqs + s)
                    after = pltpu.roll(edge, LANES - slot, 1) if slot else edge
                    long = jnp.concatenate([here, after], axis=1)
                    one = pltpu.roll(long, full - 1, 1)[:, :width]
                    two = pltpu.roll(long, full - 2, 1)[:, :width]
                    t = lane0 + 3 * j
                    r.dpv[j, s, owner, eight, :] = (
                        side[:, t : t + 1] * two
                        + side[:, t + 1 : t + 2] * one
                        + side[:, t + 2 : t + 3] * here
                    )
                    source = r.pv[j, s, rows, :]
                    sums[3 * j] = sums[3 * j] + row_sum(two * source)
                    sums[3 * j + 1] = sums[3 * j + 1] + row_sum(one * source)
                    sums[3 * j + 2] = sums[3 * j + 2] + row_sum(here * source)
                    sums[9 + j] = sums[9 + j] + row_sum(here)
            r.cols[rows, :] += put_columns([(lane0 + i, sums[i]) for i in range(12)])

        loop(n, body)
        dp_save(k).start()

    def step(k):
        @pl.when(k < groups)
        def _():
            heads(k)

        @pl.when(k > 0)
        def _():
            short(k - 1)

    loop(groups + 1, step)
    total.close()
    if not top:
        upper.arrived()
        upper.sent()
    for copy in saves:
        copy.wait()
    loop(groups, lambda k: dp_save(k).wait())
    for share in shares:
        share.wait_send()
    loop(tiles, out.sent)

    def finish(k):
        halo_copy(k).wait_send()
        back.sent(back.back_refs, k, dgch, dgpos)

    loop(groups, finish)


def back_call(z, keep, spec, gspec, x1, w, misc, chan_t, filt_t, extra, tables, n, layer, cid):
    top = layer == LAYERS - 1
    seqs, _, width = x1.shape
    chans = chan_t.shape[1]
    groups, tiles = chans // EIGHT, width // LANES
    span = tiles * EIGHT
    length = width * n
    pos = x1.shape
    by_position = (groups, n, seqs, span, LANES)
    by_channel = (groups, seqs, n * span, LANES)
    rows = round_up(9 * chans, 32) if top else 12 * chans
    held = (n, rows, D)
    half = n // 2
    if top:
        mine, places = [VMEM(pos, F32), VMEM(pos, F32)], [HBM] * 3
    else:
        mine = [
            VMEM(pos, F32), VMEM(pos, F32), VMEM(extra[6].shape, F32),
            VMEM((3, D, LANES), BF16), VMEM((3, D, LANES), BF16),
            *column_scratch(n, extra[2].shape[1]),
        ]
        places = [WHOLE] * 3 + [HBM] * 4
    dp, *rest = pl.pallas_call(
        partial(top_kernel if top else mid_kernel, n, chans, length),
        in_specs=[HBM] * 6 + [WHOLE] * 4 + places + [WHOLE] * 7,
        out_specs=[HBM] * 2 + [WHOLE] * 4 + [HBM if top else WHOLE],
        out_shape=[
            sds(3, seqs, n, chans, width), sds(*pos), sds(D, D), sds(FO, D), sds(chans, LANES),
            sds(half, rows // 4, D),
        ]
        + [sds(*pos) if top else sds(4 * extra[2].shape[1], D)],
        scratch_shapes=[
            VMEM((3, seqs, n, chans, width), F32),
            VMEM(pos, F32),
            VMEM((3,) + pos, F32),
            VMEM((3,) + pos, F32),
            VMEM(by_position, F32),
            VMEM((2, 6, FO, 512), F32),
            VMEM(spec.shape, F32),
            VMEM(spec.shape, F32),
            VMEM(pos, F32),
            VMEM(held, F32),
            VMEM(held, F32),
            VMEM(pos, F32),
            VMEM(by_position, F32),
            VMEM(by_channel, F32),
            VMEM(spec.shape, F32),
            VMEM(by_channel, F32),
            VMEM(by_position, F32),
            VMEM((groups, n * span, LANES), F32),
            VMEM((3, groups, n * span // 4, LANES), F32),
            VMEM((3, FO, LANES), F32),
            VMEM((groups, n * EIGHT, LANES), F32),
            VMEM((groups, n * EIGHT, LANES), F32),
            *pair_sems(tiles, n),
            pltpu.SemaphoreType.DMA((tiles,)),
            *pair_sems(groups, n),
            pltpu.SemaphoreType.DMA((groups,)),
            *pair_sems(groups),
            *pair_sems(3),
            pltpu.SemaphoreType.DMA((12,)),
            pltpu.SemaphoreType.DMA((2,)),
            pltpu.SemaphoreType.DMA((groups,)),
            pltpu.SemaphoreType.DMA((2,)),
            pltpu.SemaphoreType.DMA((5, tiles)),
            *group_scratch(n, rows),
        ]
        + mine,
        compiler_params=comm_params(cid),
        name="top_back" if top else "mid_back",
    )(
        z, keep, spec, gspec, x1, w, misc, chan_t, filt_t, position_table(length),
        *extra, *tables,
    )
    return (dp.reshape(3, *pos), *rest)


def total_kernel(
    n,
    part2, cols0, cols1, dnet0, dnet1, dchan0, dchan1, dp, dh, ids, late, misc,
    rows2, rows3, rows4, filt, chan, dx,
    fourth, last4, dchan, rchan, inward, sums, named, own, cs, cr, fs, fr, isem, *rest,
):
    me, b = lax.axis_index("chan"), lax.axis_index("batch")
    chans = D // n
    filter_rows = filt.shape[1]
    seqs, _, width = dh.shape
    fetch = pltpu.make_async_copy(late.at[:, 9 * chans : 12 * chans], inward, isem)
    fetch.start()
    for l, value in enumerate((dchan0, dchan1)):
        dchan[l] = value[...]
    greet(n, [lax.rem(b + d, 4) for d in range(1, 4)])

    two = ColumnSum(n, part2, rest[0], rows2, *rest[1:5])
    two.start()
    slot = lax.broadcasted_iota(jnp.int32, (LANES, width), 0)

    def by_name(s, total):
        here = ids[pl.ds(s, 1), :]
        for j in range(4):
            places = (slot == here + VOCAB * j).astype(F32)
            total = total + dot_nt(dh[s] if j == 3 else dp[j, s], places)
        return total

    by_names = lax.fori_loop(0, seqs, by_name, jnp.zeros((D, LANES), F32))
    columns = cols0[:, 0:LANES] + cols1[:, 0:LANES]
    for i in range(n):
        here = slice(i * chans, (i + 1) * chans)
        fourth[i, 0:chans, 0:LANES] = columns[here]
        fourth[i, 0:chans, LANES:] = by_names[here]
        row = i * filter_rows
        if row < LAYERS * FO:
            dnet = (dnet0, dnet1)[row // FO]
            fourth[i, chans : chans + filter_rows, :] = dnet[
                row % FO : row % FO + filter_rows, :
            ]
        else:
            fourth[i, chans : chans + filter_rows, :] = jnp.zeros((filter_rows, D), F32)
        spare = fourth.shape[1] - chans - filter_rows
        if spare:
            fourth[i, chans + filter_rows :, :] = jnp.zeros((spare, D), F32)
    four = GroupSum(n, fourth, last4, *rest[10:])
    end = ColumnSum(n, last4, rest[5], rows4, *rest[6:10])
    four.cores()
    small = [
        send(dchan, rchan.at[d - 1], (cs, cr), d - 1, {"batch": lax.rem(b + d, 4)})
        for d in range(1, 4)
    ]
    fetch.wait()
    lay = Layer(inward, None, misc, 0)

    def tile(q):
        lanes = pl.ds(pl.multiple_of(q * LANES, LANES), LANES)
        here = jnp.concatenate([ids[s : s + 1, lanes] for s in range(seqs)], axis=1)
        names = lax.broadcasted_iota(jnp.int32, (VOCAB, here.shape[1]), 0)
        value = embedded(lay.side, (names == here).astype(F32))
        grad, _ = front_backward(
            lay, value, [take(dp.at[j], q) for j in range(3)], take(dh, q)
        )
        put(dx, q, grad)

    tiles = width // LANES
    four.first()
    loop(tiles // 2, tile)
    four.second()
    loop(tiles - tiles // 2, lambda q: tile(q + tiles // 2))
    four.close()
    end.start()
    two.share()
    end.share()
    end.pass_on()
    end.arrived()
    mine = pl.ds(pl.multiple_of(me * chans, 8), chans)
    filt[me] = rows4[chans : chans + filter_rows, :]
    own[...] = rows4[0:chans, LANES:]
    named[mine, :] = own[...]
    shares = []
    for d in range(1, n):
        peer = {"chan": lax.rem(me + d, n)}
        shares.append(send(own, named.at[mine, :], (fs, fr), d - 1, peer))
        shares.append(send(filt.at[me], filt.at[me], (fs, fr), n - 2 + d, peer))
    two.pass_on()
    for copy in small + shares:
        copy.wait_recv()
    for l in range(LAYERS):
        chan[l] = dchan[l] + rchan[0, l] + rchan[1, l] + rchan[2, l]
    lane = lax.broadcasted_iota(jnp.int32, (D, LANES), 1)

    def name_lanes(value, j):
        value = pltpu.roll(value, LANES - j * VOCAB, 1) if j else value
        return jnp.where(lane[: value.shape[0]] < VOCAB, value, 0.0)

    table = jnp.where(lane < VOCAB, pltpu.roll(lay.side, D - EMB0, 1)[:, :LANES], 0.0)
    xh, scale = normalize(table)
    xh = jnp.where(lane < VOCAB, xh, 0.0)
    normed = xh * lay.vec(0) + lay.vec(1)
    everything = named[...]
    dps = [name_lanes(everything, j) for j in range(3)]
    stacked = jnp.stack([v.reshape(n, chans, LANES) for v in dps], axis=1)
    dn = dot_tn(lay.inward(), stacked.reshape(3 * D, LANES))
    grad = name_lanes(everything, 3) + normalize_back(dn * lay.vec(0), xh, scale)
    grad = jnp.where(lane < VOCAB, grad, 0.0)
    base = VEC0
    pairs = [(base + 4 + j, row_sum(dps[j])) for j in range(3)]
    pairs += [(base, row_sum(dn * xh)), (base + 1, row_sum(dn))]
    sums[...] = put_columns(pairs, LANES) + pltpu.roll(grad, EMB0, 1)
    end.sent()
    rows4[0:chans, 0:LANES] += sums[mine, :]
    for j in range(3):
        rows3[j * chans : (j + 1) * chans, :] = dot_nt(name_lanes(own[...], j), normed)
    two.arrived()
    two.sent()
    for copy in small + shares:
        copy.wait_send()


def update_kernel(n, scale, *refs):
    sem = refs[-1]
    passed = [
        pltpu.make_async_copy(refs[k], refs[k - 3], sem.at[k]) for k in range(2)
    ]
    for copy in passed:
        copy.start()
    refs = refs[2:]
    rows1, rows2, rows3, rows4, filt, chan = refs[:6]
    weights, moments, averages = refs[6:15], refs[15:24], refs[24:33]
    outs = refs[33:69]
    chans = chan.shape[1]
    filter_rows = filt.shape[1]

    def step(which, index, gradient):
        factor = STEP_RATES[which] * scale
        velocity = MOMENTUM * moments[which][index] + gradient
        updated = weights[which][index] - factor * (gradient + MOMENTUM * velocity)
        running = AVERAGING * averages[which][index] + (1.0 - AVERAGING) * updated
        base = 4 * which
        outs[base][index] = velocity
        outs[base + 1][index] = running
        outs[base + 2][index] = updated
        outs[base + 3][index] = updated.astype(BF16)

    columns = rows4[0:chans, 0:LANES]
    flat = columns
    if chans < LANES:
        flat = jnp.concatenate([columns, jnp.zeros((LANES - chans, LANES), F32)], axis=0)
    flat = flat.T
    step(0, Ellipsis, flat[EMB0 : EMB0 + VOCAB, :chans])
    lane = lax.broadcasted_iota(jnp.int32, (chans, LANES), 1)
    off = []
    for l in range(LAYERS):
        front, base = (rows3, 0) if l == 0 else (rows2, 0)
        for j in range(3):
            step(1, (l, j), front[base + j * chans : base + (j + 1) * chans, :])
        for k in range(9):
            row = VEC0 + 9 * l + k
            step(2, (k, slice(l, l + 1)), flat[row : row + 1, :chans])
        rear, base = (rows2, 3 * chans) if l == 0 else (rows1, 0)
        step(3, l, rear[base : base + chans, :])
        step(4, l, rear[base + chans : base + 5 * chans, :])
        pieces = [rear[base + (5 + c) * chans : base + (6 + c) * chans, :] for c in range(4)]
        step(6, l, fold(pieces, n, chans, back=True))
        row = jnp.zeros((1, LANES), F32)
        for c in range(4):
            piece = flat[OFF0 + 4 * l + c : OFF0 + 4 * l + c + 1, :]
            row = row + (pltpu.roll(piece, c * chans, 1) if c else piece)
        off.append(row[:, : 4 * chans])
        taps = pltpu.roll(columns, LANES - TAP0 - 12 * l, 1)
        own = chan[l]
        skip = pltpu.roll(own, LANES - FO + 12, 1)
        gradient = jnp.where(lane < 12, taps, jnp.where(lane == 12, skip, pltpu.roll(own, 13, 1)))
        step(7, l, gradient[:, : 13 + FO])
    step(5, Ellipsis, jnp.concatenate(off, axis=0))
    whole = filt[...].reshape(n * filter_rows, D)
    for l in range(LAYERS):
        step(8, l, whole[l * FO : (l + 1) * FO, :136])
    for copy in passed:
        copy.wait()


def finish(
    rows1, part2, cols, dnets, dchans, dp, dh, ids, late, misc, weights, moments, averages,
    activations, n, scale, cid,
):
    chans = D // n
    filter_rows = round_up(LAYERS * FO, n * EIGHT) // n
    fourth = round_up(chans + filter_rows, 32)
    q2, q4 = part2.shape[1], fourth // 4
    half = n // 2
    *sums, dx = pl.pallas_call(
        partial(total_kernel, n),
        in_specs=[WHOLE] * 10 + [HBM, WHOLE],
        out_specs=[WHOLE] * 6,
        out_shape=[
            sds(4 * q2, D), sds(3 * chans, D), sds(fourth, D),
            sds(n, filter_rows, D), sds(LAYERS, chans, LANES), sds(*dh.shape),
        ],
        scratch_shapes=[
            VMEM((n, fourth, D), F32),
            VMEM((half, q4, D), F32),
            VMEM((LAYERS, chans, LANES), F32),
            VMEM((3, LAYERS, chans, LANES), F32),
            VMEM((n, 3 * chans, D), F32),
            VMEM((D, LANES), F32),
            VMEM((D, LANES), F32),
            VMEM((chans, LANES), F32),
            *pair_sems(3),
            *pair_sems(2 * n),
            pltpu.SemaphoreType.DMA,
            *column_scratch(n, q2),
            *column_scratch(n, q4),
            *group_scratch(n, fourth),
        ],
        compiler_params=comm_params(cid),
        name="total",
    )(part2, *cols, *dnets, *dchans, dp, dh, ids, late, misc)
    shapes = []
    for weight in weights:
        shapes += [sds(*weight.shape)] * 3 + [jax.ShapeDtypeStruct(weight.shape, BF16)]
    shapes += [sds(*dx.shape)] * 2
    return pl.pallas_call(
        partial(update_kernel, n, scale),
        in_specs=[WHOLE] * 35,
        out_specs=[WHOLE] * 36 + [HBM, HBM],
        out_shape=shapes,
        scratch_shapes=[pltpu.SemaphoreType.DMA((2,))],
        compiler_params=pltpu.CompilerParams(vmem_limit_bytes=VMEM_LIMIT),
        name="update",
    )(activations, dx, rows1, *sums, *weights, *moments, *averages)


def onehot_rows(tokens):
    row = lax.broadcasted_iota(jnp.int32, (D, tokens.shape[1]), 0)
    return (row == tokens + EMB0).astype(F32)


class Layer:
    def __init__(self, front, rear, misc, index, base=0):
        some = rear if front is None else front
        self.n = some.shape[0]
        self.c = D // self.n
        self.front, self.rear, self.base = front, rear, base
        self.side = misc[...]
        self.index = index

    def rows(self, ref, start, count):
        return ref[:, start * self.c : (start + count) * self.c, :].reshape(
            self.n * count * self.c, D
        )

    def column(self, lane):
        return self.side[:, lane : lane + 1]

    def vec(self, k):
        return self.column(VEC0 + 9 * self.index + k)

    def off(self, k):
        return self.column(OFF0 + 4 * self.index + k)

    def inward(self):
        return self.rows(self.front, 0, 3)

    def outward(self):
        return self.rows(self.rear, self.base, 1)

    def expand(self, k):
        return self.rows(self.rear, self.base + 1 + k, 1)

    def contract(self, k):
        return self.rows(self.rear, self.base + 5 + k, 1)


def front_forward(lay, x):
    xh, _ = normalize(x)
    normed = xh * lay.vec(0) + lay.vec(1)
    p = dot(lay.inward(), normed).reshape(lay.n, 3, lay.c, x.shape[1])
    return [p[:, j].reshape(D, x.shape[1]) + lay.vec(4 + j) for j in range(3)]


def front_backward(lay, x, dp, dh, dw=None):
    xh, scale = normalize(x)
    normed = xh * lay.vec(0) + lay.vec(1)
    width = x.shape[1]
    stacked = jnp.stack([d.reshape(lay.n, lay.c, width) for d in dp], axis=1)
    stacked = stacked.reshape(3 * D, width)
    dn = dot_tn(lay.inward(), stacked)
    if dw is not None:
        dw[:, 0 : 3 * lay.c, :] += dot_nt(stacked, normed, DW).reshape(lay.n, 3 * lay.c, D)
    base = VEC0 + 9 * lay.index
    columns = [(base + 4 + j, row_sum(dp[j])) for j in range(3)]
    columns += [(base, row_sum(dn * xh)), (base + 1, row_sum(dn))]
    return dh + normalize_back(dn * lay.vec(0), xh, scale), columns


def rear_mix(lay, x, y):
    return x + dot(lay.outward(), y) + lay.vec(7)


def rear_hidden(lay, h):
    xh, scale = normalize(h)
    m = xh * lay.vec(2) + lay.vec(3)
    a = [dot(lay.expand(k), m) + lay.off(k) for k in range(4)]
    return xh, scale, m, a


def rear_out(lay, h, u):
    out = h + lay.vec(8)
    for k in range(4):
        out = out + dot(lay.contract(k), u[k])
    return out


def rear_backward(lay, h, a, y, dout, dw, base=0):
    n, c = lay.n, lay.c

    def add(row, value):
        dw[:, (base + row) * c : (base + row + 1) * c, :] += value.reshape(n, c, D)

    xh, scale = normalize(h)
    m = xh * lay.vec(2) + lay.vec(3)
    vec = VEC0 + 9 * lay.index
    columns = [(vec + 8, row_sum(dout))]
    dm = None
    for k in range(4):
        ak = a[k]
        g, t = gelu_parts(ak)
        u = ak * g
        add(5 + k, dot_nt(dout, u, DW))
        slope = g + 0.5 * ak * (1.0 - t * t) * (GELU_SCALE * (1.0 + 3.0 * GELU_CUBE * ak * ak))
        dpre = dot_tn(lay.contract(k), dout) * slope
        add(1 + k, dot_nt(dpre, m, DW))
        columns.append((OFF0 + 4 * lay.index + k, row_sum(dpre)))
        term = dot_tn(lay.expand(k), dpre)
        dm = term if dm is None else dm + term
    dh = dout + normalize_back(dm * lay.vec(2), xh, scale)
    columns += [(vec + 2, row_sum(dm * xh)), (vec + 3, row_sum(dm)), (vec + 7, row_sum(dh))]
    add(0, dot_nt(dh, y, DW))
    return dh, dot_tn(lay.outward(), dh), columns


def turned(arrays):
    out = list(arrays)
    out[2] = arrays[2].transpose(1, 0, 2)
    out[7] = arrays[7].transpose(0, 2, 1)
    out[8] = arrays[8].transpose(0, 2, 1)
    return out


def per_device(*arguments):
    token_ids, cotangent = arguments[0], arguments[28]
    weights = turned(arguments[1:10])
    moments = turned(arguments[10:19])
    averages = turned(arguments[19:28])
    n, m = lax.axis_size("chan"), lax.axis_size("batch")
    seqs, width = token_ids.shape
    length = width * n
    chan_t, filt_t = weights[7], weights[8]
    chans = chan_t.shape[1]
    groups = chans // EIGHT
    tables = fourier_tables(length)
    wall, late, spec0, spec1, gspec0, keep0, keep1, z0, misc, _, tokx, shared = prepare(
        (token_ids, *weights), tables, n, seqs, length, 1
    )
    wlate, h0, a0, x1, p1, q1, gspec1, z1 = middle(
        z0, wall, late, spec1, misc, shared, tokx, tables, n, chans, 2
    )
    dp1, dh1, cols1, dnet1, dchan1, part1, activations = back_call(
        z1, keep1, spec1, gspec1, x1, wlate, misc, chan_t, filt_t, (q1, p1, cotangent),
        tables, n, 1, 3,
    )
    dp0, dh0, cols0, dnet0, dchan0, part2, rows1 = back_call(
        z0, keep0, spec0, gspec0, x1, wall, misc, chan_t, filt_t,
        (shared, tokx, part1, dp1, dh1, h0, a0), tables, n, 0, 4,
    )
    *updates, activations, input_gradient = finish(
        rows1, part2, (cols0, cols1), (dnet0, dnet1), (dchan0, dchan1), dp0, dh0, token_ids,
        wlate, misc, weights, moments, averages, activations, n,
        1.0 / math.sqrt(seqs * m * length), 5,
    )
    kinds = [turned(updates[k::4]) for k in range(4)]
    return (activations, input_gradient) + tuple(
        kinds[k][w] for w in range(9) for k in range(4)
    )


def solution(mesh):
    in_weights = (
        P(None, "chan"),
        P(None, None, "chan", None),
        P(None, None, "chan"),
        P(None, "chan", None),
        P(None, "chan", None),
        P(None, "chan"),
        P(None, "chan", None),
        P(None, None, "chan"),
        P(),
    )
    tokens = P("batch", None, "chan")
    in_specs = (P("batch", "chan"),) + in_weights * 3 + (tokens,)
    out_specs = (tokens, tokens) + tuple(spec for spec in in_weights for _ in range(4))
    return jax.shard_map(
        per_device, mesh=mesh, in_specs=in_specs, out_specs=out_specs, check_vma=False
    )
```
